128 devices in a mesh: dp: 8 (over y_hi, x), ctx: 2 (over core), tensor: 8 (over z, y_lo).
Axes of the slice: x: 4, y: 4 (y_hi: 2, y_lo: 2; y = y_hi * 2 + y_lo), z: 4, core: 2. Of those that a mesh axis runs over, the one named last changes fastest.
Arguments:
- hidden_in: bfloat16 [16384, 1024], P(('dp', 'ctx', 'tensor')), may hold values from -6 to 6
- segment: int32 [16384], P('dp'), may hold values from 0 to 7, as said below
- norm1_gain: float32 [1024], replicated, may hold values from 0.25 to 1.75
- w_query: bfloat16 [1024, 1024], P(None, 'tensor'), may hold values from -0.1875 to 0.1875
- w_key: bfloat16 [1024, 512], P(None, 'tensor'), may hold values from -0.1875 to 0.1875
- w_value: bfloat16 [1024, 512], P(None, 'tensor'), may hold values from -0.1875 to 0.1875
- q_gain: float32 [1024], P('tensor'), may hold values from 0.25 to 1.75
- k_gain: float32 [512], P('tensor'), may hold values from 0.25 to 1.75
- w_out: bfloat16 [1024, 1024], P('tensor'), may hold values from -0.75 to 0.75
- norm2_gain: float32 [1024], replicated, may hold values from 0.25 to 1.75
- router: bfloat16 [1024, 32], replicated, may hold values from -0.09375 to 0.09375
- w_gate: bfloat16 [32, 1024, 512], P(('dp', 'ctx')), may hold values from -0.1875 to 0.1875
- w_up: bfloat16 [32, 1024, 512], P(('dp', 'ctx')), may hold values from -0.1875 to 0.1875
- w_down: bfloat16 [32, 512, 1024], P(('dp', 'ctx')), may hold values from -1.5 to 1.5
- routes: int32 [16384, 8], P(('dp', 'ctx', 'tensor')), may hold values from 0 to 31, all different within a row; in each aligned block of 128 rows (0 to 127, 128 to 255, ...) at most 64 rows name the same one
- cotangent: bfloat16 [16384, 1024], P(('dp', 'ctx', 'tensor')), may hold values from -6 to 6
Outputs:
- output: bfloat16 [16384, 1024], P(('dp', 'ctx', 'tensor'))
- grad_x: bfloat16 [16384, 1024], P(('dp', 'ctx', 'tensor'))
- grad_norm1_gain: float32 [1024], replicated
- grad_w_query: float32 [1024, 1024], P(None, 'tensor')
- grad_w_key: float32 [1024, 512], P(None, 'tensor')
- grad_w_value: float32 [1024, 512], P(None, 'tensor')
- grad_q_gain: float32 [1024], P('tensor')
- grad_k_gain: float32 [512], P('tensor')
- grad_w_out: float32 [1024, 1024], P('tensor')
- grad_norm2_gain: float32 [1024], replicated
- grad_router: float32 [1024, 32], replicated
- grad_w_gate: float32 [32, 1024, 512], P(('dp', 'ctx'))
- grad_w_up: float32 [32, 1024, 512], P(('dp', 'ctx'))
- grad_w_down: float32 [32, 512, 1024], P(('dp', 'ctx'))
The draws below stay inside these ranges and needn't reach their ends.
Inputs may be any that keep to these rules, and one draw needn't show every extreme that they name: `segment`: document number of each position within its sequence of 2048 positions: 0 at the first position, 7 at the last, never falling along the sequence. `routes`: each row names 8 different experts. Among the 128 rows of one device no expert is named more than 64 times, a bound that some block reaches.
All inputs are finite; a program needn't handle non-finite values.
Results may differ from the reference program's by a relative error of at most 0.033.
Values may be sent and summed in bfloat16 or wider, within the bound.
A program may use at most 128 MiB of HBM per device.

```python
import math
import jax
import jax.numpy as jnp
import numpy as np
from jax import lax

D = 1024
HEADS = 16
KV_HEADS = 8
HEAD_DIM = 64
FF = 512
TOP = 8
TOK_DEV = 128
DOC_CUTS = 7
EXPERTS = 32
CAP = 64
LENGTH = 2048
TOKENS = 16384
QW = 1024
KW = 512
QBLOCK = 512
N_DP = 8


def draw_segment(key, part):
    key = jax.random.fold_in(key, 7)
    seq_rows = TOKENS // LENGTH
    cut_points = jax.random.randint(key, (seq_rows, DOC_CUTS), 1, 3 * LENGTH // 4)
    cut_points = jnp.where(cut_points < 3 * LENGTH // 8, cut_points, cut_points + LENGTH // 4)
    positions = jnp.arange(LENGTH, dtype=jnp.int32)
    passed_cuts = (cut_points[:, None, :] <= positions[None, :, None]).astype(jnp.int32)
    return jnp.sum(passed_cuts, -1).reshape(-1).astype(jnp.int32)


def levels(stream_key, shape, shards, smallest, top_value):
    level, own = 1.0, jax.random.fold_in(stream_key, 6)
    for axis_at, blocks in shards:
        heights = jnp.exp(jax.random.uniform(jax.random.fold_in(own, axis_at), (blocks,), jnp.float32, smallest / len(shards), top_value / len(shards)))
        level = level * jnp.repeat(heights, shape[axis_at] // blocks).reshape([-1 if axis == axis_at else 1 for axis in range(len(shape))])
    return level


def deal_out(rng, own, number, rows, count, top, limit, skew):
    order = jax.random.permutation(rng, count)
    packed, usual = portions_of(count, rows * top, limit, skew, True), portions_of(count, rows * top, limit, skew, False)
    places = jnp.arange(count)

    def named(lengths, offset_by):
        used = int((lengths > 0).sum())
        fixed = max(1, used // 4)
        shifted = fixed + (places - fixed + offset_by * (used - fixed)) % max(1, count - fixed)
        return jnp.zeros((count,), jnp.int32).at[order[jnp.where(places < fixed, places, shifted)]].set(jnp.asarray(lengths, jnp.int32))

    lengths = jnp.where(number % 4 == 0, named(packed, number // 4), named(usual, number - number // 4 - 1))
    mixed = jax.random.permutation(jax.random.fold_in(own, 3), count)
    giver, taker = mixed[0:count // 2 * 2:2], mixed[1:count // 2 * 2:2]
    margin = jnp.minimum(lengths[giver] - 1, limit - lengths[taker]) // 2
    margin = jnp.where((giver == order[0]) | (taker == order[0]) | (lengths[taker] == 0), 0, jnp.maximum(margin, 0))
    shifted = jax.random.randint(jax.random.fold_in(own, 4), (count // 2,), 0, 1 << 20) % (margin + 1)
    lengths = lengths.at[giver].add(-shifted).at[taker].add(shifted)
    members = jnp.searchsorted(jnp.cumsum(lengths), jnp.arange(rows * top), side="right").astype(jnp.int32)
    table = members.reshape(top, rows).T
    table = table[jax.random.permutation(jax.random.fold_in(own, 1), rows)]
    offset_by = jax.random.randint(jax.random.fold_in(own, 2), (rows, 1), 0, top)
    return jnp.take_along_axis(table, (jnp.arange(top)[None, :] + offset_by) % top, axis=1)


def portions_of(amount, total, bound, slope, full):
    portions = [(1 << 20) // math.isqrt(standing ** slope) + 1 for standing in range(1, amount + 1)]
    largest = bound if full else min(bound, max(-(-total // amount), total * portions[0] // sum(portions)))
    least = 1 if total - largest >= amount - 1 else 0
    counts, surplus = [largest] + [least] * (amount - 1), total - largest - least * (amount - 1)
    while surplus > 0:
        free = [i for i in range(1, amount) if counts[i] < largest] or [i for i in range(1, amount) if counts[i] < bound]
        mass, remaining = sum([portions[i] for i in free]), surplus
        for i in free:
            more = min(bound - counts[i], max(1, remaining * portions[i] // mass), surplus)
            counts[i] = counts[i] + more
            surplus = surplus - more
    return np.array(counts)


def normal_values(key, shape, scale, reach, pieces=(), held_as=jnp.bfloat16):
    gain = levels(key, shape, pieces, -0.22, 0.18) if pieces else 1.0
    values = jax.random.normal(key, shape, jnp.float32) * scale * gain
    return jnp.minimum(jnp.maximum(values, -reach), reach).astype(held_as)


def setup_inputs(seed: int = 0) -> dict:
    splits = jax.random.split(jax.random.key(seed), 17)
    hidden_in = normal_values(splits[0], (TOKENS, D), 1.0, 6.0, ((0, 128),))
    segment = draw_segment(jax.random.fold_in(splits[16], 71), 0)
    norm1_gain = jnp.clip(1.0 + 0.15 * jax.random.normal(splits[2], (D,), jnp.float32), 0.25, 1.75)
    w_query = normal_values(splits[3], (D, QW), D ** -0.5, 0.1875, ((1, 8),))
    w_key = normal_values(splits[4], (D, KW), D ** -0.5, 0.1875, ((1, 8),))
    w_value = normal_values(splits[5], (D, KW), D ** -0.5, 0.1875, ((1, 8),))
    q_gain = jnp.clip(1.0 + 0.15 * jax.random.normal(splits[6], (QW,), jnp.float32), 0.25, 1.75)
    k_gain = jnp.clip(1.0 + 0.15 * jax.random.normal(splits[7], (KW,), jnp.float32), 0.25, 1.75)
    w_out = normal_values(splits[8], (QW, D), (QW // 16) ** -0.5, 0.75, ((0, 8),))
    norm2_gain = jnp.clip(1.0 + 0.15 * jax.random.normal(splits[9], (D,), jnp.float32), 0.25, 1.75)
    router = normal_values(splits[10], (D, EXPERTS), (4 * D) ** -0.5, 0.09375)
    w_gate = normal_values(splits[11], (EXPERTS, D, FF), D ** -0.5, 0.1875, ((0, 16),))
    w_up = normal_values(splits[12], (EXPERTS, D, FF), D ** -0.5, 0.1875, ((0, 16),))
    w_down = normal_values(splits[13], (EXPERTS, FF, D), (FF // 32) ** -0.5, 1.5, ((0, 16),))
    routes_keys = jax.random.split(jax.random.fold_in(splits[14], 1), TOKENS // TOK_DEV)
    routes_turns = jax.random.permutation(jax.random.fold_in(splits[14], 3), TOKENS // TOK_DEV)
    routes = jax.vmap(lambda own, number: deal_out(jax.random.fold_in(splits[14], 2), own, number, TOK_DEV, EXPERTS, TOP, CAP, 1))(routes_keys, routes_turns).reshape((TOKENS, TOP))
    cotangent = normal_values(splits[15], (TOKENS, D), 1.0, 6.0, ((0, 128),))
    return {"hidden_in": hidden_in, "segment": segment, "norm1_gain": norm1_gain, "w_query": w_query, "w_key": w_key, "w_value": w_value, "q_gain": q_gain, "k_gain": k_gain, "w_out": w_out, "norm2_gain": norm2_gain, "router": router, "w_gate": w_gate, "w_up": w_up, "w_down": w_down, "routes": routes, "cotangent": cotangent}


EPS = 1e-06
THETA = 10000.0
MASKED = -1e+30
HIGH = lax.Precision.HIGHEST

@jax.custom_vjp
def low(v):
    return lax.optimization_barrier(v.astype(jnp.bfloat16)).astype(jnp.float32)

@jax.custom_vjp
def low_back(v):
    return v

def low_keep(v):
    return (low(v), None)

def low_pass(kept, grad):
    return (grad,)

def back_keep(v):
    return (v, None)

def back_low(kept, grad):
    return (low(grad),)
low.defvjp(low_keep, low_pass)
low_back.defvjp(back_keep, back_low)

def matmul(left, right):
    return jnp.dot(left, right, precision=HIGH)

def normalize(values):
    return values * lax.rsqrt(lax.optimization_barrier(jnp.mean(values * values, -1, keepdims=True)) + EPS)

def softmax_rows(scores):
    largest = lax.optimization_barrier(jnp.max(scores, -1, keepdims=True))
    exponent = jnp.exp(scores - largest)
    return exponent / lax.optimization_barrier(jnp.sum(exponent, -1, keepdims=True))

def rope_tables(positions, half_dim):
    inverse = THETA ** (-(jnp.arange(half_dim, dtype=jnp.float32) * 2.0 / (2 * half_dim)))
    angles = positions.astype(jnp.float32)[:, None] * inverse[None, :]
    return (jnp.cos(angles), jnp.sin(angles))

def rotate(values, cos_table, sin_table, flip_sign):
    half_dim = values.shape[-1] // 2
    first_half = values[..., :half_dim]
    second_half = values[..., half_dim:]
    cos_part = cos_table[:, None, :]
    sin_part = sin_table[:, None, :] * flip_sign
    return jnp.concatenate([first_half * cos_part - second_half * sin_part, second_half * cos_part + first_half * sin_part], -1)

def attend(queries, keys, values, segment_row):
    group_size = HEADS // KV_HEADS
    positions = jnp.arange(LENGTH, dtype=jnp.int32)

    @jax.checkpoint
    def attend_block(block_args):
        q_block, seg_block, pos_block = block_args
        grouped = q_block.reshape(QBLOCK, KV_HEADS, group_size, HEAD_DIM)
        raw_scores = low_back(jnp.einsum('qkgd,tkd->kgqt', grouped, keys, precision=HIGH) * HEAD_DIM ** (-0.5))
        allowed = (seg_block[:, None] == segment_row[None, :]) & (positions[None, :] <= pos_block[:, None])
        probabilities = softmax_rows(jnp.where(allowed, raw_scores, MASKED))
        head_vals = jnp.einsum('kgqt,tkd->qkgd', low(probabilities), values, precision=HIGH)
        return head_vals.reshape(QBLOCK, HEADS * HEAD_DIM)
    n_blocks = LENGTH // QBLOCK
    results = lax.map(attend_block, (queries.reshape(n_blocks, QBLOCK, HEADS, HEAD_DIM), segment_row.reshape(n_blocks, QBLOCK), positions.reshape(n_blocks, QBLOCK)))
    return results.reshape(LENGTH, HEADS * HEAD_DIM)

def reference(hidden_in, segment, norm1_gain, w_query, w_key, w_value, q_gain, k_gain, w_out, norm2_gain, router, w_gate, w_up, w_down, routes, cotangent):
    assignments = TOKENS * TOP
    devices = TOKENS // TOK_DEV
    flat_ids = routes.reshape(-1).astype(jnp.int32)
    expert_hot = (flat_ids[:, None] == jnp.arange(EXPERTS, dtype=jnp.int32)[None, :]).astype(jnp.int32)
    per_device = expert_hot.reshape(devices, TOK_DEV * TOP, EXPERTS)
    earlier = jnp.cumsum(per_device, 1) - per_device
    slot_index = lax.optimization_barrier(jnp.sum(earlier * per_device, -1)).reshape(-1).astype(jnp.int32)
    column = jnp.arange(assignments, dtype=jnp.int32) // (TOK_DEV * TOP) * CAP + slot_index
    row_table = jnp.full((EXPERTS, devices * CAP), assignments, jnp.int32).at[flat_ids, column].set(jnp.arange(assignments, dtype=jnp.int32))
    row_valid = row_table < assignments
    row_clipped = jnp.minimum(row_table, assignments - 1).astype(jnp.int32)
    row_tokens = (row_clipped // TOP).astype(jnp.int32)

    def forward(x_in, gain_one, wq_in, wk_in, wv_in, gq_in, gk_in, wo_in, gain_two, router_in, gate_in, up_in, down_in):
        normed_one = low(normalize(x_in) * gain_one)
        q_raw = low_back(matmul(normed_one, wq_in))
        k_raw = low_back(matmul(normed_one, wk_in))
        value_rows = low(low_back(matmul(normed_one, wv_in)))
        q_norm = normalize(q_raw) * gq_in
        k_norm = normalize(k_raw) * gk_in
        cos_table, sin_table = rope_tables(jnp.arange(LENGTH, dtype=jnp.int32), HEAD_DIM // 2)
        queries = low(rotate(q_norm.reshape(N_DP, LENGTH, HEADS, HEAD_DIM), cos_table, sin_table, 1.0))
        keys = low(rotate(k_norm.reshape(N_DP, LENGTH, KV_HEADS, HEAD_DIM), cos_table, sin_table, 1.0))
        values = value_rows.reshape(N_DP, LENGTH, KV_HEADS, HEAD_DIM)

        def attend_row(row_args):
            return attend(row_args[0], row_args[1], row_args[2], row_args[3])
        head_vals = lax.map(attend_row, (queries, keys, values, segment.reshape(N_DP, LENGTH)))
        head_vals = low(low_back(head_vals.reshape(TOKENS, QW)))
        residual = x_in + low_back(matmul(head_vals, wo_in))
        normed_two = low(normalize(residual) * gain_two)
        logits = matmul(normed_two, router_in)
        gate_weights = softmax_rows(jnp.take_along_axis(logits, routes, 1))
        gate_flat = gate_weights.reshape(-1)

        @jax.checkpoint
        def expert(expert_args):
            gate_w, up_w, down_w, row_ids, row_keep = expert_args
            inputs = low_back(normed_two[row_ids // TOP])
            gate_h = low_back(matmul(inputs, gate_w))
            up_h = low_back(matmul(inputs, up_w))
            activation = low(gate_h * jax.nn.sigmoid(gate_h) * up_h)
            expert_out = low(low_back(matmul(activation, down_w)))
            return expert_out * jnp.where(row_keep, gate_flat[row_ids], 0.0)[:, None]
        weighted = lax.map(expert, (gate_in, up_in, down_in, row_clipped, row_valid))
        mixed = jnp.zeros((TOKENS, D), jnp.float32).at[row_tokens.reshape(-1)].add(weighted.reshape(-1, D))
        return residual + mixed
    primals = (hidden_in.astype(jnp.float32), norm1_gain, w_query.astype(jnp.float32), w_key.astype(jnp.float32), w_value.astype(jnp.float32), q_gain, k_gain, w_out.astype(jnp.float32), norm2_gain, router.astype(jnp.float32), w_gate.astype(jnp.float32), w_up.astype(jnp.float32), w_down.astype(jnp.float32))
    result, pullback = jax.vjp(forward, *primals)
    grads = pullback(cotangent.astype(jnp.float32))
    return (result.astype(jnp.bfloat16), grads[0].astype(jnp.bfloat16), grads[1], grads[2], grads[3], grads[4], grads[5], grads[6], grads[7], grads[8], grads[9], grads[10], grads[11], grads[12])
```

```python
import jax
import jax.numpy as jnp
from jax import lax
from jax.experimental import pallas as pl
from jax.experimental.pallas import tpu as pltpu
from jax.sharding import PartitionSpec as P

HEAD_DIM = 64


EPS = 1e-06
THETA = 10000.0
MASKED = -1e30
MESH = pl.DeviceIdType.MESH


def split_up(x, dim, count):
    before, after = (x.shape[:dim], x.shape[dim + 1 :])
    return jnp.moveaxis(x.reshape(*before, count, -1, *after), dim, 0)


def in_order(blocks, dim):
    lengths = list(blocks.shape[1:])
    lengths[dim] *= blocks.shape[0]
    return jnp.moveaxis(blocks, 0, dim).reshape(lengths)


def joined_exchange(x, axis, axes, splits, concats):
    sizes = [lax.axis_size(a) for a in axes]
    blocks = split_up(x, splits[0], sizes[0])
    blocks = jnp.moveaxis(split_up(blocks, splits[1] + 1, sizes[1]), 0, 1)
    inside = blocks.shape[2:]
    blocks = blocks.reshape(-1, *inside)
    blocks = lax.all_to_all(blocks, axis, split_axis=0, concat_axis=0, tiled=True)
    blocks = in_order(blocks.reshape(*sizes, *inside), concats[0] + 1)
    return in_order(blocks, concats[1])


def from_everyone(x, axis):
    copies = jnp.broadcast_to(x, (lax.axis_size(axis), *x.shape))
    return lax.all_to_all(copies, axis, split_axis=0, concat_axis=0, tiled=True)


def collect(x, axis, dim):
    blocks = from_everyone(x, axis)
    return in_order(blocks, dim)


def taken_together(x, axis):
    everything = from_everyone(x, axis)
    return jnp.sum(everything, axis=0)


def packed_total(arrays, axis):
    line, at, finished = (jnp.concatenate([a.reshape(-1) for a in arrays]), 0, [])
    so_far = taken_together(line, axis)
    for a in arrays:
        finished.append(so_far[at : at + a.size].reshape(a.shape))
        at += a.size
    return tuple(finished)


def sent_and_summed(x, axis, dim):
    count = lax.axis_size(axis)
    blocks = lax.all_to_all(split_up(x, dim, count), axis, 0, 0, tiled=True)
    return jnp.sum(blocks.astype(jnp.float32), axis=0)


def matmul(left, right):
    return jnp.dot(left, right, preferred_element_type=jnp.float32)


def matmul_tn(left, right):
    return lax.dot_general(
        left, right, (((0,), (0,)), ((), ())), preferred_element_type=jnp.float32
    )


def matmul_nt(left, right):
    return lax.dot_general(
        left, right, (((1,), (1,)), ((), ())), preferred_element_type=jnp.float32
    )


def rope_tables(positions, half_dim):
    inverse = THETA ** (-(jnp.arange(half_dim, dtype=jnp.float32) * 2.0 / (2 * half_dim)))
    angles = positions.astype(jnp.float32)[:, None] * inverse[None, :]
    return (jnp.cos(angles), jnp.sin(angles))


def rotate(values, cos_table, sin_table, flip_sign):
    half_dim = values.shape[-1] // 2
    first_half = values[..., :half_dim]
    second_half = values[..., half_dim:]
    cos_part = cos_table[:, None, :]
    sin_part = sin_table[:, None, :] * flip_sign
    return jnp.concatenate(
        [
            first_half * cos_part - second_half * sin_part,
            second_half * cos_part + first_half * sin_part,
        ],
        -1,
    )


def route_rows(buffer):
    reshaped = buffer.reshape((lax.axis_size("dp"), lax.axis_size("ctx")) + buffer.shape[1:])
    arrived = joined_exchange(reshaped, ("dp", "ctx"), ("dp", "ctx"), (0, 1), (0, 1))
    return arrived.reshape(buffer.shape)


def dot_nt(left, right):
    return lax.dot_general(
        left, right, (((1,), (1,)), ((), ())), preferred_element_type=jnp.float32
    )


def dot_tn(left, right):
    return lax.dot_general(
        left, right, (((0,), (0,)), ((), ())), preferred_element_type=jnp.float32
    )


def x_offset(a):
    return a + a // 2 - 2 * (a // 3)


def back_place(a):
    return (2 * a) % 3 + 3 * (a // 3)


def across(a, b, flip):
    dp, ctx = lax.axis_index("dp"), lax.axis_index("ctx")
    x, y = dp % 4, dp // 4
    return ((y + b) % 2) * 4 + (x + x_offset(a)) % 4, (ctx + flip) % 2


def moe_kernel(
    rows_ref,
    gate_ref,
    dy_ref,
    w_gate_ref,
    w_up_ref,
    w_down_ref,
    d_rows_ref,
    d_gate_ref,
    out_part_ref,
    grad_gu_ref,
    grad_down_ref,
    rows_all,
    gate_all,
    dy_all,
    w_gu,
    w_dn,
    acc_gu,
    acc_dn,
    out_all,
    din_all,
    sib,
    summed,
    dg_out,
    dg_in,
    places,
    x_buf,
    y_buf,
    d_buf,
    o_buf,
    i_buf,
    gs_buf,
    dgs_buf,
    load_sem,
    ag_send,
    ag_recv,
    sib_send,
    sib_recv,
    rs_send,
    rs_recv,
    dg_send,
    dg_recv,
    store_sem,
):
    tensor = lax.axis_index("tensor")
    dp, ctx = lax.axis_index("dp"), lax.axis_index("ctx")
    me = dp * 2 + ctx
    kinds = (rows_all, gate_all, dy_all)

    def to(a, b, flip):
        d, c = across(a, b, flip)
        return (d, c, tensor)

    loads = []
    for j in range(2):
        loads.append(
            pltpu.make_async_copy(w_gate_ref.at[j], w_gu.at[j, :, pl.ds(0, 512)], load_sem.at[3 * j])
        )
        loads.append(
            pltpu.make_async_copy(
                w_up_ref.at[j], w_gu.at[j, :, pl.ds(512, 512)], load_sem.at[3 * j + 1]
            )
        )
        loads.append(pltpu.make_async_copy(w_down_ref.at[j], w_dn.at[j], load_sem.at[3 * j + 2]))
    for load in loads:
        load.start()

    barrier = pltpu.get_barrier_semaphore()
    for a in range(4):
        for b in range(2):
            for flip in range(2):
                if (a, b, flip) != (0, 0, 0):
                    pl.semaphore_signal(
                        barrier, inc=1, device_id=to(a, b, flip), device_id_type=MESH
                    )
    pl.semaphore_wait(barrier, 15)

    def own_push(k, a, b, flip):
        r = 4 * a + 2 * b + flip
        back = 4 * back_place(a) + 2 * b + flip
        return pltpu.make_async_remote_copy(
            src_ref=kinds[k].at[0],
            dst_ref=kinds[k].at[back],
            send_sem=ag_send.at[k, r],
            recv_sem=ag_recv.at[k, back],
            device_id=to(a, b, flip),
            device_id_type=MESH,
        )

    def relay(k, r):
        return pltpu.make_async_remote_copy(
            src_ref=kinds[k].at[r],
            dst_ref=kinds[k].at[r + 1],
            send_sem=ag_send.at[k, r + 1],
            recv_sem=ag_recv.at[k, r + 1],
            device_id=to(0, 0, 1),
            device_id_type=MESH,
        )

    def arrival(k, r):
        return pltpu.make_async_remote_copy(
            src_ref=kinds[k].at[r],
            dst_ref=kinds[k].at[r],
            send_sem=ag_send.at[k, r],
            recv_sem=ag_recv.at[k, r],
            device_id=to(0, 0, 1),
            device_id_type=MESH,
        )

    rows_all[0] = rows_ref[...]
    gate_all[0] = gate_ref[...]
    dy_all[0] = dy_ref[...]
    for k in range(3):
        own_push(k, 0, 0, 1).start()
    for k in range(3):
        for a in range(4):
            for b in range(2):
                if (a, b) != (0, 0):
                    own_push(k, a, b, 0).start()

    acc_gu[...] = jnp.zeros_like(acc_gu)
    acc_dn[...] = jnp.zeros_like(acc_dn)

    def arrive(a, first):
        for b in range(2):
            if not (first and b == 0):
                for k in range(3):
                    arrival(k, 4 * a + 2 * b).wait_recv()
                    relay(k, 4 * a + 2 * b).start()
        for b in range(2):
            for k in range(3):
                arrival(k, 4 * a + 2 * b + 1).wait_recv()

    def sib_push(ci, r):
        return pltpu.make_async_remote_copy(
            src_ref=din_all.at[r],
            dst_ref=sib.at[ci],
            send_sem=sib_send.at[ci],
            recv_sem=sib_recv.at[ci],
            device_id=to(0, 0, 1),
            device_id_type=MESH,
        )

    def rs_push(a, b):
        back = 2 * back_place(a) + b
        return pltpu.make_async_remote_copy(
            src_ref=din_all.at[4 * a + 2 * b],
            dst_ref=summed.at[back],
            send_sem=rs_send.at[2 * a + b],
            recv_sem=rs_recv.at[back],
            device_id=to(a, b, 0),
            device_id_type=MESH,
        )

    def dg_push(a, b, flip):
        r = 4 * a + 2 * b + flip
        back = 4 * back_place(a) + 2 * b + flip
        return pltpu.make_async_remote_copy(
            src_ref=dg_out.at[r],
            dst_ref=dg_in.at[back],
            send_sem=dg_send.at[r],
            recv_sem=dg_recv.at[back],
            device_id=to(a, b, flip),
            device_id_type=MESH,
        )

    def post(a):
        for b in range(2):
            ci, r = 2 * a + b, 4 * a + 2 * b
            sib_push(ci, r + 1).wait_recv()
            total = din_all[r].astype(jnp.float32) + sib[ci].astype(jnp.float32)
            din_all[r] = total.astype(jnp.bfloat16)

            @pl.when(ci > 0)
            def _():
                rs_push(a, b).start()

    expert_row = lax.broadcasted_iota(jnp.int32, (32, 128), 0)
    slot_row = lax.broadcasted_iota(jnp.int32, (64, 128), 0).astype(jnp.float32)
    before = (
        lax.broadcasted_iota(jnp.int32, (128, 128), 0)
        < lax.broadcasted_iota(jnp.int32, (128, 128), 1)
    ).astype(jnp.float32)
    before = before.astype(jnp.bfloat16)

    def gather(a, q):
        r = 4 * a + q
        gates = gate_all[r]
        at = pl.ds(pl.multiple_of(q * 64, 64), 64)
        rows = [
            jnp.sum(jnp.where(expert_row == 2 * me + j, gates, 0.0), 0, keepdims=True)
            for j in range(2)
        ]
        both = jnp.concatenate(rows + [jnp.zeros((6, 128), jnp.float32)], 0)
        named = jnp.where(both > 0.0, 1.0, 0.0).astype(jnp.bfloat16)
        slots = jnp.dot(named, before, preferred_element_type=jnp.float32)
        hits = [
            jnp.where((slot_row == slots[j : j + 1]) & (rows[j] > 0.0), 1.0, 0.0) for j in range(2)
        ]
        place = jnp.concatenate(hits, 0).astype(jnp.bfloat16)
        places[q] = place
        x = jnp.dot(place, rows_all[r], preferred_element_type=jnp.float32).astype(jnp.bfloat16)
        y = jnp.dot(place, dy_all[r], preferred_element_type=jnp.float32)
        for j in range(2):
            gs = jnp.sum(hits[j] * rows[j], 1, keepdims=True)
            y_j = y[64 * j : 64 * j + 64]
            x_buf[j, at, :] = x[64 * j : 64 * j + 64]
            y_buf[j, at, :] = y_j.astype(jnp.bfloat16)
            d_buf[j, at, :] = (y_j * gs).astype(jnp.bfloat16)
            gs_buf[j, at, :] = gs

    def expert(j):
        x = x_buf[j]
        gu = jnp.dot(x, w_gu[j], preferred_element_type=jnp.float32)
        g, u = gu[:, :512], gu[:, 512:]
        s = jax.nn.sigmoid(g)
        silu = g * s
        act = (silu * u).astype(jnp.bfloat16)
        eout = (
            jnp.dot(act, w_dn[j], preferred_element_type=jnp.float32)
            .astype(jnp.bfloat16)
            .astype(jnp.float32)
        )
        dgs_buf[j] = jnp.sum(y_buf[j].astype(jnp.float32) * eout, 1, keepdims=True)
        o_buf[j] = (eout * gs_buf[j]).astype(jnp.bfloat16)
        d = d_buf[j]
        d_act = dot_nt(d, w_dn[j])
        d_g = (d_act * u * s * (1.0 + g * (1.0 - s))).astype(jnp.bfloat16)
        d_u = (d_act * silu).astype(jnp.bfloat16)
        d_gu = jnp.concatenate([d_g, d_u], 1)
        i_buf[j] = dot_nt(d_gu, w_gu[j]).astype(jnp.bfloat16)
        acc_gu[j] += dot_tn(x, d_gu)
        acc_dn[j] += dot_tn(act, d)

    def spread(a, q):
        r = 4 * a + q
        b, flip = q // 2, q % 2
        at = pl.ds(pl.multiple_of(q * 64, 64), 64)
        place = places[q]
        d, c = across(a, b, flip)
        o = jnp.concatenate([o_buf[0, at, :], o_buf[1, at, :]], 0)
        out_all[d * 2 + c] = dot_tn(place, o).astype(jnp.bfloat16)
        i = jnp.concatenate([i_buf[0, at, :], i_buf[1, at, :]], 0)
        din_all[r] = dot_tn(place, i).astype(jnp.bfloat16)
        hits = place.astype(jnp.float32)
        back = [
            jnp.sum(hits[64 * j : 64 * j + 64] * dgs_buf[j, at, :], 0, keepdims=True)
            for j in range(2)
        ]
        dg_out[r] = jnp.concatenate(back + [jnp.zeros((6, 128), jnp.float32)], 0)

        @pl.when(r > 0)
        def _():
            dg_push(a, b, flip).start()

    arrive(0, True)
    for load in loads:
        load.wait()

    def step(a, carry):
        lax.fori_loop(0, 4, lambda q, c: (gather(a, q), c)[1], 0)
        lax.fori_loop(0, 2, lambda j, c: (expert(j), c)[1], 0)
        lax.fori_loop(0, 4, lambda q, c: (spread(a, q), c)[1], 0)
        for b in range(2):
            sib_push(2 * a + b, 4 * a + 2 * b + 1).start()

        @pl.when(a > 0)
        def _():
            post(a - 1)

        @pl.when(a < 3)
        def _():
            arrive(a + 1, False)

        return carry

    lax.fori_loop(0, 4, step, 0)
    post(3)
    for k in range(3):
        for r in range(1, 16):
            arrival(k, r).wait_send()
    stores = []
    for j in range(2):
        for h in range(8):
            rows_all[8 * j + h] = acc_gu[j, 128 * h : 128 * h + 128, :].astype(jnp.bfloat16)
        for h in range(4):
            dy_all[4 * j + h] = acc_dn[j, 128 * h : 128 * h + 128, :].astype(jnp.bfloat16)
    stores.append(pltpu.make_async_copy(rows_all, grad_gu_ref, store_sem.at[0]))
    stores.append(pltpu.make_async_copy(dy_all.at[pl.ds(0, 8)], grad_down_ref, store_sem.at[1]))
    stores.append(pltpu.make_async_copy(out_all, out_part_ref, store_sem.at[2]))
    for store in stores:
        store.start()

    for r in range(1, 16):
        a, b, flip = r // 4, (r // 2) % 2, r % 2
        dg_push(a, b, flip).wait()
    dg_in[0] = dg_out[0]
    d_gate = jnp.zeros((32, 128), jnp.float32)
    for r in range(16):
        d, c = across(r // 4, (r // 2) % 2, r % 2)
        got = dg_in[r]
        for j in range(2):
            d_gate = jnp.where(expert_row == (d * 2 + c) * 2 + j, got[j : j + 1], d_gate)
    d_gate_ref[...] = d_gate
    total = din_all[0].astype(jnp.float32)
    for ci in range(8):
        sib_push(ci, 2 * ci + 1).wait_send()
        if ci > 0:
            rs_push(ci // 2, ci % 2).wait()
    for ci in range(1, 8):
        total = total + summed[ci].astype(jnp.float32)
    d_rows_ref[...] = total
    for store in stores:
        store.wait()


def moe(rows, gates, dy, w_gate, w_up, w_down):
    bf, f32 = jnp.bfloat16, jnp.float32
    vmem, hbm = pl.BlockSpec(memory_space=pltpu.VMEM), pl.BlockSpec(memory_space=pl.ANY)
    sem = pltpu.SemaphoreType.DMA
    return pl.pallas_call(
        moe_kernel,
        out_shape=(
            jax.ShapeDtypeStruct((128, 1024), f32),
            jax.ShapeDtypeStruct((32, 128), f32),
            jax.ShapeDtypeStruct((16, 128, 1024), bf),
            jax.ShapeDtypeStruct((16, 128, 1024), bf),
            jax.ShapeDtypeStruct((8, 128, 1024), bf),
        ),
        in_specs=[vmem] * 3 + [hbm] * 3,
        out_specs=(vmem, vmem, hbm, hbm, hbm),
        scratch_shapes=[
            pltpu.VMEM((16, 128, 1024), bf),
            pltpu.VMEM((16, 32, 128), f32),
            pltpu.VMEM((16, 128, 1024), bf),
            pltpu.VMEM((2, 1024, 1024), bf),
            pltpu.VMEM((2, 512, 1024), bf),
            pltpu.VMEM((2, 1024, 1024), f32),
            pltpu.VMEM((2, 512, 1024), f32),
            pltpu.VMEM((16, 128, 1024), bf),
            pltpu.VMEM((16, 128, 1024), bf),
            pltpu.VMEM((8, 128, 1024), bf),
            pltpu.VMEM((8, 128, 1024), bf),
            pltpu.VMEM((16, 8, 128), f32),
            pltpu.VMEM((16, 8, 128), f32),
            pltpu.VMEM((4, 128, 128), bf),
            pltpu.VMEM((2, 256, 1024), bf),
            pltpu.VMEM((2, 256, 1024), bf),
            pltpu.VMEM((2, 256, 1024), bf),
            pltpu.VMEM((2, 256, 1024), bf),
            pltpu.VMEM((2, 256, 1024), bf),
            pltpu.VMEM((2, 256, 1), f32),
            pltpu.VMEM((2, 256, 1), f32),
            sem((6,)),
            sem((3, 16)),
            sem((3, 16)),
            sem((8,)),
            sem((8,)),
            sem((8,)),
            sem((8,)),
            sem((16,)),
            sem((16,)),
            sem((3,)),
        ],
        compiler_params=pltpu.CompilerParams(
            collective_id=1, has_side_effects=True, vmem_limit_bytes=60 << 20
        ),
        cost_estimate=pl.CostEstimate(
            flops=20_000_000_000, bytes_accessed=30_000_000, transcendentals=2_000_000
        ),
    )(rows, gates, dy, w_gate, w_up, w_down)


def shards(
    hidden_in,
    segment,
    norm1_gain,
    w_query,
    w_key,
    w_value,
    q_gain,
    k_gain,
    w_out,
    norm2_gain,
    router,
    w_gate,
    w_up,
    w_down,
    routes,
    cotangent,
):
    tok_rows = hidden_in.shape[0]
    model_dim = hidden_in.shape[1]
    n_tensor = lax.axis_size("tensor")
    n_groups = lax.axis_size(("dp", "ctx"))
    seq_len = segment.shape[0]
    slab_rows = tok_rows * n_tensor
    ctx_index = lax.axis_index("ctx")
    head_dim = HEAD_DIM
    q_cols = w_query.shape[1]
    kv_cols = w_key.shape[1]
    q_heads = q_cols // head_dim
    kv_heads = kv_cols // head_dim
    group_size = q_heads // kv_heads
    q_width = q_cols * n_tensor
    k_width = kv_cols * n_tensor
    block_rows = min(512, slab_rows)
    n_blocks = slab_rows // block_rows
    scaling = head_dim ** (-0.5)
    top_k = routes.shape[1]
    exp_dev = w_gate.shape[0]
    n_experts = exp_dev * n_groups
    capacity = max(2, 2 * tok_rows * top_k // n_experts)
    x_float = hidden_in.astype(jnp.float32)
    inv_one = lax.rsqrt(jnp.mean(x_float * x_float, -1, keepdims=True) + EPS)
    x_hat = x_float * inv_one
    normed_one = (x_hat * norm1_gain).astype(jnp.bfloat16)
    rows_all = collect(normed_one, "tensor", 0)
    w_qkv = jnp.concatenate([w_query, w_key, w_value], 1)
    projected = matmul(rows_all, w_qkv)
    q_raw = projected[:, :q_cols]
    k_raw = projected[:, q_cols : q_cols + kv_cols]
    v_raw = projected[:, q_cols + kv_cols :]
    q_square, k_square = packed_total(
        (jnp.sum(q_raw * q_raw, 1), jnp.sum(k_raw * k_raw, 1)), "tensor"
    )
    inv_q = lax.rsqrt(q_square / q_width + EPS)[:, None]
    inv_k = lax.rsqrt(k_square / k_width + EPS)[:, None]
    q_hat = q_raw * inv_q
    k_hat = k_raw * inv_k
    positions = ctx_index * slab_rows + jnp.arange(slab_rows, dtype=jnp.int32)
    cos_table, sin_table = rope_tables(positions, head_dim // 2)
    queries = rotate(
        (q_hat * q_gain).reshape(slab_rows, q_heads, head_dim), cos_table, sin_table, 1.0
    ).astype(jnp.bfloat16)
    keys_local = rotate(
        (k_hat * k_gain).reshape(slab_rows, kv_heads, head_dim), cos_table, sin_table, 1.0
    ).astype(jnp.bfloat16)
    kv_local = jnp.concatenate(
        [keys_local.reshape(slab_rows, kv_cols), v_raw.astype(jnp.bfloat16)], 1
    )
    kv_all = collect(kv_local, "ctx", 0)
    key_pos = jnp.arange(seq_len, dtype=jnp.int32)
    query_seg = lax.dynamic_slice_in_dim(segment, ctx_index * slab_rows, slab_rows)
    keys_all = kv_all[:, :kv_cols].reshape(seq_len, kv_heads, head_dim)
    values_all = kv_all[:, kv_cols:].reshape(seq_len, kv_heads, head_dim)
    q_blocks = queries.reshape(n_blocks, block_rows, kv_heads, group_size, head_dim)
    seg_blocks = query_seg.reshape(n_blocks, block_rows)
    pos_blocks = positions.reshape(n_blocks, block_rows)

    def block_scores(q_block, seg_block, pos_block, keys_now):
        raw_scores = (
            jnp.einsum("qkgd,tkd->kgqt", q_block, keys_now, preferred_element_type=jnp.float32)
            * scaling
        )
        allowed = (seg_block[:, None] == segment[None, :]) & (
            key_pos[None, :] <= pos_block[:, None]
        )
        return jnp.where(allowed, raw_scores, MASKED)

    def forward_block(block_args):
        q_block, seg_block, pos_block = block_args
        scores = block_scores(q_block, seg_block, pos_block, keys_all)
        largest = jnp.max(scores, -1, keepdims=True)
        exponent = jnp.exp(scores - largest)
        row_sums = jnp.sum(exponent, -1, keepdims=True)
        probabilities = exponent / row_sums
        head_vals = jnp.einsum(
            "kgqt,tkd->qkgd",
            probabilities.astype(jnp.bfloat16),
            values_all,
            preferred_element_type=jnp.float32,
        )
        return (head_vals.reshape(block_rows, q_cols), (largest + jnp.log(row_sums))[..., 0])

    head_blocks, lse_blocks = lax.map(forward_block, (q_blocks, seg_blocks, pos_blocks))
    heads_out = head_blocks.reshape(slab_rows, q_cols).astype(jnp.bfloat16)
    attended = lax.psum_scatter(
        matmul(heads_out, w_out).astype(jnp.bfloat16), "tensor", scatter_dimension=0, tiled=True
    ).astype(jnp.float32)
    residual = x_float + attended
    inv_two = lax.rsqrt(jnp.mean(residual * residual, -1, keepdims=True) + EPS)
    res_hat = residual * inv_two
    normed_two = (res_hat * norm2_gain).astype(jnp.bfloat16)
    logits = matmul(normed_two, router)
    expert_ids = jnp.arange(n_experts, dtype=jnp.int32)
    named = jnp.any(routes[:, :, None] == expert_ids[None, None, :], 1)
    top_logit = jnp.max(jnp.where(named, logits, MASKED), -1, keepdims=True)
    gate_exp = jnp.where(named, jnp.exp(jnp.where(named, logits - top_logit, 0.0)), 0.0)
    gates = (gate_exp / jnp.sum(gate_exp, -1, keepdims=True)).T
    grad_out = cotangent.astype(jnp.float32)
    d_rows, d_gate, out_part, grad_gu, grad_down = moe(
        normed_two, gates, cotangent, w_gate, w_up, w_down
    )
    mixed = lax.psum_scatter(
        out_part.reshape(-1, model_dim), ("dp", "ctx"), scatter_dimension=0, tiled=True
    )
    output = (residual + mixed.astype(jnp.float32)).astype(jnp.bfloat16)
    d_logits = (gates * (d_gate - jnp.sum(gates * d_gate, 0, keepdims=True))).T
    router_part = lax.dot_general(
        normed_two.astype(jnp.float32),
        d_logits,
        (((0,), (0,)), ((), ())),
        precision=lax.Precision.HIGHEST,
    )
    d_normed = jnp.dot(d_logits, router.astype(jnp.float32).T, precision=lax.Precision.HIGHEST)
    d_normed = d_normed + d_rows
    grad_gu = grad_gu.reshape(2, 1024, 1024)
    grad_gate, grad_up = grad_gu[:, :, :512], grad_gu[:, :, 512:]
    grad_down = grad_down.reshape(2, 512, 1024)
    norm2_part = jnp.sum(d_normed * res_hat, 0)
    d_scaled_two = d_normed * norm2_gain
    d_resid = grad_out + inv_two * (
        d_scaled_two - res_hat * jnp.mean(d_scaled_two * res_hat, -1, keepdims=True)
    )
    d_att_all = collect(d_resid.astype(jnp.bfloat16), "tensor", 0)
    grad_wo_part = matmul_tn(heads_out, d_att_all)
    d_heads = matmul_nt(d_att_all, w_out).astype(jnp.bfloat16)
    keys_back, values_back = (keys_all, values_all)
    d_blocks = d_heads.reshape(n_blocks, block_rows, kv_heads, group_size, head_dim)

    def backward_block(carried, block_args):
        d_keys, d_values = carried
        q_block, seg_block, pos_block, lse_block, dh_block = block_args
        scores = block_scores(q_block, seg_block, pos_block, keys_back)
        probabilities = jnp.exp(scores - lse_block[..., None])
        d_probs = jnp.einsum(
            "qkgd,tkd->kgqt", dh_block, values_back, preferred_element_type=jnp.float32
        )
        d_scores = (
            probabilities * (d_probs - jnp.sum(probabilities * d_probs, -1, keepdims=True))
        ).astype(jnp.bfloat16)
        d_query = (
            jnp.einsum("kgqt,tkd->qkgd", d_scores, keys_back, preferred_element_type=jnp.float32)
            * scaling
        )
        d_keys = (
            d_keys
            + jnp.einsum("kgqt,qkgd->tkd", d_scores, q_block, preferred_element_type=jnp.float32)
            * scaling
        )
        d_values = d_values + jnp.einsum(
            "kgqt,qkgd->tkd",
            probabilities.astype(jnp.bfloat16),
            dh_block,
            preferred_element_type=jnp.float32,
        )
        return ((d_keys, d_values), d_query.reshape(block_rows, q_cols))

    zero_kv = jnp.zeros((seq_len, kv_heads, head_dim), jnp.float32)
    (d_keys_all, d_values_all), d_query_blocks = lax.scan(
        backward_block, (zero_kv, zero_kv), (q_blocks, seg_blocks, pos_blocks, lse_blocks, d_blocks)
    )
    d_kv = jnp.concatenate(
        [d_keys_all.reshape(seq_len, kv_cols), d_values_all.reshape(seq_len, kv_cols)], 1
    )
    d_kv_own = sent_and_summed(d_kv.astype(jnp.bfloat16), "ctx", 0)
    d_v_raw = d_kv_own[:, kv_cols:].astype(jnp.bfloat16)
    d_q_norm = rotate(
        d_query_blocks.reshape(slab_rows, q_heads, head_dim), cos_table, sin_table, -1.0
    ).reshape(slab_rows, q_cols)
    d_k_norm = rotate(
        d_kv_own[:, :kv_cols].reshape(slab_rows, kv_heads, head_dim), cos_table, sin_table, -1.0
    ).reshape(slab_rows, kv_cols)
    qgain_part = jnp.sum(d_q_norm * q_hat, 0)
    kgain_part = jnp.sum(d_k_norm * k_hat, 0)
    q_term = d_q_norm * q_gain
    k_term = d_k_norm * k_gain
    q_inner, k_inner = packed_total(
        (jnp.sum(q_term * q_hat, 1), jnp.sum(k_term * k_hat, 1)), "tensor"
    )
    d_q_raw = (inv_q * (q_term - q_hat * (q_inner / q_width)[:, None])).astype(jnp.bfloat16)
    d_k_raw = (inv_k * (k_term - k_hat * (k_inner / k_width)[:, None])).astype(jnp.bfloat16)
    d_qkv = jnp.concatenate([d_q_raw, d_k_raw, d_v_raw], 1)
    grad_qkv = matmul_tn(rows_all, d_qkv)
    d_normed_one = lax.psum_scatter(
        matmul_nt(d_qkv, w_qkv).astype(jnp.bfloat16), "tensor", scatter_dimension=0, tiled=True
    ).astype(jnp.float32)
    norm1_part = jnp.sum(d_normed_one * x_hat, 0)
    d_scaled_one = d_normed_one * norm1_gain
    grad_x = (
        d_resid
        + inv_one * (d_scaled_one - x_hat * jnp.mean(d_scaled_one * x_hat, -1, keepdims=True))
    ).astype(jnp.bfloat16)
    grad_gate_all, grad_up_all, grad_down_all, router_sum, norm1_sum, norm2_sum = (
        lax.psum(grad_gate.astype(jnp.bfloat16), "tensor").astype(jnp.float32),
        lax.psum(grad_up.astype(jnp.bfloat16), "tensor").astype(jnp.float32),
        lax.psum(grad_down.astype(jnp.bfloat16), "tensor").astype(jnp.float32),
        lax.psum(router_part.astype(jnp.bfloat16), "tensor").astype(jnp.float32),
        lax.psum(norm1_part.astype(jnp.bfloat16), "tensor").astype(jnp.float32),
        lax.psum(norm2_part.astype(jnp.bfloat16), "tensor").astype(jnp.float32),
    )
    totals = (
        lax.psum(grad_qkv.astype(jnp.bfloat16), ("dp", "ctx")).astype(jnp.float32),
        lax.psum(grad_wo_part.astype(jnp.bfloat16), ("dp", "ctx")).astype(jnp.float32),
        lax.psum(qgain_part.astype(jnp.bfloat16), ("dp", "ctx")).astype(jnp.float32),
        lax.psum(kgain_part.astype(jnp.bfloat16), ("dp", "ctx")).astype(jnp.float32),
        lax.psum(router_sum.astype(jnp.bfloat16), ("dp", "ctx")).astype(jnp.float32),
        lax.psum(norm1_sum.astype(jnp.bfloat16), ("dp", "ctx")).astype(jnp.float32),
        lax.psum(norm2_sum.astype(jnp.bfloat16), ("dp", "ctx")).astype(jnp.float32),
    )
    grad_qkv_all = totals[0]
    return (
        output,
        grad_x,
        totals[5],
        grad_qkv_all[:, :q_cols],
        grad_qkv_all[:, q_cols : q_cols + kv_cols],
        grad_qkv_all[:, q_cols + kv_cols :],
        totals[2],
        totals[3],
        totals[1],
        totals[6],
        totals[4],
        grad_gate_all,
        grad_up_all,
        grad_down_all,
    )


def solution(mesh):
    return jax.shard_map(
        shards,
        mesh=mesh,
        in_specs=(
            P(("dp", "ctx", "tensor"), None),
            P("dp"),
            P(),
            P(None, "tensor"),
            P(None, "tensor"),
            P(None, "tensor"),
            P("tensor"),
            P("tensor"),
            P("tensor", None),
            P(),
            P(),
            P(("dp", "ctx"), None, None),
            P(("dp", "ctx"), None, None),
            P(("dp", "ctx"), None, None),
            P(("dp", "ctx", "tensor"), None),
            P(("dp", "ctx", "tensor"), None),
        ),
        out_specs=(
            P(("dp", "ctx", "tensor"), None),
            P(("dp", "ctx", "tensor"), None),
            P(),
            P(None, "tensor"),
            P(None, "tensor"),
            P(None, "tensor"),
            P("tensor"),
            P("tensor"),
            P("tensor", None),
            P(),
            P(),
            P(("dp", "ctx"), None, None),
            P(("dp", "ctx"), None, None),
            P(("dp", "ctx"), None, None),
        ),
        check_vma=False,
    )
```

```python
import jax
import jax.numpy as jnp
import numpy as np
from jax import lax
from jax.experimental import pallas as pl
from jax.experimental.pallas import tpu as pltpu
from jax.sharding import PartitionSpec as P

EPS = 1e-06
THETA = 10000.0
MASKED = -1e30
MESH = pl.DeviceIdType.MESH


def rope_constants(length, half_dim):
    inverse = THETA ** (-(np.arange(half_dim, dtype=np.float64) * 2.0 / (2 * half_dim)))
    angles = inverse[:, None] * np.arange(length, dtype=np.float64)[None, :]
    table = np.stack([np.cos(angles), np.sin(angles)]).astype(np.float32)
    return np.ascontiguousarray(table.reshape(2, half_dim, 2, length // 2).transpose(2, 0, 1, 3))


def turn(value, cos_part, sin_part):
    parts = []
    for h in range(value.shape[0] // 64):
        a, b = value[64 * h : 64 * h + 32], value[64 * h + 32 : 64 * h + 64]
        parts += [a * cos_part - b * sin_part, b * cos_part + a * sin_part]
    return jnp.concatenate(parts, 0)


def column(row):
    return jnp.transpose(jnp.broadcast_to(row, (128, 128)))


def copy_to(src, dst, send, recv, device):
    return pltpu.make_async_remote_copy(
        src_ref=src, dst_ref=dst, send_sem=send, recv_sem=recv, device_id=device, device_id_type=MESH
    )


def dot_nt(left, right):
    return lax.dot_general(
        left, right, (((1,), (1,)), ((), ())), preferred_element_type=jnp.float32
    )


def dot_tn(left, right):
    return lax.dot_general(
        left, right, (((0,), (0,)), ((), ())), preferred_element_type=jnp.float32
    )


def x_offset(a):
    return a + a // 2 - 2 * (a // 3)


def back_place(a):
    return (2 * a) % 3 + 3 * (a // 3)


def across(a, b, flip):
    dp, ctx = lax.axis_index("dp"), lax.axis_index("ctx")
    x, y = dp % 4, dp // 4
    return ((y + b) % 2) * 4 + (x + x_offset(a)) % 4, (ctx + flip) % 2


def moe_kernel(
    rows_ref,
    gate_ref,
    dy_ref,
    w_gate_ref,
    w_up_ref,
    w_down_ref,
    w_t_ref,
    d_rows_ref,
    d_gate_ref,
    out_part_ref,
    grad_ref,
    w_all_ref,
    rows_all,
    gate_all,
    dy_all,
    w_gu,
    w_dn,
    acc_gu,
    acc_dn,
    out_all,
    din_all,
    sib,
    summed,
    dg_out,
    dg_in,
    places,
    x_buf,
    y_buf,
    d_buf,
    o_buf,
    i_buf,
    gs_buf,
    dgs_buf,
    load_sem,
    ag_send,
    ag_recv,
    sib_send,
    sib_recv,
    rs_send,
    rs_recv,
    dg_send,
    dg_recv,
    store_sem,
    w_send,
    w_recv,
):
    tensor = lax.axis_index("tensor")
    dp, ctx = lax.axis_index("dp"), lax.axis_index("ctx")
    me = dp * 2 + ctx
    kinds = (rows_all, gate_all)

    def to(a, b, flip):
        d, c = across(a, b, flip)
        return (d, c, tensor)

    def side(i):
        return (dp, ctx, (tensor + i) % 8)

    loads = []
    for j in range(2):
        loads.append(
            pltpu.make_async_copy(w_gate_ref.at[j], w_gu.at[j, :, pl.ds(0, 512)], load_sem.at[3 * j])
        )
        loads.append(
            pltpu.make_async_copy(
                w_up_ref.at[j], w_gu.at[j, :, pl.ds(512, 512)], load_sem.at[3 * j + 1]
            )
        )
        loads.append(pltpu.make_async_copy(w_down_ref.at[j], w_dn.at[j], load_sem.at[3 * j + 2]))
    loads.append(pltpu.make_async_copy(dy_ref, dy_all, load_sem.at[6]))
    for load in loads:
        load.start()

    barrier = pltpu.get_barrier_semaphore()
    for a in range(4):
        for b in range(2):
            for flip in range(2):
                if (a, b, flip) != (0, 0, 0):
                    pl.semaphore_signal(
                        barrier, inc=1, device_id=to(a, b, flip), device_id_type=MESH
                    )
    for i in range(1, 8):
        pl.semaphore_signal(barrier, inc=1, device_id=side(i), device_id_type=MESH)
    pl.semaphore_wait(barrier, 22)

    def own_push(k, a, b, flip):
        r = 4 * a + 2 * b + flip
        back = 4 * back_place(a) + 2 * b + flip
        return pltpu.make_async_remote_copy(
            src_ref=kinds[k].at[0],
            dst_ref=kinds[k].at[back],
            send_sem=ag_send.at[k, r],
            recv_sem=ag_recv.at[k, back],
            device_id=to(a, b, flip),
            device_id_type=MESH,
        )

    def relay(k, r):
        return pltpu.make_async_remote_copy(
            src_ref=kinds[k].at[r],
            dst_ref=kinds[k].at[r + 1],
            send_sem=ag_send.at[k, r + 1],
            recv_sem=ag_recv.at[k, r + 1],
            device_id=to(0, 0, 1),
            device_id_type=MESH,
        )

    def arrival(k, r):
        return pltpu.make_async_remote_copy(
            src_ref=kinds[k].at[r],
            dst_ref=kinds[k].at[r],
            send_sem=ag_send.at[k, r],
            recv_sem=ag_recv.at[k, r],
            device_id=to(0, 0, 1),
            device_id_type=MESH,
        )

    rows_all[0] = rows_ref[...]
    gate_all[0] = gate_ref[...]
    for k in range(2):
        own_push(k, 0, 0, 1).start()
    for k in range(2):
        for a in range(4):
            for b in range(2):
                if (a, b) != (0, 0):
                    own_push(k, a, b, 0).start()

    acc_gu[...] = jnp.zeros_like(acc_gu)
    acc_dn[...] = jnp.zeros_like(acc_dn)

    def arrive(a, first):
        for b in range(2):
            if not (first and b == 0):
                for k in range(2):
                    arrival(k, 4 * a + 2 * b).wait_recv()
                    relay(k, 4 * a + 2 * b).start()
        for b in range(2):
            for k in range(2):
                arrival(k, 4 * a + 2 * b + 1).wait_recv()

    half = pl.ds(pl.multiple_of(ctx * 128, 128), 128)

    def w_push(i):
        return copy_to(
            w_t_ref.at[half],
            w_all_ref.at[tensor, half],
            w_send.at[i],
            w_recv.at[tensor, ctx],
            side(i),
        )

    def w_relay(t):
        place = w_all_ref.at[t, half]
        return copy_to(place, place, w_send.at[8 + t], w_recv.at[t, ctx], to(0, 0, 1))

    def w_arrival(t, c):
        place = w_all_ref.at[t, pl.ds(pl.multiple_of(c * 128, 128), 128)]
        return copy_to(place, place, w_send.at[0], w_recv.at[t, c], to(0, 0, 1))

    for i in (1, 7, 2, 6, 3, 5, 4):
        w_push(i).start()
    w_own = pltpu.make_async_copy(w_t_ref, w_all_ref.at[tensor], load_sem.at[7])
    w_own.start()

    def sib_push(ci, r):
        return pltpu.make_async_remote_copy(
            src_ref=din_all.at[r],
            dst_ref=sib.at[ci],
            send_sem=sib_send.at[ci],
            recv_sem=sib_recv.at[ci],
            device_id=to(0, 0, 1),
            device_id_type=MESH,
        )

    def rs_push(a, b):
        back = 2 * back_place(a) + b
        return pltpu.make_async_remote_copy(
            src_ref=din_all.at[4 * a + 2 * b],
            dst_ref=summed.at[back],
            send_sem=rs_send.at[2 * a + b],
            recv_sem=rs_recv.at[back],
            device_id=to(a, b, 0),
            device_id_type=MESH,
        )

    def dg_push(a, b, flip):
        r = 4 * a + 2 * b + flip
        back = 4 * back_place(a) + 2 * b + flip
        return pltpu.make_async_remote_copy(
            src_ref=dg_out.at[r],
            dst_ref=dg_in.at[back],
            send_sem=dg_send.at[r],
            recv_sem=dg_recv.at[back],
            device_id=to(a, b, flip),
            device_id_type=MESH,
        )

    def post(a):
        for b in range(2):
            ci, r = 2 * a + b, 4 * a + 2 * b
            sib_push(ci, r + 1).wait_recv()
            total = din_all[r].astype(jnp.float32) + sib[ci].astype(jnp.float32)
            din_all[r] = total.astype(jnp.bfloat16)

            @pl.when(ci > 0)
            def _():
                rs_push(a, b).start()

    expert_row = lax.broadcasted_iota(jnp.int32, (32, 128), 0)
    slot_row = lax.broadcasted_iota(jnp.int32, (64, 128), 0).astype(jnp.float32)
    before = (
        lax.broadcasted_iota(jnp.int32, (128, 128), 0)
        < lax.broadcasted_iota(jnp.int32, (128, 128), 1)
    ).astype(jnp.float32)
    before = before.astype(jnp.bfloat16)

    def gather(a, q):
        r = 4 * a + q
        gates = gate_all[r]
        at = pl.ds(pl.multiple_of(q * 64, 64), 64)
        rows = [
            jnp.sum(jnp.where(expert_row == 2 * me + j, gates, 0.0), 0, keepdims=True)
            for j in range(2)
        ]
        both = jnp.concatenate(rows + [jnp.zeros((6, 128), jnp.float32)], 0)
        named = jnp.where(both > 0.0, 1.0, 0.0).astype(jnp.bfloat16)
        slots = jnp.dot(named, before, preferred_element_type=jnp.float32)
        hits = [
            jnp.where((slot_row == slots[j : j + 1]) & (rows[j] > 0.0), 1.0, 0.0) for j in range(2)
        ]
        place = jnp.concatenate(hits, 0).astype(jnp.bfloat16)
        places[q] = place
        x = jnp.dot(place, rows_all[r], preferred_element_type=jnp.float32).astype(jnp.bfloat16)
        y = jnp.dot(place, dy_all[r], preferred_element_type=jnp.float32)
        for j in range(2):
            gs = jnp.sum(hits[j] * rows[j], 1, keepdims=True)
            y_j = y[64 * j : 64 * j + 64]
            x_buf[j, at, :] = x[64 * j : 64 * j + 64]
            y_buf[j, at, :] = y_j.astype(jnp.bfloat16)
            d_buf[j, at, :] = (y_j * gs).astype(jnp.bfloat16)
            gs_buf[j, at, :] = gs

    def expert(j):
        x = x_buf[j]
        gu = jnp.dot(x, w_gu[j], preferred_element_type=jnp.float32)
        g, u = gu[:, :512], gu[:, 512:]
        s = jax.nn.sigmoid(g)
        silu = g * s
        act = (silu * u).astype(jnp.bfloat16)
        eout = (
            jnp.dot(act, w_dn[j], preferred_element_type=jnp.float32)
            .astype(jnp.bfloat16)
            .astype(jnp.float32)
        )
        dgs_buf[j] = jnp.sum(y_buf[j].astype(jnp.float32) * eout, 1, keepdims=True)
        o_buf[j] = (eout * gs_buf[j]).astype(jnp.bfloat16)
        d = d_buf[j]
        d_act = dot_nt(d, w_dn[j])
        d_g = (d_act * u * s * (1.0 + g * (1.0 - s))).astype(jnp.bfloat16)
        d_u = (d_act * silu).astype(jnp.bfloat16)
        d_gu = jnp.concatenate([d_g, d_u], 1)
        i_buf[j] = dot_nt(d_gu, w_gu[j]).astype(jnp.bfloat16)
        acc_gu[j] += dot_tn(x, d_gu)
        acc_dn[j] += dot_tn(act, d)

    def spread(a, q):
        r = 4 * a + q
        b, flip = q // 2, q % 2
        at = pl.ds(pl.multiple_of(q * 64, 64), 64)
        place = places[q]
        d, c = across(a, b, flip)
        o = jnp.concatenate([o_buf[0, at, :], o_buf[1, at, :]], 0)
        out_all[d * 2 + c] = dot_tn(place, o).astype(jnp.bfloat16)
        i = jnp.concatenate([i_buf[0, at, :], i_buf[1, at, :]], 0)
        din_all[r] = dot_tn(place, i).astype(jnp.bfloat16)
        hits = place.astype(jnp.float32)
        back = [
            jnp.sum(hits[64 * j : 64 * j + 64] * dgs_buf[j, at, :], 0, keepdims=True)
            for j in range(2)
        ]
        dg_out[r] = jnp.concatenate(back + [jnp.zeros((6, 128), jnp.float32)], 0)

        @pl.when(r > 0)
        def _():
            dg_push(a, b, flip).start()

    arrive(0, True)
    for load in loads:
        load.wait()

    def step(a, carry):
        lax.fori_loop(0, 4, lambda q, c: (gather(a, q), c)[1], 0)
        lax.fori_loop(0, 2, lambda j, c: (expert(j), c)[1], 0)
        lax.fori_loop(0, 4, lambda q, c: (spread(a, q), c)[1], 0)
        for b in range(2):
            sib_push(2 * a + b, 4 * a + 2 * b + 1).start()

        @pl.when(a > 0)
        def _():
            post(a - 1)

        @pl.when(a < 3)
        def _():
            arrive(a + 1, False)

        return carry

    lax.fori_loop(0, 4, step, 0)
    for i in range(1, 8):
        t = (tensor + i) % 8
        w_arrival(t, ctx).wait_recv()
        w_relay(t).start()
    post(3)
    for k in range(2):
        for r in range(1, 16):
            arrival(k, r).wait_send()
    stores = []
    for j in range(2):
        for h in range(8):
            rows_all[8 * j + h] = acc_gu[j, 128 * h : 128 * h + 128, :].astype(jnp.bfloat16)
        for h in range(4):
            dy_all[4 * j + h] = acc_dn[j, 128 * h : 128 * h + 128, :].astype(jnp.bfloat16)
    stores.append(pltpu.make_async_copy(rows_all, grad_ref.at[pl.ds(0, 16)], store_sem.at[0]))
    stores.append(
        pltpu.make_async_copy(
            dy_all.at[pl.ds(0, 8)], grad_ref.at[pl.ds(16, 8)], store_sem.at[1]
        )
    )
    stores.append(pltpu.make_async_copy(out_all, out_part_ref, store_sem.at[2]))
    for store in stores:
        store.start()

    for r in range(1, 16):
        a, b, flip = r // 4, (r // 2) % 2, r % 2
        dg_push(a, b, flip).wait()
    dg_in[0] = dg_out[0]
    d_gate = jnp.zeros((32, 128), jnp.float32)
    for r in range(16):
        d, c = across(r // 4, (r // 2) % 2, r % 2)
        got = dg_in[r]
        for j in range(2):
            d_gate = jnp.where(expert_row == (d * 2 + c) * 2 + j, got[j : j + 1], d_gate)
    d_gate_ref[...] = d_gate
    total = din_all[0].astype(jnp.float32)
    for ci in range(8):
        sib_push(ci, 2 * ci + 1).wait_send()
        if ci > 0:
            rs_push(ci // 2, ci % 2).wait()
    for ci in range(1, 8):
        total = total + summed[ci].astype(jnp.float32)
    d_rows_ref[...] = total
    for i in range(1, 8):
        t = (tensor + i) % 8
        w_arrival(t, 1 - ctx).wait_recv()
        w_push(i).wait_send()
        w_relay(t).wait_send()
    w_own.wait()
    for store in stores:
        store.wait()


def moe(rows, gates, dy, w_gate, w_up, w_down, w_t):
    bf, f32 = jnp.bfloat16, jnp.float32
    vmem, hbm = pl.BlockSpec(memory_space=pltpu.VMEM), pl.BlockSpec(memory_space=pl.ANY)
    sem = pltpu.SemaphoreType.DMA
    return pl.pallas_call(
        moe_kernel,
        out_shape=(
            jax.ShapeDtypeStruct((128, 1024), f32),
            jax.ShapeDtypeStruct((32, 128), f32),
            jax.ShapeDtypeStruct((16, 128, 1024), bf),
            jax.ShapeDtypeStruct((24, 128, 1024), bf),
            jax.ShapeDtypeStruct((8, 256, 1024), bf),
        ),
        in_specs=[vmem] * 2 + [hbm] * 5,
        out_specs=(vmem, vmem, hbm, hbm, hbm),
        scratch_shapes=[
            pltpu.VMEM((16, 128, 1024), bf),
            pltpu.VMEM((16, 32, 128), f32),
            pltpu.VMEM((16, 128, 1024), bf),
            pltpu.VMEM((2, 1024, 1024), bf),
            pltpu.VMEM((2, 512, 1024), bf),
            pltpu.VMEM((2, 1024, 1024), f32),
            pltpu.VMEM((2, 512, 1024), f32),
            pltpu.VMEM((16, 128, 1024), bf),
            pltpu.VMEM((16, 128, 1024), bf),
            pltpu.VMEM((8, 128, 1024), bf),
            pltpu.VMEM((8, 128, 1024), bf),
            pltpu.VMEM((16, 8, 128), f32),
            pltpu.VMEM((16, 8, 128), f32),
            pltpu.VMEM((4, 128, 128), bf),
            pltpu.VMEM((2, 256, 1024), bf),
            pltpu.VMEM((2, 256, 1024), bf),
            pltpu.VMEM((2, 256, 1024), bf),
            pltpu.VMEM((2, 256, 1024), bf),
            pltpu.VMEM((2, 256, 1024), bf),
            pltpu.VMEM((2, 256, 1), f32),
            pltpu.VMEM((2, 256, 1), f32),
            sem((8,)),
            sem((2, 16)),
            sem((2, 16)),
            sem((8,)),
            sem((8,)),
            sem((8,)),
            sem((8,)),
            sem((16,)),
            sem((16,)),
            sem((3,)),
            sem((16,)),
            sem((8, 2)),
        ],
        compiler_params=pltpu.CompilerParams(
            collective_id=1, has_side_effects=True, vmem_limit_bytes=60 << 20
        ),
        cost_estimate=pl.CostEstimate(
            flops=20_000_000_000, bytes_accessed=30_000_000, transcendentals=2_000_000
        ),
    )(rows, gates, dy, w_gate, w_up, w_down, w_t)


def attention_kernel(
    x_ref,
    dy_ref,
    segment_ref,
    norm1_ref,
    q_gain_ref,
    k_gain_ref,
    norm2_ref,
    router_ref,
    routes_ref,
    w_q_ref,
    w_k_ref,
    w_v_ref,
    w_out_ref,
    table_ref,
    rows2_ref,
    gates_ref,
    resid_ref,
    rows1_ref,
    raw_ref,
    inv_ref,
    q_ref,
    kv_ref,
    lse_ref,
    heads_ref,
    w_out_all_ref,
    dy_all_ref,
    w_t_ref,
    h_all,
    dy_all,
    w_all,
    w_q,
    w_k,
    w_v,
    w_t,
    raw,
    table,
    stat,
    stats,
    q_t,
    kv_own,
    kv_sib,
    k_own,
    k_sib,
    starts,
    heads,
    heads_all,
    load_sem,
    h_send,
    h_recv,
    dy_send,
    dy_recv,
    w_send,
    w_recv,
    s_send,
    s_recv,
    kv_sem,
    o_send,
    o_recv,
    store_sem,
):
    f32, bf = jnp.float32, jnp.bfloat16
    dp, ctx, me = lax.axis_index("dp"), lax.axis_index("ctx"), lax.axis_index("tensor")

    def side(i):
        return (dp, ctx, (me + i) % 8)

    def to(a, b, flip):
        d, c = across(a, b, flip)
        return (d, c, me)

    sibling = (dp, 1 - ctx, me)
    loads = [
        pltpu.make_async_copy(w_q_ref, w_q, load_sem.at[0]),
        pltpu.make_async_copy(w_k_ref, w_k, load_sem.at[1]),
        pltpu.make_async_copy(w_v_ref, w_v, load_sem.at[2]),
        pltpu.make_async_copy(w_out_ref, w_all.at[me], load_sem.at[3]),
        pltpu.make_async_copy(table_ref.at[ctx], table, load_sem.at[4]),
    ]
    for load in loads:
        load.start()
    barrier = pltpu.get_barrier_semaphore()
    for i in range(1, 8):
        pl.semaphore_signal(barrier, inc=1, device_id=side(i), device_id_type=MESH)
    for a in range(4):
        for b in range(2):
            if (a, b) != (0, 0):
                pl.semaphore_signal(barrier, inc=1, device_id=to(a, b, 0), device_id_type=MESH)
    pl.semaphore_signal(barrier, inc=1, device_id=sibling, device_id_type=MESH)
    x = x_ref[...].astype(f32)
    inv_one = lax.rsqrt(jnp.mean(x * x, -1, keepdims=True) + EPS)
    h_all[me] = (x * inv_one * norm1_ref[...]).astype(bf)
    dy_all[0] = dy_ref[...]
    pl.semaphore_wait(barrier, 15)

    def h_push(i):
        return copy_to(h_all.at[me], h_all.at[me], h_send.at[i], h_recv.at[me], side(i))

    def h_arrival(t):
        return copy_to(h_all.at[t], h_all.at[t], h_send.at[0], h_recv.at[t], sibling)

    def dy_push(a, b):
        back = 4 * back_place(a) + 2 * b
        return copy_to(
            dy_all.at[0], dy_all.at[back], dy_send.at[4 * a + 2 * b], dy_recv.at[back], to(a, b, 0)
        )

    def dy_relay(r):
        return copy_to(
            dy_all.at[r], dy_all.at[r + 1], dy_send.at[r + 1], dy_recv.at[r + 1], sibling
        )

    def dy_arrival(r):
        return copy_to(dy_all.at[r], dy_all.at[r], dy_send.at[r], dy_recv.at[r], sibling)

    for i in (1, 7, 2, 6, 3, 5, 4):
        h_push(i).start()
    dy_relay(0).start()
    for a in range(4):
        for b in range(2):
            if (a, b) != (0, 0):
                dy_push(a, b).start()

    for load in loads:
        load.wait()
    w_t[0:128, :] = jnp.transpose(w_q[...])
    w_t[128:192, :] = jnp.transpose(w_k[...])
    w_t[192:256, :] = jnp.transpose(w_v[...])
    seg = segment_ref[...]
    start = jnp.zeros((16, 128), f32)
    for s in range(1, 8):
        below = jnp.where(seg < s, 1.0, 0.0)
        count = jnp.sum(jnp.sum(below, 1, keepdims=True), 0, keepdims=True)
        start = jnp.where(seg == s, count, start)
    start = jnp.where(ctx == 0, start[:8], start[8:])
    for t in range(8):
        starts[0:1, 128 * t : 128 * t + 128] = start[t : t + 1]

    def project(i, carry):
        t = (me + i) % 8

        @pl.when(i > 0)
        def _():
            h_arrival(t).wait_recv()

        value = dot_nt(w_t[...], h_all[t])
        raw[t] = value
        square = value * value
        sums = [
            jnp.sum(square[0:128], 0, keepdims=True),
            jnp.sum(square[128:192], 0, keepdims=True),
            jnp.zeros((6, 128), f32),
        ]
        stat[t] = jnp.concatenate(sums, 0)
        return carry

    lax.fori_loop(0, 8, project, 0)
    stats[me] = stat[...]

    def s_push(i):
        return copy_to(stats.at[me], stats.at[me], s_send.at[i], s_recv.at[me], side(i))

    def s_arrival(t):
        return copy_to(stats.at[t], stats.at[t], s_send.at[0], s_recv.at[t], sibling)

    for i in range(1, 8):
        s_push(i).start()
    store_rows = pltpu.make_async_copy(h_all, rows1_ref, store_sem.at[0])
    store_raw = pltpu.make_async_copy(raw, raw_ref, store_sem.at[1])
    store_wt = pltpu.make_async_copy(w_t, w_t_ref, store_sem.at[8])
    store_rows.start()
    store_raw.start()
    store_wt.start()

    def w_push(i):
        half = w_all.at[me, pl.ds(pl.multiple_of(ctx * 64, 64), 64)]
        return copy_to(half, half, w_send.at[i], w_recv.at[me, ctx], side(i))

    def w_relay(t):
        half = w_all.at[t, pl.ds(pl.multiple_of(ctx * 64, 64), 64)]
        return copy_to(half, half, w_send.at[8 + t], w_recv.at[t, ctx], sibling)

    def w_arrival(t, c):
        half = w_all.at[t, pl.ds(pl.multiple_of(c * 64, 64), 64)]
        return copy_to(half, half, w_send.at[0], w_recv.at[t, c], sibling)

    for i in (1, 7, 2, 6, 3, 5, 4):
        w_push(i).start()
    gain_q = column(q_gain_ref[...])
    gain_k = column(jnp.concatenate([k_gain_ref[...], jnp.zeros((1, 64), f32)], 1))[:64]
    for i in range(1, 8):
        s_arrival((me + i) % 8).wait_recv()

    def finish(t, carry):
        at = pl.ds(pl.multiple_of(t * 128, 128), 128)
        sums = stats[0, t]
        for s in range(1, 8):
            sums = sums + stats[s, t]
        width = jnp.where(lax.broadcasted_iota(jnp.int32, (8, 128), 0) == 0, 1024.0, 512.0)
        inv = lax.rsqrt(sums / width + EPS)
        inv_ref[t] = inv
        value = raw[t]
        cos_part, sin_part = table[0, :, at], table[1, :, at]
        queries = turn(value[0:128] * inv[0:1] * gain_q, cos_part, sin_part).astype(bf)
        keys = turn(value[128:192] * inv[1:2] * gain_k, cos_part, sin_part).astype(bf)
        q_t[:, at] = queries
        kv_own[0:64, at] = keys
        kv_own[64:128, at] = value[192:256].astype(bf)
        k_own[at, :] = jnp.transpose(keys)
        return carry

    lax.fori_loop(0, 8, finish, 0)
    kv_push = copy_to(kv_own, kv_sib, kv_sem.at[0], kv_sem.at[1], sibling)
    kv_push.start()

    key_row = lax.broadcasted_iota(jnp.int32, (256, 256), 0).astype(f32)
    query_lane = lax.broadcasted_iota(jnp.int32, (256, 256), 1).astype(f32)
    base = (ctx * 1024).astype(f32)

    def attend(n, carry):
        i, h = n // 2, n % 2
        at = pl.ds(pl.multiple_of(i * 256, 256), 256)
        q = q_t[pl.ds(pl.multiple_of(h * 64, 64), 64), at] * 0.125
        begin = starts[0:1, at]

        def block(keys, values, first_key, state, causal):
            top, total, acc = state
            s = jnp.dot(keys, q, preferred_element_type=f32)
            ok = key_row >= begin - first_key
            if causal:
                ok = ok & (key_row <= query_lane)
            s = jnp.where(ok, s, MASKED)
            new_top = jnp.maximum(top, jnp.max(s, 0, keepdims=True))
            e = jnp.exp(s - new_top)
            shrink = jnp.exp(top - new_top)
            total = total * shrink + jnp.sum(e, 0, keepdims=True)
            acc = acc * shrink + jnp.dot(values, e.astype(bf), preferred_element_type=f32)
            return new_top, total, acc

        state = (jnp.full((1, 256), MASKED, f32), jnp.zeros((1, 256), f32), jnp.zeros((64, 256), f32))
        state = block(
            k_own[at, :], kv_own[64:128, at], base + (i * 256).astype(f32), state, True
        )

        def own(j, state):
            ks = pl.ds(pl.multiple_of(j * 256, 256), 256)
            return block(k_own[ks, :], kv_own[64:128, ks], base + (j * 256).astype(f32), state, False)

        state = lax.fori_loop(0, i, own, state)

        def other(j, state):
            ks = pl.ds(pl.multiple_of(j * 256, 256), 256)
            return block(k_sib[ks, :], kv_sib[64:128, ks], (j * 256).astype(f32), state, False)

        top, total, acc = lax.fori_loop(0, 4 * ctx, other, state)
        out = (acc / total).astype(bf)
        hs = pl.ds(pl.multiple_of(h * 64, 64), 64)
        heads[2 * i, hs, :] = out[:, :128]
        heads[2 * i + 1, hs, :] = out[:, 128:]
        lse_ref[h, 0:1, at] = top + jnp.log(total)
        return carry

    kv_push.wait()

    def straighten(t, carry):
        at = pl.ds(pl.multiple_of(t * 128, 128), 128)
        k_sib[at, :] = jnp.transpose(kv_sib[0:64, at])
        return carry

    lax.fori_loop(0, 8, straighten, 0)
    lax.fori_loop(0, 8, attend, 0)

    def o_push(i):
        return copy_to(
            heads.at[(me + i) % 8], heads_all.at[me], o_send.at[i], o_recv.at[me], side(i)
        )

    def o_arrival(t):
        return copy_to(heads_all.at[t], heads_all.at[t], o_send.at[0], o_recv.at[t], sibling)

    for i in range(1, 8):
        o_push(i).start()
    heads_all[me] = heads[me]
    stores = [
        pltpu.make_async_copy(q_t, q_ref, store_sem.at[2]),
        pltpu.make_async_copy(kv_own, kv_ref.at[0], store_sem.at[3]),
        pltpu.make_async_copy(kv_sib, kv_ref.at[1], store_sem.at[4]),
        pltpu.make_async_copy(heads, heads_ref, store_sem.at[5]),
    ]
    for store in stores:
        store.start()

    def pass_on(i, carry):
        t = (me + i) % 8
        w_arrival(t, ctx).wait_recv()
        w_relay(t).start()
        return carry

    lax.fori_loop(1, 8, pass_on, 0)

    def pass_dy(c, carry):
        dy_arrival(2 * c).wait_recv()
        dy_relay(2 * c).start()
        return carry

    lax.fori_loop(1, 8, pass_dy, 0)
    for i in range(1, 8):
        t = (me + i) % 8
        w_arrival(t, 1 - ctx).wait_recv()
        o_arrival(t).wait_recv()
    store_w = pltpu.make_async_copy(w_all, w_out_all_ref, store_sem.at[6])
    store_w.start()
    attended = dot_tn(heads_all[...].reshape(1024, 128), w_all[...].reshape(1024, 1024))
    resid = x + attended
    resid_ref[...] = resid
    inv_two = lax.rsqrt(jnp.mean(resid * resid, -1, keepdims=True) + EPS)
    rows2 = (resid * inv_two * norm2_ref[...]).astype(bf)
    rows2_ref[...] = rows2
    logits = jnp.transpose(jnp.dot(rows2, router_ref[...], preferred_element_type=f32))
    expert_row = lax.broadcasted_iota(jnp.int32, (32, 128), 0)
    routes = jnp.transpose(routes_ref[...])
    named = routes[0:1] == expert_row
    for k in range(1, 8):
        named = named | (routes[k : k + 1] == expert_row)
    chosen = jnp.where(named, logits, MASKED)
    weight = jnp.where(named, jnp.exp(chosen - jnp.max(chosen, 0, keepdims=True)), 0.0)
    gates_ref[...] = weight / jnp.sum(weight, 0, keepdims=True)

    for c in range(8):
        dy_arrival(2 * c + 1).wait_recv()
    store_dy = pltpu.make_async_copy(dy_all, dy_all_ref, store_sem.at[7])
    store_dy.start()
    for i in range(1, 8):
        h_push(i).wait_send()
        s_push(i).wait_send()
        w_push(i).wait_send()
        w_relay((me + i) % 8).wait_send()
        o_push(i).wait_send()
        dy_push(i // 2, i % 2).wait_send()
    for c in range(8):
        dy_relay(2 * c).wait_send()
    for store in [store_rows, store_raw, store_wt, store_w, store_dy] + stores:
        store.wait()


def attention(x, dy, segment, norm1, q_gain, k_gain, norm2, router, routes, w_q, w_k, w_v, w_out):
    bf, f32 = jnp.bfloat16, jnp.float32
    vmem, hbm = pl.BlockSpec(memory_space=pltpu.VMEM), pl.BlockSpec(memory_space=pl.ANY)
    sem = pltpu.SemaphoreType.DMA
    shape = jax.ShapeDtypeStruct
    table = jnp.asarray(rope_constants(2048, 32))
    return pl.pallas_call(
        attention_kernel,
        out_shape=(
            shape((128, 1024), bf),
            shape((32, 128), f32),
            shape((128, 1024), f32),
            shape((8, 128, 1024), bf),
            shape((8, 256, 128), f32),
            shape((8, 8, 128), f32),
            shape((128, 1024), bf),
            shape((2, 128, 1024), bf),
            shape((2, 8, 1024), f32),
            shape((8, 128, 128), bf),
            shape((8, 128, 1024), bf),
            shape((16, 128, 1024), bf),
            shape((256, 1024), bf),
        ),
        in_specs=[vmem] * 9 + [hbm] * 5,
        out_specs=(vmem, vmem, vmem, hbm, hbm, vmem, hbm, hbm, vmem, hbm, hbm, hbm, hbm),
        scratch_shapes=[
            pltpu.VMEM((8, 128, 1024), bf),
            pltpu.VMEM((16, 128, 1024), bf),
            pltpu.VMEM((8, 128, 1024), bf),
            pltpu.VMEM((1024, 128), bf),
            pltpu.VMEM((1024, 64), bf),
            pltpu.VMEM((1024, 64), bf),
            pltpu.VMEM((256, 1024), bf),
            pltpu.VMEM((8, 256, 128), f32),
            pltpu.VMEM((2, 32, 1024), f32),
            pltpu.VMEM((8, 8, 128), f32),
            pltpu.VMEM((8, 8, 8, 128), f32),
            pltpu.VMEM((128, 1024), bf),
            pltpu.VMEM((128, 1024), bf),
            pltpu.VMEM((128, 1024), bf),
            pltpu.VMEM((1024, 64), bf),
            pltpu.VMEM((1024, 64), bf),
            pltpu.VMEM((8, 1024), f32),
            pltpu.VMEM((8, 128, 128), bf),
            pltpu.VMEM((8, 128, 128), bf),
            sem((5,)),
            sem((8,)),
            sem((8,)),
            sem((16,)),
            sem((16,)),
            sem((16,)),
            sem((8, 2)),
            sem((8,)),
            sem((8,)),
            sem((2,)),
            sem((8,)),
            sem((8,)),
            sem((9,)),
        ],
        compiler_params=pltpu.CompilerParams(
            collective_id=2, has_side_effects=True, vmem_limit_bytes=56 << 20
        ),
        cost_estimate=pl.CostEstimate(
            flops=5_000_000_000, bytes_accessed=20_000_000, transcendentals=4_000_000
        ),
    )(
        x,
        dy,
        segment.reshape(16, 128),
        norm1.reshape(1, 1024),
        q_gain.reshape(1, 128),
        k_gain.reshape(1, 64),
        norm2.reshape(1, 1024),
        router,
        routes,
        w_q,
        w_k,
        w_v,
        w_out,
        table,
    )


def backward_kernel(
    x_ref,
    dy_ref,
    d_rows_ref,
    d_gate_ref,
    gates_ref,
    rows2_ref,
    resid_ref,
    router_ref,
    norm1_ref,
    norm2_ref,
    q_gain_ref,
    k_gain_ref,
    segment_ref,
    inv_ref,
    lse_ref,
    rows1_ref,
    raw_ref,
    q_ref,
    kv_ref,
    heads_ref,
    w_out_ref,
    w_all_ref,
    table_ref,
    grad_x_ref,
    norm1_out_ref,
    pack_ref,
    rows1,
    raw,
    q_t,
    kv_own,
    kv_sib,
    heads,
    w_out,
    w_all,
    table,
    starts,
    d_resid,
    datt_all,
    dh_send,
    dh_all,
    tiny,
    q_cat,
    q_nat,
    d_cat,
    d_nat,
    lanes,
    k_nat,
    v_nat,
    dq_acc,
    dk_acc,
    dv_acc,
    dkv_out,
    dkv_in,
    terms,
    stat,
    stats,
    dqkv,
    dqkv_all,
    heads2,
    pack,
    pack_sib,
    pack_in,
    result,
    n1,
    n1_chips,
    n1_sib,
    load_sem,
    a_send,
    a_recv,
    dh_send_sem,
    dh_recv,
    t_send,
    t_recv,
    s_send,
    s_recv,
    dkv_sem,
    o_send,
    o_recv,
    p_sem,
    rs_send,
    rs_recv,
    g_send,
    g_recv,
    gs_send,
    gs_recv,
    n_send,
    n_recv,
    m_send,
    m_recv,
    ns_sem,
):
    f32, bf = jnp.float32, jnp.bfloat16
    dp, ctx, me = lax.axis_index("dp"), lax.axis_index("ctx"), lax.axis_index("tensor")
    sibling = (dp, 1 - ctx, me)

    def side(i):
        return (dp, ctx, (me + i) % 8)

    def chip(i):
        return ((dp + i) % 8, ctx, me)

    sources = (rows1_ref, raw_ref, q_ref, kv_ref.at[0], kv_ref.at[1], heads_ref, w_out_ref)
    targets = (rows1, raw, q_t, kv_own, kv_sib, heads, w_out)
    loads = [
        pltpu.make_async_copy(s, t, load_sem.at[n])
        for n, (s, t) in enumerate(zip(sources, targets, strict=True))
    ]
    loads.append(pltpu.make_async_copy(w_all_ref, w_all, load_sem.at[7]))
    loads.append(pltpu.make_async_copy(table_ref.at[ctx], table, load_sem.at[8]))
    for load in loads:
        load.start()
    barrier = pltpu.get_barrier_semaphore()
    for i in range(1, 8):
        pl.semaphore_signal(barrier, inc=1, device_id=side(i), device_id_type=MESH)
        pl.semaphore_signal(barrier, inc=1, device_id=chip(i), device_id_type=MESH)
    pl.semaphore_signal(barrier, inc=1, device_id=sibling, device_id_type=MESH)

    gates, d_gate = gates_ref[...], d_gate_ref[...]
    d_logits = gates * (d_gate - jnp.sum(gates * d_gate, 0, keepdims=True))
    d_normed = d_rows_ref[...] + lax.dot_general(
        jnp.transpose(d_logits),
        router_ref[...].astype(f32),
        (((1,), (1,)), ((), ())),
        preferred_element_type=f32,
        precision=lax.Precision.HIGHEST,
    )
    resid = resid_ref[...]
    inv_two = lax.rsqrt(jnp.mean(resid * resid, -1, keepdims=True) + EPS)
    res_hat = resid * inv_two
    scaled = d_normed * norm2_ref[...]
    d_res = dy_ref[...].astype(f32) + inv_two * (
        scaled - res_hat * jnp.mean(scaled * res_hat, -1, keepdims=True)
    )
    d_resid[...] = d_res
    datt = d_res.astype(bf)
    datt_all[me] = datt
    for n in (6,):
        loads[n].wait()
    d_heads = dot_nt(w_out[...].reshape(1024, 1024), datt).astype(bf)
    dh_send[...] = d_heads.reshape(8, 128, 128)
    dh_all[me] = dh_send[me]
    pl.semaphore_wait(barrier, 15)

    def dh_push(i):
        return copy_to(
            dh_send.at[(me + i) % 8], dh_all.at[me], dh_send_sem.at[i], dh_recv.at[me], side(i)
        )

    def dh_arrival(t):
        return copy_to(dh_all.at[t], dh_all.at[t], dh_send_sem.at[0], dh_recv.at[t], sibling)

    for i in range(1, 8):
        dh_push(i).start()

    norm2_part = jnp.sum(d_normed * res_hat, 0, keepdims=True)
    router_part = jnp.dot(
        d_logits,
        rows2_ref[...].astype(f32),
        preferred_element_type=f32,
        precision=lax.Precision.HIGHEST,
    )
    tiny[me] = jnp.concatenate(
        [router_part, norm2_part, jnp.zeros((15, 1024), f32)], 0
    ).astype(bf)

    def t_push(i):
        return copy_to(tiny.at[me], tiny.at[me], t_send.at[i], t_recv.at[me], side(i))

    def t_arrival(t):
        return copy_to(tiny.at[t], tiny.at[t], t_send.at[0], t_recv.at[t], sibling)

    def a_push(i):
        return copy_to(datt_all.at[me], datt_all.at[me], a_send.at[i], a_recv.at[me], side(i))

    def a_arrival(t):
        return copy_to(datt_all.at[t], datt_all.at[t], a_send.at[0], a_recv.at[t], sibling)

    for i in range(1, 8):
        t_push(i).start()
    for i in (1, 7, 2, 6, 3, 5, 4):
        a_push(i).start()

    for n in (0, 1, 2, 3, 4, 5, 7, 8):
        loads[n].wait()
    seg = segment_ref[...]
    start = jnp.zeros((16, 128), f32)
    for s in range(1, 8):
        below = jnp.where(seg < s, 1.0, 0.0)
        count = jnp.sum(jnp.sum(below, 1, keepdims=True), 0, keepdims=True)
        start = jnp.where(seg == s, count, start)
    start = jnp.where(ctx == 0, start[:8], start[8:])
    for t in range(8):
        starts[0:1, 128 * t : 128 * t + 128] = start[t : t + 1]

    def lay_out(t, carry):
        at = pl.ds(pl.multiple_of(t * 128, 128), 128)
        i, half = t // 2, t % 2
        q = q_t[:, at] * 0.125
        for h in range(2):
            spot = pl.ds(pl.multiple_of(h * 256 + half * 128, 128), 128)
            q_h = q[64 * h : 64 * h + 64]
            q_cat[i, :, spot] = q_h
            q_nat[i, spot, :] = jnp.transpose(q_h)
            lanes[i, 0:1, spot] = lse_ref[h, 0:1, at]
            lanes[i, 2:3, spot] = starts[0:1, at]
        for n, kv in enumerate((kv_own, kv_sib)):
            k_nat[n, at, :] = jnp.transpose(kv[0:64, at])
            v_nat[n, at, :] = jnp.transpose(kv[64:128, at])
        heads2[:, at] = heads[t]
        return carry

    lax.fori_loop(0, 8, lay_out, 0)
    dk_acc[...] = jnp.zeros_like(dk_acc)
    dv_acc[...] = jnp.zeros_like(dv_acc)
    dq_acc[...] = jnp.zeros_like(dq_acc)
    for i in range(1, 8):
        dh_arrival((me + i) % 8).wait_recv()

    def lay_dh(t, carry):
        i, half = t // 2, t % 2
        d, o = dh_all[t], heads[t]
        product = d.astype(f32) * o.astype(f32)
        for h in range(2):
            spot = pl.ds(pl.multiple_of(h * 256 + half * 128, 128), 128)
            d_h = d[64 * h : 64 * h + 64]
            d_cat[i, :, spot] = d_h
            d_nat[i, spot, :] = jnp.transpose(d_h)
            lanes[i, 1:2, spot] = jnp.sum(product[64 * h : 64 * h + 64], 0, keepdims=True)
        return carry

    lax.fori_loop(0, 8, lay_dh, 0)
    key_row = lax.broadcasted_iota(jnp.int32, (256, 512), 0).astype(f32)
    query_lane = (lax.broadcasted_iota(jnp.int32, (256, 512), 1) % 256).astype(f32)
    base = (ctx * 1024).astype(f32)

    def block(n, i, j, first_key, causal):
        ks = pl.ds(pl.multiple_of(j * 256, 256), 256)
        kv = (kv_own, kv_sib)[n]
        s = jnp.dot(k_nat[n, ks, :], q_cat[i], preferred_element_type=f32)
        ok = key_row >= lanes[i, 2:3, :] - first_key
        if causal:
            ok = ok & (key_row <= query_lane)
        p = jnp.exp(jnp.where(ok, s, MASKED) - lanes[i, 0:1, :])
        dp_ = jnp.dot(v_nat[n, ks, :], d_cat[i], preferred_element_type=f32)
        ds = (p * (dp_ - lanes[i, 1:2, :])).astype(bf)
        dv_acc[n, ks, :] += jnp.dot(p.astype(bf), d_nat[i], preferred_element_type=f32)
        dk_acc[n, ks, :] += jnp.dot(ds, q_nat[i], preferred_element_type=f32)
        dq_acc[i] += jnp.dot(kv[0:64, ks], ds, preferred_element_type=f32)

    def cross(n, carry):
        block(1, n // 4, n % 4, ((n % 4) * 256).astype(f32), False)
        return carry

    lax.fori_loop(0, 16 * ctx, cross, 0)
    dkv_push = copy_to(dkv_out, dkv_in, dkv_sem.at[0], dkv_sem.at[1], sibling)

    def upright(t, carry):
        at = pl.ds(pl.multiple_of(t * 128, 128), 128)
        dkv_out[0:64, at] = jnp.transpose(dk_acc[1, at, :]).astype(bf)
        dkv_out[64:128, at] = jnp.transpose(dv_acc[1, at, :]).astype(bf)
        return carry

    lax.fori_loop(0, 8, upright, 0)
    dkv_push.start()

    def within(i, carry):
        def full(j, c):
            block(0, i, j, base + (j * 256).astype(f32), False)
            return c

        lax.fori_loop(0, i, full, 0)
        block(0, i, i, base + (i * 256).astype(f32), True)
        return carry

    lax.fori_loop(0, 4, within, 0)
    gain_q = column(q_gain_ref[...])
    gain_k = column(jnp.concatenate([k_gain_ref[...], jnp.zeros((1, 64), f32)], 1))[:64]
    dkv_push.wait()

    def unturn(t, sums):
        at = pl.ds(pl.multiple_of(t * 128, 128), 128)
        i, half = t // 2, t % 2
        parts = [
            dq_acc[i, :, pl.ds(pl.multiple_of(h * 256 + half * 128, 128), 128)] for h in range(2)
        ]
        cos_part, sin_part = table[0, :, at], -table[1, :, at]
        inv = inv_ref[t]
        d_q = turn(jnp.concatenate(parts, 0) * 0.125, cos_part, sin_part)
        came = dkv_in[:, at].astype(f32)
        d_k = turn(jnp.transpose(dk_acc[0, at, :]) + came[0:64], cos_part, sin_part)
        d_v = jnp.transpose(dv_acc[0, at, :]) + came[64:128]
        q_hat, k_hat = raw[t, 0:128] * inv[0:1], raw[t, 128:192] * inv[1:2]
        q_sum, k_sum = sums[0] + d_q * q_hat, sums[1] + d_k * k_hat
        q_term, k_term = d_q * gain_q, d_k * gain_k
        terms[t, 0:128] = q_term
        terms[t, 128:192] = k_term
        dqkv[t, 192:256] = d_v.astype(bf)
        rows = [
            jnp.sum(q_term * q_hat, 0, keepdims=True),
            jnp.sum(k_term * k_hat, 0, keepdims=True),
            jnp.zeros((6, 128), f32),
        ]
        stat[t] = jnp.concatenate(rows, 0)
        return q_sum, k_sum

    q_sum, k_sum = lax.fori_loop(
        0, 8, unturn, (jnp.zeros((128, 128), f32), jnp.zeros((64, 128), f32))
    )
    stats[me] = stat[...]

    def s_push(i):
        return copy_to(stats.at[me], stats.at[me], s_send.at[i], s_recv.at[me], side(i))

    def s_arrival(t):
        return copy_to(stats.at[t], stats.at[t], s_send.at[0], s_recv.at[t], sibling)

    for i in range(1, 8):
        s_push(i).start()
    for i in range(1, 8):
        a_arrival((me + i) % 8).wait_recv()
    pack[256:384, :] = jnp.dot(
        heads2[...], datt_all[...].reshape(1024, 1024), preferred_element_type=f32
    ).astype(bf)
    for i in range(1, 8):
        t_arrival((me + i) % 8).wait_recv()
    total = tiny[0].astype(f32)
    for t in range(1, 8):
        total = total + tiny[t].astype(f32)
    q_row = jnp.sum(jnp.transpose(q_sum), 0, keepdims=True)
    k_row = jnp.sum(jnp.transpose(k_sum), 0, keepdims=True)
    gain_row = jnp.concatenate([q_row, k_row, jnp.zeros((1, 1024 - 192), f32)], 1)
    extra = jnp.concatenate([total[0:33], gain_row, jnp.zeros((94, 1024), f32)], 0)
    pack[384:512, :] = extra.astype(bf)
    for i in range(1, 8):
        s_arrival((me + i) % 8).wait_recv()

    def finish(t, carry):
        at = pl.ds(pl.multiple_of(t * 128, 128), 128)
        inner = stats[0, t]
        for s in range(1, 8):
            inner = inner + stats[s, t]
        inv = inv_ref[t]
        q_hat, k_hat = raw[t, 0:128] * inv[0:1], raw[t, 128:192] * inv[1:2]
        d_q = inv[0:1] * (terms[t, 0:128] - q_hat * (inner[0:1] / 1024.0))
        d_k = inv[1:2] * (terms[t, 128:192] - k_hat * (inner[1:2] / 512.0))
        dqkv[t, 0:128] = d_q.astype(bf)
        dqkv[t, 128:192] = d_k.astype(bf)
        return carry

    lax.fori_loop(0, 8, finish, 0)

    def o_push(i):
        return copy_to(
            dqkv.at[(me + i) % 8], dqkv_all.at[me], o_send.at[i], o_recv.at[me], side(i)
        )

    def o_arrival(t):
        return copy_to(dqkv_all.at[t], dqkv_all.at[t], o_send.at[0], o_recv.at[t], sibling)

    for i in range(1, 8):
        o_push(i).start()
    dqkv_all[me] = dqkv[me]
    grad_qkv = jnp.zeros((256, 1024), f32)
    for t in range(8):
        grad_qkv = grad_qkv + jnp.dot(dqkv[t], rows1[t], preferred_element_type=f32)
    pack[0:256, :] = grad_qkv.astype(bf)
    mine = pl.ds(pl.multiple_of(ctx * 256, 256), 256)
    theirs = pl.ds(pl.multiple_of((1 - ctx) * 256, 256), 256)
    p_push = copy_to(pack.at[theirs], pack_sib, p_sem.at[0], p_sem.at[1], sibling)
    p_push.start()
    for i in range(1, 8):
        o_arrival((me + i) % 8).wait_recv()
    d_rows1 = dot_tn(dqkv_all[...].reshape(2048, 128), w_all[...].reshape(2048, 1024))
    x = x_ref[...].astype(f32)
    inv_one = lax.rsqrt(jnp.mean(x * x, -1, keepdims=True) + EPS)
    x_hat = x * inv_one
    norm1_part = jnp.sum(d_rows1 * x_hat, 0, keepdims=True)
    n1[me] = jnp.concatenate([norm1_part[:, 128 * t : 128 * t + 128] for t in range(8)], 0)

    def n_push(i):
        return copy_to(n1.at[me], n1.at[me], n_send.at[i], n_recv.at[me], side(i))

    def n_arrival(t):
        return copy_to(n1.at[t], n1.at[t], n_send.at[0], n_recv.at[t], sibling)

    for i in range(1, 8):
        n_push(i).start()
    p_push.wait()
    pack[mine, :] = (pack[mine, :].astype(f32) + pack_sib[...].astype(f32)).astype(bf)

    def rs_push(i):
        to = (dp + i) % 8
        rows = pack.at[pl.ds(pl.multiple_of(ctx * 256 + to * 32, 32), 32)]
        return copy_to(rows, pack_in.at[dp], rs_send.at[i], rs_recv.at[dp], chip(i))

    def rs_arrival(d):
        return copy_to(pack_in.at[d], pack_in.at[d], rs_send.at[0], rs_recv.at[d], sibling)

    for i in range(1, 8):
        rs_push(i).start()
    scaled = d_rows1 * norm1_ref[...]
    grad_x_ref[...] = (
        d_resid[...] + inv_one * (scaled - x_hat * jnp.mean(scaled * x_hat, -1, keepdims=True))
    ).astype(bf)
    for i in range(1, 8):
        n_arrival((me + i) % 8).wait_recv()
    norm1_sum = n1[0]
    for t in range(1, 8):
        norm1_sum = norm1_sum + n1[t]
    n1_chips[dp] = norm1_sum

    def m_push(i):
        return copy_to(n1_chips.at[dp], n1_chips.at[dp], m_send.at[i], m_recv.at[dp], chip(i))

    def m_arrival(d):
        return copy_to(n1_chips.at[d], n1_chips.at[d], m_send.at[0], m_recv.at[d], sibling)

    for i in range(1, 8):
        m_push(i).start()
    pack_in[dp] = pack[pl.ds(pl.multiple_of(ctx * 256 + dp * 32, 32), 32), :]
    for i in range(1, 8):
        rs_arrival((dp + i) % 8).wait_recv()
    owned = pack_in[0].astype(f32)
    for d in range(1, 8):
        owned = owned + pack_in[d].astype(f32)
    result[ctx, dp] = owned.astype(bf)

    def g_push(i):
        return copy_to(
            result.at[ctx, dp], result.at[ctx, dp], g_send.at[i], g_recv.at[dp], chip(i)
        )

    def g_arrival(d):
        return copy_to(result.at[ctx, d], result.at[ctx, d], g_send.at[0], g_recv.at[d], sibling)

    def g_relay(d):
        return copy_to(
            result.at[ctx, d], result.at[ctx, d], gs_send.at[d], gs_recv.at[d], sibling
        )

    def g_sib_arrival(d):
        place = result.at[1 - ctx, d]
        return copy_to(place, place, gs_send.at[d], gs_recv.at[d], sibling)

    for i in range(1, 8):
        g_push(i).start()
    g_relay(dp).start()
    for i in range(1, 8):
        m_arrival((dp + i) % 8).wait_recv()
    norm1_sum = n1_chips[0]
    for d in range(1, 8):
        norm1_sum = norm1_sum + n1_chips[d]
    n1_sib[0] = norm1_sum
    ns_push = copy_to(n1_sib.at[0], n1_sib.at[1], ns_sem.at[0], ns_sem.at[1], sibling)
    ns_push.start()

    def pass_on(i, carry):
        d = (dp + i) % 8
        g_arrival(d).wait_recv()
        g_relay(d).start()
        return carry

    lax.fori_loop(1, 8, pass_on, 0)
    ns_push.wait()
    norm1_out_ref[...] = n1_sib[0] + n1_sib[1]
    for d in range(8):
        g_sib_arrival(d).wait_recv()
        g_relay(d).wait_send()
    pack_ref[...] = result[...].reshape(512, 1024)
    for i in range(1, 8):
        dh_push(i).wait_send()
        t_push(i).wait_send()
        a_push(i).wait_send()
        s_push(i).wait_send()
        o_push(i).wait_send()
        n_push(i).wait_send()
        rs_push(i).wait_send()
        m_push(i).wait_send()
        g_push(i).wait_send()


def backward(small, large):
    bf, f32 = jnp.bfloat16, jnp.float32
    vmem, hbm = pl.BlockSpec(memory_space=pltpu.VMEM), pl.BlockSpec(memory_space=pl.ANY)
    sem = pltpu.SemaphoreType.DMA
    shape = jax.ShapeDtypeStruct
    table = jnp.asarray(rope_constants(2048, 32))
    return pl.pallas_call(
        backward_kernel,
        out_shape=(shape((128, 1024), bf), shape((8, 128), f32), shape((512, 1024), bf)),
        in_specs=[vmem] * 15 + [hbm] * 8,
        out_specs=(vmem, vmem, vmem),
        scratch_shapes=[
            pltpu.VMEM((8, 128, 1024), bf),
            pltpu.VMEM((8, 256, 128), f32),
            pltpu.VMEM((128, 1024), bf),
            pltpu.VMEM((128, 1024), bf),
            pltpu.VMEM((128, 1024), bf),
            pltpu.VMEM((8, 128, 128), bf),
            pltpu.VMEM((8, 128, 1024), bf),
            pltpu.VMEM((8, 256, 1024), bf),
            pltpu.VMEM((2, 32, 1024), f32),
            pltpu.VMEM((8, 1024), f32),
            pltpu.VMEM((128, 1024), f32),
            pltpu.VMEM((8, 128, 1024), bf),
            pltpu.VMEM((8, 128, 128), bf),
            pltpu.VMEM((8, 128, 128), bf),
            pltpu.VMEM((8, 48, 1024), bf),
            pltpu.VMEM((4, 64, 512), bf),
            pltpu.VMEM((4, 512, 64), bf),
            pltpu.VMEM((4, 64, 512), bf),
            pltpu.VMEM((4, 512, 64), bf),
            pltpu.VMEM((4, 8, 512), f32),
            pltpu.VMEM((2, 1024, 64), bf),
            pltpu.VMEM((2, 1024, 64), bf),
            pltpu.VMEM((4, 64, 512), f32),
            pltpu.VMEM((2, 1024, 64), f32),
            pltpu.VMEM((2, 1024, 64), f32),
            pltpu.VMEM((128, 1024), bf),
            pltpu.VMEM((128, 1024), bf),
            pltpu.VMEM((8, 192, 128), f32),
            pltpu.VMEM((8, 8, 128), f32),
            pltpu.VMEM((8, 8, 8, 128), f32),
            pltpu.VMEM((8, 256, 128), bf),
            pltpu.VMEM((8, 256, 128), bf),
            pltpu.VMEM((128, 1024), bf),
            pltpu.VMEM((512, 1024), bf),
            pltpu.VMEM((256, 1024), bf),
            pltpu.VMEM((8, 32, 1024), bf),
            pltpu.VMEM((2, 8, 32, 1024), bf),
            pltpu.VMEM((8, 8, 128), f32),
            pltpu.VMEM((8, 8, 128), f32),
            pltpu.VMEM((2, 8, 128), f32),
            sem((9,)),
        ]
        + [sem((8,))] * 8
        + [sem((2,))]
        + [sem((8,))] * 2
        + [sem((2,))]
        + [sem((8,))] * 10
        + [sem((2,))],
        compiler_params=pltpu.CompilerParams(
            collective_id=3, has_side_effects=True, vmem_limit_bytes=56 << 20
        ),
        cost_estimate=pl.CostEstimate(
            flops=10_000_000_000, bytes_accessed=20_000_000, transcendentals=4_000_000
        ),
    )(*small, *large, table)


def shards(
    hidden_in,
    segment,
    norm1_gain,
    w_query,
    w_key,
    w_value,
    q_gain,
    k_gain,
    w_out,
    norm2_gain,
    router,
    w_gate,
    w_up,
    w_down,
    routes,
    cotangent,
):
    f32, bf = jnp.float32, jnp.bfloat16
    rows2, gates, resid, rows1, raw, inv, q_t, kv, lse, heads, w_out_all, dy_all, w_t = attention(
        hidden_in,
        cotangent,
        segment,
        norm1_gain,
        q_gain,
        k_gain,
        norm2_gain,
        router,
        routes,
        w_query,
        w_key,
        w_value,
        w_out,
    )
    d_rows, d_gate, out_part, grads, w_all = moe(
        rows2, gates, dy_all, w_gate, w_up, w_down, w_t
    )
    mixed = lax.psum_scatter(
        out_part.reshape(-1, 1024), ("dp", "ctx"), scatter_dimension=0, tiled=True
    )
    output = (resid + mixed.astype(f32)).astype(bf)
    grad_x, norm1_sum, pack = backward(
        (
            hidden_in,
            cotangent,
            d_rows,
            d_gate,
            gates,
            rows2,
            resid,
            router,
            norm1_gain.reshape(1, 1024),
            norm2_gain.reshape(1, 1024),
            q_gain.reshape(1, 128),
            k_gain.reshape(1, 64),
            segment.reshape(16, 128),
            inv,
            lse,
        ),
        (rows1, raw, q_t, kv, heads, w_out_all, w_all),
    )
    grads = lax.psum(grads, "tensor").astype(f32).reshape(3072, 1024)
    gate_up = grads[:2048].reshape(2, 1024, 1024)
    return (
        output,
        grad_x,
        norm1_sum.reshape(1024),
        pack[0:128].T.astype(f32),
        pack[128:192].T.astype(f32),
        pack[192:256].T.astype(f32),
        pack[417, :128].astype(f32),
        pack[417, 128:192].astype(f32),
        pack[256:384].astype(f32),
        pack[416].astype(f32),
        pack[384:416].T.astype(f32),
        gate_up[:, :, :512],
        gate_up[:, :, 512:],
        grads[2048:].reshape(2, 512, 1024),
    )


def solution(mesh):
    return jax.shard_map(
        shards,
        mesh=mesh,
        in_specs=(
            P(("dp", "ctx", "tensor"), None),
            P("dp"),
            P(),
            P(None, "tensor"),
            P(None, "tensor"),
            P(None, "tensor"),
            P("tensor"),
            P("tensor"),
            P("tensor", None),
            P(),
            P(),
            P(("dp", "ctx"), None, None),
            P(("dp", "ctx"), None, None),
            P(("dp", "ctx"), None, None),
            P(("dp", "ctx", "tensor"), None),
            P(("dp", "ctx", "tensor"), None),
        ),
        out_specs=(
            P(("dp", "ctx", "tensor"), None),
            P(("dp", "ctx", "tensor"), None),
            P(),
            P(None, "tensor"),
            P(None, "tensor"),
            P(None, "tensor"),
            P("tensor"),
            P("tensor"),
            P("tensor", None),
            P(),
            P(),
            P(("dp", "ctx"), None, None),
            P(("dp", "ctx"), None, None),
            P(("dp", "ctx"), None, None),
        ),
        check_vma=False,
    )
```

```python
import jax
import jax.numpy as jnp
import numpy as np
from jax import lax
from jax.experimental import pallas as pl
from jax.experimental.pallas import tpu as pltpu
from jax.sharding import PartitionSpec as P

EPS = 1e-06
THETA = 10000.0
MASKED = -1e30
MESH = pl.DeviceIdType.MESH


def rope_constants(length, half_dim):
    inverse = THETA ** (-(np.arange(half_dim, dtype=np.float64) * 2.0 / (2 * half_dim)))
    angles = inverse[:, None] * np.arange(length, dtype=np.float64)[None, :]
    table = np.stack([np.cos(angles), np.sin(angles)]).astype(np.float32)
    return np.ascontiguousarray(table.reshape(2, half_dim, 2, length // 2).transpose(2, 0, 1, 3))


def turn(value, cos_part, sin_part):
    parts = []
    for h in range(value.shape[0] // 64):
        a, b = value[64 * h : 64 * h + 32], value[64 * h + 32 : 64 * h + 64]
        parts += [a * cos_part - b * sin_part, b * cos_part + a * sin_part]
    return jnp.concatenate(parts, 0)


def column(row):
    return jnp.transpose(jnp.broadcast_to(row, (128, 128)))


def copy_to(src, dst, send, recv, device):
    return pltpu.make_async_remote_copy(
        src_ref=src, dst_ref=dst, send_sem=send, recv_sem=recv, device_id=device, device_id_type=MESH
    )


def dot_nt(left, right):
    return lax.dot_general(
        left, right, (((1,), (1,)), ((), ())), preferred_element_type=jnp.float32
    )


def dot_tn(left, right):
    return lax.dot_general(
        left, right, (((0,), (0,)), ((), ())), preferred_element_type=jnp.float32
    )


def across(a, b, flip):
    dp, ctx = lax.axis_index("dp"), lax.axis_index("ctx")
    x, y = dp % 4, dp // 4
    odd = a % 2
    by_x = odd * (1 + 2 * b) + (1 - odd) * a
    by_y = (1 - odd) * b + odd * (1 - a // 2)
    return ((y + by_y) % 2) * 4 + (x + by_x) % 4, (ctx + flip) % 2


def opposite(a, b):
    return b + (a % 2) * (1 - 2 * b)


def moe_kernel(
    rows_ref,
    gate_ref,
    dy_ref,
    w_gate_ref,
    w_up_ref,
    w_down_ref,
    w_t_ref,
    d_rows_ref,
    d_gate_ref,
    out_part_ref,
    grad_ref,
    w_all_ref,
    rows_all,
    gate_all,
    dy_all,
    w_gu,
    w_dn,
    acc_gu,
    acc_dn,
    out_all,
    din_all,
    sib,
    rs_a,
    rs_b,
    rs_c,
    rs_d,
    rs_e,
    dg_out,
    dg_in,
    places,
    x_buf,
    y_buf,
    d_buf,
    o_buf,
    i_buf,
    gs_buf,
    dgs_buf,
    load_sem,
    ag_send,
    ag_recv,
    g_send,
    g_recv,
    sib_send,
    sib_recv,
    rs_send,
    rs_recv,
    dg_send,
    dg_recv,
    store_sem,
    w_send,
    w_recv,
):
    tensor = lax.axis_index("tensor")
    dp, ctx = lax.axis_index("dp"), lax.axis_index("ctx")
    me = dp * 2 + ctx

    def to(a, b, flip):
        d, c = across(a, b, flip)
        return (d, c, tensor)

    def side(i):
        return (dp, ctx, (tensor + i) % 8)

    loads = []
    for j in range(2):
        loads.append(
            pltpu.make_async_copy(w_gate_ref.at[j], w_gu.at[j, :, pl.ds(0, 512)], load_sem.at[3 * j])
        )
        loads.append(
            pltpu.make_async_copy(
                w_up_ref.at[j], w_gu.at[j, :, pl.ds(512, 512)], load_sem.at[3 * j + 1]
            )
        )
        loads.append(pltpu.make_async_copy(w_down_ref.at[j], w_dn.at[j], load_sem.at[3 * j + 2]))
    loads.append(pltpu.make_async_copy(dy_ref, dy_all, load_sem.at[6]))
    for load in loads:
        load.start()

    barrier = pltpu.get_barrier_semaphore()
    for a in range(4):
        for b in range(2):
            for flip in range(2):
                if (a, b, flip) != (0, 0, 0):
                    pl.semaphore_signal(
                        barrier, inc=1, device_id=to(a, b, flip), device_id_type=MESH
                    )
    for i in range(1, 8):
        pl.semaphore_signal(barrier, inc=1, device_id=side(i), device_id_type=MESH)
    pl.semaphore_wait(barrier, 22)

    right, left, partner = to(3, 0, 0), to(3, 1, 0), to(0, 1, 0)
    sibling = to(0, 0, 1)
    low, high = pl.ds(0, 64), pl.ds(64, 64)

    def hop(n):
        src, dst, device = (
            (rows_all.at[0], rows_all.at[14], right),
            (rows_all.at[0], rows_all.at[12], left),
            (rows_all.at[0], rows_all.at[2], partner),
            (rows_all.at[14, low], rows_all.at[8, low], right),
            (rows_all.at[12, high], rows_all.at[8, high], left),
            (rows_all.at[2], rows_all.at[6], right),
            (rows_all.at[2], rows_all.at[4], left),
            (rows_all.at[8], rows_all.at[10], partner),
        )[n]
        return copy_to(src, dst, ag_send.at[n], ag_recv.at[n], device)

    def relay(ci):
        r = 2 * ci
        return copy_to(
            rows_all.at[r], rows_all.at[r + 1], ag_send.at[8 + ci], ag_recv.at[8 + ci], sibling
        )

    def gate_push(a, b, flip):
        r = 4 * a + 2 * b + flip
        back = 4 * a + 2 * opposite(a, b) + flip
        return copy_to(
            gate_all.at[0], gate_all.at[back], g_send.at[r], g_recv.at[back], to(a, b, flip)
        )

    rows_all[0] = rows_ref[...]
    gate_all[0] = gate_ref[...]
    for n in range(3):
        hop(n).start()
    relay(0).start()
    for r in range(1, 16):
        gate_push(r // 4, (r // 2) % 2, r % 2).start()

    acc_gu[...] = jnp.zeros_like(acc_gu)
    acc_dn[...] = jnp.zeros_like(acc_dn)

    half = pl.ds(pl.multiple_of(ctx * 128, 128), 128)

    def w_push(i):
        return copy_to(
            w_t_ref.at[half],
            w_all_ref.at[tensor, half],
            w_send.at[i],
            w_recv.at[tensor, ctx],
            side(i),
        )

    def w_relay(t):
        place = w_all_ref.at[t, half]
        return copy_to(place, place, w_send.at[8 + t], w_recv.at[t, ctx], to(0, 0, 1))

    def w_arrival(t, c):
        place = w_all_ref.at[t, pl.ds(pl.multiple_of(c * 128, 128), 128)]
        return copy_to(place, place, w_send.at[0], w_recv.at[t, c], to(0, 0, 1))

    for i in (1, 7, 2, 6, 3, 5, 4):
        w_push(i).start()
    w_own = pltpu.make_async_copy(w_t_ref, w_all_ref.at[tensor], load_sem.at[7])
    w_own.start()

    def sib_push(ci):
        return copy_to(
            din_all.at[2 * ci + 1], sib.at[ci], sib_send.at[ci], sib_recv.at[ci], sibling
        )

    def rs_hop(n):
        src, dst, device = (
            (din_all.at[4], rs_a.at[0], right),
            (din_all.at[6], rs_a.at[1], left),
            (din_all.at[10], rs_b, partner),
            (din_all.at[2], rs_c, partner),
            (din_all.at[8, low], rs_d.at[0], right),
            (din_all.at[8, high], rs_d.at[1], left),
            (din_all.at[12], rs_e.at[0], right),
            (din_all.at[14], rs_e.at[1], left),
        )[n]
        return copy_to(src, dst, rs_send.at[n], rs_recv.at[n], device)

    def rs_go(*hops):
        for n in hops:
            rs_hop(n).start()

    def rs_got(*hops):
        for n in hops:
            rs_hop(n).wait_recv()

    def plus(r, rows, *parts):
        total = din_all[r, rows].astype(jnp.float32)
        for part in parts:
            total = total + part.astype(jnp.float32)
        din_all[r, rows] = total.astype(jnp.bfloat16)

    def post(*cis):
        for ci in cis:
            sib_push(ci).wait_recv()
            plus(2 * ci, slice(None), sib[ci])

    def dg_push(a, b, flip):
        r = 4 * a + 2 * b + flip
        back = 4 * a + 2 * opposite(a, b) + flip
        return pltpu.make_async_remote_copy(
            src_ref=dg_out.at[r],
            dst_ref=dg_in.at[back],
            send_sem=dg_send.at[r],
            recv_sem=dg_recv.at[back],
            device_id=to(a, b, flip),
            device_id_type=MESH,
        )

    expert_row = lax.broadcasted_iota(jnp.int32, (32, 128), 0)
    slot_row = lax.broadcasted_iota(jnp.int32, (64, 128), 0).astype(jnp.float32)
    before = (
        lax.broadcasted_iota(jnp.int32, (128, 128), 0)
        < lax.broadcasted_iota(jnp.int32, (128, 128), 1)
    ).astype(jnp.float32)
    before = before.astype(jnp.bfloat16)

    def gather(a, q):
        r = 4 * a + q
        gates = gate_all[r]
        at = pl.ds(pl.multiple_of(q * 64, 64), 64)
        rows = [
            jnp.sum(jnp.where(expert_row == 2 * me + j, gates, 0.0), 0, keepdims=True)
            for j in range(2)
        ]
        both = jnp.concatenate(rows + [jnp.zeros((6, 128), jnp.float32)], 0)
        named = jnp.where(both > 0.0, 1.0, 0.0).astype(jnp.bfloat16)
        slots = jnp.dot(named, before, preferred_element_type=jnp.float32)
        hits = [
            jnp.where((slot_row == slots[j : j + 1]) & (rows[j] > 0.0), 1.0, 0.0) for j in range(2)
        ]
        place = jnp.concatenate(hits, 0).astype(jnp.bfloat16)
        places[q] = place
        x = jnp.dot(place, rows_all[r], preferred_element_type=jnp.float32).astype(jnp.bfloat16)
        y = jnp.dot(place, dy_all[r], preferred_element_type=jnp.float32)
        for j in range(2):
            gs = jnp.sum(hits[j] * rows[j], 1, keepdims=True)
            y_j = y[64 * j : 64 * j + 64]
            x_buf[j, at, :] = x[64 * j : 64 * j + 64]
            y_buf[j, at, :] = y_j.astype(jnp.bfloat16)
            d_buf[j, at, :] = (y_j * gs).astype(jnp.bfloat16)
            gs_buf[j, at, :] = gs

    def expert(j):
        x = x_buf[j]
        gu = jnp.dot(x, w_gu[j], preferred_element_type=jnp.float32)
        g, u = gu[:, :512], gu[:, 512:]
        s = jax.nn.sigmoid(g)
        silu = g * s
        act = (silu * u).astype(jnp.bfloat16)
        eout = (
            jnp.dot(act, w_dn[j], preferred_element_type=jnp.float32)
            .astype(jnp.bfloat16)
            .astype(jnp.float32)
        )
        dgs_buf[j] = jnp.sum(y_buf[j].astype(jnp.float32) * eout, 1, keepdims=True)
        o_buf[j] = (eout * gs_buf[j]).astype(jnp.bfloat16)
        d = d_buf[j]
        d_act = dot_nt(d, w_dn[j])
        d_g = (d_act * u * s * (1.0 + g * (1.0 - s))).astype(jnp.bfloat16)
        d_u = (d_act * silu).astype(jnp.bfloat16)
        d_gu = jnp.concatenate([d_g, d_u], 1)
        i_buf[j] = dot_nt(d_gu, w_gu[j]).astype(jnp.bfloat16)
        acc_gu[j] += dot_tn(x, d_gu)
        acc_dn[j] += dot_tn(act, d)

    def spread(a, q):
        r = 4 * a + q
        b, flip = q // 2, q % 2
        at = pl.ds(pl.multiple_of(q * 64, 64), 64)
        place = places[q]
        d, c = across(a, b, flip)
        o = jnp.concatenate([o_buf[0, at, :], o_buf[1, at, :]], 0)
        out_all[c * 8 + d] = dot_tn(place, o).astype(jnp.bfloat16)
        i = jnp.concatenate([i_buf[0, at, :], i_buf[1, at, :]], 0)
        din_all[r] = dot_tn(place, i).astype(jnp.bfloat16)
        hits = place.astype(jnp.float32)
        back = [
            jnp.sum(hits[64 * j : 64 * j + 64] * dgs_buf[j, at, :], 0, keepdims=True)
            for j in range(2)
        ]
        dg_out[r] = jnp.concatenate(back + [jnp.zeros((6, 128), jnp.float32)], 0)

        @pl.when(r > 0)
        def _():
            dg_push(a, b, flip).start()

    for n, ci in ((0, 7), (1, 6)):
        hop(n).wait_recv()
        hop(3 + n).start()
        relay(ci).start()
    hop(2).wait_recv()
    hop(5).start()
    hop(6).start()
    relay(1).start()
    relay(0).wait_recv()
    for r in range(1, 16):
        gate_push(r // 4, (r // 2) % 2, r % 2).wait_recv()
    for load in loads:
        load.wait()
    relay(1).wait_recv()

    def step(a, carry):
        lax.fori_loop(0, 4, lambda q, c: (gather(a, q), c)[1], 0)

        @pl.when(a == 1)
        def _():
            post(0, 1)

        @pl.when(a == 2)
        def _():
            post(2, 3)
            rs_go(0, 1)

        @pl.when(a == 3)
        def _():
            post(4, 5)
            rs_go(2)
            rs_got(0, 1)
            plus(2, slice(None), rs_a[0], rs_a[1])
            rs_go(3)

        lax.fori_loop(0, 2, lambda j, c: (expert(j), c)[1], 0)
        lax.fori_loop(0, 4, lambda q, c: (spread(a, q), c)[1], 0)
        for b in range(2):
            sib_push(2 * a + b).start()

        @pl.when(a == 0)
        def _():
            hop(3).wait_recv()
            hop(4).wait_recv()
            hop(7).start()
            relay(4).start()
            for n, ci in ((5, 3), (6, 2)):
                hop(n).wait_recv()
                relay(ci).start()
            for ci in (2, 3):
                relay(ci).wait_recv()

        @pl.when(a == 1)
        def _():
            hop(7).wait_recv()
            relay(5).start()
            for ci in (4, 5, 6, 7):
                relay(ci).wait_recv()

        return carry

    lax.fori_loop(0, 4, step, 0)
    rs_got(2)
    plus(8, slice(None), rs_b[...])
    rs_go(4, 5)
    post(6, 7)
    rs_got(4)
    plus(12, low, rs_d[0])
    rs_go(6)
    rs_got(5)
    plus(14, high, rs_d[1])
    rs_go(7)
    for i in range(1, 8):
        t = (tensor + i) % 8
        w_arrival(t, ctx).wait_recv()
        w_relay(t).start()
    for n in range(8):
        hop(n).wait_send()
        relay(n).wait_send()
    for r in range(1, 16):
        gate_push(r // 4, (r // 2) % 2, r % 2).wait_send()
    stores = []
    for j in range(2):
        for h in range(8):
            rows_all[8 * j + h] = acc_gu[j, 128 * h : 128 * h + 128, :].astype(jnp.bfloat16)
        for h in range(4):
            dy_all[4 * j + h] = acc_dn[j, 128 * h : 128 * h + 128, :].astype(jnp.bfloat16)
    stores.append(pltpu.make_async_copy(rows_all, grad_ref.at[pl.ds(0, 16)], store_sem.at[0]))
    stores.append(
        pltpu.make_async_copy(
            dy_all.at[pl.ds(0, 8)], grad_ref.at[pl.ds(16, 8)], store_sem.at[1]
        )
    )
    stores.append(pltpu.make_async_copy(out_all, out_part_ref, store_sem.at[2]))
    for store in stores:
        store.start()

    for r in range(1, 16):
        a, b, flip = r // 4, (r // 2) % 2, r % 2
        dg_push(a, b, flip).wait()
    dg_in[0] = dg_out[0]
    d_gate = jnp.zeros((32, 128), jnp.float32)
    for r in range(16):
        d, c = across(r // 4, (r // 2) % 2, r % 2)
        got = dg_in[r]
        for j in range(2):
            d_gate = jnp.where(expert_row == (d * 2 + c) * 2 + j, got[j : j + 1], d_gate)
    d_gate_ref[...] = d_gate
    for ci in range(8):
        sib_push(ci).wait_send()
    rs_got(3, 6, 7)
    total = din_all[0].astype(jnp.float32) + rs_c[...].astype(jnp.float32)
    d_rows_ref[...] = total + rs_e[0].astype(jnp.float32) + rs_e[1].astype(jnp.float32)
    for n in range(8):
        rs_hop(n).wait_send()
    for i in range(1, 8):
        t = (tensor + i) % 8
        w_arrival(t, 1 - ctx).wait_recv()
        w_push(i).wait_send()
        w_relay(t).wait_send()
    w_own.wait()
    for store in stores:
        store.wait()


def moe(rows, gates, dy, w_gate, w_up, w_down, w_t):
    bf, f32 = jnp.bfloat16, jnp.float32
    vmem, hbm = pl.BlockSpec(memory_space=pltpu.VMEM), pl.BlockSpec(memory_space=pl.ANY)
    sem = pltpu.SemaphoreType.DMA
    return pl.pallas_call(
        moe_kernel,
        out_shape=(
            jax.ShapeDtypeStruct((128, 1024), f32),
            jax.ShapeDtypeStruct((32, 128), f32),
            jax.ShapeDtypeStruct((16, 128, 1024), bf),
            jax.ShapeDtypeStruct((24, 128, 1024), bf),
            jax.ShapeDtypeStruct((8, 256, 1024), bf),
        ),
        in_specs=[vmem] * 2 + [hbm] * 5,
        out_specs=(vmem, vmem, hbm, hbm, hbm),
        scratch_shapes=[
            pltpu.VMEM((16, 128, 1024), bf),
            pltpu.VMEM((16, 32, 128), f32),
            pltpu.VMEM((16, 128, 1024), bf),
            pltpu.VMEM((2, 1024, 1024), bf),
            pltpu.VMEM((2, 512, 1024), bf),
            pltpu.VMEM((2, 1024, 1024), f32),
            pltpu.VMEM((2, 512, 1024), f32),
            pltpu.VMEM((16, 128, 1024), bf),
            pltpu.VMEM((16, 128, 1024), bf),
            pltpu.VMEM((8, 128, 1024), bf),
            pltpu.VMEM((2, 128, 1024), bf),
            pltpu.VMEM((128, 1024), bf),
            pltpu.VMEM((128, 1024), bf),
            pltpu.VMEM((2, 64, 1024), bf),
            pltpu.VMEM((2, 128, 1024), bf),
            pltpu.VMEM((16, 8, 128), f32),
            pltpu.VMEM((16, 8, 128), f32),
            pltpu.VMEM((4, 128, 128), bf),
            pltpu.VMEM((2, 256, 1024), bf),
            pltpu.VMEM((2, 256, 1024), bf),
            pltpu.VMEM((2, 256, 1024), bf),
            pltpu.VMEM((2, 256, 1024), bf),
            pltpu.VMEM((2, 256, 1024), bf),
            pltpu.VMEM((2, 256, 1), f32),
            pltpu.VMEM((2, 256, 1), f32),
            sem((8,)),
            sem((16,)),
            sem((16,)),
            sem((16,)),
            sem((16,)),
            sem((8,)),
            sem((8,)),
            sem((8,)),
            sem((8,)),
            sem((16,)),
            sem((16,)),
            sem((3,)),
            sem((16,)),
            sem((8, 2)),
        ],
        compiler_params=pltpu.CompilerParams(
            collective_id=1, has_side_effects=True, vmem_limit_bytes=60 << 20
        ),
        cost_estimate=pl.CostEstimate(
            flops=20_000_000_000, bytes_accessed=30_000_000, transcendentals=2_000_000
        ),
    )(rows, gates, dy, w_gate, w_up, w_down, w_t)


def attention_kernel(
    x_ref,
    dy_ref,
    segment_ref,
    norm1_ref,
    q_gain_ref,
    k_gain_ref,
    norm2_ref,
    router_ref,
    routes_ref,
    w_q_ref,
    w_k_ref,
    w_v_ref,
    w_out_ref,
    table_ref,
    rows2_ref,
    gates_ref,
    resid_ref,
    rows1_ref,
    raw_ref,
    inv_ref,
    q_ref,
    kv_ref,
    lse_ref,
    heads_ref,
    w_out_all_ref,
    dy_all_ref,
    w_t_ref,
    h_all,
    dy_all,
    w_all,
    w_q,
    w_t,
    raw,
    table,
    stat,
    stats,
    q_t,
    kv_own,
    kv_sib,
    k_own,
    k_sib,
    starts,
    heads,
    heads_all,
    load_sem,
    h_send,
    h_recv,
    dy_send,
    dy_recv,
    w_send,
    w_recv,
    s_send,
    s_recv,
    kv_sem,
    o_send,
    o_recv,
    store_sem,
):
    f32, bf = jnp.float32, jnp.bfloat16
    dp, ctx, me = lax.axis_index("dp"), lax.axis_index("ctx"), lax.axis_index("tensor")

    def side(i):
        return (dp, ctx, (me + i) % 8)

    def to(a, b, flip):
        d, c = across(a, b, flip)
        return (d, c, me)

    sibling = (dp, 1 - ctx, me)
    loads = [
        pltpu.make_async_copy(w_q_ref, w_q, load_sem.at[0]),
        pltpu.make_async_copy(w_k_ref, w_t.at[pl.ds(128, 64)], load_sem.at[1]),
        pltpu.make_async_copy(w_v_ref, w_t.at[pl.ds(192, 64)], load_sem.at[2]),
        pltpu.make_async_copy(w_out_ref, w_all.at[me], load_sem.at[3]),
        pltpu.make_async_copy(table_ref.at[ctx], table, load_sem.at[4]),
    ]
    for load in loads:
        load.start()
    barrier = pltpu.get_barrier_semaphore()
    for i in range(1, 8):
        pl.semaphore_signal(barrier, inc=1, device_id=side(i), device_id_type=MESH)
    for a in range(4):
        for b in range(2):
            if (a, b) != (0, 0):
                pl.semaphore_signal(barrier, inc=1, device_id=to(a, b, 0), device_id_type=MESH)
    pl.semaphore_signal(barrier, inc=1, device_id=sibling, device_id_type=MESH)
    x = x_ref[...].astype(f32)
    inv_one = lax.rsqrt(jnp.mean(x * x, -1, keepdims=True) + EPS)
    h_all[me] = (x * inv_one * norm1_ref[...]).astype(bf)
    dy_all[0] = dy_ref[...]
    pl.semaphore_wait(barrier, 15)

    z, y = me // 2, me % 2
    up, down, pair = (
        (dp, ctx, ((z + 1) % 4) * 2 + y),
        (dp, ctx, ((z + 3) % 4) * 2 + y),
        (dp, ctx, z * 2 + 1 - y),
    )
    low, high = pl.ds(0, 64), pl.ds(64, 64)

    def block_at(k, flip):
        return ((z + k) % 4) * 2 + (y + flip) % 2

    def h_hop(n):
        place, device = (
            (h_all.at[me], up),
            (h_all.at[me], down),
            (h_all.at[me], pair),
            (h_all.at[block_at(3, 0), low], up),
            (h_all.at[block_at(1, 0), high], down),
            (h_all.at[block_at(0, 1)], up),
            (h_all.at[block_at(0, 1)], down),
            (h_all.at[block_at(2, 0)], pair),
        )[n]
        return copy_to(place, place, h_send.at[n], h_recv.at[n], device)

    right, left, partner = to(3, 0, 0), to(3, 1, 0), to(0, 1, 0)

    def dy_hop(n):
        src, dst, device = (
            (dy_all.at[0], dy_all.at[14], right),
            (dy_all.at[0], dy_all.at[12], left),
            (dy_all.at[0], dy_all.at[2], partner),
            (dy_all.at[14, low], dy_all.at[8, low], right),
            (dy_all.at[12, high], dy_all.at[8, high], left),
            (dy_all.at[2], dy_all.at[6], right),
            (dy_all.at[2], dy_all.at[4], left),
            (dy_all.at[8], dy_all.at[10], partner),
        )[n]
        return copy_to(src, dst, dy_send.at[n], dy_recv.at[n], device)

    def dy_relay(ci):
        r = 2 * ci
        return copy_to(
            dy_all.at[r], dy_all.at[r + 1], dy_send.at[8 + ci], dy_recv.at[8 + ci], sibling
        )

    for n in range(3):
        h_hop(n).start()
    for n in range(3):
        dy_hop(n).start()
    dy_relay(0).start()

    for load in loads:
        load.wait()
    w_t[0:128, :] = jnp.transpose(w_q[...])
    seg = segment_ref[...]
    start = jnp.zeros((16, 128), f32)
    for s in range(1, 8):
        below = jnp.where(seg < s, 1.0, 0.0)
        count = jnp.sum(jnp.sum(below, 1, keepdims=True), 0, keepdims=True)
        start = jnp.where(seg == s, count, start)
    start = jnp.where(ctx == 0, start[:8], start[8:])
    for t in range(8):
        starts[0:1, 128 * t : 128 * t + 128] = start[t : t + 1]

    def project(t):
        value = dot_nt(w_t[...], h_all[t])
        raw[t] = value
        square = value * value
        sums = [
            jnp.sum(square[0:128], 0, keepdims=True),
            jnp.sum(square[128:192], 0, keepdims=True),
            jnp.zeros((6, 128), f32),
        ]
        stat[t] = jnp.concatenate(sums, 0)

    project(me)
    for n in range(2):
        h_hop(n).wait_recv()
        h_hop(3 + n).start()
    h_hop(2).wait_recv()
    h_hop(5).start()
    h_hop(6).start()
    for k, flip in ((3, 0), (1, 0), (0, 1)):
        project(block_at(k, flip))
    h_hop(3).wait_recv()
    h_hop(4).wait_recv()
    h_hop(7).start()
    project(block_at(2, 0))
    for n, k in ((5, 3), (6, 1), (7, 2)):
        h_hop(n).wait_recv()
        project(block_at(k, 1))
    stats[me] = stat[...]

    def s_push(i):
        return copy_to(stats.at[me], stats.at[me], s_send.at[i], s_recv.at[me], side(i))

    def s_arrival(t):
        return copy_to(stats.at[t], stats.at[t], s_send.at[0], s_recv.at[t], sibling)

    for i in range(1, 8):
        s_push(i).start()
    store_rows = pltpu.make_async_copy(h_all, rows1_ref, store_sem.at[0])
    store_raw = pltpu.make_async_copy(raw, raw_ref, store_sem.at[1])
    store_wt = pltpu.make_async_copy(w_t, w_t_ref, store_sem.at[8])
    store_rows.start()
    store_raw.start()
    store_wt.start()

    def w_push(i):
        half = w_all.at[me, pl.ds(pl.multiple_of(ctx * 64, 64), 64)]
        return copy_to(half, half, w_send.at[i], w_recv.at[me, ctx], side(i))

    def w_relay(t):
        half = w_all.at[t, pl.ds(pl.multiple_of(ctx * 64, 64), 64)]
        return copy_to(half, half, w_send.at[8 + t], w_recv.at[t, ctx], sibling)

    def w_arrival(t, c):
        half = w_all.at[t, pl.ds(pl.multiple_of(c * 64, 64), 64)]
        return copy_to(half, half, w_send.at[0], w_recv.at[t, c], sibling)

    for n, ci in ((0, 7), (1, 6)):
        dy_hop(n).wait_recv()
        dy_hop(3 + n).start()
        dy_relay(ci).start()
    dy_hop(2).wait_recv()
    dy_hop(5).start()
    dy_hop(6).start()
    dy_relay(1).start()
    for i in (1, 7, 2, 6, 3, 5, 4):
        w_push(i).start()
    gain_q = column(q_gain_ref[...])
    gain_k = column(jnp.concatenate([k_gain_ref[...], jnp.zeros((1, 64), f32)], 1))[:64]
    for i in range(1, 8):
        s_arrival((me + i) % 8).wait_recv()

    def finish(t, carry):
        at = pl.ds(pl.multiple_of(t * 128, 128), 128)
        sums = stats[0, t]
        for s in range(1, 8):
            sums = sums + stats[s, t]
        width = jnp.where(lax.broadcasted_iota(jnp.int32, (8, 128), 0) == 0, 1024.0, 512.0)
        inv = lax.rsqrt(sums / width + EPS)
        inv_ref[t] = inv
        value = raw[t]
        cos_part, sin_part = table[0, :, at], table[1, :, at]
        queries = turn(value[0:128] * inv[0:1] * gain_q, cos_part, sin_part).astype(bf)
        keys = turn(value[128:192] * inv[1:2] * gain_k, cos_part, sin_part).astype(bf)
        q_t[:, at] = queries
        kv_own[0:64, at] = keys
        kv_own[64:128, at] = value[192:256].astype(bf)
        k_own[at, :] = jnp.transpose(keys)
        return carry

    lax.fori_loop(0, 8, finish, 0)
    kv_push = copy_to(kv_own, kv_sib, kv_sem.at[0], kv_sem.at[1], sibling)
    kv_push.start()

    key_row = lax.broadcasted_iota(jnp.int32, (256, 256), 0).astype(f32)
    query_lane = lax.broadcasted_iota(jnp.int32, (256, 256), 1).astype(f32)
    base = (ctx * 1024).astype(f32)

    def attend(n, carry):
        i, h = n // 2, n % 2
        at = pl.ds(pl.multiple_of(i * 256, 256), 256)
        q = q_t[pl.ds(pl.multiple_of(h * 64, 64), 64), at] * 0.125
        begin = starts[0:1, at]

        def block(keys, values, first_key, state, causal):
            top, total, acc = state
            s = jnp.dot(keys, q, preferred_element_type=f32)
            ok = key_row >= begin - first_key
            if causal:
                ok = ok & (key_row <= query_lane)
            s = jnp.where(ok, s, MASKED)
            new_top = jnp.maximum(top, jnp.max(s, 0, keepdims=True))
            e = jnp.exp(s - new_top)
            shrink = jnp.exp(top - new_top)
            total = total * shrink + jnp.sum(e, 0, keepdims=True)
            acc = acc * shrink + jnp.dot(values, e.astype(bf), preferred_element_type=f32)
            return new_top, total, acc

        state = (jnp.full((1, 256), MASKED, f32), jnp.zeros((1, 256), f32), jnp.zeros((64, 256), f32))
        state = block(
            k_own[at, :], kv_own[64:128, at], base + (i * 256).astype(f32), state, True
        )

        def own(j, state):
            ks = pl.ds(pl.multiple_of(j * 256, 256), 256)
            return block(k_own[ks, :], kv_own[64:128, ks], base + (j * 256).astype(f32), state, False)

        state = lax.fori_loop(0, i, own, state)

        def other(j, state):
            ks = pl.ds(pl.multiple_of(j * 256, 256), 256)
            return block(k_sib[ks, :], kv_sib[64:128, ks], (j * 256).astype(f32), state, False)

        top, total, acc = lax.fori_loop(0, 4 * ctx, other, state)
        out = (acc / total).astype(bf)
        hs = pl.ds(pl.multiple_of(h * 64, 64), 64)
        heads[2 * i, hs, :] = out[:, :128]
        heads[2 * i + 1, hs, :] = out[:, 128:]
        lse_ref[h, 0:1, at] = top + jnp.log(total)
        return carry

    kv_push.wait()

    def straighten(t, carry):
        at = pl.ds(pl.multiple_of(t * 128, 128), 128)
        k_sib[at, :] = jnp.transpose(kv_sib[0:64, at])
        return carry

    dy_hop(3).wait_recv()
    dy_hop(4).wait_recv()
    dy_hop(7).start()
    dy_relay(4).start()
    lax.fori_loop(0, 8, straighten, 0)
    lax.fori_loop(0, 8, attend, 0)

    def o_push(i):
        return copy_to(
            heads.at[(me + i) % 8], heads_all.at[me], o_send.at[i], o_recv.at[me], side(i)
        )

    def o_arrival(t):
        return copy_to(heads_all.at[t], heads_all.at[t], o_send.at[0], o_recv.at[t], sibling)

    for i in range(1, 8):
        o_push(i).start()
    heads_all[me] = heads[me]
    stores = [
        pltpu.make_async_copy(q_t, q_ref, store_sem.at[2]),
        pltpu.make_async_copy(kv_own, kv_ref.at[0], store_sem.at[3]),
        pltpu.make_async_copy(kv_sib, kv_ref.at[1], store_sem.at[4]),
        pltpu.make_async_copy(heads, heads_ref, store_sem.at[5]),
    ]
    for store in stores:
        store.start()

    def pass_on(i, carry):
        t = (me + i) % 8
        w_arrival(t, ctx).wait_recv()
        w_relay(t).start()
        return carry

    lax.fori_loop(1, 8, pass_on, 0)

    for n, ci in ((5, 3), (6, 2), (7, 5)):
        dy_hop(n).wait_recv()
        dy_relay(ci).start()
    for i in range(1, 8):
        t = (me + i) % 8
        w_arrival(t, 1 - ctx).wait_recv()
        o_arrival(t).wait_recv()
    store_w = pltpu.make_async_copy(w_all, w_out_all_ref, store_sem.at[6])
    store_w.start()
    attended = dot_tn(heads_all[...].reshape(1024, 128), w_all[...].reshape(1024, 1024))
    resid = x + attended
    resid_ref[...] = resid
    inv_two = lax.rsqrt(jnp.mean(resid * resid, -1, keepdims=True) + EPS)
    rows2 = (resid * inv_two * norm2_ref[...]).astype(bf)
    rows2_ref[...] = rows2
    logits = dot_nt(router_ref[...], rows2)
    expert_row = lax.broadcasted_iota(jnp.int32, (32, 128), 0)
    routes = routes_ref[...]
    named = routes[0:1] == expert_row
    for k in range(1, 8):
        named = named | (routes[k : k + 1] == expert_row)
    chosen = jnp.where(named, logits, MASKED)
    weight = jnp.where(named, jnp.exp(chosen - jnp.max(chosen, 0, keepdims=True)), 0.0)
    gates_ref[...] = weight / jnp.sum(weight, 0, keepdims=True)

    for ci in range(8):
        dy_relay(ci).wait_recv()
    store_dy = pltpu.make_async_copy(dy_all, dy_all_ref, store_sem.at[7])
    store_dy.start()
    for i in range(1, 8):
        s_push(i).wait_send()
        w_push(i).wait_send()
        w_relay((me + i) % 8).wait_send()
        o_push(i).wait_send()
    for n in range(8):
        h_hop(n).wait_send()
        dy_hop(n).wait_send()
        dy_relay(n).wait_send()
    for store in [store_rows, store_raw, store_wt, store_w, store_dy] + stores:
        store.wait()


def attention(x, dy, segment, norm1, q_gain, k_gain, norm2, router, routes, w_q, w_k, w_v, w_out):
    bf, f32 = jnp.bfloat16, jnp.float32
    vmem, hbm = pl.BlockSpec(memory_space=pltpu.VMEM), pl.BlockSpec(memory_space=pl.ANY)
    sem = pltpu.SemaphoreType.DMA
    shape = jax.ShapeDtypeStruct
    table = jnp.asarray(rope_constants(2048, 32))
    return pl.pallas_call(
        attention_kernel,
        out_shape=(
            shape((128, 1024), bf),
            shape((32, 128), f32),
            shape((128, 1024), f32),
            shape((8, 128, 1024), bf),
            shape((8, 256, 128), f32),
            shape((8, 8, 128), f32),
            shape((128, 1024), bf),
            shape((2, 128, 1024), bf),
            shape((2, 8, 1024), f32),
            shape((8, 128, 128), bf),
            shape((8, 128, 1024), bf),
            shape((16, 128, 1024), bf),
            shape((256, 1024), bf),
        ),
        in_specs=[vmem] * 9 + [hbm] * 5,
        out_specs=(vmem, vmem, vmem, hbm, hbm, vmem, hbm, hbm, vmem, hbm, hbm, hbm, hbm),
        scratch_shapes=[
            pltpu.VMEM((8, 128, 1024), bf),
            pltpu.VMEM((16, 128, 1024), bf),
            pltpu.VMEM((8, 128, 1024), bf),
            pltpu.VMEM((1024, 128), bf),
            pltpu.VMEM((256, 1024), bf),
            pltpu.VMEM((8, 256, 128), f32),
            pltpu.VMEM((2, 32, 1024), f32),
            pltpu.VMEM((8, 8, 128), f32),
            pltpu.VMEM((8, 8, 8, 128), f32),
            pltpu.VMEM((128, 1024), bf),
            pltpu.VMEM((128, 1024), bf),
            pltpu.VMEM((128, 1024), bf),
            pltpu.VMEM((1024, 64), bf),
            pltpu.VMEM((1024, 64), bf),
            pltpu.VMEM((8, 1024), f32),
            pltpu.VMEM((8, 128, 128), bf),
            pltpu.VMEM((8, 128, 128), bf),
            sem((5,)),
            sem((8,)),
            sem((8,)),
            sem((16,)),
            sem((16,)),
            sem((16,)),
            sem((8, 2)),
            sem((8,)),
            sem((8,)),
            sem((2,)),
            sem((8,)),
            sem((8,)),
            sem((9,)),
        ],
        compiler_params=pltpu.CompilerParams(
            collective_id=2, has_side_effects=True, vmem_limit_bytes=56 << 20
        ),
        cost_estimate=pl.CostEstimate(
            flops=5_000_000_000, bytes_accessed=20_000_000, transcendentals=4_000_000
        ),
    )(
        x,
        dy,
        segment.reshape(16, 128),
        norm1.reshape(1, 1024),
        q_gain.reshape(1, 128),
        k_gain.reshape(1, 64),
        norm2.reshape(1, 1024),
        router.T,
        routes.T,
        w_q,
        w_k.T,
        w_v.T,
        w_out,
        table,
    )


def backward_kernel(
    x_ref,
    dy_ref,
    d_rows_ref,
    d_gate_ref,
    gates_ref,
    rows2_ref,
    resid_ref,
    router_ref,
    norm1_ref,
    norm2_ref,
    q_gain_ref,
    k_gain_ref,
    segment_ref,
    inv_ref,
    lse_ref,
    rows1_ref,
    raw_ref,
    q_ref,
    kv_ref,
    heads_ref,
    w_out_ref,
    w_all_ref,
    grads_ref,
    out_part_ref,
    table_ref,
    grad_x_ref,
    norm1_out_ref,
    pack_ref,
    output_ref,
    reduced_ref,
    rows1,
    raw,
    q_t,
    kv_own,
    kv_sib,
    heads,
    w_out,
    w_all,
    table,
    starts,
    d_resid,
    datt_all,
    dh_send,
    dh_all,
    tiny,
    q_cat,
    q_nat,
    d_cat,
    d_nat,
    lanes,
    k_nat,
    v_nat,
    dq_acc,
    dk_acc,
    dv_acc,
    dkv_out,
    dkv_in,
    terms,
    stat,
    stats,
    dqkv,
    dqkv_all,
    heads2,
    pack,
    pack_sib,
    pack_in,
    result,
    n1,
    n1_chips,
    n1_sib,
    load_sem,
    a_send,
    a_recv,
    dh_send_sem,
    dh_recv,
    t_send,
    t_recv,
    s_send,
    s_recv,
    dkv_sem,
    o_send,
    o_recv,
    p_sem,
    rs_send,
    rs_recv,
    g_send,
    g_recv,
    gs_send,
    gs_recv,
    n_send,
    n_recv,
    m_send,
    m_recv,
    ns_sem,
    grads,
    reduced,
    ra1,
    ra2,
    ra4,
    rb1,
    rb2,
    rb3,
    r_send,
    r_recv,
    out_own,
    out_sib,
    out_in,
    os_sem,
    out_send,
    out_recv,
):
    f32, bf = jnp.float32, jnp.bfloat16
    dp, ctx, me = lax.axis_index("dp"), lax.axis_index("ctx"), lax.axis_index("tensor")
    sibling = (dp, 1 - ctx, me)

    def side(i):
        return (dp, ctx, (me + i) % 8)

    z, y = me // 2, me % 2
    other = 1 - y
    up, down, across_y = (
        (dp, ctx, ((z + 1) % 4) * 2 + y),
        (dp, ctx, ((z + 3) % 4) * 2 + y),
        (dp, ctx, z * 2 + other),
    )

    def unit(k, c, first=0):
        return pl.ds(pl.multiple_of((first + ((z + k) % 4) * 2 + c) * 192, 64), 192)

    def half_unit(k, c, part):
        return pl.ds(pl.multiple_of((8 + ((z + k) % 4) * 2 + c) * 192 + part * 96, 32), 96)

    def hop(n):
        if n < 2:
            src, dst = grads.at[unit(2, n)], ra1.at[n]
            to = (up, down)[n]
        elif n < 4:
            src, dst, to = grads.at[unit(1, n - 2)], ra2.at[0, n - 2], up
        elif n < 6:
            src, dst, to = grads.at[unit(3, n - 4)], ra2.at[1, n - 4], down
        elif n == 6:
            src, dst, to = grads.at[unit(0, other)], ra4, across_y
        elif n == 7:
            src = dst = reduced.at[unit(0, y)]
            to = across_y
        elif n < 12:
            src = dst = reduced.at[unit(0, n % 2)]
            to = up if n < 10 else down
        elif n == 12:
            src = dst = reduced.at[unit(3, 0)]
            to = up
        elif n == 13:
            src = dst = reduced.at[unit(1, 1)]
            to = down
        elif n < 18:
            src, dst, to = grads.at[unit(n - 14, other, 8)], rb1.at[(z + n - 14) % 4], across_y
        elif n < 20:
            src, dst, to = grads.at[half_unit(2, y, n - 18)], rb2.at[n - 18], (up, down)[n - 18]
        elif n == 20:
            src, dst, to = grads.at[unit(1, y, 8)], rb3.at[0], up
        elif n == 21:
            src, dst, to = grads.at[unit(3, y, 8)], rb3.at[1], down
        elif n < 24:
            src = dst = reduced.at[unit(0, y, 8)]
            to = (up, down)[n - 22]
        elif n == 24:
            src = dst = reduced.at[half_unit(3, y, 0)]
            to = up
        elif n == 25:
            src = dst = reduced.at[half_unit(1, y, 1)]
            to = down
        else:
            src = dst = reduced.at[unit((0, 3, 1, 2)[n - 26], y, 8)]
            to = across_y
        return copy_to(src, dst, r_send.at[n], r_recv.at[n], to)

    def go(*hops):
        for n in hops:
            hop(n).start()

    def got(*hops):
        for n in hops:
            hop(n).wait_recv()

    def plus(place, *parts):
        total = grads[place, :].astype(jnp.float32)
        for part in parts:
            total = total + part.astype(jnp.float32)
        grads[place, :] = total.astype(jnp.bfloat16)

    def reduce_0():
        go(0, 1, 14, 15, 16, 17, 3, 4)

    def reduce_1():
        got(0)
        plus(unit(1, 0), ra1[0])
        go(2)
        got(1)
        plus(unit(3, 1), ra1[1])
        go(5)

    def reduce_2():
        for k in (2, 1, 3, 0):
            got(14 + k)
            plus(unit(k, y, 8), rb1[(z + k) % 4])
            if k == 2:
                go(18, 19)

    def reduce_3():
        got(2, 3, 4, 5)
        for c in range(2):
            plus(unit(0, c), ra2[0, c], ra2[1, c])
        go(6)

    def reduce_4():
        got(18, 19)
        plus(half_unit(1, y, 0), rb2[0])
        plus(half_unit(3, y, 1), rb2[1])
        go(20, 21)

    def reduce_5():
        got(6)
        plus(unit(0, y), ra4[...])
        reduced[unit(0, y), :] = grads[unit(0, y), :]
        go(7)

    def reduce_6():
        got(20, 21)
        plus(unit(0, y, 8), rb3[0], rb3[1])
        reduced[unit(0, y, 8), :] = grads[unit(0, y, 8), :]
        go(22, 23, 26)

    def reduce_7():
        got(7)
        go(8, 11, 9, 10)

    def reduce_8():
        got(22)
        go(24, 27)
        got(23)
        go(25, 28)
        got(8)
        go(12)
        got(11)
        go(13)

    def reduce_9():
        got(24, 25)
        go(29)

    def reduce_10():
        got(9, 10, 12, 13, 26, 27, 28, 29)
        for n in range(30):
            hop(n).wait_send()

    theirs_out = out_part_ref.at[pl.ds(pl.multiple_of((1 - ctx) * 8, 8), 8)]
    os_push = copy_to(theirs_out, out_sib, os_sem.at[0], os_sem.at[1], sibling)

    def out_push(i):
        return copy_to(
            out_own.at[(dp + i) % 8], out_in.at[dp], out_send.at[i], out_recv.at[dp], chip(i)
        )

    def out_arrival(d):
        return copy_to(out_in.at[d], out_in.at[d], out_send.at[0], out_recv.at[d], sibling)

    def chip(i):
        return ((dp + i) % 8, ctx, me)

    sources = (rows1_ref, raw_ref, q_ref, kv_ref.at[0], kv_ref.at[1], heads_ref, w_out_ref)
    targets = (rows1, raw, q_t, kv_own, kv_sib, heads, w_out)
    loads = [
        pltpu.make_async_copy(s, t, load_sem.at[n])
        for n, (s, t) in enumerate(zip(sources, targets, strict=True))
    ]
    loads.append(pltpu.make_async_copy(w_all_ref, w_all, load_sem.at[7]))
    loads.append(pltpu.make_async_copy(table_ref.at[ctx], table, load_sem.at[8]))
    loads.append(pltpu.make_async_copy(grads_ref, grads, load_sem.at[9]))
    own_blocks = out_part_ref.at[pl.ds(pl.multiple_of(ctx * 8, 8), 8)]
    loads.append(pltpu.make_async_copy(own_blocks, out_own, load_sem.at[10]))
    for load in loads:
        load.start()
    barrier = pltpu.get_barrier_semaphore()
    for i in range(1, 8):
        pl.semaphore_signal(barrier, inc=1, device_id=side(i), device_id_type=MESH)
        pl.semaphore_signal(barrier, inc=1, device_id=chip(i), device_id_type=MESH)
    pl.semaphore_signal(barrier, inc=1, device_id=sibling, device_id_type=MESH)

    gates, d_gate = gates_ref[...], d_gate_ref[...]
    d_logits = gates * (d_gate - jnp.sum(gates * d_gate, 0, keepdims=True))
    d_normed = d_rows_ref[...] + lax.dot_general(
        jnp.transpose(d_logits),
        router_ref[...].astype(f32),
        (((1,), (0,)), ((), ())),
        preferred_element_type=f32,
        precision=lax.Precision.HIGHEST,
    )
    resid = resid_ref[...]
    inv_two = lax.rsqrt(jnp.mean(resid * resid, -1, keepdims=True) + EPS)
    res_hat = resid * inv_two
    scaled = d_normed * norm2_ref[...]
    d_res = dy_ref[...].astype(f32) + inv_two * (
        scaled - res_hat * jnp.mean(scaled * res_hat, -1, keepdims=True)
    )
    d_resid[...] = d_res
    datt = d_res.astype(bf)
    datt_all[me] = datt
    for n in (6,):
        loads[n].wait()
    d_heads = dot_nt(w_out[...].reshape(1024, 1024), datt).astype(bf)
    dh_send[...] = d_heads.reshape(8, 128, 128)
    dh_all[me] = dh_send[me]
    pl.semaphore_wait(barrier, 15)

    def dh_push(i):
        return copy_to(
            dh_send.at[(me + i) % 8], dh_all.at[me], dh_send_sem.at[i], dh_recv.at[me], side(i)
        )

    def dh_arrival(t):
        return copy_to(dh_all.at[t], dh_all.at[t], dh_send_sem.at[0], dh_recv.at[t], sibling)

    for i in range(1, 8):
        dh_push(i).start()

    norm2_part = jnp.sum(d_normed * res_hat, 0, keepdims=True)
    router_part = jnp.dot(
        d_logits,
        rows2_ref[...].astype(f32),
        preferred_element_type=f32,
        precision=lax.Precision.HIGHEST,
    )
    tiny[me] = jnp.concatenate(
        [router_part, norm2_part, jnp.zeros((15, 1024), f32)], 0
    ).astype(bf)

    def t_push(i):
        return copy_to(tiny.at[me], tiny.at[me], t_send.at[i], t_recv.at[me], side(i))

    def t_arrival(t):
        return copy_to(tiny.at[t], tiny.at[t], t_send.at[0], t_recv.at[t], sibling)

    def a_push(i):
        return copy_to(datt_all.at[me], datt_all.at[me], a_send.at[i], a_recv.at[me], side(i))

    def a_arrival(t):
        return copy_to(datt_all.at[t], datt_all.at[t], a_send.at[0], a_recv.at[t], sibling)

    loads[9].wait()
    reduce_0()
    os_push.start()
    for i in range(1, 8):
        t_push(i).start()
    for i in (1, 7, 2, 6, 3, 5, 4):
        a_push(i).start()

    for n in (0, 1, 2, 3, 4, 5, 7, 8, 10):
        loads[n].wait()
    seg = segment_ref[...]
    start = jnp.zeros((16, 128), f32)
    for s in range(1, 8):
        below = jnp.where(seg < s, 1.0, 0.0)
        count = jnp.sum(jnp.sum(below, 1, keepdims=True), 0, keepdims=True)
        start = jnp.where(seg == s, count, start)
    start = jnp.where(ctx == 0, start[:8], start[8:])
    for t in range(8):
        starts[0:1, 128 * t : 128 * t + 128] = start[t : t + 1]

    def lay_out(t, carry):
        at = pl.ds(pl.multiple_of(t * 128, 128), 128)
        i, half = t // 2, t % 2
        q = q_t[:, at] * 0.125
        for h in range(2):
            spot = pl.ds(pl.multiple_of(h * 256 + half * 128, 128), 128)
            q_h = q[64 * h : 64 * h + 64]
            q_cat[i, :, spot] = q_h
            q_nat[i, spot, :] = jnp.transpose(q_h)
            lanes[i, 0:1, spot] = lse_ref[h, 0:1, at]
            lanes[i, 2:3, spot] = starts[0:1, at]
        for n, kv in enumerate((kv_own, kv_sib)):
            k_nat[n, at, :] = jnp.transpose(kv[0:64, at])
            v_nat[n, at, :] = jnp.transpose(kv[64:128, at])
        heads2[:, at] = heads[t]
        return carry

    lax.fori_loop(0, 8, lay_out, 0)
    dk_acc[...] = jnp.zeros_like(dk_acc)
    dv_acc[...] = jnp.zeros_like(dv_acc)
    dq_acc[...] = jnp.zeros_like(dq_acc)
    for i in range(1, 8):
        dh_arrival((me + i) % 8).wait_recv()

    def lay_dh(t, carry):
        i, half = t // 2, t % 2
        d, o = dh_all[t], heads[t]
        product = d.astype(f32) * o.astype(f32)
        for h in range(2):
            spot = pl.ds(pl.multiple_of(h * 256 + half * 128, 128), 128)
            d_h = d[64 * h : 64 * h + 64]
            d_cat[i, :, spot] = d_h
            d_nat[i, spot, :] = jnp.transpose(d_h)
            lanes[i, 1:2, spot] = jnp.sum(product[64 * h : 64 * h + 64], 0, keepdims=True)
        return carry

    lax.fori_loop(0, 8, lay_dh, 0)
    reduce_1()
    key_row = lax.broadcasted_iota(jnp.int32, (256, 512), 0).astype(f32)
    query_lane = (lax.broadcasted_iota(jnp.int32, (256, 512), 1) % 256).astype(f32)
    base = (ctx * 1024).astype(f32)

    def block(n, i, j, first_key, causal):
        ks = pl.ds(pl.multiple_of(j * 256, 256), 256)
        kv = (kv_own, kv_sib)[n]
        s = jnp.dot(k_nat[n, ks, :], q_cat[i], preferred_element_type=f32)
        ok = key_row >= lanes[i, 2:3, :] - first_key
        if causal:
            ok = ok & (key_row <= query_lane)
        p = jnp.exp(jnp.where(ok, s, MASKED) - lanes[i, 0:1, :])
        dp_ = jnp.dot(v_nat[n, ks, :], d_cat[i], preferred_element_type=f32)
        ds = (p * (dp_ - lanes[i, 1:2, :])).astype(bf)
        dv_acc[n, ks, :] += jnp.dot(p.astype(bf), d_nat[i], preferred_element_type=f32)
        dk_acc[n, ks, :] += jnp.dot(ds, q_nat[i], preferred_element_type=f32)
        dq_acc[i] += jnp.dot(kv[0:64, ks], ds, preferred_element_type=f32)

    def cross(n, carry):
        block(1, n // 4, n % 4, ((n % 4) * 256).astype(f32), False)
        return carry

    lax.fori_loop(0, 16 * ctx, cross, 0)
    dkv_push = copy_to(dkv_out, dkv_in, dkv_sem.at[0], dkv_sem.at[1], sibling)

    def upright(t, carry):
        at = pl.ds(pl.multiple_of(t * 128, 128), 128)
        dkv_out[0:64, at] = jnp.transpose(dk_acc[1, at, :]).astype(bf)
        dkv_out[64:128, at] = jnp.transpose(dv_acc[1, at, :]).astype(bf)
        return carry

    lax.fori_loop(0, 8, upright, 0)
    dkv_push.start()
    os_push.wait()

    def add_sib(d, carry):
        out_own[d] = (out_own[d].astype(f32) + out_sib[d].astype(f32)).astype(bf)
        return carry

    lax.fori_loop(0, 8, add_sib, 0)
    for i in range(1, 8):
        out_push(i).start()
    reduce_3()

    def within(i, carry):
        def full(j, c):
            block(0, i, j, base + (j * 256).astype(f32), False)
            return c

        lax.fori_loop(0, i, full, 0)
        block(0, i, i, base + (i * 256).astype(f32), True)
        return carry

    lax.fori_loop(0, 4, within, 0)
    reduce_2()
    gain_q = column(q_gain_ref[...])
    gain_k = column(jnp.concatenate([k_gain_ref[...], jnp.zeros((1, 64), f32)], 1))[:64]
    dkv_push.wait()

    def unturn(t, sums):
        at = pl.ds(pl.multiple_of(t * 128, 128), 128)
        i, half = t // 2, t % 2
        parts = [
            dq_acc[i, :, pl.ds(pl.multiple_of(h * 256 + half * 128, 128), 128)] for h in range(2)
        ]
        cos_part, sin_part = table[0, :, at], -table[1, :, at]
        inv = inv_ref[t]
        d_q = turn(jnp.concatenate(parts, 0) * 0.125, cos_part, sin_part)
        came = dkv_in[:, at].astype(f32)
        d_k = turn(jnp.transpose(dk_acc[0, at, :]) + came[0:64], cos_part, sin_part)
        d_v = jnp.transpose(dv_acc[0, at, :]) + came[64:128]
        q_hat, k_hat = raw[t, 0:128] * inv[0:1], raw[t, 128:192] * inv[1:2]
        q_sum, k_sum = sums[0] + d_q * q_hat, sums[1] + d_k * k_hat
        q_term, k_term = d_q * gain_q, d_k * gain_k
        terms[t, 0:128] = q_term
        terms[t, 128:192] = k_term
        dqkv[t, 192:256] = d_v.astype(bf)
        rows = [
            jnp.sum(q_term * q_hat, 0, keepdims=True),
            jnp.sum(k_term * k_hat, 0, keepdims=True),
            jnp.zeros((6, 128), f32),
        ]
        stat[t] = jnp.concatenate(rows, 0)
        return q_sum, k_sum

    q_sum, k_sum = lax.fori_loop(
        0, 8, unturn, (jnp.zeros((128, 128), f32), jnp.zeros((64, 128), f32))
    )
    stats[me] = stat[...]

    def s_push(i):
        return copy_to(stats.at[me], stats.at[me], s_send.at[i], s_recv.at[me], side(i))

    def s_arrival(t):
        return copy_to(stats.at[t], stats.at[t], s_send.at[0], s_recv.at[t], sibling)

    for i in range(1, 8):
        s_push(i).start()
    reduce_4()
    reduce_5()
    for i in range(1, 8):
        a_arrival((me + i) % 8).wait_recv()
    pack[256:384, :] = jnp.dot(
        heads2[...], datt_all[...].reshape(1024, 1024), preferred_element_type=f32
    ).astype(bf)
    reduce_6()
    for i in range(1, 8):
        t_arrival((me + i) % 8).wait_recv()
    total = tiny[0].astype(f32)
    for t in range(1, 8):
        total = total + tiny[t].astype(f32)
    q_row = jnp.sum(jnp.transpose(q_sum), 0, keepdims=True)
    k_row = jnp.sum(jnp.transpose(k_sum), 0, keepdims=True)
    gain_row = jnp.concatenate([q_row, k_row, jnp.zeros((1, 1024 - 192), f32)], 1)
    extra = jnp.concatenate([total[0:33], gain_row, jnp.zeros((94, 1024), f32)], 0)
    pack[384:512, :] = extra.astype(bf)
    for i in range(1, 8):
        s_arrival((me + i) % 8).wait_recv()

    def finish(t, carry):
        at = pl.ds(pl.multiple_of(t * 128, 128), 128)
        inner = stats[0, t]
        for s in range(1, 8):
            inner = inner + stats[s, t]
        inv = inv_ref[t]
        q_hat, k_hat = raw[t, 0:128] * inv[0:1], raw[t, 128:192] * inv[1:2]
        d_q = inv[0:1] * (terms[t, 0:128] - q_hat * (inner[0:1] / 1024.0))
        d_k = inv[1:2] * (terms[t, 128:192] - k_hat * (inner[1:2] / 512.0))
        dqkv[t, 0:128] = d_q.astype(bf)
        dqkv[t, 128:192] = d_k.astype(bf)
        return carry

    lax.fori_loop(0, 8, finish, 0)

    def o_push(i):
        return copy_to(
            dqkv.at[(me + i) % 8], dqkv_all.at[me], o_send.at[i], o_recv.at[me], side(i)
        )

    def o_arrival(t):
        return copy_to(dqkv_all.at[t], dqkv_all.at[t], o_send.at[0], o_recv.at[t], sibling)

    for i in range(1, 8):
        o_push(i).start()
    reduce_7()
    dqkv_all[me] = dqkv[me]
    grad_qkv = jnp.zeros((256, 1024), f32)
    for t in range(8):
        grad_qkv = grad_qkv + jnp.dot(dqkv[t], rows1[t], preferred_element_type=f32)
    pack[0:256, :] = grad_qkv.astype(bf)
    mine = pl.ds(pl.multiple_of(ctx * 256, 256), 256)
    theirs = pl.ds(pl.multiple_of((1 - ctx) * 256, 256), 256)
    p_push = copy_to(pack.at[theirs], pack_sib, p_sem.at[0], p_sem.at[1], sibling)
    p_push.start()
    for i in range(1, 8):
        o_arrival((me + i) % 8).wait_recv()
    d_rows1 = dot_tn(dqkv_all[...].reshape(2048, 128), w_all[...].reshape(2048, 1024))
    x = x_ref[...].astype(f32)
    inv_one = lax.rsqrt(jnp.mean(x * x, -1, keepdims=True) + EPS)
    x_hat = x * inv_one
    norm1_part = jnp.sum(d_rows1 * x_hat, 0, keepdims=True)
    n1[me] = jnp.concatenate([norm1_part[:, 128 * t : 128 * t + 128] for t in range(8)], 0)

    def n_push(i):
        return copy_to(n1.at[me], n1.at[me], n_send.at[i], n_recv.at[me], side(i))

    def n_arrival(t):
        return copy_to(n1.at[t], n1.at[t], n_send.at[0], n_recv.at[t], sibling)

    for i in range(1, 8):
        n_push(i).start()
    reduce_8()
    p_push.wait()
    pack[mine, :] = (pack[mine, :].astype(f32) + pack_sib[...].astype(f32)).astype(bf)

    def rs_push(i):
        to = (dp + i) % 8
        rows = pack.at[pl.ds(pl.multiple_of(ctx * 256 + to * 32, 32), 32)]
        return copy_to(rows, pack_in.at[dp], rs_send.at[i], rs_recv.at[dp], chip(i))

    def rs_arrival(d):
        return copy_to(pack_in.at[d], pack_in.at[d], rs_send.at[0], rs_recv.at[d], sibling)

    for i in range(1, 8):
        rs_push(i).start()
    scaled = d_rows1 * norm1_ref[...]
    grad_x_ref[...] = (
        d_resid[...] + inv_one * (scaled - x_hat * jnp.mean(scaled * x_hat, -1, keepdims=True))
    ).astype(bf)
    for i in range(1, 8):
        n_arrival((me + i) % 8).wait_recv()
    norm1_sum = n1[0]
    for t in range(1, 8):
        norm1_sum = norm1_sum + n1[t]
    n1_chips[dp] = norm1_sum

    def m_push(i):
        return copy_to(n1_chips.at[dp], n1_chips.at[dp], m_send.at[i], m_recv.at[dp], chip(i))

    def m_arrival(d):
        return copy_to(n1_chips.at[d], n1_chips.at[d], m_send.at[0], m_recv.at[d], sibling)

    for i in range(1, 8):
        m_push(i).start()
    pack_in[dp] = pack[pl.ds(pl.multiple_of(ctx * 256 + dp * 32, 32), 32), :]
    reduce_9()
    for i in range(1, 8):
        rs_arrival((dp + i) % 8).wait_recv()
    owned = pack_in[0].astype(f32)
    for d in range(1, 8):
        owned = owned + pack_in[d].astype(f32)
    result[ctx, dp] = owned.astype(bf)

    def g_push(i):
        return copy_to(
            result.at[ctx, dp], result.at[ctx, dp], g_send.at[i], g_recv.at[dp], chip(i)
        )

    def g_arrival(d):
        return copy_to(result.at[ctx, d], result.at[ctx, d], g_send.at[0], g_recv.at[d], sibling)

    def g_relay(d):
        return copy_to(
            result.at[ctx, d], result.at[ctx, d], gs_send.at[d], gs_recv.at[d], sibling
        )

    def g_sib_arrival(d):
        place = result.at[1 - ctx, d]
        return copy_to(place, place, gs_send.at[d], gs_recv.at[d], sibling)

    for i in range(1, 8):
        g_push(i).start()
    g_relay(dp).start()
    for i in range(1, 8):
        m_arrival((dp + i) % 8).wait_recv()
    norm1_sum = n1_chips[0]
    for d in range(1, 8):
        norm1_sum = norm1_sum + n1_chips[d]
    n1_sib[0] = norm1_sum
    ns_push = copy_to(n1_sib.at[0], n1_sib.at[1], ns_sem.at[0], ns_sem.at[1], sibling)
    ns_push.start()

    def pass_on(i, carry):
        d = (dp + i) % 8
        g_arrival(d).wait_recv()
        g_relay(d).start()
        return carry

    lax.fori_loop(1, 8, pass_on, 0)
    ns_push.wait()
    norm1_out_ref[...] = n1_sib[0] + n1_sib[1]
    for d in range(8):
        g_sib_arrival(d).wait_recv()
        g_relay(d).wait_send()
    for i in range(1, 8):
        out_arrival((dp + i) % 8).wait_recv()
    total = resid_ref[...] + out_own[dp].astype(f32)
    for i in range(1, 8):
        total = total + out_in[(dp + i) % 8].astype(f32)
    output_ref[...] = total.astype(bf)
    reduce_10()
    store = pltpu.make_async_copy(reduced, reduced_ref, load_sem.at[9])
    store.start()
    pack_ref[...] = result[...].reshape(512, 1024)
    for i in range(1, 8):
        dh_push(i).wait_send()
        t_push(i).wait_send()
        a_push(i).wait_send()
        s_push(i).wait_send()
        o_push(i).wait_send()
        n_push(i).wait_send()
        rs_push(i).wait_send()
        m_push(i).wait_send()
        g_push(i).wait_send()
        out_push(i).wait_send()
    store.wait()


def backward(small, large):
    bf, f32 = jnp.bfloat16, jnp.float32
    vmem, hbm = pl.BlockSpec(memory_space=pltpu.VMEM), pl.BlockSpec(memory_space=pl.ANY)
    sem = pltpu.SemaphoreType.DMA
    shape = jax.ShapeDtypeStruct
    table = jnp.asarray(rope_constants(2048, 32))
    return pl.pallas_call(
        backward_kernel,
        out_shape=(
            shape((128, 1024), bf),
            shape((8, 128), f32),
            shape((512, 1024), bf),
            shape((128, 1024), bf),
            shape((3072, 1024), bf),
        ),
        in_specs=[vmem] * 15 + [hbm] * 10,
        out_specs=(vmem, vmem, vmem, vmem, hbm),
        scratch_shapes=[
            pltpu.VMEM((8, 128, 1024), bf),
            pltpu.VMEM((8, 256, 128), f32),
            pltpu.VMEM((128, 1024), bf),
            pltpu.VMEM((128, 1024), bf),
            pltpu.VMEM((128, 1024), bf),
            pltpu.VMEM((8, 128, 128), bf),
            pltpu.VMEM((8, 128, 1024), bf),
            pltpu.VMEM((8, 256, 1024), bf),
            pltpu.VMEM((2, 32, 1024), f32),
            pltpu.VMEM((8, 1024), f32),
            pltpu.VMEM((128, 1024), f32),
            pltpu.VMEM((8, 128, 1024), bf),
            pltpu.VMEM((8, 128, 128), bf),
            pltpu.VMEM((8, 128, 128), bf),
            pltpu.VMEM((8, 48, 1024), bf),
            pltpu.VMEM((4, 64, 512), bf),
            pltpu.VMEM((4, 512, 64), bf),
            pltpu.VMEM((4, 64, 512), bf),
            pltpu.VMEM((4, 512, 64), bf),
            pltpu.VMEM((4, 8, 512), f32),
            pltpu.VMEM((2, 1024, 64), bf),
            pltpu.VMEM((2, 1024, 64), bf),
            pltpu.VMEM((4, 64, 512), f32),
            pltpu.VMEM((2, 1024, 64), f32),
            pltpu.VMEM((2, 1024, 64), f32),
            pltpu.VMEM((128, 1024), bf),
            pltpu.VMEM((128, 1024), bf),
            pltpu.VMEM((8, 192, 128), f32),
            pltpu.VMEM((8, 8, 128), f32),
            pltpu.VMEM((8, 8, 8, 128), f32),
            pltpu.VMEM((8, 256, 128), bf),
            pltpu.VMEM((8, 256, 128), bf),
            pltpu.VMEM((128, 1024), bf),
            pltpu.VMEM((512, 1024), bf),
            pltpu.VMEM((256, 1024), bf),
            pltpu.VMEM((8, 32, 1024), bf),
            pltpu.VMEM((2, 8, 32, 1024), bf),
            pltpu.VMEM((8, 8, 128), f32),
            pltpu.VMEM((8, 8, 128), f32),
            pltpu.VMEM((2, 8, 128), f32),
            sem((11,)),
        ]
        + [sem((8,))] * 8
        + [sem((2,))]
        + [sem((8,))] * 2
        + [sem((2,))]
        + [sem((8,))] * 10
        + [sem((2,))]
        + [
            pltpu.VMEM((3072, 1024), bf),
            pltpu.VMEM((3072, 1024), bf),
            pltpu.VMEM((2, 192, 1024), bf),
            pltpu.VMEM((2, 2, 192, 1024), bf),
            pltpu.VMEM((192, 1024), bf),
            pltpu.VMEM((4, 192, 1024), bf),
            pltpu.VMEM((2, 96, 1024), bf),
            pltpu.VMEM((2, 192, 1024), bf),
            sem((30,)),
            sem((30,)),
            pltpu.VMEM((8, 128, 1024), bf),
            pltpu.VMEM((8, 128, 1024), bf),
            pltpu.VMEM((8, 128, 1024), bf),
            sem((2,)),
            sem((8,)),
            sem((8,)),
        ],
        compiler_params=pltpu.CompilerParams(
            collective_id=3, has_side_effects=True, vmem_limit_bytes=56 << 20
        ),
        cost_estimate=pl.CostEstimate(
            flops=10_000_000_000, bytes_accessed=20_000_000, transcendentals=4_000_000
        ),
    )(*small, *large, table)


def shards(
    hidden_in,
    segment,
    norm1_gain,
    w_query,
    w_key,
    w_value,
    q_gain,
    k_gain,
    w_out,
    norm2_gain,
    router,
    w_gate,
    w_up,
    w_down,
    routes,
    cotangent,
):
    f32, bf = jnp.float32, jnp.bfloat16
    rows2, gates, resid, rows1, raw, inv, q_t, kv, lse, heads, w_out_all, dy_all, w_t = attention(
        hidden_in,
        cotangent,
        segment,
        norm1_gain,
        q_gain,
        k_gain,
        norm2_gain,
        router,
        routes,
        w_query,
        w_key,
        w_value,
        w_out,
    )
    d_rows, d_gate, out_part, grads, w_all = moe(
        rows2, gates, dy_all, w_gate, w_up, w_down, w_t
    )
    grad_x, norm1_sum, pack, output, grads = backward(
        (
            hidden_in,
            cotangent,
            d_rows,
            d_gate,
            gates,
            rows2,
            resid,
            router.T,
            norm1_gain.reshape(1, 1024),
            norm2_gain.reshape(1, 1024),
            q_gain.reshape(1, 128),
            k_gain.reshape(1, 64),
            segment.reshape(16, 128),
            inv,
            lse,
        ),
        (rows1, raw, q_t, kv, heads, w_out_all, w_all, grads.reshape(3072, 1024), out_part),
    )
    grads = grads.astype(f32)
    gate_up = grads[:2048].reshape(2, 1024, 1024)
    return (
        output,
        grad_x,
        norm1_sum.reshape(1024),
        pack[0:128].T.astype(f32),
        pack[128:192].T.astype(f32),
        pack[192:256].T.astype(f32),
        pack[417, :128].astype(f32),
        pack[417, 128:192].astype(f32),
        pack[256:384].astype(f32),
        pack[416].astype(f32),
        pack[384:416].T.astype(f32),
        gate_up[:, :, :512],
        gate_up[:, :, 512:],
        grads[2048:].reshape(2, 512, 1024),
    )


def solution(mesh):
    return jax.shard_map(
        shards,
        mesh=mesh,
        in_specs=(
            P(("dp", "ctx", "tensor"), None),
            P("dp"),
            P(),
            P(None, "tensor"),
            P(None, "tensor"),
            P(None, "tensor"),
            P("tensor"),
            P("tensor"),
            P("tensor", None),
            P(),
            P(),
            P(("dp", "ctx"), None, None),
            P(("dp", "ctx"), None, None),
            P(("dp", "ctx"), None, None),
            P(("dp", "ctx", "tensor"), None),
            P(("dp", "ctx", "tensor"), None),
        ),
        out_specs=(
            P(("dp", "ctx", "tensor"), None),
            P(("dp", "ctx", "tensor"), None),
            P(),
            P(None, "tensor"),
            P(None, "tensor"),
            P(None, "tensor"),
            P("tensor"),
            P("tensor"),
            P("tensor", None),
            P(),
            P(),
            P(("dp", "ctx"), None, None),
            P(("dp", "ctx"), None, None),
            P(("dp", "ctx"), None, None),
        ),
        check_vma=False,
    )
```

```python
import jax
import jax.numpy as jnp
import numpy as np
from jax import lax
from jax.experimental import pallas as pl
from jax.experimental.pallas import tpu as pltpu
from jax.sharding import PartitionSpec as P

EPS = 1e-06
THETA = 10000.0
MASKED = -1e30
MESH = pl.DeviceIdType.MESH


def rope_constants(length, half_dim):
    inverse = THETA ** (-(np.arange(half_dim, dtype=np.float64) * 2.0 / (2 * half_dim)))
    angles = inverse[:, None] * np.arange(length, dtype=np.float64)[None, :]
    table = np.stack([np.cos(angles), np.sin(angles)]).astype(np.float32)
    return np.ascontiguousarray(table.reshape(2, half_dim, 2, length // 2).transpose(2, 0, 1, 3))


def turn(value, cos_part, sin_part):
    parts = []
    for h in range(value.shape[0] // 64):
        a, b = value[64 * h : 64 * h + 32], value[64 * h + 32 : 64 * h + 64]
        parts += [a * cos_part - b * sin_part, b * cos_part + a * sin_part]
    return jnp.concatenate(parts, 0)


def column(row):
    return jnp.transpose(jnp.broadcast_to(row, (128, 128)))


def copy_to(src, dst, send, recv, device):
    return pltpu.make_async_remote_copy(
        src_ref=src, dst_ref=dst, send_sem=send, recv_sem=recv, device_id=device, device_id_type=MESH
    )


def dot_nt(left, right):
    return lax.dot_general(
        left, right, (((1,), (1,)), ((), ())), preferred_element_type=jnp.float32
    )


def dot_tn(left, right):
    return lax.dot_general(
        left, right, (((0,), (0,)), ((), ())), preferred_element_type=jnp.float32
    )


def across(a, b, flip):
    dp, ctx = lax.axis_index("dp"), lax.axis_index("ctx")
    x, y = dp % 4, dp // 4
    odd = a % 2
    by_x = odd * (1 + 2 * b) + (1 - odd) * a
    by_y = (1 - odd) * b + odd * (1 - a // 2)
    return ((y + by_y) % 2) * 4 + (x + by_x) % 4, (ctx + flip) % 2


def opposite(a, b):
    return b + (a % 2) * (1 - 2 * b)


def first_half(z, y, k, c):
    return pl.ds(pl.multiple_of(240 * (((z + k) % 4) * 2 + c), 16), 240)


def second_half(z, y, k, c):
    return pl.ds(pl.multiple_of(1920 + 144 * (((z + k) % 4) * 2 + c), 16), 144)


def piece(z, y, k, c, part):
    start = 1920 + 144 * (((z + k) % 4) * 2 + c) + 80 * part
    return pl.ds(pl.multiple_of(start, 16), (80, 64)[part])


def add_rows(ref, place, *parts):
    total = ref[place, :].astype(jnp.float32)
    for part in parts:
        total = total + part.astype(jnp.float32)
    ref[place, :] = total.astype(jnp.bfloat16)


def moe_kernel(
    rows_ref,
    gate_ref,
    dy_ref,
    w_gate_ref,
    w_up_ref,
    w_down_ref,
    w_t_ref,
    d_rows_ref,
    d_gate_ref,
    out_part_ref,
    grad_ref,
    w_all_ref,
    rows_all,
    gate_all,
    dy_all,
    w_full,
    acc,
    out_all,
    din_all,
    sib,
    rs_a,
    rs_b,
    rs_c,
    rs_d,
    rs_e,
    dg_out,
    dg_in,
    places,
    x_buf,
    y_buf,
    d_buf,
    o_buf,
    i_buf,
    gs_buf,
    dgs_buf,
    load_sem,
    ag_send,
    ag_recv,
    g_send,
    g_recv,
    sib_send,
    sib_recv,
    rs_send,
    rs_recv,
    dg_send,
    dg_recv,
    store_sem,
    w_send,
    w_recv,
    ra_0,
    ra_1,
    rb,
    r_send,
    r_recv,
):
    tensor = lax.axis_index("tensor")
    dp, ctx = lax.axis_index("dp"), lax.axis_index("ctx")
    me = dp * 2 + ctx

    def to(a, b, flip):
        d, c = across(a, b, flip)
        return (d, c, tensor)

    def side(i):
        return (dp, ctx, (tensor + i) % 8)

    loads = []
    for j in range(2):
        loads.append(
            pltpu.make_async_copy(w_gate_ref.at[j], w_full.at[pl.ds(1024 * j, 1024), pl.ds(0, 512)], load_sem.at[3 * j])
        )
        loads.append(
            pltpu.make_async_copy(
                w_up_ref.at[j], w_full.at[pl.ds(1024 * j, 1024), pl.ds(512, 512)], load_sem.at[3 * j + 1]
            )
        )
        loads.append(pltpu.make_async_copy(w_down_ref.at[j], w_full.at[pl.ds(2048 + 512 * j, 512)], load_sem.at[3 * j + 2]))
    loads.append(pltpu.make_async_copy(dy_ref, dy_all, load_sem.at[6]))
    for load in loads:
        load.start()

    barrier = pltpu.get_barrier_semaphore()
    for a in range(4):
        for b in range(2):
            for flip in range(2):
                if (a, b, flip) != (0, 0, 0):
                    pl.semaphore_signal(
                        barrier, inc=1, device_id=to(a, b, flip), device_id_type=MESH
                    )
    for i in range(1, 8):
        pl.semaphore_signal(barrier, inc=1, device_id=side(i), device_id_type=MESH)
    pl.semaphore_wait(barrier, 22)

    right, left, partner = to(3, 0, 0), to(3, 1, 0), to(0, 1, 0)
    sibling = to(0, 0, 1)
    low, high = pl.ds(0, 64), pl.ds(64, 64)

    def hop(n):
        src, dst, device = (
            (rows_all.at[0], rows_all.at[14], right),
            (rows_all.at[0], rows_all.at[12], left),
            (rows_all.at[0], rows_all.at[2], partner),
            (rows_all.at[14, low], rows_all.at[8, low], right),
            (rows_all.at[12, high], rows_all.at[8, high], left),
            (rows_all.at[2], rows_all.at[6], right),
            (rows_all.at[2], rows_all.at[4], left),
            (rows_all.at[8], rows_all.at[10], partner),
        )[n]
        return copy_to(src, dst, ag_send.at[n], ag_recv.at[n], device)

    def relay(ci):
        r = 2 * ci
        return copy_to(
            rows_all.at[r], rows_all.at[r + 1], ag_send.at[8 + ci], ag_recv.at[8 + ci], sibling
        )

    def gate_push(a, b, flip):
        r = 4 * a + 2 * b + flip
        back = 4 * a + 2 * opposite(a, b) + flip
        return copy_to(
            gate_all.at[0], gate_all.at[back], g_send.at[r], g_recv.at[back], to(a, b, flip)
        )

    rows_all[0] = rows_ref[...]
    gate_all[0] = gate_ref[...]
    for n in range(3):
        hop(n).start()
    relay(0).start()
    for r in range(1, 16):
        gate_push(r // 4, (r // 2) % 2, r % 2).start()

    acc[...] = jnp.zeros_like(acc)

    half = pl.ds(pl.multiple_of(ctx * 128, 128), 128)

    def w_push(i):
        return copy_to(
            w_t_ref.at[half],
            w_all_ref.at[tensor, half],
            w_send.at[i],
            w_recv.at[tensor, ctx],
            side(i),
        )

    def w_relay(t):
        place = w_all_ref.at[t, half]
        return copy_to(place, place, w_send.at[8 + t], w_recv.at[t, ctx], to(0, 0, 1))

    def w_arrival(t, c):
        place = w_all_ref.at[t, pl.ds(pl.multiple_of(c * 128, 128), 128)]
        return copy_to(place, place, w_send.at[0], w_recv.at[t, c], to(0, 0, 1))

    for i in (1, 7, 2, 6, 3, 5, 4):
        w_push(i).start()
    w_own = pltpu.make_async_copy(w_t_ref, w_all_ref.at[tensor], load_sem.at[7])
    w_own.start()

    def sib_push(ci):
        return copy_to(
            din_all.at[2 * ci + 1], sib.at[ci], sib_send.at[ci], sib_recv.at[ci], sibling
        )

    def rs_hop(n):
        src, dst, device = (
            (din_all.at[4], rs_a.at[0], right),
            (din_all.at[6], rs_a.at[1], left),
            (din_all.at[10], rs_b, partner),
            (din_all.at[2], rs_c, partner),
            (din_all.at[8, low], rs_d.at[0], right),
            (din_all.at[8, high], rs_d.at[1], left),
            (din_all.at[12], rs_e.at[0], right),
            (din_all.at[14], rs_e.at[1], left),
        )[n]
        return copy_to(src, dst, rs_send.at[n], rs_recv.at[n], device)

    def rs_go(*hops):
        for n in hops:
            rs_hop(n).start()

    def rs_got(*hops):
        for n in hops:
            rs_hop(n).wait_recv()

    def plus(r, rows, *parts):
        total = din_all[r, rows].astype(jnp.float32)
        for part in parts:
            total = total + part.astype(jnp.float32)
        din_all[r, rows] = total.astype(jnp.bfloat16)

    def post(*cis):
        for ci in cis:
            sib_push(ci).wait_recv()
            plus(2 * ci, slice(None), sib[ci])

    def dg_push(a, b, flip):
        r = 4 * a + 2 * b + flip
        back = 4 * a + 2 * opposite(a, b) + flip
        return pltpu.make_async_remote_copy(
            src_ref=dg_out.at[r],
            dst_ref=dg_in.at[back],
            send_sem=dg_send.at[r],
            recv_sem=dg_recv.at[back],
            device_id=to(a, b, flip),
            device_id_type=MESH,
        )

    expert_row = lax.broadcasted_iota(jnp.int32, (32, 128), 0)
    slot_row = lax.broadcasted_iota(jnp.int32, (64, 128), 0).astype(jnp.float32)
    before = (
        lax.broadcasted_iota(jnp.int32, (128, 128), 0)
        < lax.broadcasted_iota(jnp.int32, (128, 128), 1)
    ).astype(jnp.float32)
    before = before.astype(jnp.bfloat16)

    def gather(a, q):
        r = 4 * a + q
        gates = gate_all[r]
        at = pl.ds(pl.multiple_of(q * 64, 64), 64)
        rows = [
            jnp.sum(jnp.where(expert_row == 2 * me + j, gates, 0.0), 0, keepdims=True)
            for j in range(2)
        ]
        both = jnp.concatenate(rows + [jnp.zeros((6, 128), jnp.float32)], 0)
        named = jnp.where(both > 0.0, 1.0, 0.0).astype(jnp.bfloat16)
        slots = jnp.dot(named, before, preferred_element_type=jnp.float32)
        hits = [
            jnp.where((slot_row == slots[j : j + 1]) & (rows[j] > 0.0), 1.0, 0.0) for j in range(2)
        ]
        place = jnp.concatenate(hits, 0).astype(jnp.bfloat16)
        places[q] = place
        x = jnp.dot(place, rows_all[r], preferred_element_type=jnp.float32).astype(jnp.bfloat16)
        y = jnp.dot(place, dy_all[r], preferred_element_type=jnp.float32)
        for j in range(2):
            gs = jnp.sum(hits[j] * rows[j], 1, keepdims=True)
            y_j = y[64 * j : 64 * j + 64]
            x_buf[j, at, :] = x[64 * j : 64 * j + 64]
            y_buf[j, at, :] = y_j.astype(jnp.bfloat16)
            d_buf[j, at, :] = (y_j * gs).astype(jnp.bfloat16)
            gs_buf[j, at, :] = gs

    def expert(j):
        of_gu = pl.ds(pl.multiple_of(j * 1024, 1024), 1024)
        of_dn = pl.ds(pl.multiple_of(2048 + j * 512, 512), 512)
        x = x_buf[j]
        gu = jnp.dot(x, w_full[of_gu, :], preferred_element_type=jnp.float32)
        g, u = gu[:, :512], gu[:, 512:]
        s = jax.nn.sigmoid(g)
        silu = g * s
        act = (silu * u).astype(jnp.bfloat16)
        eout = (
            jnp.dot(act, w_full[of_dn, :], preferred_element_type=jnp.float32)
            .astype(jnp.bfloat16)
            .astype(jnp.float32)
        )
        dgs_buf[j] = jnp.sum(y_buf[j].astype(jnp.float32) * eout, 1, keepdims=True)
        o_buf[j] = (eout * gs_buf[j]).astype(jnp.bfloat16)
        d = d_buf[j]
        d_act = dot_nt(d, w_full[of_dn, :])
        d_g = (d_act * u * s * (1.0 + g * (1.0 - s))).astype(jnp.bfloat16)
        d_u = (d_act * silu).astype(jnp.bfloat16)
        d_gu = jnp.concatenate([d_g, d_u], 1)
        i_buf[j] = dot_nt(d_gu, w_full[of_gu, :]).astype(jnp.bfloat16)
        acc[of_gu, :] += dot_tn(x, d_gu)
        acc[of_dn, :] += dot_tn(act, d)

    def spread(a, q):
        r = 4 * a + q
        b, flip = q // 2, q % 2
        at = pl.ds(pl.multiple_of(q * 64, 64), 64)
        place = places[q]
        d, c = across(a, b, flip)
        o = jnp.concatenate([o_buf[0, at, :], o_buf[1, at, :]], 0)
        out_all[c * 8 + d] = dot_tn(place, o).astype(jnp.bfloat16)
        i = jnp.concatenate([i_buf[0, at, :], i_buf[1, at, :]], 0)
        din_all[r] = dot_tn(place, i).astype(jnp.bfloat16)
        hits = place.astype(jnp.float32)
        back = [
            jnp.sum(hits[64 * j : 64 * j + 64] * dgs_buf[j, at, :], 0, keepdims=True)
            for j in range(2)
        ]
        dg_out[r] = jnp.concatenate(back + [jnp.zeros((6, 128), jnp.float32)], 0)

        @pl.when(r > 0)
        def _():
            dg_push(a, b, flip).start()

    for n, ci in ((0, 7), (1, 6)):
        hop(n).wait_recv()
        hop(3 + n).start()
        relay(ci).start()
    hop(2).wait_recv()
    hop(5).start()
    hop(6).start()
    relay(1).start()
    relay(0).wait_recv()
    for r in range(1, 16):
        gate_push(r // 4, (r // 2) % 2, r % 2).wait_recv()
    for load in loads:
        load.wait()
    relay(1).wait_recv()

    def step(a, carry):
        lax.fori_loop(0, 4, lambda q, c: (gather(a, q), c)[1], 0)

        @pl.when(a == 1)
        def _():
            post(0, 1)

        @pl.when(a == 2)
        def _():
            post(2, 3)
            rs_go(0, 1)

        @pl.when(a == 3)
        def _():
            post(4, 5)
            rs_go(2)
            rs_got(0, 1)
            plus(2, slice(None), rs_a[0], rs_a[1])
            rs_go(3)

        lax.fori_loop(0, 2, lambda j, c: (expert(j), c)[1], 0)
        lax.fori_loop(0, 4, lambda q, c: (spread(a, q), c)[1], 0)
        for b in range(2):
            sib_push(2 * a + b).start()

        @pl.when(a == 0)
        def _():
            hop(3).wait_recv()
            hop(4).wait_recv()
            hop(7).start()
            relay(4).start()
            for n, ci in ((5, 3), (6, 2)):
                hop(n).wait_recv()
                relay(ci).start()
            for ci in (2, 3):
                relay(ci).wait_recv()

        @pl.when(a == 1)
        def _():
            hop(7).wait_recv()
            relay(5).start()
            for ci in (4, 5, 6, 7):
                relay(ci).wait_recv()

        return carry

    lax.fori_loop(0, 4, step, 0)
    rs_got(2)
    plus(8, slice(None), rs_b[...])
    rs_go(4, 5)

    def round_rows(n, carry):
        place = pl.ds(pl.multiple_of(n * 128, 128), 128)
        w_full[place, :] = acc[place, :].astype(jnp.bfloat16)
        return carry

    lax.fori_loop(0, 24, round_rows, 0)
    z, y = tensor // 2, tensor % 2
    up, down, pair = (
        (dp, ctx, ((z + 1) % 4) * 2 + y),
        (dp, ctx, ((z + 3) % 4) * 2 + y),
        (dp, ctx, z * 2 + 1 - y),
    )

    def grad_hop(n):
        place, dst, device = (
            (first_half(z, y, 2, 0), ra_0.at[0], up),
            (first_half(z, y, 2, 1), ra_0.at[1], down),
            (first_half(z, y, 1, 1), ra_1.at[0], up),
            (first_half(z, y, 3, 0), ra_1.at[1], down),
            (second_half(z, y, 2, 1 - y), rb.at[0], pair),
            (second_half(z, y, 1, 1 - y), rb.at[1], pair),
            (second_half(z, y, 3, 1 - y), rb.at[2], pair),
        )[n]
        return copy_to(w_full.at[place], dst, r_send.at[n], r_recv.at[n], device)

    for n in (0, 1, 4, 2, 3, 5, 6):
        grad_hop(n).start()
    post(6, 7)
    rs_got(4)
    plus(12, low, rs_d[0])
    rs_go(6)
    rs_got(5)
    plus(14, high, rs_d[1])
    rs_go(7)
    for i in range(1, 8):
        t = (tensor + i) % 8
        w_arrival(t, ctx).wait_recv()
        w_relay(t).start()
    for n in range(8):
        hop(n).wait_send()
        relay(n).wait_send()
    for r in range(1, 16):
        gate_push(r // 4, (r // 2) % 2, r % 2).wait_send()
    store_out = pltpu.make_async_copy(out_all, out_part_ref, store_sem.at[0])
    store_out.start()

    for r in range(1, 16):
        a, b, flip = r // 4, (r // 2) % 2, r % 2
        dg_push(a, b, flip).wait()
    dg_in[0] = dg_out[0]
    d_gate = jnp.zeros((32, 128), jnp.float32)
    for r in range(16):
        d, c = across(r // 4, (r // 2) % 2, r % 2)
        got = dg_in[r]
        for j in range(2):
            d_gate = jnp.where(expert_row == (d * 2 + c) * 2 + j, got[j : j + 1], d_gate)
    d_gate_ref[...] = d_gate
    for ci in range(8):
        sib_push(ci).wait_send()
    rs_got(3, 6, 7)
    total = din_all[0].astype(jnp.float32) + rs_c[...].astype(jnp.float32)
    d_rows_ref[...] = total + rs_e[0].astype(jnp.float32) + rs_e[1].astype(jnp.float32)
    for n in range(8):
        rs_hop(n).wait_send()
    for i in range(1, 8):
        t = (tensor + i) % 8
        w_arrival(t, 1 - ctx).wait_recv()
        w_push(i).wait_send()
        w_relay(t).wait_send()
    w_own.wait()
    grad_hop(0).wait_recv()
    add_rows(w_full, first_half(z, y, 1, 0), ra_0[0])
    grad_hop(1).wait_recv()
    add_rows(w_full, first_half(z, y, 3, 1), ra_0[1])
    grad_hop(4).wait_recv()
    add_rows(w_full, second_half(z, y, 2, y), rb[0])
    grad_hop(2).wait_recv()
    add_rows(w_full, first_half(z, y, 0, 1), ra_1[0])
    grad_hop(3).wait_recv()
    add_rows(w_full, first_half(z, y, 0, 0), ra_1[1])
    grad_hop(5).wait_recv()
    add_rows(w_full, second_half(z, y, 1, y), rb[1])
    grad_hop(6).wait_recv()
    add_rows(w_full, second_half(z, y, 3, y), rb[2])
    store_grad = pltpu.make_async_copy(w_full, grad_ref, store_sem.at[1])
    store_grad.start()
    for n in range(7):
        grad_hop(n).wait_send()
    store_out.wait()
    store_grad.wait()


def moe(rows, gates, dy, w_gate, w_up, w_down, w_t):
    bf, f32 = jnp.bfloat16, jnp.float32
    vmem, hbm = pl.BlockSpec(memory_space=pltpu.VMEM), pl.BlockSpec(memory_space=pl.ANY)
    sem = pltpu.SemaphoreType.DMA
    return pl.pallas_call(
        moe_kernel,
        out_shape=(
            jax.ShapeDtypeStruct((128, 1024), f32),
            jax.ShapeDtypeStruct((32, 128), f32),
            jax.ShapeDtypeStruct((16, 128, 1024), bf),
            jax.ShapeDtypeStruct((3072, 1024), bf),
            jax.ShapeDtypeStruct((8, 256, 1024), bf),
        ),
        in_specs=[vmem] * 2 + [hbm] * 4 + [vmem],
        out_specs=(vmem, vmem, hbm, hbm, hbm),
        scratch_shapes=[
            pltpu.VMEM((16, 128, 1024), bf),
            pltpu.VMEM((16, 32, 128), f32),
            pltpu.VMEM((16, 128, 1024), bf),
            pltpu.VMEM((3072, 1024), bf),
            pltpu.VMEM((3072, 1024), f32),
            pltpu.VMEM((16, 128, 1024), bf),
            pltpu.VMEM((16, 128, 1024), bf),
            pltpu.VMEM((8, 128, 1024), bf),
            pltpu.VMEM((2, 128, 1024), bf),
            pltpu.VMEM((128, 1024), bf),
            pltpu.VMEM((128, 1024), bf),
            pltpu.VMEM((2, 64, 1024), bf),
            pltpu.VMEM((2, 128, 1024), bf),
            pltpu.VMEM((16, 8, 128), f32),
            pltpu.VMEM((16, 8, 128), f32),
            pltpu.VMEM((4, 128, 128), bf),
            pltpu.VMEM((2, 256, 1024), bf),
            pltpu.VMEM((2, 256, 1024), bf),
            pltpu.VMEM((2, 256, 1024), bf),
            pltpu.VMEM((2, 256, 1024), bf),
            pltpu.VMEM((2, 256, 1024), bf),
            pltpu.VMEM((2, 256, 1), f32),
            pltpu.VMEM((2, 256, 1), f32),
            sem((8,)),
            sem((16,)),
            sem((16,)),
            sem((16,)),
            sem((16,)),
            sem((8,)),
            sem((8,)),
            sem((8,)),
            sem((8,)),
            sem((16,)),
            sem((16,)),
            sem((2,)),
            sem((16,)),
            sem((8, 2)),
            pltpu.VMEM((2, 240, 1024), bf),
            pltpu.VMEM((2, 240, 1024), bf),
            pltpu.VMEM((3, 144, 1024), bf),
            sem((7,)),
            sem((7,)),
        ],
        compiler_params=pltpu.CompilerParams(
            collective_id=1, has_side_effects=True, vmem_limit_bytes=60 << 20
        ),
        cost_estimate=pl.CostEstimate(
            flops=20_000_000_000, bytes_accessed=30_000_000, transcendentals=2_000_000
        ),
    )(rows, gates, dy, w_gate, w_up, w_down, w_t)


def attention_kernel(
    x_ref,
    dy_ref,
    segment_ref,
    norm1_ref,
    q_gain_ref,
    k_gain_ref,
    norm2_ref,
    router_ref,
    routes_ref,
    w_q_ref,
    w_k_ref,
    w_v_ref,
    w_out_ref,
    table_ref,
    rows2_ref,
    gates_ref,
    resid_ref,
    rows1_ref,
    raw_ref,
    inv_ref,
    q_ref,
    kv_ref,
    lse_ref,
    heads_ref,
    w_out_all_ref,
    dy_all_ref,
    w_t_ref,
    heads_all_ref,
    h_all,
    dy_all,
    w_all,
    w_q,
    w_t,
    raw,
    table,
    stat,
    stats,
    q_t,
    kv_own,
    kv_sib,
    k_own,
    k_sib,
    starts,
    heads,
    heads_all,
    load_sem,
    h_send,
    h_recv,
    dy_send,
    dy_recv,
    w_send,
    w_recv,
    s_send,
    s_recv,
    kv_sem,
    o_send,
    o_recv,
    store_sem,
):
    f32, bf = jnp.float32, jnp.bfloat16
    dp, ctx, me = lax.axis_index("dp"), lax.axis_index("ctx"), lax.axis_index("tensor")

    def side(i):
        return (dp, ctx, (me + i) % 8)

    def to(a, b, flip):
        d, c = across(a, b, flip)
        return (d, c, me)

    sibling = (dp, 1 - ctx, me)
    loads = [
        pltpu.make_async_copy(w_q_ref, w_q, load_sem.at[0]),
        pltpu.make_async_copy(w_k_ref, w_t.at[pl.ds(128, 64)], load_sem.at[1]),
        pltpu.make_async_copy(w_v_ref, w_t.at[pl.ds(192, 64)], load_sem.at[2]),
        pltpu.make_async_copy(w_out_ref, w_all.at[me], load_sem.at[3]),
        pltpu.make_async_copy(table_ref.at[ctx], table, load_sem.at[4]),
    ]
    for load in loads:
        load.start()
    barrier = pltpu.get_barrier_semaphore()
    for i in range(1, 8):
        pl.semaphore_signal(barrier, inc=1, device_id=side(i), device_id_type=MESH)
    for a in range(4):
        for b in range(2):
            if (a, b) != (0, 0):
                pl.semaphore_signal(barrier, inc=1, device_id=to(a, b, 0), device_id_type=MESH)
    pl.semaphore_signal(barrier, inc=1, device_id=sibling, device_id_type=MESH)
    x = x_ref[...].astype(f32)
    inv_one = lax.rsqrt(jnp.mean(x * x, -1, keepdims=True) + EPS)
    h_all[me] = (x * inv_one * norm1_ref[...]).astype(bf)
    dy_all[0] = dy_ref[...]
    pl.semaphore_wait(barrier, 15)

    z, y = me // 2, me % 2
    up, down, pair = (
        (dp, ctx, ((z + 1) % 4) * 2 + y),
        (dp, ctx, ((z + 3) % 4) * 2 + y),
        (dp, ctx, z * 2 + 1 - y),
    )
    low, high = pl.ds(0, 64), pl.ds(64, 64)

    def block_at(k, flip):
        return ((z + k) % 4) * 2 + (y + flip) % 2

    def h_hop(n):
        place, device = (
            (h_all.at[me], up),
            (h_all.at[me], down),
            (h_all.at[me], pair),
            (h_all.at[block_at(3, 0), low], up),
            (h_all.at[block_at(1, 0), high], down),
            (h_all.at[block_at(0, 1)], up),
            (h_all.at[block_at(0, 1)], down),
            (h_all.at[block_at(2, 0)], pair),
        )[n]
        return copy_to(place, place, h_send.at[n], h_recv.at[n], device)

    right, left, partner = to(3, 0, 0), to(3, 1, 0), to(0, 1, 0)

    def dy_hop(n):
        src, dst, device = (
            (dy_all.at[0], dy_all.at[14], right),
            (dy_all.at[0], dy_all.at[12], left),
            (dy_all.at[0], dy_all.at[2], partner),
            (dy_all.at[14, low], dy_all.at[8, low], right),
            (dy_all.at[12, high], dy_all.at[8, high], left),
            (dy_all.at[2], dy_all.at[6], right),
            (dy_all.at[2], dy_all.at[4], left),
            (dy_all.at[8], dy_all.at[10], partner),
        )[n]
        return copy_to(src, dst, dy_send.at[n], dy_recv.at[n], device)

    def dy_relay(ci):
        r = 2 * ci
        return copy_to(
            dy_all.at[r], dy_all.at[r + 1], dy_send.at[8 + ci], dy_recv.at[8 + ci], sibling
        )

    for n in range(3):
        h_hop(n).start()
    for n in range(3):
        dy_hop(n).start()
    dy_relay(0).start()

    for load in loads:
        load.wait()
    w_t[0:128, :] = jnp.transpose(w_q[...])
    seg = segment_ref[...]
    start = jnp.zeros((16, 128), f32)
    for s in range(1, 8):
        below = jnp.where(seg < s, 1.0, 0.0)
        count = jnp.sum(jnp.sum(below, 1, keepdims=True), 0, keepdims=True)
        start = jnp.where(seg == s, count, start)
    start = jnp.where(ctx == 0, start[:8], start[8:])
    for t in range(8):
        starts[0:1, 128 * t : 128 * t + 128] = start[t : t + 1]

    def project(t):
        value = dot_nt(w_t[...], h_all[t])
        raw[t] = value
        square = value * value
        stat[0, pl.ds(t, 1), :] = jnp.sum(square[0:128], 0, keepdims=True)
        stat[1, pl.ds(t, 1), :] = jnp.sum(square[128:192], 0, keepdims=True)

    project(me)
    for n in range(2):
        h_hop(n).wait_recv()
        h_hop(3 + n).start()
    h_hop(2).wait_recv()
    h_hop(5).start()
    h_hop(6).start()
    for k, flip in ((3, 0), (1, 0), (0, 1)):
        project(block_at(k, flip))
    h_hop(3).wait_recv()
    h_hop(4).wait_recv()
    h_hop(7).start()
    project(block_at(2, 0))
    for n, k in ((5, 3), (6, 1), (7, 2)):
        h_hop(n).wait_recv()
        project(block_at(k, 1))
    stats[me] = stat[...]

    def s_push(i):
        return copy_to(stats.at[me], stats.at[me], s_send.at[i], s_recv.at[me], side(i))

    def s_arrival(t):
        return copy_to(stats.at[t], stats.at[t], s_send.at[0], s_recv.at[t], sibling)

    for i in range(1, 8):
        s_push(i).start()
    store_rows = pltpu.make_async_copy(h_all, rows1_ref, store_sem.at[0])
    store_raw = pltpu.make_async_copy(raw, raw_ref, store_sem.at[1])
    store_wt = pltpu.make_async_copy(w_t, w_t_ref, store_sem.at[8])
    store_rows.start()
    store_raw.start()
    store_wt.start()

    def w_push(i):
        half = w_all.at[me, pl.ds(pl.multiple_of(ctx * 64, 64), 64)]
        return copy_to(half, half, w_send.at[i], w_recv.at[me, ctx], side(i))

    def w_relay(t):
        half = w_all.at[t, pl.ds(pl.multiple_of(ctx * 64, 64), 64)]
        return copy_to(half, half, w_send.at[8 + t], w_recv.at[t, ctx], sibling)

    def w_arrival(t, c):
        half = w_all.at[t, pl.ds(pl.multiple_of(c * 64, 64), 64)]
        return copy_to(half, half, w_send.at[0], w_recv.at[t, c], sibling)

    for n, ci in ((0, 7), (1, 6)):
        dy_hop(n).wait_recv()
        dy_hop(3 + n).start()
        dy_relay(ci).start()
    dy_hop(2).wait_recv()
    dy_hop(5).start()
    dy_hop(6).start()
    dy_relay(1).start()
    for i in (1, 7, 2, 6, 3, 5, 4):
        w_push(i).start()
    gain_q = column(q_gain_ref[...])
    gain_k = column(jnp.concatenate([k_gain_ref[...], jnp.zeros((1, 64), f32)], 1))[:64]
    for i in range(1, 8):
        s_arrival((me + i) % 8).wait_recv()

    def finish(t, carry):
        at = pl.ds(pl.multiple_of(t * 128, 128), 128)
        rows = []
        for n, width in enumerate((1024.0, 512.0)):
            total = stats[0, n, pl.ds(t, 1), :]
            for s in range(1, 8):
                total = total + stats[s, n, pl.ds(t, 1), :]
            rows.append(lax.rsqrt(total / width + EPS))
        inv = jnp.concatenate(rows + [jnp.zeros((6, 128), f32)], 0)
        inv_ref[t] = inv
        value = raw[t]
        cos_part, sin_part = table[0, :, at], table[1, :, at]
        queries = turn(value[0:128] * inv[0:1] * gain_q, cos_part, sin_part).astype(bf)
        keys = turn(value[128:192] * inv[1:2] * gain_k, cos_part, sin_part).astype(bf)
        q_t[:, at] = queries
        kv_own[0:64, at] = keys
        kv_own[64:128, at] = value[192:256].astype(bf)
        k_own[at, :] = jnp.transpose(keys)
        return carry

    lax.fori_loop(0, 8, finish, 0)
    kv_push = copy_to(kv_own, kv_sib, kv_sem.at[0], kv_sem.at[1], sibling)
    kv_push.start()

    key_row = lax.broadcasted_iota(jnp.int32, (256, 256), 0).astype(f32)
    query_lane = lax.broadcasted_iota(jnp.int32, (256, 256), 1).astype(f32)
    base = (ctx * 1024).astype(f32)

    def attend(n, carry):
        i, h = n // 2, n % 2
        at = pl.ds(pl.multiple_of(i * 256, 256), 256)
        q = q_t[pl.ds(pl.multiple_of(h * 64, 64), 64), at] * 0.125
        begin = starts[0:1, at]

        def block(keys, values, first_key, state, causal):
            top, total, acc = state
            s = jnp.dot(keys, q, preferred_element_type=f32)
            ok = key_row >= begin - first_key
            if causal:
                ok = ok & (key_row <= query_lane)
            s = jnp.where(ok, s, MASKED)
            new_top = jnp.maximum(top, jnp.max(s, 0, keepdims=True))
            e = jnp.exp(s - new_top)
            shrink = jnp.exp(top - new_top)
            total = total * shrink + jnp.sum(e, 0, keepdims=True)
            acc = acc * shrink + jnp.dot(values, e.astype(bf), preferred_element_type=f32)
            return new_top, total, acc

        state = (jnp.full((1, 256), MASKED, f32), jnp.zeros((1, 256), f32), jnp.zeros((64, 256), f32))
        state = block(
            k_own[at, :], kv_own[64:128, at], base + (i * 256).astype(f32), state, True
        )

        def own(j, state):
            ks = pl.ds(pl.multiple_of(j * 256, 256), 256)
            return block(k_own[ks, :], kv_own[64:128, ks], base + (j * 256).astype(f32), state, False)

        state = lax.fori_loop(0, i, own, state)

        def other(j, state):
            ks = pl.ds(pl.multiple_of(j * 256, 256), 256)
            return block(k_sib[ks, :], kv_sib[64:128, ks], (j * 256).astype(f32), state, False)

        top, total, acc = lax.fori_loop(0, 4 * ctx, other, state)
        out = (acc / total).astype(bf)
        hs = pl.ds(pl.multiple_of(h * 64, 64), 64)
        heads[2 * i, hs, :] = out[:, :128]
        heads[2 * i + 1, hs, :] = out[:, 128:]
        lse_ref[h, 0:1, at] = top + jnp.log(total)
        return carry

    kv_push.wait()

    def straighten(t, carry):
        at = pl.ds(pl.multiple_of(t * 128, 128), 128)
        k_sib[at, :] = jnp.transpose(kv_sib[0:64, at])
        return carry

    dy_hop(3).wait_recv()
    dy_hop(4).wait_recv()
    dy_hop(7).start()
    dy_relay(4).start()
    lax.fori_loop(0, 8, straighten, 0)
    lax.fori_loop(0, 8, attend, 0)

    def o_push(i):
        return copy_to(
            heads.at[(me + i) % 8], heads_all.at[me], o_send.at[i], o_recv.at[me], side(i)
        )

    def o_arrival(t):
        return copy_to(heads_all.at[t], heads_all.at[t], o_send.at[0], o_recv.at[t], sibling)

    for i in range(1, 8):
        o_push(i).start()
    heads_all[me] = heads[me]
    stores = [
        pltpu.make_async_copy(q_t, q_ref, store_sem.at[2]),
        pltpu.make_async_copy(kv_own, kv_ref.at[0], store_sem.at[3]),
        pltpu.make_async_copy(kv_sib, kv_ref.at[1], store_sem.at[4]),
        pltpu.make_async_copy(heads, heads_ref, store_sem.at[5]),
    ]
    for store in stores:
        store.start()

    def pass_on(i, carry):
        t = (me + i) % 8
        w_arrival(t, ctx).wait_recv()
        w_relay(t).start()
        return carry

    lax.fori_loop(1, 8, pass_on, 0)

    for n, ci in ((5, 3), (6, 2), (7, 5)):
        dy_hop(n).wait_recv()
        dy_relay(ci).start()
    for i in range(1, 8):
        t = (me + i) % 8
        w_arrival(t, 1 - ctx).wait_recv()
        o_arrival(t).wait_recv()
    store_w = pltpu.make_async_copy(w_all, w_out_all_ref, store_sem.at[6])
    store_w.start()
    store_heads = pltpu.make_async_copy(heads_all, heads_all_ref, store_sem.at[9])
    store_heads.start()
    attended = dot_tn(heads_all[...].reshape(1024, 128), w_all[...].reshape(1024, 1024))
    resid = x + attended
    resid_ref[...] = resid
    inv_two = lax.rsqrt(jnp.mean(resid * resid, -1, keepdims=True) + EPS)
    rows2 = (resid * inv_two * norm2_ref[...]).astype(bf)
    rows2_ref[...] = rows2
    logits = dot_nt(router_ref[...], rows2)
    expert_row = lax.broadcasted_iota(jnp.int32, (32, 128), 0)
    routes = routes_ref[...]
    named = routes[0:1] == expert_row
    for k in range(1, 8):
        named = named | (routes[k : k + 1] == expert_row)
    chosen = jnp.where(named, logits, MASKED)
    weight = jnp.where(named, jnp.exp(chosen - jnp.max(chosen, 0, keepdims=True)), 0.0)
    gates_ref[...] = weight / jnp.sum(weight, 0, keepdims=True)

    for ci in range(8):
        dy_relay(ci).wait_recv()
    store_dy = pltpu.make_async_copy(dy_all, dy_all_ref, store_sem.at[7])
    store_dy.start()
    for i in range(1, 8):
        s_push(i).wait_send()
        w_push(i).wait_send()
        w_relay((me + i) % 8).wait_send()
        o_push(i).wait_send()
    for n in range(8):
        h_hop(n).wait_send()
        dy_hop(n).wait_send()
        dy_relay(n).wait_send()
    for store in [store_rows, store_raw, store_wt, store_w, store_dy, store_heads] + stores:
        store.wait()


def attention(x, dy, segment, norm1, q_gain, k_gain, norm2, router, routes, w_q, w_k, w_v, w_out):
    bf, f32 = jnp.bfloat16, jnp.float32
    vmem, hbm = pl.BlockSpec(memory_space=pltpu.VMEM), pl.BlockSpec(memory_space=pl.ANY)
    sem = pltpu.SemaphoreType.DMA
    shape = jax.ShapeDtypeStruct
    table = jnp.asarray(rope_constants(2048, 32))
    return pl.pallas_call(
        attention_kernel,
        out_shape=(
            shape((128, 1024), bf),
            shape((32, 128), f32),
            shape((128, 1024), f32),
            shape((8, 128, 1024), bf),
            shape((8, 256, 128), f32),
            shape((8, 8, 128), f32),
            shape((128, 1024), bf),
            shape((2, 128, 1024), bf),
            shape((2, 8, 1024), f32),
            shape((8, 128, 128), bf),
            shape((8, 128, 1024), bf),
            shape((16, 128, 1024), bf),
            shape((256, 1024), bf),
            shape((8, 128, 128), bf),
        ),
        in_specs=[vmem] * 9 + [hbm] * 5,
        out_specs=(vmem, vmem, vmem, hbm, hbm, vmem, hbm, hbm, vmem, hbm, hbm, hbm, hbm, hbm),
        scratch_shapes=[
            pltpu.VMEM((8, 128, 1024), bf),
            pltpu.VMEM((16, 128, 1024), bf),
            pltpu.VMEM((8, 128, 1024), bf),
            pltpu.VMEM((1024, 128), bf),
            pltpu.VMEM((256, 1024), bf),
            pltpu.VMEM((8, 256, 128), f32),
            pltpu.VMEM((2, 32, 1024), f32),
            pltpu.VMEM((2, 8, 128), f32),
            pltpu.VMEM((8, 2, 8, 128), f32),
            pltpu.VMEM((128, 1024), bf),
            pltpu.VMEM((128, 1024), bf),
            pltpu.VMEM((128, 1024), bf),
            pltpu.VMEM((1024, 64), bf),
            pltpu.VMEM((1024, 64), bf),
            pltpu.VMEM((8, 1024), f32),
            pltpu.VMEM((8, 128, 128), bf),
            pltpu.VMEM((8, 128, 128), bf),
            sem((5,)),
            sem((8,)),
            sem((8,)),
            sem((16,)),
            sem((16,)),
            sem((16,)),
            sem((8, 2)),
            sem((8,)),
            sem((8,)),
            sem((2,)),
            sem((8,)),
            sem((8,)),
            sem((10,)),
        ],
        compiler_params=pltpu.CompilerParams(
            collective_id=2, has_side_effects=True, vmem_limit_bytes=56 << 20
        ),
        cost_estimate=pl.CostEstimate(
            flops=5_000_000_000, bytes_accessed=20_000_000, transcendentals=4_000_000
        ),
    )(
        x,
        dy,
        segment.reshape(16, 128),
        norm1.reshape(1, 1024),
        q_gain.reshape(1, 128),
        k_gain.reshape(1, 64),
        norm2.reshape(1, 1024),
        router.T,
        routes.T,
        w_q,
        w_k.T,
        w_v.T,
        w_out,
        table,
    )


def backward_kernel(
    x_ref,
    dy_ref,
    d_rows_ref,
    d_gate_ref,
    gates_ref,
    rows2_ref,
    resid_ref,
    router_ref,
    norm1_ref,
    norm2_ref,
    q_gain_ref,
    k_gain_ref,
    segment_ref,
    inv_ref,
    lse_ref,
    rows1_ref,
    raw_ref,
    q_ref,
    kv_ref,
    heads_ref,
    heads_all_ref,
    w_out_ref,
    w_all_ref,
    grads_ref,
    out_part_ref,
    table_ref,
    grad_x_ref,
    norm1_out_ref,
    pack_ref,
    output_ref,
    reduced_ref,
    rows1,
    raw,
    q_t,
    kv_own,
    kv_sib,
    heads,
    w_out,
    w_all,
    table,
    starts,
    d_resid,
    heads_all,
    wo_part,
    wo_in,
    dh_send,
    dh_all,
    tiny,
    q_cat,
    q_nat,
    d_cat,
    d_nat,
    lanes,
    k_nat,
    v_nat,
    dq_acc,
    dk_acc,
    dv_acc,
    dkv_out,
    dkv_in,
    terms,
    stat,
    stats,
    dqkv,
    dqkv_all,
    pack,
    pack_sib,
    pack_in,
    result,
    n1,
    n1_chips,
    n1_sib,
    load_sem,
    a_send,
    a_recv,
    dh_send_sem,
    dh_recv,
    t_send,
    t_recv,
    s_send,
    s_recv,
    dkv_sem,
    o_send,
    o_recv,
    p_sem,
    rs_send,
    rs_recv,
    g_send,
    g_recv,
    gs_send,
    gs_recv,
    n_send,
    n_recv,
    m_send,
    m_recv,
    ns_sem,
    grads,
    reduced,
    ra2,
    ra4,
    rb1,
    rb2,
    rb3,
    r_send,
    r_recv,
    out_own,
    out_sib,
    out_a,
    out_b,
    out_c,
    os_sem,
    out_send,
    out_recv,
):
    f32, bf = jnp.float32, jnp.bfloat16
    dp, ctx, me = lax.axis_index("dp"), lax.axis_index("ctx"), lax.axis_index("tensor")
    sibling = (dp, 1 - ctx, me)

    def side(i):
        return (dp, ctx, (me + i) % 8)

    def chip(i):
        return ((dp + i) % 8, ctx, me)

    z, y = me // 2, me % 2
    other = 1 - y
    up, down, pair = (
        (dp, ctx, ((z + 1) % 4) * 2 + y),
        (dp, ctx, ((z + 3) % 4) * 2 + y),
        (dp, ctx, z * 2 + other),
    )

    def a_rows(k, c, s=0):
        start = 240 * (((z + k) % 4) * 2 + c) + 128 * s
        return pl.ds(pl.multiple_of(start, 16), (128, 112)[s])

    def of_part(s):
        return pl.ds(128 * s, (128, 112)[s])

    def b_rows(k, c):
        return second_half(z, y, k, c)

    def hop(n, s=0):
        if n < 2:
            src, dst = grads.at[a_rows((1, 3)[n], n, s)], ra2.at[n, of_part(s)]
            to = (up, down)[n]
        elif n == 2:
            src, dst, to = grads.at[b_rows(0, other)], rb1, pair
        elif n < 5:
            part = n - 3
            src, to = grads.at[piece(z, y, 2, y, part)], (up, down)[part]
            dst = (rb2.at[pl.ds(0, 80)], rb2.at[pl.ds(80, 64)])[part]
        elif n == 5:
            src, dst, to = grads.at[a_rows(0, other, s)], ra4.at[of_part(s)], pair
        elif n == 6:
            src, dst, to = grads.at[b_rows(1, y)], rb3.at[0], up
        elif n == 7:
            src, dst, to = grads.at[b_rows(3, y)], rb3.at[1], down
        else:
            place, to = (
                (a_rows(0, y, s), pair),
                (a_rows(0, y, s), up),
                (a_rows(0, y, s), down),
                (a_rows(0, other, s), up),
                (a_rows(0, other, s), down),
                (a_rows(3, 0, s), up),
                (a_rows(1, 1, s), down),
                (b_rows(0, y), up),
                (b_rows(0, y), down),
                (piece(z, y, 3, y, 0), up),
                (piece(z, y, 1, y, 1), down),
                (b_rows(0, y), pair),
                (b_rows(3, y), pair),
                (b_rows(1, y), pair),
                (b_rows(2, y), pair),
            )[n - 8]
            src = dst = reduced.at[place]
        return copy_to(src, dst, r_send.at[n + 23 * s], r_recv.at[n + 23 * s], to)

    def go(*hops, s=0):
        for n in hops:
            hop(n, s).start()

    def got(*hops, s=0):
        for n in hops:
            hop(n, s).wait_recv()

    def reduce_0():
        go(0, 1, 3, 4, 2)

    def reduce_1(s):
        got(0, 1, s=s)
        for c in range(2):
            add_rows(grads, a_rows(0, c, s), ra2[c, of_part(s)])
        go(5, s=s)

    def reduce_2():
        got(3, 4)
        add_rows(grads, piece(z, y, 1, y, 0), rb2[0:80])
        add_rows(grads, piece(z, y, 3, y, 1), rb2[80:144])
        go(6, 7)
        got(2)
        add_rows(grads, b_rows(0, y), rb1[...])

    def reduce_3(s):
        got(5, s=s)
        add_rows(grads, a_rows(0, y, s), ra4[of_part(s)])
        reduced[a_rows(0, y, s), :] = grads[a_rows(0, y, s), :]
        go(8, 9, 10, s=s)

    def reduce_4():
        got(6, 7)
        add_rows(grads, b_rows(0, y), rb3[0], rb3[1])
        reduced[b_rows(0, y), :] = grads[b_rows(0, y), :]
        go(15, 16, 19)

    def reduce_5(s):
        got(8, s=s)
        go(11, 12, s=s)

    def reduce_6():
        got(15)
        go(17, 20)
        got(16)
        go(18, 21)

    def reduce_7(s):
        @pl.when(y == 0)
        def _():
            got(9, 12, s=s)

        @pl.when(y == 1)
        def _():
            got(11, 10, s=s)

        go(13, 14, s=s)

    def reduce_8():
        got(17, 18)
        go(22)

    def reduce_9():
        for s in range(2):

            @pl.when(y == 0)
            def _():
                got(10, 11, s=s)

            @pl.when(y == 1)
            def _():
                got(9, 12, s=s)

            got(13, 14, s=s)
        got(19, 20, 21, 22)
        for n in range(23):
            hop(n).wait_send()
        for n in (0, 1, 5, 8, 9, 10, 11, 12, 13, 14):
            hop(n, 1).wait_send()

    def x_side(i):
        return ((dp // 4) * 4 + (dp + i) % 4, ctx, me)

    right, left, partner = x_side(1), x_side(3), ((dp + 4) % 8, ctx, me)
    theirs_out = out_part_ref.at[pl.ds(pl.multiple_of((1 - ctx) * 8, 8), 8)]
    os_push = copy_to(
        theirs_out, out_sib.at[:, :, pl.ds(0, 1024)], os_sem.at[0], os_sem.at[1], sibling
    )
    wo_push = copy_to(
        wo_part.at[1 - ctx],
        out_sib.at[:, :, pl.ds(1024, 512)],
        os_sem.at[2],
        os_sem.at[3],
        sibling,
    )

    def out_at(i, b):
        return (dp // 4 + b) % 2 * 4 + (dp + i) % 4

    def out_hop(n):
        b = n % 2
        if n < 2:
            src, dst, to = out_own.at[out_at(2, b), pl.ds(0, 64)], out_a.at[0, b], right
        elif n < 4:
            src, dst, to = out_own.at[out_at(2, b), pl.ds(64, 64)], out_a.at[1, b], left
        elif n < 6:
            src, dst, to = out_own.at[out_at(1, b)], out_b.at[0, b], right
        elif n < 8:
            src, dst, to = out_own.at[out_at(3, b)], out_b.at[1, b], left
        else:
            src, dst, to = out_own.at[out_at(0, 1)], out_c, partner
        return copy_to(src, dst, out_send.at[n], out_recv.at[n], to)

    def out_0():
        os_push.wait()
        wo_push.wait()

        def add_sib(d, carry):
            left_part = out_own[d, :, 0:1024].astype(f32)
            right_part = wo_part[ctx, d].astype(f32)
            total = jnp.concatenate([left_part, right_part], 1) + out_sib[d].astype(f32)
            out_own[d] = total.astype(bf)
            return carry

        lax.fori_loop(0, 8, add_sib, 0)
        for n in range(4):
            out_hop(n).start()

    def out_add(at, rows, *parts):
        total = out_own[at, rows].astype(f32)
        for part in parts:
            total = total + part.astype(f32)
        out_own[at, rows] = total.astype(bf)

    def out_1():
        for b in range(2):
            out_hop(b).wait_recv()
            out_add(out_at(1, b), pl.ds(0, 64), out_a[0, b])
            out_hop(4 + b).start()
            out_hop(2 + b).wait_recv()
            out_add(out_at(3, b), pl.ds(64, 64), out_a[1, b])
            out_hop(6 + b).start()

    def out_2():
        for b in (1, 0):
            out_hop(4 + b).wait_recv()
            out_hop(6 + b).wait_recv()
            out_add(out_at(0, b), slice(None), out_b[0, b], out_b[1, b])
            if b == 1:
                out_hop(8).start()

    def out_3():
        out_hop(8).wait_recv()
        total = out_own[dp].astype(f32) + out_c[...].astype(f32)
        output_ref[...] = (resid_ref[...] + total[:, 0:1024]).astype(bf)
        wo_sum = total[:, 1024:1536].astype(bf)
        for t in range(8):
            wo_part[0, 0, 16 * t : 16 * t + 16, :] = wo_sum[16 * t : 16 * t + 16]
        for i in range(1, 8):
            wo_hop(i).start()
        wo_in[me] = wo_part[0, 0, pl.ds(pl.multiple_of(me * 16, 16), 16), :]
        for n in range(9):
            out_hop(n).wait_send()

    def wo_hop(i):
        rows = pl.ds(pl.multiple_of((me + i) % 8 * 16, 16), 16)
        return copy_to(wo_part.at[0, 0, rows], wo_in.at[me], a_send.at[i], a_recv.at[me], side(i))

    def wo_arrival(t):
        return copy_to(wo_in.at[t], wo_in.at[t], a_send.at[0], a_recv.at[t], sibling)

    early = pltpu.make_async_copy(grads_ref, grads, load_sem.at[9])
    early.start()
    sources = (rows1_ref, raw_ref, q_ref, kv_ref.at[0], kv_ref.at[1], heads_ref, w_out_ref)
    targets = (rows1, raw, q_t, kv_own, kv_sib, heads, w_out)
    loads = [
        pltpu.make_async_copy(s, t, load_sem.at[n])
        for n, (s, t) in enumerate(zip(sources, targets, strict=True))
    ]
    loads.append(pltpu.make_async_copy(w_all_ref, w_all, load_sem.at[7]))
    loads.append(pltpu.make_async_copy(table_ref.at[ctx], table, load_sem.at[8]))
    loads.append(early)
    loads.append(pltpu.make_async_copy(heads_all_ref, heads_all, load_sem.at[11]))
    own_blocks = out_part_ref.at[pl.ds(pl.multiple_of(ctx * 8, 8), 8)]
    loads.append(pltpu.make_async_copy(own_blocks, out_own.at[:, :, pl.ds(0, 1024)], load_sem.at[10]))
    for n, load in enumerate(loads):
        if n != 9:
            load.start()
    barrier = pltpu.get_barrier_semaphore()
    for i in range(1, 8):
        pl.semaphore_signal(barrier, inc=1, device_id=side(i), device_id_type=MESH)
        pl.semaphore_signal(barrier, inc=1, device_id=chip(i), device_id_type=MESH)
    pl.semaphore_signal(barrier, inc=1, device_id=sibling, device_id_type=MESH)

    gates, d_gate = gates_ref[...], d_gate_ref[...]
    d_logits = gates * (d_gate - jnp.sum(gates * d_gate, 0, keepdims=True))
    d_normed = d_rows_ref[...] + lax.dot_general(
        jnp.transpose(d_logits),
        router_ref[...].astype(f32),
        (((1,), (0,)), ((), ())),
        preferred_element_type=f32,
        precision=lax.Precision.HIGHEST,
    )
    resid = resid_ref[...]
    inv_two = lax.rsqrt(jnp.mean(resid * resid, -1, keepdims=True) + EPS)
    res_hat = resid * inv_two
    scaled = d_normed * norm2_ref[...]
    d_res = dy_ref[...].astype(f32) + inv_two * (
        scaled - res_hat * jnp.mean(scaled * res_hat, -1, keepdims=True)
    )
    d_resid[...] = d_res
    datt = d_res.astype(bf)
    for n in (6,):
        loads[n].wait()
    d_heads = dot_nt(w_out[...].reshape(1024, 1024), datt).astype(bf)
    dh_send[...] = d_heads.reshape(8, 128, 128)
    dh_all[me] = dh_send[me]
    pl.semaphore_wait(barrier, 15)

    def dh_push(i):
        return copy_to(
            dh_send.at[(me + i) % 8], dh_all.at[me], dh_send_sem.at[i], dh_recv.at[me], side(i)
        )

    def dh_arrival(t):
        return copy_to(dh_all.at[t], dh_all.at[t], dh_send_sem.at[0], dh_recv.at[t], sibling)

    for i in range(1, 8):
        dh_push(i).start()

    norm2_part = jnp.sum(d_normed * res_hat, 0, keepdims=True)
    router_part = jnp.dot(
        d_logits,
        rows2_ref[...].astype(f32),
        preferred_element_type=f32,
        precision=lax.Precision.HIGHEST,
    )
    def pack_rows(place, value):
        for c in range(2):
            pack[c, place, :] = value[:, 512 * c : 512 * c + 512].astype(bf)

    pack_rows(pl.ds(256, 32), router_part)
    pack_rows(pl.ds(288, 16), jnp.concatenate([norm2_part, jnp.zeros((15, 1024), f32)], 0))
    pack_rows(pl.ds(320, 64), jnp.zeros((64, 1024), f32))

    loads[9].wait()
    reduce_0()
    os_push.start()
    loads[10].wait()

    def wo_rows(t, carry):
        value = jnp.dot(heads_all[t], datt, preferred_element_type=f32).astype(bf)
        rows = pl.ds(pl.multiple_of(t * 16, 16), 16)
        for d in range(8):
            for c in range(2):
                wo_part[c, d, rows, :] = value[16 * d : 16 * d + 16, 512 * c : 512 * c + 512]
        return carry

    lax.fori_loop(0, 8, wo_rows, 0)
    wo_push.start()
    go(0, 1, s=1)
    for n in (0, 1, 2, 3, 4, 5, 7, 8, 11):
        loads[n].wait()
    seg = segment_ref[...]
    start = jnp.zeros((16, 128), f32)
    for s in range(1, 8):
        below = jnp.where(seg < s, 1.0, 0.0)
        count = jnp.sum(jnp.sum(below, 1, keepdims=True), 0, keepdims=True)
        start = jnp.where(seg == s, count, start)
    start = jnp.where(ctx == 0, start[:8], start[8:])
    for t in range(8):
        starts[0:1, 128 * t : 128 * t + 128] = start[t : t + 1]

    def lay_out(t, carry):
        at = pl.ds(pl.multiple_of(t * 128, 128), 128)
        i, half = t // 2, t % 2
        q = q_t[:, at] * 0.125
        for h in range(2):
            spot = pl.ds(pl.multiple_of(h * 256 + half * 128, 128), 128)
            q_h = q[64 * h : 64 * h + 64]
            q_cat[i, :, spot] = q_h
            q_nat[i, spot, :] = jnp.transpose(q_h)
            lanes[i, 0:1, spot] = lse_ref[h, 0:1, at]
            lanes[i, 2:3, spot] = starts[0:1, at]
        for n, kv in enumerate((kv_own, kv_sib)):
            k_nat[n, at, :] = jnp.transpose(kv[0:64, at])
            v_nat[n, at, :] = jnp.transpose(kv[64:128, at])
        return carry

    lax.fori_loop(0, 8, lay_out, 0)
    dk_acc[...] = jnp.zeros_like(dk_acc)
    dv_acc[...] = jnp.zeros_like(dv_acc)
    dq_acc[...] = jnp.zeros_like(dq_acc)
    for i in range(1, 8):
        dh_arrival((me + i) % 8).wait_recv()

    def lay_dh(t, carry):
        i, half = t // 2, t % 2
        d, o = dh_all[t], heads[t]
        product = d.astype(f32) * o.astype(f32)
        for h in range(2):
            spot = pl.ds(pl.multiple_of(h * 256 + half * 128, 128), 128)
            d_h = d[64 * h : 64 * h + 64]
            d_cat[i, :, spot] = d_h
            d_nat[i, spot, :] = jnp.transpose(d_h)
            lanes[i, 1:2, spot] = jnp.sum(product[64 * h : 64 * h + 64], 0, keepdims=True)
        return carry

    lax.fori_loop(0, 8, lay_dh, 0)
    key_row = lax.broadcasted_iota(jnp.int32, (256, 512), 0).astype(f32)
    query_lane = (lax.broadcasted_iota(jnp.int32, (256, 512), 1) % 256).astype(f32)
    base = (ctx * 1024).astype(f32)

    def block(n, i, j, first_key, causal):
        ks = pl.ds(pl.multiple_of(j * 256, 256), 256)
        kv = (kv_own, kv_sib)[n]
        s = jnp.dot(k_nat[n, ks, :], q_cat[i], preferred_element_type=f32)
        ok = key_row >= lanes[i, 2:3, :] - first_key
        if causal:
            ok = ok & (key_row <= query_lane)
        p = jnp.exp(jnp.where(ok, s, MASKED) - lanes[i, 0:1, :])
        dp_ = jnp.dot(v_nat[n, ks, :], d_cat[i], preferred_element_type=f32)
        ds = (p * (dp_ - lanes[i, 1:2, :])).astype(bf)
        dv_acc[n, ks, :] += jnp.dot(p.astype(bf), d_nat[i], preferred_element_type=f32)
        dk_acc[n, ks, :] += jnp.dot(ds, q_nat[i], preferred_element_type=f32)
        dq_acc[i] += jnp.dot(kv[0:64, ks], ds, preferred_element_type=f32)

    def hook_0():
        reduce_1(0)
        reduce_2()

    def hook_1():
        out_0()
        reduce_1(1)

    def hook_2():
        reduce_3(0)
        reduce_4()

    def hook_3():
        reduce_3(1)
        out_1()

    for i in range(4):

        def cross(j, carry, i=i):
            block(1, i, j, (j * 256).astype(f32), False)
            return carry

        lax.fori_loop(0, 4 * ctx, cross, 0)
        (hook_0, hook_1, hook_2, hook_3)[i]()
    dkv_push = copy_to(dkv_out, dkv_in, dkv_sem.at[0], dkv_sem.at[1], sibling)

    def upright(t, carry):
        at = pl.ds(pl.multiple_of(t * 128, 128), 128)
        dkv_out[0:64, at] = jnp.transpose(dk_acc[1, at, :]).astype(bf)
        dkv_out[64:128, at] = jnp.transpose(dv_acc[1, at, :]).astype(bf)
        return carry

    lax.fori_loop(0, 8, upright, 0)
    dkv_push.start()

    def within(i):
        def full(j, c):
            block(0, i, j, base + (j * 256).astype(f32), False)
            return c

        lax.fori_loop(0, i, full, 0)
        block(0, i, i, base + 256.0 * i, True)

    within(0)
    within(1)
    within(2)
    within(3)
    reduce_5(0)
    reduce_6()
    gain_q = column(q_gain_ref[...])
    gain_k = column(jnp.concatenate([k_gain_ref[...], jnp.zeros((1, 64), f32)], 1))[:64]
    dkv_push.wait()

    def unturn(t, sums):
        at = pl.ds(pl.multiple_of(t * 128, 128), 128)
        i, half = t // 2, t % 2
        parts = [
            dq_acc[i, :, pl.ds(pl.multiple_of(h * 256 + half * 128, 128), 128)] for h in range(2)
        ]
        cos_part, sin_part = table[0, :, at], -table[1, :, at]
        inv = inv_ref[t]
        d_q = turn(jnp.concatenate(parts, 0) * 0.125, cos_part, sin_part)
        came = dkv_in[:, at].astype(f32)
        d_k = turn(jnp.transpose(dk_acc[0, at, :]) + came[0:64], cos_part, sin_part)
        d_v = jnp.transpose(dv_acc[0, at, :]) + came[64:128]
        q_hat, k_hat = raw[t, 0:128] * inv[0:1], raw[t, 128:192] * inv[1:2]
        q_sum, k_sum = sums[0] + d_q * q_hat, sums[1] + d_k * k_hat
        q_term, k_term = d_q * gain_q, d_k * gain_k
        terms[t, 0:128] = q_term
        terms[t, 128:192] = k_term
        dqkv[t, 192:256] = d_v.astype(bf)
        stat[0, pl.ds(t, 1), :] = jnp.sum(q_term * q_hat, 0, keepdims=True)
        stat[1, pl.ds(t, 1), :] = jnp.sum(k_term * k_hat, 0, keepdims=True)
        return q_sum, k_sum

    q_sum, k_sum = lax.fori_loop(
        0, 8, unturn, (jnp.zeros((128, 128), f32), jnp.zeros((64, 128), f32))
    )
    stats[me] = stat[...]

    def s_push(i):
        return copy_to(stats.at[me], stats.at[me], s_send.at[i], s_recv.at[me], side(i))

    def s_arrival(t):
        return copy_to(stats.at[t], stats.at[t], s_send.at[0], s_recv.at[t], sibling)

    for i in range(1, 8):
        s_push(i).start()
    out_2()
    q_row = jnp.sum(jnp.transpose(q_sum), 0, keepdims=True)
    k_row = jnp.sum(jnp.transpose(k_sum), 0, keepdims=True)
    gain_row = jnp.concatenate([q_row, k_row, jnp.zeros((1, 1024 - 192), f32)], 1)
    pack_rows(pl.ds(304, 16), jnp.concatenate([gain_row, jnp.zeros((15, 1024), f32)], 0))
    reduce_5(1)
    for i in range(1, 8):
        s_arrival((me + i) % 8).wait_recv()

    def finish(t, carry):
        at = pl.ds(pl.multiple_of(t * 128, 128), 128)
        inner = []
        for n in range(2):
            part = stats[0, n, pl.ds(t, 1), :]
            for s in range(1, 8):
                part = part + stats[s, n, pl.ds(t, 1), :]
            inner.append(part)
        inv = inv_ref[t]
        q_hat, k_hat = raw[t, 0:128] * inv[0:1], raw[t, 128:192] * inv[1:2]
        d_q = inv[0:1] * (terms[t, 0:128] - q_hat * (inner[0] / 1024.0))
        d_k = inv[1:2] * (terms[t, 128:192] - k_hat * (inner[1] / 512.0))
        dqkv[t, 0:128] = d_q.astype(bf)
        dqkv[t, 128:192] = d_k.astype(bf)
        return carry

    lax.fori_loop(0, 8, finish, 0)

    def o_push(i):
        return copy_to(
            dqkv.at[(me + i) % 8], dqkv_all.at[me], o_send.at[i], o_recv.at[me], side(i)
        )

    def o_arrival(t):
        return copy_to(dqkv_all.at[t], dqkv_all.at[t], o_send.at[0], o_recv.at[t], sibling)

    for i in range(1, 8):
        o_push(i).start()
    dqkv_all[me] = dqkv[me]
    grad_qkv = jnp.zeros((256, 1024), f32)
    for t in range(8):
        grad_qkv = grad_qkv + jnp.dot(dqkv[t], rows1[t], preferred_element_type=f32)
    pack_rows(pl.ds(0, 256), grad_qkv)
    p_push = copy_to(pack.at[1 - ctx], pack_sib, p_sem.at[0], p_sem.at[1], sibling)
    p_push.start()
    reduce_7(0)
    for i in range(1, 8):
        o_arrival((me + i) % 8).wait_recv()
    d_rows1 = dot_tn(dqkv_all[...].reshape(2048, 128), w_all[...].reshape(2048, 1024))
    x = x_ref[...].astype(f32)
    inv_one = lax.rsqrt(jnp.mean(x * x, -1, keepdims=True) + EPS)
    x_hat = x * inv_one
    norm1_part = jnp.sum(d_rows1 * x_hat, 0, keepdims=True)
    n1[me] = jnp.concatenate([norm1_part[:, 128 * t : 128 * t + 128] for t in range(8)], 0)

    def n_push(i):
        return copy_to(n1.at[me], n1.at[me], n_send.at[i], n_recv.at[me], side(i))

    def n_arrival(t):
        return copy_to(n1.at[t], n1.at[t], n_send.at[0], n_recv.at[t], sibling)

    for i in range(1, 8):
        n_push(i).start()
    p_push.wait()
    pack[ctx] = (pack[ctx].astype(f32) + pack_sib[...].astype(f32)).astype(bf)
    out_3()

    def rs_push(i):
        to = (dp + i) % 8
        rows = pack.at[ctx, pl.ds(pl.multiple_of(to * 48, 16), 48)]
        return copy_to(rows, pack_in.at[dp], rs_send.at[i], rs_recv.at[dp], chip(i))

    def rs_arrival(d):
        return copy_to(pack_in.at[d], pack_in.at[d], rs_send.at[0], rs_recv.at[d], sibling)

    for i in range(1, 8):
        rs_push(i).start()
    scaled = d_rows1 * norm1_ref[...]
    grad_x_ref[...] = (
        d_resid[...] + inv_one * (scaled - x_hat * jnp.mean(scaled * x_hat, -1, keepdims=True))
    ).astype(bf)
    reduce_8()
    reduce_7(1)
    for i in range(1, 8):
        n_arrival((me + i) % 8).wait_recv()
    norm1_sum = n1[0]
    for t in range(1, 8):
        norm1_sum = norm1_sum + n1[t]
    n1_chips[dp] = norm1_sum

    def m_push(i):
        return copy_to(n1_chips.at[dp], n1_chips.at[dp], m_send.at[i], m_recv.at[dp], chip(i))

    def m_arrival(d):
        return copy_to(n1_chips.at[d], n1_chips.at[d], m_send.at[0], m_recv.at[d], sibling)

    for i in range(1, 8):
        m_push(i).start()
    pack_in[dp] = pack[ctx, pl.ds(pl.multiple_of(dp * 48, 16), 48), :]
    for i in range(1, 8):
        rs_arrival((dp + i) % 8).wait_recv()
    owned = pack_in[0].astype(f32)
    for d in range(1, 8):
        owned = owned + pack_in[d].astype(f32)
    top = pl.ds(0, 48)
    result[ctx, dp, top] = owned.astype(bf)
    wide = (dp == 5) | (dp == 6)

    def t_push(i):
        return copy_to(result.at[ctx, dp, top], tiny.at[me], t_send.at[i], t_recv.at[me], side(i))

    def t_arrival(t):
        return copy_to(tiny.at[t], tiny.at[t], t_send.at[0], t_recv.at[t], sibling)

    @pl.when(wide)
    def _():
        for i in range(1, 8):
            t_push(i).start()
        tiny[me] = result[ctx, dp, top]
        for i in range(1, 8):
            t_arrival((me + i) % 8).wait_recv()
            t_push(i).wait_send()
        total = tiny[0].astype(f32)
        for t in range(1, 8):
            total = total + tiny[t].astype(f32)
        row = lax.broadcasted_iota(jnp.int32, (48, 512), 0)
        shared = ((dp == 5) & (row >= 16)) | ((dp == 6) & (row < 16))
        result[ctx, dp, top] = jnp.where(shared, total, owned).astype(bf)

    for i in range(1, 8):
        wo_arrival((me + i) % 8).wait_recv()
    total = wo_in[0].astype(f32)
    for t in range(1, 8):
        total = total + wo_in[t].astype(f32)
    result[ctx, dp, pl.ds(48, 16)] = total.astype(bf)


    def g_push(i):
        return copy_to(
            result.at[ctx, dp], result.at[ctx, dp], g_send.at[i], g_recv.at[dp], chip(i)
        )

    def g_arrival(d):
        return copy_to(result.at[ctx, d], result.at[ctx, d], g_send.at[0], g_recv.at[d], sibling)

    def g_relay(d):
        return copy_to(
            result.at[ctx, d], result.at[ctx, d], gs_send.at[d], gs_recv.at[d], sibling
        )

    def g_sib_arrival(d):
        place = result.at[1 - ctx, d]
        return copy_to(place, place, gs_send.at[d], gs_recv.at[d], sibling)

    for i in range(1, 8):
        g_push(i).start()
    g_relay(dp).start()
    for i in range(1, 8):
        m_arrival((dp + i) % 8).wait_recv()
    norm1_sum = n1_chips[0]
    for d in range(1, 8):
        norm1_sum = norm1_sum + n1_chips[d]
    n1_sib[0] = norm1_sum
    ns_push = copy_to(n1_sib.at[0], n1_sib.at[1], ns_sem.at[0], ns_sem.at[1], sibling)
    ns_push.start()

    def pass_on(i, carry):
        d = (dp + i) % 8
        g_arrival(d).wait_recv()
        g_relay(d).start()
        return carry

    lax.fori_loop(1, 8, pass_on, 0)
    ns_push.wait()
    norm1_out_ref[...] = n1_sib[0] + n1_sib[1]
    for d in range(8):
        g_sib_arrival(d).wait_recv()
        g_relay(d).wait_send()
    reduce_9()
    store = pltpu.make_async_copy(reduced, reduced_ref, load_sem.at[9])
    store.start()
    pack_ref[...] = result[...]
    for i in range(1, 8):
        dh_push(i).wait_send()
        s_push(i).wait_send()
        o_push(i).wait_send()
        n_push(i).wait_send()
        rs_push(i).wait_send()
        m_push(i).wait_send()
        g_push(i).wait_send()
    for i in range(1, 8):
        wo_hop(i).wait_send()
    store.wait()


def backward(small, large):
    bf, f32 = jnp.bfloat16, jnp.float32
    vmem, hbm = pl.BlockSpec(memory_space=pltpu.VMEM), pl.BlockSpec(memory_space=pl.ANY)
    sem = pltpu.SemaphoreType.DMA
    shape = jax.ShapeDtypeStruct
    table = jnp.asarray(rope_constants(2048, 32))
    return pl.pallas_call(
        backward_kernel,
        out_shape=(
            shape((128, 1024), bf),
            shape((8, 128), f32),
            shape((2, 8, 64, 512), bf),
            shape((128, 1024), bf),
            shape((3072, 1024), bf),
        ),
        in_specs=[vmem] * 15 + [hbm] * 11,
        out_specs=(vmem, vmem, vmem, vmem, hbm),
        scratch_shapes=[
            pltpu.VMEM((8, 128, 1024), bf),
            pltpu.VMEM((8, 256, 128), f32),
            pltpu.VMEM((128, 1024), bf),
            pltpu.VMEM((128, 1024), bf),
            pltpu.VMEM((128, 1024), bf),
            pltpu.VMEM((8, 128, 128), bf),
            pltpu.VMEM((8, 128, 1024), bf),
            pltpu.VMEM((8, 256, 1024), bf),
            pltpu.VMEM((2, 32, 1024), f32),
            pltpu.VMEM((8, 1024), f32),
            pltpu.VMEM((128, 1024), f32),
            pltpu.VMEM((8, 128, 128), bf),
            pltpu.VMEM((2, 8, 128, 512), bf),
            pltpu.VMEM((8, 16, 512), bf),
            pltpu.VMEM((8, 128, 128), bf),
            pltpu.VMEM((8, 128, 128), bf),
            pltpu.VMEM((8, 48, 512), bf),
            pltpu.VMEM((4, 64, 512), bf),
            pltpu.VMEM((4, 512, 64), bf),
            pltpu.VMEM((4, 64, 512), bf),
            pltpu.VMEM((4, 512, 64), bf),
            pltpu.VMEM((4, 8, 512), f32),
            pltpu.VMEM((2, 1024, 64), bf),
            pltpu.VMEM((2, 1024, 64), bf),
            pltpu.VMEM((4, 64, 512), f32),
            pltpu.VMEM((2, 1024, 64), f32),
            pltpu.VMEM((2, 1024, 64), f32),
            pltpu.VMEM((128, 1024), bf),
            pltpu.VMEM((128, 1024), bf),
            pltpu.VMEM((8, 192, 128), f32),
            pltpu.VMEM((2, 8, 128), f32),
            pltpu.VMEM((8, 2, 8, 128), f32),
            pltpu.VMEM((8, 256, 128), bf),
            pltpu.VMEM((8, 256, 128), bf),
            pltpu.VMEM((2, 384, 512), bf),
            pltpu.VMEM((384, 512), bf),
            pltpu.VMEM((8, 48, 512), bf),
            pltpu.VMEM((2, 8, 64, 512), bf),
            pltpu.VMEM((8, 8, 128), f32),
            pltpu.VMEM((8, 8, 128), f32),
            pltpu.VMEM((2, 8, 128), f32),
            sem((12,)),
        ]
        + [sem((8,))] * 8
        + [sem((2,))]
        + [sem((8,))] * 2
        + [sem((2,))]
        + [sem((8,))] * 10
        + [sem((2,))]
        + [
            pltpu.VMEM((3072, 1024), bf),
            pltpu.VMEM((3072, 1024), bf),
            pltpu.VMEM((2, 240, 1024), bf),
            pltpu.VMEM((240, 1024), bf),
            pltpu.VMEM((144, 1024), bf),
            pltpu.VMEM((144, 1024), bf),
            pltpu.VMEM((2, 144, 1024), bf),
            sem((46,)),
            sem((46,)),
            pltpu.VMEM((8, 128, 1536), bf),
            pltpu.VMEM((8, 128, 1536), bf),
            pltpu.VMEM((2, 2, 64, 1536), bf),
            pltpu.VMEM((2, 2, 128, 1536), bf),
            pltpu.VMEM((128, 1536), bf),
            sem((4,)),
            sem((9,)),
            sem((9,)),
        ],
        compiler_params=pltpu.CompilerParams(
            collective_id=3, has_side_effects=True, vmem_limit_bytes=56 << 20
        ),
        cost_estimate=pl.CostEstimate(
            flops=10_000_000_000, bytes_accessed=20_000_000, transcendentals=4_000_000
        ),
    )(*small, *large, table)


def finish_kernel(
    reduced_ref,
    out_ref,
    grad_x_ref,
    pack_ref,
    norm1_ref,
    gate_ref,
    up_ref,
    down_ref,
    out_copy_ref,
    grad_x_copy_ref,
    w_q_ref,
    w_k_ref,
    w_v_ref,
    q_gain_ref,
    k_gain_ref,
    w_out_ref,
    norm2_ref,
    router_ref,
    norm1_copy_ref,
    rounded,
    wide,
    load_sem,
    store_sem,
):
    f32 = jnp.float32
    loads = [
        pltpu.make_async_copy(reduced_ref.at[pl.ds(256 * n, 256)], rounded.at[n], load_sem.at[n])
        for n in range(12)
    ]
    passed = [
        pltpu.make_async_copy(out_ref, out_copy_ref, load_sem.at[12]),
        pltpu.make_async_copy(grad_x_ref, grad_x_copy_ref, load_sem.at[13]),
    ]
    for copy in loads + passed:
        copy.start()
    def rows(start, count):
        parts = []
        for c in range(2):
            pieces = []
            for d in range(start // 48, (start + count - 1) // 48 + 1):
                first, last = max(start, 48 * d) - 48 * d, min(start + count, 48 * d + 48) - 48 * d
                pieces.append(pack_ref[c, d, first:last, :])
            parts.append(jnp.concatenate(pieces, 0))
        return jnp.concatenate(parts, 1).astype(f32)

    w_q_ref[...] = jnp.transpose(rows(0, 128))
    w_k_ref[...] = rows(128, 64)
    w_v_ref[...] = rows(192, 64)
    router_ref[...] = rows(256, 32)
    norm2_ref[...] = rows(288, 16)[0:1]
    gains = rows(304, 16)
    q_gain_ref[...] = gains[0:1, 0:128]
    k_gain_ref[...] = gains[0:1, 128:192]
    for d in range(8):
        for c in range(2):
            w_out_ref[16 * d : 16 * d + 16, 512 * c : 512 * c + 512] = pack_ref[c, d, 48:64, :].astype(f32)
    norm1_copy_ref[...] = norm1_ref[...]
    stores = []
    for n in range(12):
        loads[n].wait()
        wide[n] = rounded[n].astype(f32)
        if n < 8:
            rows = pl.ds(256 * (n % 4), 256)
            for m, ref in enumerate((gate_ref, up_ref)):
                src = wide.at[n, :, pl.ds(512 * m, 512)]
                stores.append(pltpu.make_async_copy(src, ref.at[n // 4, rows], store_sem.at[2 * n + m]))
        else:
            rows = pl.ds(256 * (n % 2), 256)
            stores.append(
                pltpu.make_async_copy(wide.at[n], down_ref.at[n // 2 - 4, rows], store_sem.at[n + 8])
            )
        for store in stores[-2:] if n < 8 else stores[-1:]:
            store.start()
    for copy in stores + passed:
        copy.wait()


def finish(reduced, out, grad_x, pack, norm1):
    bf, f32 = jnp.bfloat16, jnp.float32
    vmem, hbm = pl.BlockSpec(memory_space=pltpu.VMEM), pl.BlockSpec(memory_space=pl.ANY)
    shape = jax.ShapeDtypeStruct
    return pl.pallas_call(
        finish_kernel,
        out_shape=(
            shape((2, 1024, 512), f32),
            shape((2, 1024, 512), f32),
            shape((2, 512, 1024), f32),
            shape((128, 1024), bf),
            shape((128, 1024), bf),
            shape((1024, 128), f32),
            shape((64, 1024), f32),
            shape((64, 1024), f32),
            shape((1, 128), f32),
            shape((1, 64), f32),
            shape((128, 1024), f32),
            shape((1, 1024), f32),
            shape((32, 1024), f32),
            shape((8, 128), f32),
        ),
        in_specs=[hbm] + [vmem] * 4,
        out_specs=(hbm,) * 5 + (vmem,) * 9,
        scratch_shapes=[
            pltpu.VMEM((12, 256, 1024), bf),
            pltpu.VMEM((12, 256, 1024), f32),
            pltpu.SemaphoreType.DMA((14,)),
            pltpu.SemaphoreType.DMA((20,)),
        ],
        compiler_params=pltpu.CompilerParams(vmem_limit_bytes=62 << 20),
    )(reduced, out, grad_x, pack, norm1)


def shards(
    hidden_in,
    segment,
    norm1_gain,
    w_query,
    w_key,
    w_value,
    q_gain,
    k_gain,
    w_out,
    norm2_gain,
    router,
    w_gate,
    w_up,
    w_down,
    routes,
    cotangent,
):
    f32, bf = jnp.float32, jnp.bfloat16
    rows2, gates, resid, rows1, raw, inv, q_t, kv, lse, heads, w_out_all, dy_all, w_t, heads_all = attention(
        hidden_in,
        cotangent,
        segment,
        norm1_gain,
        q_gain,
        k_gain,
        norm2_gain,
        router,
        routes,
        w_query,
        w_key,
        w_value,
        w_out,
    )
    d_rows, d_gate, out_part, grads, w_all = moe(
        rows2, gates, dy_all, w_gate, w_up, w_down, w_t
    )
    grad_x, norm1_sum, pack, output, grads = backward(
        (
            hidden_in,
            cotangent,
            d_rows,
            d_gate,
            gates,
            rows2,
            resid,
            router.T,
            norm1_gain.reshape(1, 1024),
            norm2_gain.reshape(1, 1024),
            q_gain.reshape(1, 128),
            k_gain.reshape(1, 64),
            segment.reshape(16, 128),
            inv,
            lse,
        ),
        (rows1, raw, q_t, kv, heads, heads_all, w_out_all, w_all, grads, out_part),
    )
    (
        gate,
        up,
        down,
        output,
        grad_x,
        w_q,
        w_k,
        w_v,
        q_g,
        k_g,
        w_o,
        norm2_sum,
        grad_router,
        norm1_sum,
    ) = finish(grads, output, grad_x, pack, norm1_sum)
    return (
        output,
        grad_x,
        norm1_sum.reshape(1024),
        w_q,
        w_k.T,
        w_v.T,
        q_g.reshape(128),
        k_g.reshape(64),
        w_o,
        norm2_sum.reshape(1024),
        grad_router.T,
        gate,
        up,
        down,
    )


def solution(mesh):
    return jax.shard_map(
        shards,
        mesh=mesh,
        in_specs=(
            P(("dp", "ctx", "tensor"), None),
            P("dp"),
            P(),
            P(None, "tensor"),
            P(None, "tensor"),
            P(None, "tensor"),
            P("tensor"),
            P("tensor"),
            P("tensor", None),
            P(),
            P(),
            P(("dp", "ctx"), None, None),
            P(("dp", "ctx"), None, None),
            P(("dp", "ctx"), None, None),
            P(("dp", "ctx", "tensor"), None),
            P(("dp", "ctx", "tensor"), None),
        ),
        out_specs=(
            P(("dp", "ctx", "tensor"), None),
            P(("dp", "ctx", "tensor"), None),
            P(),
            P(None, "tensor"),
            P(None, "tensor"),
            P(None, "tensor"),
            P("tensor"),
            P("tensor"),
            P("tensor", None),
            P(),
            P(),
            P(("dp", "ctx"), None, None),
            P(("dp", "ctx"), None, None),
            P(("dp", "ctx"), None, None),
        ),
        check_vma=False,
    )
```

```python
import jax
import jax.numpy as jnp
import numpy as np
from jax import lax
from jax.experimental import pallas as pl
from jax.experimental.pallas import tpu as pltpu
from jax.sharding import PartitionSpec as P

EPS = 1e-06
THETA = 10000.0
MASKED = -1e30
MESH = pl.DeviceIdType.MESH


def rope_constants(length, half_dim):
    inverse = THETA ** (-(np.arange(half_dim, dtype=np.float64) * 2.0 / (2 * half_dim)))
    angles = inverse[:, None] * np.arange(length, dtype=np.float64)[None, :]
    table = np.stack([np.cos(angles), np.sin(angles)]).astype(np.float32)
    return np.ascontiguousarray(table.reshape(2, half_dim, 2, length // 2).transpose(2, 0, 1, 3))


def turn(value, cos_part, sin_part):
    parts = []
    for h in range(value.shape[0] // 64):
        a, b = value[64 * h : 64 * h + 32], value[64 * h + 32 : 64 * h + 64]
        parts += [a * cos_part - b * sin_part, b * cos_part + a * sin_part]
    return jnp.concatenate(parts, 0)


def column(row):
    return jnp.transpose(jnp.broadcast_to(row, (128, 128)))


def copy_to(src, dst, send, recv, device):
    return pltpu.make_async_remote_copy(
        src_ref=src, dst_ref=dst, send_sem=send, recv_sem=recv, device_id=device, device_id_type=MESH
    )


def dot_nt(left, right):
    return lax.dot_general(
        left, right, (((1,), (1,)), ((), ())), preferred_element_type=jnp.float32
    )


def dot_tn(left, right):
    return lax.dot_general(
        left, right, (((0,), (0,)), ((), ())), preferred_element_type=jnp.float32
    )


def across(a, b, flip):
    dp, ctx = lax.axis_index("dp"), lax.axis_index("ctx")
    x, y = dp % 4, dp // 4
    mid = ((a + 1) // 2) % 2
    by_x = mid * (1 + 2 * b) + (1 - mid) * 2 * (a // 3)
    by_y = mid * (a // 2) + (1 - mid) * b
    return ((y + by_y) % 2) * 4 + (x + by_x) % 4, (ctx + flip) % 2


def opposite(a, b):
    return b + (((a + 1) // 2) % 2) * (1 - 2 * b)


def first_half(z, y, k, c):
    return pl.ds(pl.multiple_of(304 * (((z + k) % 4) * 2 + c), 16), 304)


def second_half(z, y, k, c):
    return pl.ds(pl.multiple_of(2432 + 80 * (((z + k) % 4) * 2 + c), 16), 80)


def piece(z, y, k, c, part):
    start = 2432 + 80 * (((z + k) % 4) * 2 + c) + 48 * part
    return pl.ds(pl.multiple_of(start, 16), (48, 32)[part])


def add_rows(ref, place, *parts):
    total = ref[place, :].astype(jnp.float32)
    for part in parts:
        total = total + part.astype(jnp.float32)
    ref[place, :] = total.astype(jnp.bfloat16)


def moe_kernel(
    rows_ref,
    gate_ref,
    dy_ref,
    w_gate_ref,
    w_up_ref,
    w_down_ref,
    w_t_ref,
    d_rows_ref,
    d_gate_ref,
    out_part_ref,
    grad_ref,
    w_all_ref,
    rows_all,
    gate_all,
    dy_all,
    w_full,
    acc,
    out_all,
    din_all,
    sib,
    rs_a,
    rs_b,
    rs_c,
    rs_d,
    rs_e,
    dg_out,
    dg_in,
    places,
    x_buf,
    y_buf,
    d_buf,
    o_buf,
    i_buf,
    gs_buf,
    dgs_buf,
    load_sem,
    ag_send,
    ag_recv,
    g_send,
    g_recv,
    sib_send,
    sib_recv,
    rs_send,
    rs_recv,
    dg_send,
    dg_recv,
    store_sem,
    w_send,
    w_recv,
    ra_0,
    ra_1,
    rb,
    r_send,
    r_recv,
    keep_sem,
):
    tensor = lax.axis_index("tensor")
    dp, ctx = lax.axis_index("dp"), lax.axis_index("ctx")
    me = dp * 2 + ctx

    def to(a, b, flip):
        d, c = across(a, b, flip)
        return (d, c, tensor)

    def side(i):
        return (dp, ctx, (tensor + i) % 8)

    loads = []
    for j in range(2):
        loads.append(
            pltpu.make_async_copy(w_gate_ref.at[j], w_full.at[pl.ds(1024 * j, 1024), pl.ds(0, 512)], load_sem.at[3 * j])
        )
        loads.append(
            pltpu.make_async_copy(
                w_up_ref.at[j], w_full.at[pl.ds(1024 * j, 1024), pl.ds(512, 512)], load_sem.at[3 * j + 1]
            )
        )
        loads.append(pltpu.make_async_copy(w_down_ref.at[j], w_full.at[pl.ds(2048 + 512 * j, 512)], load_sem.at[3 * j + 2]))
    loads.append(pltpu.make_async_copy(dy_ref, dy_all, load_sem.at[6]))
    for load in loads:
        load.start()

    barrier = pltpu.get_barrier_semaphore()
    for a in range(4):
        for b in range(2):
            for flip in range(2):
                if (a, b, flip) != (0, 0, 0):
                    pl.semaphore_signal(
                        barrier, inc=1, device_id=to(a, b, flip), device_id_type=MESH
                    )
    for i in range(1, 8):
        pl.semaphore_signal(barrier, inc=1, device_id=side(i), device_id_type=MESH)
    pl.semaphore_wait(barrier, 22)

    right, left, partner = to(1, 0, 0), to(1, 1, 0), to(0, 1, 0)
    sibling = to(0, 0, 1)
    low, high = pl.ds(0, 64), pl.ds(64, 64)

    def hop(n):
        src, dst, device = (
            (rows_all.at[0], rows_all.at[6], right),
            (rows_all.at[0], rows_all.at[4], left),
            (rows_all.at[0], rows_all.at[2], partner),
            (rows_all.at[6, low], rows_all.at[12, low], right),
            (rows_all.at[4, high], rows_all.at[12, high], left),
            (rows_all.at[2], rows_all.at[10], right),
            (rows_all.at[2], rows_all.at[8], left),
            (rows_all.at[12], rows_all.at[14], partner),
        )[n]
        return copy_to(src, dst, ag_send.at[n], ag_recv.at[n], device)

    def relay(ci):
        r = 2 * ci
        return copy_to(
            rows_all.at[r], rows_all.at[r + 1], ag_send.at[8 + ci], ag_recv.at[8 + ci], sibling
        )

    def gate_push(a, b, flip):
        r = 4 * a + 2 * b + flip
        back = 4 * a + 2 * opposite(a, b) + flip
        return copy_to(
            gate_all.at[0], gate_all.at[back], g_send.at[r], g_recv.at[back], to(a, b, flip)
        )

    rows_all[0] = rows_ref[...]
    gate_all[0] = gate_ref[...]
    for n in range(3):
        hop(n).start()
    relay(0).start()
    for r in range(1, 16):
        gate_push(r // 4, (r // 2) % 2, r % 2).start()

    acc[...] = jnp.zeros_like(acc)

    half = pl.ds(pl.multiple_of(ctx * 128, 128), 128)

    def w_push(i):
        return copy_to(
            w_t_ref.at[half],
            w_all_ref.at[tensor, half],
            w_send.at[i],
            w_recv.at[tensor, ctx],
            side(i),
        )

    def w_relay(t):
        place = w_all_ref.at[t, half]
        return copy_to(place, place, w_send.at[8 + t], w_recv.at[t, ctx], to(0, 0, 1))

    def w_arrival(t, c):
        place = w_all_ref.at[t, pl.ds(pl.multiple_of(c * 128, 128), 128)]
        return copy_to(place, place, w_send.at[0], w_recv.at[t, c], to(0, 0, 1))

    for i in (1, 7, 2, 6, 3, 5, 4):
        w_push(i).start()
    w_own = pltpu.make_async_copy(w_t_ref, w_all_ref.at[tensor], load_sem.at[7])
    w_own.start()

    def sib_push(ci):
        return copy_to(
            din_all.at[2 * ci + 1], sib.at[ci], sib_send.at[ci], sib_recv.at[ci], sibling
        )

    def rs_hop(n):
        src, dst, device = (
            (din_all.at[8], rs_a.at[0], right),
            (din_all.at[10], rs_a.at[1], left),
            (din_all.at[14], rs_b, partner),
            (din_all.at[2], rs_c, partner),
            (din_all.at[12, low], rs_d.at[0], right),
            (din_all.at[12, high], rs_d.at[1], left),
            (din_all.at[4], rs_e.at[0], right),
            (din_all.at[6], rs_e.at[1], left),
        )[n]
        return copy_to(src, dst, rs_send.at[n], rs_recv.at[n], device)

    def rs_go(*hops):
        for n in hops:
            rs_hop(n).start()

    def rs_got(*hops):
        for n in hops:
            rs_hop(n).wait_recv()

    def plus(r, rows, *parts):
        total = din_all[r, rows].astype(jnp.float32)
        for part in parts:
            total = total + part.astype(jnp.float32)
        din_all[r, rows] = total.astype(jnp.bfloat16)

    def post(*cis):
        for ci in cis:
            sib_push(ci).wait_recv()
            plus(2 * ci, slice(None), sib[ci])

    def dg_push(a, b, flip):
        r = 4 * a + 2 * b + flip
        back = 4 * a + 2 * opposite(a, b) + flip
        return pltpu.make_async_remote_copy(
            src_ref=dg_out.at[r],
            dst_ref=dg_in.at[back],
            send_sem=dg_send.at[r],
            recv_sem=dg_recv.at[back],
            device_id=to(a, b, flip),
            device_id_type=MESH,
        )

    expert_row = lax.broadcasted_iota(jnp.int32, (32, 128), 0)
    slot_row = lax.broadcasted_iota(jnp.int32, (64, 128), 0).astype(jnp.float32)
    before = (
        lax.broadcasted_iota(jnp.int32, (128, 128), 0)
        < lax.broadcasted_iota(jnp.int32, (128, 128), 1)
    ).astype(jnp.float32)
    before = before.astype(jnp.bfloat16)

    def gather(a, q):
        r = 4 * a + q
        gates = gate_all[r]
        at = pl.ds(pl.multiple_of(q * 64, 64), 64)
        rows = [
            jnp.sum(jnp.where(expert_row == 2 * me + j, gates, 0.0), 0, keepdims=True)
            for j in range(2)
        ]
        both = jnp.concatenate(rows + [jnp.zeros((6, 128), jnp.float32)], 0)
        named = jnp.where(both > 0.0, 1.0, 0.0).astype(jnp.bfloat16)
        slots = jnp.dot(named, before, preferred_element_type=jnp.float32)
        hits = [
            jnp.where((slot_row == slots[j : j + 1]) & (rows[j] > 0.0), 1.0, 0.0) for j in range(2)
        ]
        place = jnp.concatenate(hits, 0).astype(jnp.bfloat16)
        places[q] = place
        x = jnp.dot(place, rows_all[r], preferred_element_type=jnp.float32).astype(jnp.bfloat16)
        y = jnp.dot(place, dy_all[r], preferred_element_type=jnp.float32)
        for j in range(2):
            gs = jnp.sum(hits[j] * rows[j], 1, keepdims=True)
            y_j = y[64 * j : 64 * j + 64]
            x_buf[j, at, :] = x[64 * j : 64 * j + 64]
            y_buf[j, at, :] = y_j.astype(jnp.bfloat16)
            d_buf[j, at, :] = (y_j * gs).astype(jnp.bfloat16)
            gs_buf[j, at, :] = gs

    def expert(j):
        of_gu = pl.ds(pl.multiple_of(j * 1024, 1024), 1024)
        of_dn = pl.ds(pl.multiple_of(2048 + j * 512, 512), 512)
        x = x_buf[j]
        gu = jnp.dot(x, w_full[of_gu, :], preferred_element_type=jnp.float32)
        g, u = gu[:, :512], gu[:, 512:]
        s = jax.nn.sigmoid(g)
        silu = g * s
        act = (silu * u).astype(jnp.bfloat16)
        eout = (
            jnp.dot(act, w_full[of_dn, :], preferred_element_type=jnp.float32)
            .astype(jnp.bfloat16)
            .astype(jnp.float32)
        )
        dgs_buf[j] = jnp.sum(y_buf[j].astype(jnp.float32) * eout, 1, keepdims=True)
        o_buf[j] = (eout * gs_buf[j]).astype(jnp.bfloat16)
        d = d_buf[j]
        d_act = dot_nt(d, w_full[of_dn, :])
        d_g = (d_act * u * s * (1.0 + g * (1.0 - s))).astype(jnp.bfloat16)
        d_u = (d_act * silu).astype(jnp.bfloat16)
        d_gu = jnp.concatenate([d_g, d_u], 1)
        i_buf[j] = dot_nt(d_gu, w_full[of_gu, :]).astype(jnp.bfloat16)
        acc[of_gu, :] += dot_tn(x, d_gu)
        acc[of_dn, :] += dot_tn(act, d)

    def spread(a, q):
        r = 4 * a + q
        b, flip = q // 2, q % 2
        at = pl.ds(pl.multiple_of(q * 64, 64), 64)
        place = places[q]
        d, c = across(a, b, flip)
        o = jnp.concatenate([o_buf[0, at, :], o_buf[1, at, :]], 0)
        out_all[c * 8 + d] = dot_tn(place, o).astype(jnp.bfloat16)
        i = jnp.concatenate([i_buf[0, at, :], i_buf[1, at, :]], 0)
        din_all[r] = dot_tn(place, i).astype(jnp.bfloat16)
        hits = place.astype(jnp.float32)
        back = [
            jnp.sum(hits[64 * j : 64 * j + 64] * dgs_buf[j, at, :], 0, keepdims=True)
            for j in range(2)
        ]
        dg_out[r] = jnp.concatenate(back + [jnp.zeros((6, 128), jnp.float32)], 0)

        @pl.when(r > 0)
        def _():
            dg_push(a, b, flip).start()

    for n, ci in ((0, 3), (1, 2)):
        hop(n).wait_recv()
        hop(3 + n).start()
        relay(ci).start()
    hop(2).wait_recv()
    hop(5).start()
    hop(6).start()
    relay(1).start()
    relay(0).wait_recv()
    for r in range(1, 16):
        gate_push(r // 4, (r // 2) % 2, r % 2).wait_recv()
    for load in loads:
        load.wait()
    relay(1).wait_recv()

    def step(a, carry):
        lax.fori_loop(0, 4, lambda q, c: (gather(a, q), c)[1], 0)

        @pl.when(a == 1)
        def _():
            post(0, 1)

        @pl.when(a == 2)
        def _():
            post(2, 3)

        @pl.when(a == 3)
        def _():
            post(4, 5)
            rs_go(0, 1)

        lax.fori_loop(0, 2, lambda j, c: (expert(j), c)[1], 0)
        lax.fori_loop(0, 4, lambda q, c: (spread(a, q), c)[1], 0)
        for b in range(2):
            sib_push(2 * a + b).start()

        @pl.when(a == 0)
        def _():
            hop(3).wait_recv()
            hop(4).wait_recv()
            hop(7).start()
            relay(6).start()
            for ci in (2, 3):
                relay(ci).wait_recv()

        @pl.when(a == 1)
        def _():
            for n, ci in ((5, 5), (6, 4)):
                hop(n).wait_recv()
                relay(ci).start()
            for ci in (4, 5):
                relay(ci).wait_recv()

        @pl.when(a == 2)
        def _():
            hop(7).wait_recv()
            relay(7).start()
            for ci in (6, 7):
                relay(ci).wait_recv()

        return carry

    lax.fori_loop(0, 4, step, 0)
    post(7, 6)
    rs_go(2)
    rs_got(0, 1)
    plus(2, slice(None), rs_a[0], rs_a[1])
    rs_go(3)

    def round_rows(n, carry):
        place = pl.ds(pl.multiple_of(n * 128, 128), 128)
        w_full[place, :] = acc[place, :].astype(jnp.bfloat16)
        return carry

    lax.fori_loop(0, 24, round_rows, 0)
    z, y = tensor // 2, tensor % 2
    up, down, pair = (
        (dp, ctx, ((z + 1) % 4) * 2 + y),
        (dp, ctx, ((z + 3) % 4) * 2 + y),
        (dp, ctx, z * 2 + 1 - y),
    )

    def grad_hop(n):
        place, dst, device = (
            (first_half(z, y, 2, 0), ra_0.at[0], up),
            (first_half(z, y, 2, 1), ra_0.at[1], down),
            (first_half(z, y, 1, 1), ra_1.at[0], up),
            (first_half(z, y, 3, 0), ra_1.at[1], down),
            (second_half(z, y, 2, 1 - y), rb.at[0], pair),
            (second_half(z, y, 1, 1 - y), rb.at[1], pair),
            (second_half(z, y, 3, 1 - y), rb.at[2], pair),
        )[n]
        return copy_to(w_full.at[place], dst, r_send.at[n], r_recv.at[n], device)

    for n in range(4):
        grad_hop(n).start()

    def keep(n, place):
        return pltpu.make_async_copy(w_full.at[place], grad_ref.at[place], keep_sem.at[n])

    first_places = [first_half(z, y, k, c) for k, c in ((1, 1), (3, 0), (2, 0), (2, 1))]
    first_places += [second_half(z, y, k, 1 - y) for k in range(4)] + [second_half(z, y, 0, y)]
    last_places = [
        first_half(z, y, 1, 0),
        first_half(z, y, 3, 1),
        second_half(z, y, 2, y),
        first_half(z, y, 0, 1),
        first_half(z, y, 0, 0),
        second_half(z, y, 1, y),
        second_half(z, y, 3, y),
    ]
    for n, place in enumerate(first_places):
        keep(n, place).start()
    rs_got(2)
    plus(12, slice(None), rs_b[...])
    rs_go(4, 5)
    grad_hop(4).start()
    grad_hop(5).start()
    grad_hop(6).start()
    rs_got(4)
    plus(4, low, rs_d[0])
    rs_go(6)
    rs_got(5)
    plus(6, high, rs_d[1])
    rs_go(7)
    for i in range(1, 8):
        t = (tensor + i) % 8
        w_arrival(t, ctx).wait_recv()
        w_relay(t).start()
    for n in range(8):
        hop(n).wait_send()
        relay(n).wait_send()
    for r in range(1, 16):
        gate_push(r // 4, (r // 2) % 2, r % 2).wait_send()
    store_out = pltpu.make_async_copy(out_all, out_part_ref, store_sem.at[0])
    store_out.start()

    for r in range(1, 16):
        a, b, flip = r // 4, (r // 2) % 2, r % 2
        dg_push(a, b, flip).wait()
    dg_in[0] = dg_out[0]
    d_gate = jnp.zeros((32, 128), jnp.float32)
    for r in range(16):
        d, c = across(r // 4, (r // 2) % 2, r % 2)
        got = dg_in[r]
        for j in range(2):
            d_gate = jnp.where(expert_row == (d * 2 + c) * 2 + j, got[j : j + 1], d_gate)
    d_gate_ref[...] = d_gate
    for ci in range(8):
        sib_push(ci).wait_send()
    rs_got(3, 6, 7)
    total = din_all[0].astype(jnp.float32) + rs_c[...].astype(jnp.float32)
    d_rows_ref[...] = total + rs_e[0].astype(jnp.float32) + rs_e[1].astype(jnp.float32)
    for n in range(8):
        rs_hop(n).wait_send()
    for i in range(1, 8):
        t = (tensor + i) % 8
        w_arrival(t, 1 - ctx).wait_recv()
        w_push(i).wait_send()
        w_relay(t).wait_send()
    w_own.wait()
    for n, (arrived, got) in enumerate(
        ((0, ra_0.at[0]), (1, ra_0.at[1]), (4, rb.at[0]), (2, ra_1.at[0]), (3, ra_1.at[1]), (5, rb.at[1]), (6, rb.at[2]))
    ):
        grad_hop(arrived).wait_recv()
        add_rows(w_full, last_places[n], got[...])
        keep(9 + n, last_places[n]).start()
    for n in range(7):
        grad_hop(n).wait_send()
    store_out.wait()
    for n, place in enumerate(first_places + last_places):
        keep(n, place).wait()


def moe(rows, gates, dy, w_gate, w_up, w_down, w_t):
    bf, f32 = jnp.bfloat16, jnp.float32
    vmem, hbm = pl.BlockSpec(memory_space=pltpu.VMEM), pl.BlockSpec(memory_space=pl.ANY)
    sem = pltpu.SemaphoreType.DMA
    return pl.pallas_call(
        moe_kernel,
        out_shape=(
            jax.ShapeDtypeStruct((128, 1024), f32),
            jax.ShapeDtypeStruct((32, 128), f32),
            jax.ShapeDtypeStruct((16, 128, 1024), bf),
            jax.ShapeDtypeStruct((3072, 1024), bf),
            jax.ShapeDtypeStruct((8, 256, 1024), bf),
        ),
        in_specs=[vmem] * 2 + [hbm] * 4 + [vmem],
        out_specs=(vmem, vmem, hbm, hbm, hbm),
        scratch_shapes=[
            pltpu.VMEM((16, 128, 1024), bf),
            pltpu.VMEM((16, 32, 128), f32),
            pltpu.VMEM((16, 128, 1024), bf),
            pltpu.VMEM((3072, 1024), bf),
            pltpu.VMEM((3072, 1024), f32),
            pltpu.VMEM((16, 128, 1024), bf),
            pltpu.VMEM((16, 128, 1024), bf),
            pltpu.VMEM((8, 128, 1024), bf),
            pltpu.VMEM((2, 128, 1024), bf),
            pltpu.VMEM((128, 1024), bf),
            pltpu.VMEM((128, 1024), bf),
            pltpu.VMEM((2, 64, 1024), bf),
            pltpu.VMEM((2, 128, 1024), bf),
            pltpu.VMEM((16, 8, 128), f32),
            pltpu.VMEM((16, 8, 128), f32),
            pltpu.VMEM((4, 128, 128), bf),
            pltpu.VMEM((2, 256, 1024), bf),
            pltpu.VMEM((2, 256, 1024), bf),
            pltpu.VMEM((2, 256, 1024), bf),
            pltpu.VMEM((2, 256, 1024), bf),
            pltpu.VMEM((2, 256, 1024), bf),
            pltpu.VMEM((2, 256, 1), f32),
            pltpu.VMEM((2, 256, 1), f32),
            sem((8,)),
            sem((16,)),
            sem((16,)),
            sem((16,)),
            sem((16,)),
            sem((8,)),
            sem((8,)),
            sem((8,)),
            sem((8,)),
            sem((16,)),
            sem((16,)),
            sem((2,)),
            sem((16,)),
            sem((8, 2)),
            pltpu.VMEM((2, 304, 1024), bf),
            pltpu.VMEM((2, 304, 1024), bf),
            pltpu.VMEM((3, 80, 1024), bf),
            sem((7,)),
            sem((7,)),
            sem((16,)),
        ],
        compiler_params=pltpu.CompilerParams(
            collective_id=1, has_side_effects=True, vmem_limit_bytes=60 << 20
        ),
        cost_estimate=pl.CostEstimate(
            flops=20_000_000_000, bytes_accessed=30_000_000, transcendentals=2_000_000
        ),
    )(rows, gates, dy, w_gate, w_up, w_down, w_t)


def attention_kernel(
    x_ref,
    dy_ref,
    segment_ref,
    norm1_ref,
    q_gain_ref,
    k_gain_ref,
    norm2_ref,
    router_ref,
    routes_ref,
    w_q_ref,
    w_k_ref,
    w_v_ref,
    w_out_ref,
    table_ref,
    rows2_ref,
    gates_ref,
    resid_ref,
    rows1_ref,
    raw_ref,
    inv_ref,
    q_ref,
    kv_ref,
    lse_ref,
    heads_ref,
    w_out_all_ref,
    dy_all_ref,
    w_t_ref,
    heads_all_ref,
    h_all,
    dy_all,
    w_all,
    w_q,
    w_t,
    raw,
    table,
    stat,
    stats,
    q_t,
    kv_own,
    kv_sib,
    k_own,
    k_sib,
    starts,
    heads,
    heads_all,
    load_sem,
    h_send,
    h_recv,
    dy_send,
    dy_recv,
    w_send,
    w_recv,
    s_send,
    s_recv,
    kv_sem,
    o_send,
    o_recv,
    store_sem,
):
    f32, bf = jnp.float32, jnp.bfloat16
    dp, ctx, me = lax.axis_index("dp"), lax.axis_index("ctx"), lax.axis_index("tensor")

    def side(i):
        return (dp, ctx, (me + i) % 8)

    def to(a, b, flip):
        d, c = across(a, b, flip)
        return (d, c, me)

    sibling = (dp, 1 - ctx, me)
    loads = [
        pltpu.make_async_copy(w_q_ref, w_q, load_sem.at[0]),
        pltpu.make_async_copy(w_k_ref, w_t.at[pl.ds(128, 64)], load_sem.at[1]),
        pltpu.make_async_copy(w_v_ref, w_t.at[pl.ds(192, 64)], load_sem.at[2]),
        pltpu.make_async_copy(w_out_ref, w_all.at[me], load_sem.at[3]),
        pltpu.make_async_copy(table_ref.at[ctx], table, load_sem.at[4]),
    ]
    for load in loads:
        load.start()
    barrier = pltpu.get_barrier_semaphore()
    for i in range(1, 8):
        pl.semaphore_signal(barrier, inc=1, device_id=side(i), device_id_type=MESH)
    for a in range(4):
        for b in range(2):
            if (a, b) != (0, 0):
                pl.semaphore_signal(barrier, inc=1, device_id=to(a, b, 0), device_id_type=MESH)
    pl.semaphore_signal(barrier, inc=1, device_id=sibling, device_id_type=MESH)
    x = x_ref[...].astype(f32)
    inv_one = lax.rsqrt(jnp.mean(x * x, -1, keepdims=True) + EPS)
    h_all[me] = (x * inv_one * norm1_ref[...]).astype(bf)
    dy_all[0] = dy_ref[...]
    pl.semaphore_wait(barrier, 15)

    z, y = me // 2, me % 2
    up, down, pair = (
        (dp, ctx, ((z + 1) % 4) * 2 + y),
        (dp, ctx, ((z + 3) % 4) * 2 + y),
        (dp, ctx, z * 2 + 1 - y),
    )
    low, high = pl.ds(0, 64), pl.ds(64, 64)

    def block_at(k, flip):
        return ((z + k) % 4) * 2 + (y + flip) % 2

    def h_hop(n):
        place, device = (
            (h_all.at[me], up),
            (h_all.at[me], down),
            (h_all.at[me], pair),
            (h_all.at[block_at(3, 0), low], up),
            (h_all.at[block_at(1, 0), high], down),
            (h_all.at[block_at(0, 1)], up),
            (h_all.at[block_at(0, 1)], down),
            (h_all.at[block_at(2, 0)], pair),
        )[n]
        return copy_to(place, place, h_send.at[n], h_recv.at[n], device)

    right, left, partner = to(1, 0, 0), to(1, 1, 0), to(0, 1, 0)

    def dy_hop(n):
        src, dst, device = (
            (dy_all.at[0], dy_all.at[6], right),
            (dy_all.at[0], dy_all.at[4], left),
            (dy_all.at[0], dy_all.at[2], partner),
            (dy_all.at[6, low], dy_all.at[12, low], right),
            (dy_all.at[4, high], dy_all.at[12, high], left),
            (dy_all.at[2], dy_all.at[10], right),
            (dy_all.at[2], dy_all.at[8], left),
            (dy_all.at[12], dy_all.at[14], partner),
        )[n]
        return copy_to(src, dst, dy_send.at[n], dy_recv.at[n], device)

    def dy_relay(ci):
        r = 2 * ci
        return copy_to(
            dy_all.at[r], dy_all.at[r + 1], dy_send.at[8 + ci], dy_recv.at[8 + ci], sibling
        )

    for n in range(3):
        h_hop(n).start()
    for n in range(3):
        dy_hop(n).start()
    dy_relay(0).start()

    for load in loads:
        load.wait()
    w_t[0:128, :] = jnp.transpose(w_q[...])
    seg = segment_ref[...]
    start = jnp.zeros((16, 128), f32)
    for s in range(1, 8):
        below = jnp.where(seg < s, 1.0, 0.0)
        count = jnp.sum(jnp.sum(below, 1, keepdims=True), 0, keepdims=True)
        start = jnp.where(seg == s, count, start)
    start = jnp.where(ctx == 0, start[:8], start[8:])
    for t in range(8):
        starts[0:1, 128 * t : 128 * t + 128] = start[t : t + 1]

    def project(t):
        value = dot_nt(w_t[...], h_all[t])
        raw[t] = value
        square = value * value
        stat[0, pl.ds(t, 1), :] = jnp.sum(square[0:128], 0, keepdims=True)
        stat[1, pl.ds(t, 1), :] = jnp.sum(square[128:192], 0, keepdims=True)

    project(me)
    for n in range(2):
        h_hop(n).wait_recv()
        h_hop(3 + n).start()
    h_hop(2).wait_recv()
    h_hop(5).start()
    h_hop(6).start()
    for k, flip in ((3, 0), (1, 0), (0, 1)):
        project(block_at(k, flip))
    h_hop(3).wait_recv()
    h_hop(4).wait_recv()
    h_hop(7).start()
    project(block_at(2, 0))
    for n, k in ((5, 3), (6, 1), (7, 2)):
        h_hop(n).wait_recv()
        project(block_at(k, 1))
    stats[me] = stat[...]

    def s_push(i):
        return copy_to(stats.at[me], stats.at[me], s_send.at[i], s_recv.at[me], side(i))

    def s_arrival(t):
        return copy_to(stats.at[t], stats.at[t], s_send.at[0], s_recv.at[t], sibling)

    for i in range(1, 8):
        s_push(i).start()
    store_rows = pltpu.make_async_copy(h_all, rows1_ref, store_sem.at[0])
    store_raw = pltpu.make_async_copy(raw, raw_ref, store_sem.at[1])
    store_wt = pltpu.make_async_copy(w_t, w_t_ref, store_sem.at[8])
    store_rows.start()
    store_raw.start()
    store_wt.start()

    def w_push(i):
        half = w_all.at[me, pl.ds(pl.multiple_of(ctx * 64, 64), 64)]
        return copy_to(half, half, w_send.at[i], w_recv.at[me, ctx], side(i))

    def w_relay(t):
        half = w_all.at[t, pl.ds(pl.multiple_of(ctx * 64, 64), 64)]
        return copy_to(half, half, w_send.at[8 + t], w_recv.at[t, ctx], sibling)

    def w_arrival(t, c):
        half = w_all.at[t, pl.ds(pl.multiple_of(c * 64, 64), 64)]
        return copy_to(half, half, w_send.at[0], w_recv.at[t, c], sibling)

    for n, ci in ((0, 3), (1, 2)):
        dy_hop(n).wait_recv()
        dy_hop(3 + n).start()
        dy_relay(ci).start()
    dy_hop(2).wait_recv()
    dy_hop(5).start()
    dy_hop(6).start()
    dy_relay(1).start()
    for i in (1, 7, 2, 6, 3, 5, 4):
        w_push(i).start()
    gain_q = column(q_gain_ref[...])
    gain_k = column(jnp.concatenate([k_gain_ref[...], jnp.zeros((1, 64), f32)], 1))[:64]
    for i in range(1, 8):
        s_arrival((me + i) % 8).wait_recv()

    def finish(t, carry):
        at = pl.ds(pl.multiple_of(t * 128, 128), 128)
        rows = []
        for n, width in enumerate((1024.0, 512.0)):
            total = stats[0, n, pl.ds(t, 1), :]
            for s in range(1, 8):
                total = total + stats[s, n, pl.ds(t, 1), :]
            rows.append(lax.rsqrt(total / width + EPS))
        inv = jnp.concatenate(rows + [jnp.zeros((6, 128), f32)], 0)
        inv_ref[t] = inv
        value = raw[t]
        cos_part, sin_part = table[0, :, at], table[1, :, at]
        queries = turn(value[0:128] * inv[0:1] * gain_q, cos_part, sin_part).astype(bf)
        keys = turn(value[128:192] * inv[1:2] * gain_k, cos_part, sin_part).astype(bf)
        q_t[:, at] = queries
        kv_own[0:64, at] = keys
        kv_own[64:128, at] = value[192:256].astype(bf)
        k_own[at, :] = jnp.transpose(keys)
        return carry

    lax.fori_loop(0, 8, finish, 0)
    kv_push = copy_to(kv_own, kv_sib, kv_sem.at[0], kv_sem.at[1], sibling)
    kv_push.start()

    key_row = lax.broadcasted_iota(jnp.int32, (256, 512), 0).astype(f32)
    query_lane = (lax.broadcasted_iota(jnp.int32, (256, 512), 1) % 256).astype(f32)
    base = (ctx * 1024).astype(f32)

    def attend(i, carry):
        at = pl.ds(pl.multiple_of(i * 256, 256), 256)
        q = jnp.concatenate([q_t[0:64, at], q_t[64:128, at]], 1) * 0.125
        begin = jnp.concatenate([starts[0:1, at]] * 2, 1)

        def block(keys, values, first_key, state, causal):
            top, total, acc = state
            s = jnp.dot(keys, q, preferred_element_type=f32)
            ok = key_row >= begin - first_key
            if causal:
                ok = ok & (key_row <= query_lane)
            s = jnp.where(ok, s, MASKED)
            new_top = jnp.maximum(top, jnp.max(s, 0, keepdims=True))
            e = jnp.exp(s - new_top)
            shrink = jnp.exp(top - new_top)
            total = total * shrink + jnp.sum(e, 0, keepdims=True)
            acc = acc * shrink + jnp.dot(values, e.astype(bf), preferred_element_type=f32)
            return new_top, total, acc

        state = (jnp.full((1, 512), MASKED, f32), jnp.zeros((1, 512), f32), jnp.zeros((64, 512), f32))
        state = block(
            k_own[at, :], kv_own[64:128, at], base + (i * 256).astype(f32), state, True
        )

        def own(j, state):
            ks = pl.ds(pl.multiple_of(j * 256, 256), 256)
            return block(k_own[ks, :], kv_own[64:128, ks], base + (j * 256).astype(f32), state, False)

        state = lax.fori_loop(0, i, own, state)

        def other(j, state):
            ks = pl.ds(pl.multiple_of(j * 256, 256), 256)
            return block(k_sib[ks, :], kv_sib[64:128, ks], (j * 256).astype(f32), state, False)

        top, total, acc = lax.fori_loop(0, 4 * ctx, other, state)
        out = (acc / total).astype(bf)
        lse = top + jnp.log(total)
        for h in range(2):
            for n in range(2):
                heads[2 * i + n, 64 * h : 64 * h + 64, :] = out[
                    :, 256 * h + 128 * n : 256 * h + 128 * n + 128
                ]
            lse_ref[h, 0:1, at] = lse[:, 256 * h : 256 * h + 256]
        return carry

    kv_push.wait()

    def straighten(t, carry):
        at = pl.ds(pl.multiple_of(t * 128, 128), 128)
        k_sib[at, :] = jnp.transpose(kv_sib[0:64, at])
        return carry

    dy_hop(3).wait_recv()
    dy_hop(4).wait_recv()
    dy_hop(7).start()
    dy_relay(6).start()
    lax.fori_loop(0, 8, straighten, 0)
    lax.fori_loop(0, 4, attend, 0)

    def o_push(i):
        return copy_to(
            heads.at[(me + i) % 8], heads_all.at[me], o_send.at[i], o_recv.at[me], side(i)
        )

    def o_arrival(t):
        return copy_to(heads_all.at[t], heads_all.at[t], o_send.at[0], o_recv.at[t], sibling)

    for i in range(1, 8):
        o_push(i).start()
    heads_all[me] = heads[me]
    stores = [
        pltpu.make_async_copy(q_t, q_ref, store_sem.at[2]),
        pltpu.make_async_copy(kv_own, kv_ref.at[0], store_sem.at[3]),
        pltpu.make_async_copy(kv_sib, kv_ref.at[1], store_sem.at[4]),
        pltpu.make_async_copy(heads, heads_ref, store_sem.at[5]),
    ]
    for store in stores:
        store.start()

    def pass_on(i, carry):
        t = (me + i) % 8
        w_arrival(t, ctx).wait_recv()
        w_relay(t).start()
        return carry

    lax.fori_loop(1, 8, pass_on, 0)

    for n, ci in ((5, 5), (6, 4), (7, 7)):
        dy_hop(n).wait_recv()
        dy_relay(ci).start()
    for i in range(1, 8):
        t = (me + i) % 8
        w_arrival(t, 1 - ctx).wait_recv()
        o_arrival(t).wait_recv()
    store_w = pltpu.make_async_copy(w_all, w_out_all_ref, store_sem.at[6])
    store_w.start()
    store_heads = pltpu.make_async_copy(heads_all, heads_all_ref, store_sem.at[9])
    store_heads.start()
    attended = dot_tn(heads_all[...].reshape(1024, 128), w_all[...].reshape(1024, 1024))
    resid = x + attended
    resid_ref[...] = resid
    inv_two = lax.rsqrt(jnp.mean(resid * resid, -1, keepdims=True) + EPS)
    rows2 = (resid * inv_two * norm2_ref[...]).astype(bf)
    rows2_ref[...] = rows2
    logits = dot_nt(router_ref[...], rows2)
    expert_row = lax.broadcasted_iota(jnp.int32, (32, 128), 0)
    routes = routes_ref[...]
    named = routes[0:1] == expert_row
    for k in range(1, 8):
        named = named | (routes[k : k + 1] == expert_row)
    chosen = jnp.where(named, logits, MASKED)
    weight = jnp.where(named, jnp.exp(chosen - jnp.max(chosen, 0, keepdims=True)), 0.0)
    gates_ref[...] = weight / jnp.sum(weight, 0, keepdims=True)

    for ci in range(8):
        dy_relay(ci).wait_recv()
    store_dy = pltpu.make_async_copy(dy_all, dy_all_ref, store_sem.at[7])
    store_dy.start()
    for i in range(1, 8):
        s_push(i).wait_send()
        w_push(i).wait_send()
        w_relay((me + i) % 8).wait_send()
        o_push(i).wait_send()
    for n in range(8):
        h_hop(n).wait_send()
        dy_hop(n).wait_send()
        dy_relay(n).wait_send()
    for store in [store_rows, store_raw, store_wt, store_w, store_dy, store_heads] + stores:
        store.wait()


def attention(x, dy, segment, norm1, q_gain, k_gain, norm2, router, routes, w_q, w_k, w_v, w_out):
    bf, f32 = jnp.bfloat16, jnp.float32
    vmem, hbm = pl.BlockSpec(memory_space=pltpu.VMEM), pl.BlockSpec(memory_space=pl.ANY)
    sem = pltpu.SemaphoreType.DMA
    shape = jax.ShapeDtypeStruct
    table = jnp.asarray(rope_constants(2048, 32))
    return pl.pallas_call(
        attention_kernel,
        out_shape=(
            shape((128, 1024), bf),
            shape((32, 128), f32),
            shape((128, 1024), f32),
            shape((8, 128, 1024), bf),
            shape((8, 256, 128), f32),
            shape((8, 8, 128), f32),
            shape((128, 1024), bf),
            shape((2, 128, 1024), bf),
            shape((2, 8, 1024), f32),
            shape((8, 128, 128), bf),
            shape((8, 128, 1024), bf),
            shape((16, 128, 1024), bf),
            shape((256, 1024), bf),
            shape((8, 128, 128), bf),
        ),
        in_specs=[vmem] * 9 + [hbm] * 5,
        out_specs=(vmem, vmem, vmem, hbm, hbm, vmem, hbm, hbm, vmem, hbm, hbm, hbm, hbm, hbm),
        scratch_shapes=[
            pltpu.VMEM((8, 128, 1024), bf),
            pltpu.VMEM((16, 128, 1024), bf),
            pltpu.VMEM((8, 128, 1024), bf),
            pltpu.VMEM((1024, 128), bf),
            pltpu.VMEM((256, 1024), bf),
            pltpu.VMEM((8, 256, 128), f32),
            pltpu.VMEM((2, 32, 1024), f32),
            pltpu.VMEM((2, 8, 128), f32),
            pltpu.VMEM((8, 2, 8, 128), f32),
            pltpu.VMEM((128, 1024), bf),
            pltpu.VMEM((128, 1024), bf),
            pltpu.VMEM((128, 1024), bf),
            pltpu.VMEM((1024, 64), bf),
            pltpu.VMEM((1024, 64), bf),
            pltpu.VMEM((8, 1024), f32),
            pltpu.VMEM((8, 128, 128), bf),
            pltpu.VMEM((8, 128, 128), bf),
            sem((5,)),
            sem((8,)),
            sem((8,)),
            sem((16,)),
            sem((16,)),
            sem((16,)),
            sem((8, 2)),
            sem((8,)),
            sem((8,)),
            sem((2,)),
            sem((8,)),
            sem((8,)),
            sem((10,)),
        ],
        compiler_params=pltpu.CompilerParams(
            collective_id=2, has_side_effects=True, vmem_limit_bytes=56 << 20
        ),
        cost_estimate=pl.CostEstimate(
            flops=5_000_000_000, bytes_accessed=20_000_000, transcendentals=4_000_000
        ),
    )(
        x,
        dy,
        segment.reshape(16, 128),
        norm1.reshape(1, 1024),
        q_gain.reshape(1, 128),
        k_gain.reshape(1, 64),
        norm2.reshape(1, 1024),
        router.T,
        routes.T,
        w_q,
        w_k.T,
        w_v.T,
        w_out,
        table,
    )


def backward_kernel(
    x_ref,
    dy_ref,
    d_rows_ref,
    d_gate_ref,
    gates_ref,
    rows2_ref,
    resid_ref,
    router_ref,
    norm1_ref,
    norm2_ref,
    q_gain_ref,
    k_gain_ref,
    segment_ref,
    inv_ref,
    lse_ref,
    rows1_ref,
    raw_ref,
    q_ref,
    kv_ref,
    heads_ref,
    heads_all_ref,
    w_out_ref,
    w_all_ref,
    grads_ref,
    out_part_ref,
    table_ref,
    grad_x_ref,
    norm1_out_ref,
    pack_ref,
    output_ref,
    reduced_ref,
    rows1,
    raw,
    q_t,
    kv_own,
    kv_sib,
    heads,
    w_out,
    w_all,
    table,
    starts,
    d_resid,
    heads_all,
    wo_part,
    wo_in,
    dh_send,
    dh_all,
    tiny,
    q_cat,
    q_nat,
    d_cat,
    d_nat,
    lanes,
    k_nat,
    v_nat,
    dq_acc,
    dk_acc,
    dv_acc,
    dkv_out,
    dkv_in,
    terms,
    stat,
    stats,
    dqkv,
    dqkv_all,
    pack,
    pack_sib,
    pack_in,
    result,
    n1,
    n1_chips,
    n1_sib,
    load_sem,
    a_send,
    a_recv,
    dh_send_sem,
    dh_recv,
    t_send,
    t_recv,
    s_send,
    s_recv,
    dkv_sem,
    o_send,
    o_recv,
    p_sem,
    rs_send,
    rs_recv,
    g_send,
    g_recv,
    gs_send,
    gs_recv,
    n_send,
    n_recv,
    m_send,
    m_recv,
    ns_sem,
    grads,
    reduced,
    ra2,
    ra4,
    rb1,
    rb2,
    rb3,
    r_send,
    r_recv,
    out_own,
    out_sib,
    out_a,
    out_b,
    out_c,
    os_sem,
    out_send,
    out_recv,
    keep_sem,
):
    f32, bf = jnp.float32, jnp.bfloat16
    dp, ctx, me = lax.axis_index("dp"), lax.axis_index("ctx"), lax.axis_index("tensor")
    sibling = (dp, 1 - ctx, me)

    def side(i):
        return (dp, ctx, (me + i) % 8)

    def chip(i):
        return ((dp + i) % 8, ctx, me)

    z, y = me // 2, me % 2
    other = 1 - y
    up, down, pair = (
        (dp, ctx, ((z + 1) % 4) * 2 + y),
        (dp, ctx, ((z + 3) % 4) * 2 + y),
        (dp, ctx, z * 2 + other),
    )

    def a_rows(k, c, s=0):
        start = 304 * (((z + k) % 4) * 2 + c) + 160 * s
        return pl.ds(pl.multiple_of(start, 16), (160, 144)[s])

    def of_part(s):
        return pl.ds(160 * s, (160, 144)[s])

    def b_rows(k, c):
        return second_half(z, y, k, c)

    def hop(n, s=0):
        if n < 2:
            src, dst = grads.at[a_rows((1, 3)[n], n, s)], ra2.at[n, of_part(s)]
            to = (up, down)[n]
        elif n == 2:
            src, dst, to = grads.at[b_rows(0, other)], rb1, pair
        elif n < 5:
            part = n - 3
            src, to = grads.at[piece(z, y, 2, y, part)], (up, down)[part]
            dst = (rb2.at[pl.ds(0, 48)], rb2.at[pl.ds(48, 32)])[part]
        elif n == 5:
            src, dst, to = grads.at[a_rows(0, other, s)], ra4.at[of_part(s)], pair
        elif n == 6:
            src, dst, to = grads.at[b_rows(1, y)], rb3.at[0], up
        elif n == 7:
            src, dst, to = grads.at[b_rows(3, y)], rb3.at[1], down
        else:
            place, to = (
                (a_rows(0, y, s), pair),
                (a_rows(0, y, s), up),
                (a_rows(0, y, s), down),
                (a_rows(0, other, s), up),
                (a_rows(0, other, s), down),
                (a_rows(3, 0, s), up),
                (a_rows(1, 1, s), down),
                (b_rows(0, y), up),
                (b_rows(0, y), down),
                (piece(z, y, 3, y, 0), up),
                (piece(z, y, 1, y, 1), down),
                (b_rows(0, y), pair),
                (b_rows(3, y), pair),
                (b_rows(1, y), pair),
                (b_rows(2, y), pair),
            )[n - 8]
            src = dst = reduced.at[place]
        return copy_to(src, dst, r_send.at[n + 23 * s], r_recv.at[n + 23 * s], to)

    def go(*hops, s=0):
        for n in hops:
            hop(n, s).start()

    def got(*hops, s=0):
        for n in hops:
            hop(n, s).wait_recv()

    def reduce_0():
        go(0, 1, 3, 4, 2)

    def reduce_1(s):
        got(0, 1, s=s)
        for c in range(2):
            add_rows(grads, a_rows(0, c, s), ra2[c, of_part(s)])
        go(5, s=s)

    def reduce_2():
        got(3, 4)
        add_rows(grads, piece(z, y, 1, y, 0), rb2[0:48])
        add_rows(grads, piece(z, y, 3, y, 1), rb2[48:80])
        go(6, 7)

    def reduce_3(s):
        got(5, s=s)
        add_rows(grads, a_rows(0, y, s), ra4[of_part(s)])
        reduced[a_rows(0, y, s), :] = grads[a_rows(0, y, s), :]
        go(8, 9, 10, s=s)

    def reduce_4():
        got(6, 7, 2)
        add_rows(grads, b_rows(0, y), rb1[...], rb3[0], rb3[1])
        reduced[b_rows(0, y), :] = grads[b_rows(0, y), :]
        go(15, 16, 19)

    def reduce_5(s):
        got(8, s=s)
        go(11, 12, s=s)

    def reduce_6():
        got(15)
        go(17, 20)
        got(16)
        go(18, 21)

    def reduce_7(s):
        @pl.when(y == 0)
        def _():
            got(9, 12, s=s)

        @pl.when(y == 1)
        def _():
            got(11, 10, s=s)

        go(13, 14, s=s)

    def reduce_8():
        got(17, 18)
        go(22)

    def keep(n, place):
        return pltpu.make_async_copy(reduced.at[place], reduced_ref.at[place], keep_sem.at[n])

    keep_places = (
        [a_rows(0, c, s) for c in range(2) for s in range(2)]
        + [a_rows(k, c, s) for k in (1, 3) for c in range(2) for s in range(2)]
        + [a_rows(2, c, s) for c in range(2) for s in range(2)]
        + [pl.ds(2432, 640)]
    )

    def reduce_9():
        for n in range(4):
            keep(n, keep_places[n]).start()
        for s in range(2):

            @pl.when(y == 0)
            def _():
                got(10, 11, s=s)

            @pl.when(y == 1)
            def _():
                got(9, 12, s=s)

        for n in range(4, 12):
            keep(n, keep_places[n]).start()
        got(19, 20, 21, 22)
        keep(16, keep_places[16]).start()
        for s in range(2):
            got(13, 14, s=s)
        for n in range(12, 16):
            keep(n, keep_places[n]).start()
        for n in range(23):
            hop(n).wait_send()
        for n in (0, 1, 5, 8, 9, 10, 11, 12, 13, 14):
            hop(n, 1).wait_send()

    def x_side(i):
        return ((dp // 4) * 4 + (dp + i) % 4, ctx, me)

    right, left, partner = x_side(1), x_side(3), ((dp + 4) % 8, ctx, me)
    theirs_out = out_part_ref.at[pl.ds(pl.multiple_of((1 - ctx) * 8, 8), 8)]
    os_push = copy_to(
        theirs_out, out_sib.at[:, :, pl.ds(0, 1024)], os_sem.at[0], os_sem.at[1], sibling
    )
    wo_push = copy_to(
        wo_part.at[1 - ctx],
        out_sib.at[:, :, pl.ds(1024, 512)],
        os_sem.at[2],
        os_sem.at[3],
        sibling,
    )

    def out_at(i, b):
        return (dp // 4 + b) % 2 * 4 + (dp + i) % 4

    def out_hop(n):
        b = n % 2
        if n < 2:
            src, dst, to = out_own.at[out_at(2, b), pl.ds(0, 64)], out_a.at[0, b], right
        elif n < 4:
            src, dst, to = out_own.at[out_at(2, b), pl.ds(64, 64)], out_a.at[1, b], left
        elif n < 6:
            src, dst, to = out_own.at[out_at(1, b)], out_b.at[0, b], right
        elif n < 8:
            src, dst, to = out_own.at[out_at(3, b)], out_b.at[1, b], left
        else:
            src, dst, to = out_own.at[out_at(0, 1)], out_c, partner
        return copy_to(src, dst, out_send.at[n], out_recv.at[n], to)

    def out_0():
        os_push.wait()
        wo_push.wait()

        def add_sib(d, carry):
            left_part = out_own[d, :, 0:1024].astype(f32)
            right_part = wo_part[ctx, d].astype(f32)
            total = jnp.concatenate([left_part, right_part], 1) + out_sib[d].astype(f32)
            out_own[d] = total.astype(bf)
            return carry

        lax.fori_loop(0, 8, add_sib, 0)
        for n in range(4):
            out_hop(n).start()

    def out_add(at, rows, *parts):
        total = out_own[at, rows].astype(f32)
        for part in parts:
            total = total + part.astype(f32)
        out_own[at, rows] = total.astype(bf)

    def out_1():
        for b in range(2):
            out_hop(b).wait_recv()
            out_add(out_at(1, b), pl.ds(0, 64), out_a[0, b])
            out_hop(4 + b).start()
            out_hop(2 + b).wait_recv()
            out_add(out_at(3, b), pl.ds(64, 64), out_a[1, b])
            out_hop(6 + b).start()

    def out_2():
        for b in (1, 0):
            out_hop(4 + b).wait_recv()
            out_hop(6 + b).wait_recv()
            out_add(out_at(0, b), slice(None), out_b[0, b], out_b[1, b])
            if b == 1:
                out_hop(8).start()

    def out_3():
        out_hop(8).wait_recv()
        total = out_own[dp].astype(f32) + out_c[...].astype(f32)
        output_ref[...] = (resid_ref[...] + total[:, 0:1024]).astype(bf)
        wo_sum = total[:, 1024:1536].astype(bf)
        for t in range(8):
            wo_part[0, 0, 16 * t : 16 * t + 16, :] = wo_sum[16 * t : 16 * t + 16]
        for i in range(1, 8):
            wo_hop(i).start()
        wo_in[me] = wo_part[0, 0, pl.ds(pl.multiple_of(me * 16, 16), 16), :]
        for n in range(9):
            out_hop(n).wait_send()

    def wo_hop(i):
        rows = pl.ds(pl.multiple_of((me + i) % 8 * 16, 16), 16)
        return copy_to(wo_part.at[0, 0, rows], wo_in.at[me], a_send.at[i], a_recv.at[me], side(i))

    def wo_arrival(t):
        return copy_to(wo_in.at[t], wo_in.at[t], a_send.at[0], a_recv.at[t], sibling)

    early = pltpu.make_async_copy(grads_ref, grads, load_sem.at[9])
    early.start()
    sources = (rows1_ref, raw_ref, q_ref, kv_ref.at[0], kv_ref.at[1], heads_ref, w_out_ref)
    targets = (rows1, raw, q_t, kv_own, kv_sib, heads, w_out)
    loads = [
        pltpu.make_async_copy(s, t, load_sem.at[n])
        for n, (s, t) in enumerate(zip(sources, targets, strict=True))
    ]
    loads.append(pltpu.make_async_copy(w_all_ref, w_all, load_sem.at[7]))
    loads.append(pltpu.make_async_copy(table_ref.at[ctx], table, load_sem.at[8]))
    loads.append(early)
    loads.append(pltpu.make_async_copy(heads_all_ref, heads_all, load_sem.at[11]))
    own_blocks = out_part_ref.at[pl.ds(pl.multiple_of(ctx * 8, 8), 8)]
    loads.append(pltpu.make_async_copy(own_blocks, out_own.at[:, :, pl.ds(0, 1024)], load_sem.at[10]))
    for n, load in enumerate(loads):
        if n != 9:
            load.start()
    barrier = pltpu.get_barrier_semaphore()
    for i in range(1, 8):
        pl.semaphore_signal(barrier, inc=1, device_id=side(i), device_id_type=MESH)
        pl.semaphore_signal(barrier, inc=1, device_id=chip(i), device_id_type=MESH)
    pl.semaphore_signal(barrier, inc=1, device_id=sibling, device_id_type=MESH)

    pl.semaphore_wait(barrier, 15)
    early.wait()
    reduce_0()
    gates, d_gate = gates_ref[...], d_gate_ref[...]
    d_logits = gates * (d_gate - jnp.sum(gates * d_gate, 0, keepdims=True))
    d_normed = d_rows_ref[...] + lax.dot_general(
        jnp.transpose(d_logits),
        router_ref[...].astype(f32),
        (((1,), (0,)), ((), ())),
        preferred_element_type=f32,
        precision=lax.Precision.HIGHEST,
    )
    resid = resid_ref[...]
    inv_two = lax.rsqrt(jnp.mean(resid * resid, -1, keepdims=True) + EPS)
    res_hat = resid * inv_two
    scaled = d_normed * norm2_ref[...]
    d_res = dy_ref[...].astype(f32) + inv_two * (
        scaled - res_hat * jnp.mean(scaled * res_hat, -1, keepdims=True)
    )
    d_resid[...] = d_res
    datt = d_res.astype(bf)
    for n in (6,):
        loads[n].wait()
    d_heads = dot_nt(w_out[...].reshape(1024, 1024), datt).astype(bf)
    dh_send[...] = d_heads.reshape(8, 128, 128)
    dh_all[me] = dh_send[me]

    def dh_push(i):
        return copy_to(
            dh_send.at[(me + i) % 8], dh_all.at[me], dh_send_sem.at[i], dh_recv.at[me], side(i)
        )

    def dh_arrival(t):
        return copy_to(dh_all.at[t], dh_all.at[t], dh_send_sem.at[0], dh_recv.at[t], sibling)

    for i in range(1, 8):
        dh_push(i).start()

    norm2_part = jnp.sum(d_normed * res_hat, 0, keepdims=True)
    router_part = jnp.dot(
        d_logits,
        rows2_ref[...].astype(f32),
        preferred_element_type=f32,
        precision=lax.Precision.HIGHEST,
    )
    def pack_rows(place, value):
        for c in range(2):
            pack[c, place, :] = value[:, 512 * c : 512 * c + 512].astype(bf)

    pack_rows(pl.ds(256, 32), router_part)
    pack_rows(pl.ds(288, 16), jnp.concatenate([norm2_part, jnp.zeros((15, 1024), f32)], 0))
    pack_rows(pl.ds(320, 64), jnp.zeros((64, 1024), f32))

    os_push.start()
    loads[10].wait()

    def wo_rows(t, carry):
        value = jnp.dot(heads_all[t], datt, preferred_element_type=f32).astype(bf)
        rows = pl.ds(pl.multiple_of(t * 16, 16), 16)
        for d in range(8):
            for c in range(2):
                wo_part[c, d, rows, :] = value[16 * d : 16 * d + 16, 512 * c : 512 * c + 512]
        return carry

    lax.fori_loop(0, 8, wo_rows, 0)
    wo_push.start()
    go(0, 1, s=1)
    for n in (0, 1, 2, 3, 4, 5, 7, 8, 11):
        loads[n].wait()
    seg = segment_ref[...]
    start = jnp.zeros((16, 128), f32)
    for s in range(1, 8):
        below = jnp.where(seg < s, 1.0, 0.0)
        count = jnp.sum(jnp.sum(below, 1, keepdims=True), 0, keepdims=True)
        start = jnp.where(seg == s, count, start)
    start = jnp.where(ctx == 0, start[:8], start[8:])
    for t in range(8):
        starts[0:1, 128 * t : 128 * t + 128] = start[t : t + 1]

    def lay_out(t, carry):
        at = pl.ds(pl.multiple_of(t * 128, 128), 128)
        i, half = t // 2, t % 2
        q = q_t[:, at] * 0.125
        for h in range(2):
            spot = pl.ds(pl.multiple_of(h * 256 + half * 128, 128), 128)
            q_h = q[64 * h : 64 * h + 64]
            q_cat[i, :, spot] = q_h
            q_nat[i, spot, :] = jnp.transpose(q_h)
            lanes[i, 0:1, spot] = lse_ref[h, 0:1, at]
            lanes[i, 2:3, spot] = starts[0:1, at]
        for n, kv in enumerate((kv_own, kv_sib)):
            k_nat[n, at, :] = jnp.transpose(kv[0:64, at])
            v_nat[n, at, :] = jnp.transpose(kv[64:128, at])
        return carry

    lax.fori_loop(0, 8, lay_out, 0)
    dk_acc[...] = jnp.zeros_like(dk_acc)
    dv_acc[...] = jnp.zeros_like(dv_acc)
    dq_acc[...] = jnp.zeros_like(dq_acc)
    for i in range(1, 8):
        dh_arrival((me + i) % 8).wait_recv()

    def lay_dh(t, carry):
        i, half = t // 2, t % 2
        d, o = dh_all[t], heads[t]
        product = d.astype(f32) * o.astype(f32)
        for h in range(2):
            spot = pl.ds(pl.multiple_of(h * 256 + half * 128, 128), 128)
            d_h = d[64 * h : 64 * h + 64]
            d_cat[i, :, spot] = d_h
            d_nat[i, spot, :] = jnp.transpose(d_h)
            lanes[i, 1:2, spot] = jnp.sum(product[64 * h : 64 * h + 64], 0, keepdims=True)
        return carry

    lax.fori_loop(0, 8, lay_dh, 0)
    reduce_1(0)
    key_row = lax.broadcasted_iota(jnp.int32, (256, 512), 0).astype(f32)
    query_lane = (lax.broadcasted_iota(jnp.int32, (256, 512), 1) % 256).astype(f32)
    base = (ctx * 1024).astype(f32)

    def block(n, i, j, first_key, causal):
        ks = pl.ds(pl.multiple_of(j * 256, 256), 256)
        kv = (kv_own, kv_sib)[n]
        s = jnp.dot(k_nat[n, ks, :], q_cat[i], preferred_element_type=f32)
        ok = key_row >= lanes[i, 2:3, :] - first_key
        if causal:
            ok = ok & (key_row <= query_lane)
        p = jnp.exp(jnp.where(ok, s, MASKED) - lanes[i, 0:1, :])
        dp_ = jnp.dot(v_nat[n, ks, :], d_cat[i], preferred_element_type=f32)
        ds = (p * (dp_ - lanes[i, 1:2, :])).astype(bf)
        dv_acc[n, ks, :] += jnp.dot(p.astype(bf), d_nat[i], preferred_element_type=f32)
        dk_acc[n, ks, :] += jnp.dot(ds, q_nat[i], preferred_element_type=f32)
        dq_acc[i] += jnp.dot(kv[0:64, ks], ds, preferred_element_type=f32)

    def hook_0():
        reduce_2()
        reduce_1(1)

    def hook_1():
        out_0()
        reduce_3(0)

    def hook_2():
        reduce_4()

    def hook_3():
        reduce_3(1)
        out_1()

    for i in range(4):

        def cross(j, carry, i=i):
            block(1, i, j, (j * 256).astype(f32), False)
            return carry

        lax.fori_loop(0, 4 * ctx, cross, 0)
        (hook_0, hook_1, hook_2, hook_3)[i]()
    dkv_push = copy_to(dkv_out, dkv_in, dkv_sem.at[0], dkv_sem.at[1], sibling)

    def upright(t, carry):
        at = pl.ds(pl.multiple_of(t * 128, 128), 128)
        dkv_out[0:64, at] = jnp.transpose(dk_acc[1, at, :]).astype(bf)
        dkv_out[64:128, at] = jnp.transpose(dv_acc[1, at, :]).astype(bf)
        return carry

    lax.fori_loop(0, 8, upright, 0)
    dkv_push.start()

    def within(i):
        def full(j, c):
            block(0, i, j, base + (j * 256).astype(f32), False)
            return c

        lax.fori_loop(0, i, full, 0)
        block(0, i, i, base + 256.0 * i, True)

    within(0)
    within(1)
    within(2)
    within(3)
    reduce_5(0)
    reduce_6()
    gain_q = column(q_gain_ref[...])
    gain_k = column(jnp.concatenate([k_gain_ref[...], jnp.zeros((1, 64), f32)], 1))[:64]
    dkv_push.wait()

    def unturn(t, sums):
        at = pl.ds(pl.multiple_of(t * 128, 128), 128)
        i, half = t // 2, t % 2
        parts = [
            dq_acc[i, :, pl.ds(pl.multiple_of(h * 256 + half * 128, 128), 128)] for h in range(2)
        ]
        cos_part, sin_part = table[0, :, at], -table[1, :, at]
        inv = inv_ref[t]
        d_q = turn(jnp.concatenate(parts, 0) * 0.125, cos_part, sin_part)
        came = dkv_in[:, at].astype(f32)
        d_k = turn(jnp.transpose(dk_acc[0, at, :]) + came[0:64], cos_part, sin_part)
        d_v = jnp.transpose(dv_acc[0, at, :]) + came[64:128]
        q_hat, k_hat = raw[t, 0:128] * inv[0:1], raw[t, 128:192] * inv[1:2]
        q_sum, k_sum = sums[0] + d_q * q_hat, sums[1] + d_k * k_hat
        q_term, k_term = d_q * gain_q, d_k * gain_k
        terms[t, 0:128] = q_term
        terms[t, 128:192] = k_term
        dqkv[t, 192:256] = d_v.astype(bf)
        stat[0, pl.ds(t, 1), :] = jnp.sum(q_term * q_hat, 0, keepdims=True)
        stat[1, pl.ds(t, 1), :] = jnp.sum(k_term * k_hat, 0, keepdims=True)
        return q_sum, k_sum

    q_sum, k_sum = lax.fori_loop(
        0, 8, unturn, (jnp.zeros((128, 128), f32), jnp.zeros((64, 128), f32))
    )
    stats[me] = stat[...]

    def s_push(i):
        return copy_to(stats.at[me], stats.at[me], s_send.at[i], s_recv.at[me], side(i))

    def s_arrival(t):
        return copy_to(stats.at[t], stats.at[t], s_send.at[0], s_recv.at[t], sibling)

    for i in range(1, 8):
        s_push(i).start()
    out_2()
    q_row = jnp.sum(jnp.transpose(q_sum), 0, keepdims=True)
    k_row = jnp.sum(jnp.transpose(k_sum), 0, keepdims=True)
    gain_row = jnp.concatenate([q_row, k_row, jnp.zeros((1, 1024 - 192), f32)], 1)
    pack_rows(pl.ds(304, 16), jnp.concatenate([gain_row, jnp.zeros((15, 1024), f32)], 0))
    reduce_5(1)
    for i in range(1, 8):
        s_arrival((me + i) % 8).wait_recv()

    def finish(t, carry):
        at = pl.ds(pl.multiple_of(t * 128, 128), 128)
        inner = []
        for n in range(2):
            part = stats[0, n, pl.ds(t, 1), :]
            for s in range(1, 8):
                part = part + stats[s, n, pl.ds(t, 1), :]
            inner.append(part)
        inv = inv_ref[t]
        q_hat, k_hat = raw[t, 0:128] * inv[0:1], raw[t, 128:192] * inv[1:2]
        d_q = inv[0:1] * (terms[t, 0:128] - q_hat * (inner[0] / 1024.0))
        d_k = inv[1:2] * (terms[t, 128:192] - k_hat * (inner[1] / 512.0))
        dqkv[t, 0:128] = d_q.astype(bf)
        dqkv[t, 128:192] = d_k.astype(bf)
        return carry

    lax.fori_loop(0, 8, finish, 0)

    def o_push(i):
        return copy_to(
            dqkv.at[(me + i) % 8], dqkv_all.at[me], o_send.at[i], o_recv.at[me], side(i)
        )

    def o_arrival(t):
        return copy_to(dqkv_all.at[t], dqkv_all.at[t], o_send.at[0], o_recv.at[t], sibling)

    for i in range(1, 8):
        o_push(i).start()
    dqkv_all[me] = dqkv[me]
    grad_qkv = jnp.zeros((256, 1024), f32)
    for t in range(8):
        grad_qkv = grad_qkv + jnp.dot(dqkv[t], rows1[t], preferred_element_type=f32)
    pack_rows(pl.ds(0, 256), grad_qkv)
    p_push = copy_to(pack.at[1 - ctx], pack_sib, p_sem.at[0], p_sem.at[1], sibling)
    p_push.start()
    reduce_7(0)
    for i in range(1, 8):
        o_arrival((me + i) % 8).wait_recv()
    d_rows1 = dot_tn(dqkv_all[...].reshape(2048, 128), w_all[...].reshape(2048, 1024))
    x = x_ref[...].astype(f32)
    inv_one = lax.rsqrt(jnp.mean(x * x, -1, keepdims=True) + EPS)
    x_hat = x * inv_one
    norm1_part = jnp.sum(d_rows1 * x_hat, 0, keepdims=True)
    n1[me] = jnp.concatenate([norm1_part[:, 128 * t : 128 * t + 128] for t in range(8)], 0)

    def n_push(i):
        return copy_to(n1.at[me], n1.at[me], n_send.at[i], n_recv.at[me], side(i))

    def n_arrival(t):
        return copy_to(n1.at[t], n1.at[t], n_send.at[0], n_recv.at[t], sibling)

    for i in range(1, 8):
        n_push(i).start()
    p_push.wait()
    pack[ctx] = (pack[ctx].astype(f32) + pack_sib[...].astype(f32)).astype(bf)
    out_3()

    def rs_push(i):
        to = (dp + i) % 8
        rows = pack.at[ctx, pl.ds(pl.multiple_of(to * 48, 16), 48)]
        return copy_to(rows, pack_in.at[dp], rs_send.at[i], rs_recv.at[dp], chip(i))

    def rs_arrival(d):
        return copy_to(pack_in.at[d], pack_in.at[d], rs_send.at[0], rs_recv.at[d], sibling)

    for i in range(1, 8):
        rs_push(i).start()
    scaled = d_rows1 * norm1_ref[...]
    grad_x_ref[...] = (
        d_resid[...] + inv_one * (scaled - x_hat * jnp.mean(scaled * x_hat, -1, keepdims=True))
    ).astype(bf)
    reduce_8()
    reduce_7(1)
    for i in range(1, 8):
        n_arrival((me + i) % 8).wait_recv()
    norm1_sum = n1[0]
    for t in range(1, 8):
        norm1_sum = norm1_sum + n1[t]
    n1_chips[dp] = norm1_sum

    def m_push(i):
        return copy_to(n1_chips.at[dp], n1_chips.at[dp], m_send.at[i], m_recv.at[dp], chip(i))

    def m_arrival(d):
        return copy_to(n1_chips.at[d], n1_chips.at[d], m_send.at[0], m_recv.at[d], sibling)

    for i in range(1, 8):
        m_push(i).start()
    pack_in[dp] = pack[ctx, pl.ds(pl.multiple_of(dp * 48, 16), 48), :]
    for i in range(1, 8):
        rs_arrival((dp + i) % 8).wait_recv()
    owned = pack_in[0].astype(f32)
    for d in range(1, 8):
        owned = owned + pack_in[d].astype(f32)
    top = pl.ds(0, 48)
    result[ctx, dp, top] = owned.astype(bf)
    wide = (dp == 5) | (dp == 6)

    def t_push(i):
        return copy_to(result.at[ctx, dp, top], tiny.at[me], t_send.at[i], t_recv.at[me], side(i))

    def t_arrival(t):
        return copy_to(tiny.at[t], tiny.at[t], t_send.at[0], t_recv.at[t], sibling)

    @pl.when(wide)
    def _():
        for i in range(1, 8):
            t_push(i).start()
        tiny[me] = result[ctx, dp, top]
        for i in range(1, 8):
            t_arrival((me + i) % 8).wait_recv()
            t_push(i).wait_send()
        total = tiny[0].astype(f32)
        for t in range(1, 8):
            total = total + tiny[t].astype(f32)
        row = lax.broadcasted_iota(jnp.int32, (48, 512), 0)
        shared = ((dp == 5) & (row >= 16)) | ((dp == 6) & (row < 16))
        result[ctx, dp, top] = jnp.where(shared, total, owned).astype(bf)

    for i in range(1, 8):
        wo_arrival((me + i) % 8).wait_recv()
    total = wo_in[0].astype(f32)
    for t in range(1, 8):
        total = total + wo_in[t].astype(f32)
    result[ctx, dp, pl.ds(48, 16)] = total.astype(bf)


    def g_push(i):
        return copy_to(
            result.at[ctx, dp], result.at[ctx, dp], g_send.at[i], g_recv.at[dp], chip(i)
        )

    def g_arrival(d):
        return copy_to(result.at[ctx, d], result.at[ctx, d], g_send.at[0], g_recv.at[d], sibling)

    def g_relay(d):
        return copy_to(
            result.at[ctx, d], result.at[ctx, d], gs_send.at[d], gs_recv.at[d], sibling
        )

    def g_sib_arrival(d):
        place = result.at[1 - ctx, d]
        return copy_to(place, place, gs_send.at[d], gs_recv.at[d], sibling)

    for i in range(1, 8):
        g_push(i).start()
    g_relay(dp).start()
    for i in range(1, 8):
        m_arrival((dp + i) % 8).wait_recv()
    norm1_sum = n1_chips[0]
    for d in range(1, 8):
        norm1_sum = norm1_sum + n1_chips[d]
    n1_sib[0] = norm1_sum
    ns_push = copy_to(n1_sib.at[0], n1_sib.at[1], ns_sem.at[0], ns_sem.at[1], sibling)
    ns_push.start()

    def pass_on(i, carry):
        d = (dp + i) % 8
        g_arrival(d).wait_recv()
        g_relay(d).start()
        return carry

    lax.fori_loop(1, 8, pass_on, 0)
    ns_push.wait()
    norm1_out_ref[...] = n1_sib[0] + n1_sib[1]
    for d in range(8):
        g_sib_arrival(d).wait_recv()
        g_relay(d).wait_send()
    reduce_9()
    pack_ref[...] = result[...]
    for i in range(1, 8):
        dh_push(i).wait_send()
        s_push(i).wait_send()
        o_push(i).wait_send()
        n_push(i).wait_send()
        rs_push(i).wait_send()
        m_push(i).wait_send()
        g_push(i).wait_send()
    for i in range(1, 8):
        wo_hop(i).wait_send()
    for n, place in enumerate(keep_places):
        keep(n, place).wait()


def backward(small, large):
    bf, f32 = jnp.bfloat16, jnp.float32
    vmem, hbm = pl.BlockSpec(memory_space=pltpu.VMEM), pl.BlockSpec(memory_space=pl.ANY)
    sem = pltpu.SemaphoreType.DMA
    shape = jax.ShapeDtypeStruct
    table = jnp.asarray(rope_constants(2048, 32))
    return pl.pallas_call(
        backward_kernel,
        out_shape=(
            shape((128, 1024), bf),
            shape((8, 128), f32),
            shape((2, 8, 64, 512), bf),
            shape((128, 1024), bf),
            shape((3072, 1024), bf),
        ),
        in_specs=[vmem] * 15 + [hbm] * 11,
        out_specs=(vmem, vmem, vmem, vmem, hbm),
        scratch_shapes=[
            pltpu.VMEM((8, 128, 1024), bf),
            pltpu.VMEM((8, 256, 128), f32),
            pltpu.VMEM((128, 1024), bf),
            pltpu.VMEM((128, 1024), bf),
            pltpu.VMEM((128, 1024), bf),
            pltpu.VMEM((8, 128, 128), bf),
            pltpu.VMEM((8, 128, 1024), bf),
            pltpu.VMEM((8, 256, 1024), bf),
            pltpu.VMEM((2, 32, 1024), f32),
            pltpu.VMEM((8, 1024), f32),
            pltpu.VMEM((128, 1024), f32),
            pltpu.VMEM((8, 128, 128), bf),
            pltpu.VMEM((2, 8, 128, 512), bf),
            pltpu.VMEM((8, 16, 512), bf),
            pltpu.VMEM((8, 128, 128), bf),
            pltpu.VMEM((8, 128, 128), bf),
            pltpu.VMEM((8, 48, 512), bf),
            pltpu.VMEM((4, 64, 512), bf),
            pltpu.VMEM((4, 512, 64), bf),
            pltpu.VMEM((4, 64, 512), bf),
            pltpu.VMEM((4, 512, 64), bf),
            pltpu.VMEM((4, 8, 512), f32),
            pltpu.VMEM((2, 1024, 64), bf),
            pltpu.VMEM((2, 1024, 64), bf),
            pltpu.VMEM((4, 64, 512), f32),
            pltpu.VMEM((2, 1024, 64), f32),
            pltpu.VMEM((2, 1024, 64), f32),
            pltpu.VMEM((128, 1024), bf),
            pltpu.VMEM((128, 1024), bf),
            pltpu.VMEM((8, 192, 128), f32),
            pltpu.VMEM((2, 8, 128), f32),
            pltpu.VMEM((8, 2, 8, 128), f32),
            pltpu.VMEM((8, 256, 128), bf),
            pltpu.VMEM((8, 256, 128), bf),
            pltpu.VMEM((2, 384, 512), bf),
            pltpu.VMEM((384, 512), bf),
            pltpu.VMEM((8, 48, 512), bf),
            pltpu.VMEM((2, 8, 64, 512), bf),
            pltpu.VMEM((8, 8, 128), f32),
            pltpu.VMEM((8, 8, 128), f32),
            pltpu.VMEM((2, 8, 128), f32),
            sem((12,)),
        ]
        + [sem((8,))] * 8
        + [sem((2,))]
        + [sem((8,))] * 2
        + [sem((2,))]
        + [sem((8,))] * 10
        + [sem((2,))]
        + [
            pltpu.VMEM((3072, 1024), bf),
            pltpu.VMEM((3072, 1024), bf),
            pltpu.VMEM((2, 304, 1024), bf),
            pltpu.VMEM((304, 1024), bf),
            pltpu.VMEM((80, 1024), bf),
            pltpu.VMEM((80, 1024), bf),
            pltpu.VMEM((2, 80, 1024), bf),
            sem((46,)),
            sem((46,)),
            pltpu.VMEM((8, 128, 1536), bf),
            pltpu.VMEM((8, 128, 1536), bf),
            pltpu.VMEM((2, 2, 64, 1536), bf),
            pltpu.VMEM((2, 2, 128, 1536), bf),
            pltpu.VMEM((128, 1536), bf),
            sem((4,)),
            sem((9,)),
            sem((9,)),
            sem((17,)),
        ],
        compiler_params=pltpu.CompilerParams(
            collective_id=3, has_side_effects=True, vmem_limit_bytes=56 << 20
        ),
        cost_estimate=pl.CostEstimate(
            flops=10_000_000_000, bytes_accessed=20_000_000, transcendentals=4_000_000
        ),
    )(*small, *large, table)


def finish_kernel(
    reduced_ref,
    out_ref,
    grad_x_ref,
    pack_ref,
    norm1_ref,
    gate_ref,
    up_ref,
    down_ref,
    out_copy_ref,
    grad_x_copy_ref,
    w_q_ref,
    w_k_ref,
    w_v_ref,
    q_gain_ref,
    k_gain_ref,
    w_out_ref,
    norm2_ref,
    router_ref,
    norm1_copy_ref,
    rounded,
    wide,
    load_sem,
    store_sem,
):
    f32 = jnp.float32
    loads = [
        pltpu.make_async_copy(reduced_ref.at[pl.ds(256 * n, 256)], rounded.at[n], load_sem.at[n])
        for n in range(12)
    ]
    passed = [
        pltpu.make_async_copy(out_ref, out_copy_ref, load_sem.at[12]),
        pltpu.make_async_copy(grad_x_ref, grad_x_copy_ref, load_sem.at[13]),
    ]
    for copy in loads + passed:
        copy.start()
    def rows(start, count):
        parts = []
        for c in range(2):
            pieces = []
            for d in range(start // 48, (start + count - 1) // 48 + 1):
                first, last = max(start, 48 * d) - 48 * d, min(start + count, 48 * d + 48) - 48 * d
                pieces.append(pack_ref[c, d, first:last, :])
            parts.append(jnp.concatenate(pieces, 0))
        return jnp.concatenate(parts, 1).astype(f32)

    w_q_ref[...] = jnp.transpose(rows(0, 128))
    w_k_ref[...] = rows(128, 64)
    w_v_ref[...] = rows(192, 64)
    router_ref[...] = rows(256, 32)
    norm2_ref[...] = rows(288, 16)[0:1]
    gains = rows(304, 16)
    q_gain_ref[...] = gains[0:1, 0:128]
    k_gain_ref[...] = gains[0:1, 128:192]
    for d in range(8):
        for c in range(2):
            w_out_ref[16 * d : 16 * d + 16, 512 * c : 512 * c + 512] = pack_ref[c, d, 48:64, :].astype(f32)
    norm1_copy_ref[...] = norm1_ref[...]
    stores = []
    for n in range(12):
        loads[n].wait()
        wide[n] = rounded[n].astype(f32)
        if n < 8:
            rows = pl.ds(256 * (n % 4), 256)
            for m, ref in enumerate((gate_ref, up_ref)):
                src = wide.at[n, :, pl.ds(512 * m, 512)]
                stores.append(pltpu.make_async_copy(src, ref.at[n // 4, rows], store_sem.at[2 * n + m]))
        else:
            rows = pl.ds(256 * (n % 2), 256)
            stores.append(
                pltpu.make_async_copy(wide.at[n], down_ref.at[n // 2 - 4, rows], store_sem.at[n + 8])
            )
        for store in stores[-2:] if n < 8 else stores[-1:]:
            store.start()
    for copy in stores + passed:
        copy.wait()


def finish(reduced, out, grad_x, pack, norm1):
    bf, f32 = jnp.bfloat16, jnp.float32
    vmem, hbm = pl.BlockSpec(memory_space=pltpu.VMEM), pl.BlockSpec(memory_space=pl.ANY)
    shape = jax.ShapeDtypeStruct
    return pl.pallas_call(
        finish_kernel,
        out_shape=(
            shape((2, 1024, 512), f32),
            shape((2, 1024, 512), f32),
            shape((2, 512, 1024), f32),
            shape((128, 1024), bf),
            shape((128, 1024), bf),
            shape((1024, 128), f32),
            shape((64, 1024), f32),
            shape((64, 1024), f32),
            shape((1, 128), f32),
            shape((1, 64), f32),
            shape((128, 1024), f32),
            shape((1, 1024), f32),
            shape((32, 1024), f32),
            shape((8, 128), f32),
        ),
        in_specs=[hbm] + [vmem] * 4,
        out_specs=(hbm,) * 5 + (vmem,) * 9,
        scratch_shapes=[
            pltpu.VMEM((12, 256, 1024), bf),
            pltpu.VMEM((12, 256, 1024), f32),
            pltpu.SemaphoreType.DMA((14,)),
            pltpu.SemaphoreType.DMA((20,)),
        ],
        compiler_params=pltpu.CompilerParams(vmem_limit_bytes=62 << 20),
    )(reduced, out, grad_x, pack, norm1)


def shards(
    hidden_in,
    segment,
    norm1_gain,
    w_query,
    w_key,
    w_value,
    q_gain,
    k_gain,
    w_out,
    norm2_gain,
    router,
    w_gate,
    w_up,
    w_down,
    routes,
    cotangent,
):
    f32, bf = jnp.float32, jnp.bfloat16
    rows2, gates, resid, rows1, raw, inv, q_t, kv, lse, heads, w_out_all, dy_all, w_t, heads_all = attention(
        hidden_in,
        cotangent,
        segment,
        norm1_gain,
        q_gain,
        k_gain,
        norm2_gain,
        router,
        routes,
        w_query,
        w_key,
        w_value,
        w_out,
    )
    d_rows, d_gate, out_part, grads, w_all = moe(
        rows2, gates, dy_all, w_gate, w_up, w_down, w_t
    )
    grad_x, norm1_sum, pack, output, grads = backward(
        (
            hidden_in,
            cotangent,
            d_rows,
            d_gate,
            gates,
            rows2,
            resid,
            router.T,
            norm1_gain.reshape(1, 1024),
            norm2_gain.reshape(1, 1024),
            q_gain.reshape(1, 128),
            k_gain.reshape(1, 64),
            segment.reshape(16, 128),
            inv,
            lse,
        ),
        (rows1, raw, q_t, kv, heads, heads_all, w_out_all, w_all, grads, out_part),
    )
    (
        gate,
        up,
        down,
        output,
        grad_x,
        w_q,
        w_k,
        w_v,
        q_g,
        k_g,
        w_o,
        norm2_sum,
        grad_router,
        norm1_sum,
    ) = finish(grads, output, grad_x, pack, norm1_sum)
    return (
        output,
        grad_x,
        norm1_sum.reshape(1024),
        w_q,
        w_k.T,
        w_v.T,
        q_g.reshape(128),
        k_g.reshape(64),
        w_o,
        norm2_sum.reshape(1024),
        grad_router.T,
        gate,
        up,
        down,
    )


def solution(mesh):
    return jax.shard_map(
        shards,
        mesh=mesh,
        in_specs=(
            P(("dp", "ctx", "tensor"), None),
            P("dp"),
            P(),
            P(None, "tensor"),
            P(None, "tensor"),
            P(None, "tensor"),
            P("tensor"),
            P("tensor"),
            P("tensor", None),
            P(),
            P(),
            P(("dp", "ctx"), None, None),
            P(("dp", "ctx"), None, None),
            P(("dp", "ctx"), None, None),
            P(("dp", "ctx", "tensor"), None),
            P(("dp", "ctx", "tensor"), None),
        ),
        out_specs=(
            P(("dp", "ctx", "tensor"), None),
            P(("dp", "ctx", "tensor"), None),
            P(),
            P(None, "tensor"),
            P(None, "tensor"),
            P(None, "tensor"),
            P("tensor"),
            P("tensor"),
            P("tensor", None),
            P(),
            P(),
            P(("dp", "ctx"), None, None),
            P(("dp", "ctx"), None, None),
            P(("dp", "ctx"), None, None),
        ),
        check_vma=False,
    )
```

```python
import jax
import jax.numpy as jnp
import numpy as np
from jax import lax
from jax.experimental import pallas as pl
from jax.experimental.pallas import tpu as pltpu
from jax.sharding import PartitionSpec as P

EPS = 1e-06
THETA = 10000.0
MASKED = -1e30
MESH = pl.DeviceIdType.MESH


def rope_constants(length, half_dim):
    inverse = THETA ** (-(np.arange(half_dim, dtype=np.float64) * 2.0 / (2 * half_dim)))
    angles = inverse[:, None] * np.arange(length, dtype=np.float64)[None, :]
    table = np.stack([np.cos(angles), np.sin(angles)]).astype(np.float32)
    return np.ascontiguousarray(table.reshape(2, half_dim, 2, length // 2).transpose(2, 0, 1, 3))


def turn(value, cos_part, sin_part):
    parts = []
    for h in range(value.shape[0] // 64):
        a, b = value[64 * h : 64 * h + 32], value[64 * h + 32 : 64 * h + 64]
        parts += [a * cos_part - b * sin_part, b * cos_part + a * sin_part]
    return jnp.concatenate(parts, 0)


def column(row):
    return jnp.transpose(jnp.broadcast_to(row, (128, 128)))


def copy_to(src, dst, send, recv, device):
    return pltpu.make_async_remote_copy(
        src_ref=src, dst_ref=dst, send_sem=send, recv_sem=recv, device_id=device, device_id_type=MESH
    )


def dot_nt(left, right):
    return lax.dot_general(
        left, right, (((1,), (1,)), ((), ())), preferred_element_type=jnp.float32
    )


def dot_tn(left, right):
    return lax.dot_general(
        left, right, (((0,), (0,)), ((), ())), preferred_element_type=jnp.float32
    )


def across(a, b, flip):
    dp, ctx = lax.axis_index("dp"), lax.axis_index("ctx")
    x, y = dp % 4, dp // 4
    mid = ((a + 1) // 2) % 2
    by_x = mid * (1 + 2 * b) + (1 - mid) * 2 * (a // 3)
    by_y = mid * (a // 2) + (1 - mid) * b
    return ((y + by_y) % 2) * 4 + (x + by_x) % 4, (ctx + flip) % 2


def opposite(a, b):
    return b + (((a + 1) // 2) % 2) * (1 - 2 * b)


def first_half(z, y, k, c):
    return pl.ds(pl.multiple_of(304 * (((z + k) % 4) * 2 + c), 16), 304)


def second_half(z, y, k, c):
    return pl.ds(pl.multiple_of(2432 + 80 * (((z + k) % 4) * 2 + c), 16), 80)


def piece(z, y, k, c, part):
    start = 2432 + 80 * (((z + k) % 4) * 2 + c) + 48 * part
    return pl.ds(pl.multiple_of(start, 16), (48, 32)[part])


def add_rows(ref, place, *parts):
    total = ref[place, :].astype(jnp.float32)
    for part in parts:
        total = total + part.astype(jnp.float32)
    ref[place, :] = total.astype(jnp.bfloat16)


def moe_kernel(
    rows_ref,
    gate_ref,
    dy_ref,
    w_gate_ref,
    w_up_ref,
    w_down_ref,
    w_t_ref,
    d_rows_ref,
    d_gate_ref,
    out_part_ref,
    grad_ref,
    w_all_ref,
    rows_all,
    gate_all,
    dy_all,
    w_full,
    acc,
    out_all,
    din_all,
    sib,
    rs_a,
    rs_b,
    rs_c,
    rs_d,
    rs_e,
    dg_out,
    dg_in,
    places,
    x_buf,
    y_buf,
    d_buf,
    o_buf,
    i_buf,
    gs_buf,
    dgs_buf,
    load_sem,
    ag_send,
    ag_recv,
    g_send,
    g_recv,
    sib_send,
    sib_recv,
    rs_send,
    rs_recv,
    dg_send,
    dg_recv,
    store_sem,
    w_send,
    w_recv,
    ra_0,
    ra_1,
    rb,
    r_send,
    r_recv,
    keep_sem,
):
    tensor = lax.axis_index("tensor")
    dp, ctx = lax.axis_index("dp"), lax.axis_index("ctx")
    me = dp * 2 + ctx

    def to(a, b, flip):
        d, c = across(a, b, flip)
        return (d, c, tensor)

    def side(i):
        return (dp, ctx, (tensor + i) % 8)

    loads = []
    for j in range(2):
        loads.append(
            pltpu.make_async_copy(w_gate_ref.at[j], w_full.at[pl.ds(1024 * j, 1024), pl.ds(0, 512)], load_sem.at[3 * j])
        )
        loads.append(
            pltpu.make_async_copy(
                w_up_ref.at[j], w_full.at[pl.ds(1024 * j, 1024), pl.ds(512, 512)], load_sem.at[3 * j + 1]
            )
        )
        loads.append(pltpu.make_async_copy(w_down_ref.at[j], w_full.at[pl.ds(2048 + 512 * j, 512)], load_sem.at[3 * j + 2]))
    loads.append(pltpu.make_async_copy(dy_ref, dy_all, load_sem.at[6]))
    for load in loads:
        load.start()

    barrier = pltpu.get_barrier_semaphore()
    for a in range(4):
        for b in range(2):
            for flip in range(2):
                if (a, b, flip) != (0, 0, 0):
                    pl.semaphore_signal(
                        barrier, inc=1, device_id=to(a, b, flip), device_id_type=MESH
                    )
    for i in range(1, 8):
        pl.semaphore_signal(barrier, inc=1, device_id=side(i), device_id_type=MESH)
    pl.semaphore_wait(barrier, 22)

    right, left, partner = to(1, 0, 0), to(1, 1, 0), to(0, 1, 0)
    sibling = to(0, 0, 1)
    low, high = pl.ds(0, 64), pl.ds(64, 64)

    def hop(n):
        src, dst, device = (
            (rows_all.at[0], rows_all.at[6], right),
            (rows_all.at[0], rows_all.at[4], left),
            (rows_all.at[0], rows_all.at[2], partner),
            (rows_all.at[6, low], rows_all.at[12, low], right),
            (rows_all.at[4, high], rows_all.at[12, high], left),
            (rows_all.at[2], rows_all.at[10], right),
            (rows_all.at[2], rows_all.at[8], left),
            (rows_all.at[12], rows_all.at[14], partner),
        )[n]
        return copy_to(src, dst, ag_send.at[n], ag_recv.at[n], device)

    def relay(ci):
        r = 2 * ci
        return copy_to(
            rows_all.at[r], rows_all.at[r + 1], ag_send.at[8 + ci], ag_recv.at[8 + ci], sibling
        )

    def gate_push(a, b, flip):
        r = 4 * a + 2 * b + flip
        back = 4 * a + 2 * opposite(a, b) + flip
        return copy_to(
            gate_all.at[0], gate_all.at[back], g_send.at[r], g_recv.at[back], to(a, b, flip)
        )

    rows_all[0] = rows_ref[...]
    gate_all[0] = gate_ref[...]
    for n in range(3):
        hop(n).start()
    relay(0).start()
    for r in range(1, 16):
        gate_push(r // 4, (r // 2) % 2, r % 2).start()

    acc[...] = jnp.zeros_like(acc)

    half = pl.ds(pl.multiple_of(ctx * 128, 128), 128)

    def w_push(i):
        return copy_to(
            w_t_ref.at[half],
            w_all_ref.at[tensor, half],
            w_send.at[i],
            w_recv.at[tensor, ctx],
            side(i),
        )

    def w_relay(t):
        place = w_all_ref.at[t, half]
        return copy_to(place, place, w_send.at[8 + t], w_recv.at[t, ctx], to(0, 0, 1))

    def w_arrival(t, c):
        place = w_all_ref.at[t, pl.ds(pl.multiple_of(c * 128, 128), 128)]
        return copy_to(place, place, w_send.at[0], w_recv.at[t, c], to(0, 0, 1))

    for i in (1, 7, 2, 6, 3, 5, 4):
        w_push(i).start()
    w_own = pltpu.make_async_copy(w_t_ref, w_all_ref.at[tensor], load_sem.at[7])
    w_own.start()

    def sib_push(ci):
        return copy_to(
            din_all.at[2 * ci + 1], sib.at[ci], sib_send.at[ci], sib_recv.at[ci], sibling
        )

    def rs_hop(n):
        src, dst, device = (
            (din_all.at[8], rs_a.at[0], right),
            (din_all.at[10], rs_a.at[1], left),
            (din_all.at[14], rs_b, partner),
            (din_all.at[2], rs_c, partner),
            (din_all.at[12, low], rs_d.at[0], right),
            (din_all.at[12, high], rs_d.at[1], left),
            (din_all.at[4], rs_e.at[0], right),
            (din_all.at[6], rs_e.at[1], left),
        )[n]
        return copy_to(src, dst, rs_send.at[n], rs_recv.at[n], device)

    def rs_go(*hops):
        for n in hops:
            rs_hop(n).start()

    def rs_got(*hops):
        for n in hops:
            rs_hop(n).wait_recv()

    def plus(r, rows, *parts):
        total = din_all[r, rows].astype(jnp.float32)
        for part in parts:
            total = total + part.astype(jnp.float32)
        din_all[r, rows] = total.astype(jnp.bfloat16)

    def post(*cis):
        for ci in cis:
            sib_push(ci).wait_recv()
            plus(2 * ci, slice(None), sib[ci])

    def dg_push(a, b, flip):
        r = 4 * a + 2 * b + flip
        back = 4 * a + 2 * opposite(a, b) + flip
        return pltpu.make_async_remote_copy(
            src_ref=dg_out.at[r],
            dst_ref=dg_in.at[back],
            send_sem=dg_send.at[r],
            recv_sem=dg_recv.at[back],
            device_id=to(a, b, flip),
            device_id_type=MESH,
        )

    expert_row = lax.broadcasted_iota(jnp.int32, (32, 128), 0)
    slot_row = lax.broadcasted_iota(jnp.int32, (64, 128), 0).astype(jnp.float32)
    before = (
        lax.broadcasted_iota(jnp.int32, (128, 128), 0)
        < lax.broadcasted_iota(jnp.int32, (128, 128), 1)
    ).astype(jnp.float32)
    before = before.astype(jnp.bfloat16)

    def gather(a, q):
        r = 4 * a + q
        gates = gate_all[r]
        at = pl.ds(pl.multiple_of(q * 64, 64), 64)
        rows = [
            jnp.sum(jnp.where(expert_row == 2 * me + j, gates, 0.0), 0, keepdims=True)
            for j in range(2)
        ]
        both = jnp.concatenate(rows + [jnp.zeros((6, 128), jnp.float32)], 0)
        named = jnp.where(both > 0.0, 1.0, 0.0).astype(jnp.bfloat16)
        slots = jnp.dot(named, before, preferred_element_type=jnp.float32)
        hits = [
            jnp.where((slot_row == slots[j : j + 1]) & (rows[j] > 0.0), 1.0, 0.0) for j in range(2)
        ]
        place = jnp.concatenate(hits, 0).astype(jnp.bfloat16)
        places[q] = place
        x = jnp.dot(place, rows_all[r], preferred_element_type=jnp.float32).astype(jnp.bfloat16)
        y = jnp.dot(place, dy_all[r], preferred_element_type=jnp.float32)
        for j in range(2):
            gs = jnp.sum(hits[j] * rows[j], 1, keepdims=True)
            y_j = y[64 * j : 64 * j + 64]
            x_buf[j, at, :] = x[64 * j : 64 * j + 64]
            y_buf[j, at, :] = y_j.astype(jnp.bfloat16)
            d_buf[j, at, :] = (y_j * gs).astype(jnp.bfloat16)
            gs_buf[j, at, :] = gs

    def expert(j):
        of_gu = pl.ds(pl.multiple_of(j * 1024, 1024), 1024)
        of_dn = pl.ds(pl.multiple_of(2048 + j * 512, 512), 512)
        x = x_buf[j]
        gu = jnp.dot(x, w_full[of_gu, :], preferred_element_type=jnp.float32)
        g, u = gu[:, :512], gu[:, 512:]
        s = jax.nn.sigmoid(g)
        silu = g * s
        act = (silu * u).astype(jnp.bfloat16)
        eout = (
            jnp.dot(act, w_full[of_dn, :], preferred_element_type=jnp.float32)
            .astype(jnp.bfloat16)
            .astype(jnp.float32)
        )
        dgs_buf[j] = jnp.sum(y_buf[j].astype(jnp.float32) * eout, 1, keepdims=True)
        o_buf[j] = (eout * gs_buf[j]).astype(jnp.bfloat16)
        d = d_buf[j]
        d_act = dot_nt(d, w_full[of_dn, :])
        d_g = (d_act * u * s * (1.0 + g * (1.0 - s))).astype(jnp.bfloat16)
        d_u = (d_act * silu).astype(jnp.bfloat16)
        d_gu = jnp.concatenate([d_g, d_u], 1)
        i_buf[j] = dot_nt(d_gu, w_full[of_gu, :]).astype(jnp.bfloat16)
        acc[of_gu, :] += dot_tn(x, d_gu)
        acc[of_dn, :] += dot_tn(act, d)

    def spread(a, q):
        r = 4 * a + q
        b, flip = q // 2, q % 2
        at = pl.ds(pl.multiple_of(q * 64, 64), 64)
        place = places[q]
        d, c = across(a, b, flip)
        o = jnp.concatenate([o_buf[0, at, :], o_buf[1, at, :]], 0)
        out_all[c * 8 + d] = dot_tn(place, o).astype(jnp.bfloat16)
        i = jnp.concatenate([i_buf[0, at, :], i_buf[1, at, :]], 0)
        din_all[r] = dot_tn(place, i).astype(jnp.bfloat16)
        hits = place.astype(jnp.float32)
        back = [
            jnp.sum(hits[64 * j : 64 * j + 64] * dgs_buf[j, at, :], 0, keepdims=True)
            for j in range(2)
        ]
        dg_out[r] = jnp.concatenate(back + [jnp.zeros((6, 128), jnp.float32)], 0)

        @pl.when(r > 0)
        def _():
            dg_push(a, b, flip).start()

    for n, ci in ((0, 3), (1, 2)):
        hop(n).wait_recv()
        hop(3 + n).start()
        relay(ci).start()
    hop(2).wait_recv()
    hop(5).start()
    hop(6).start()
    relay(1).start()
    relay(0).wait_recv()
    for r in range(1, 16):
        gate_push(r // 4, (r // 2) % 2, r % 2).wait_recv()
    for load in loads:
        load.wait()
    relay(1).wait_recv()

    def step(a, carry):
        lax.fori_loop(0, 4, lambda q, c: (gather(a, q), c)[1], 0)

        @pl.when(a == 1)
        def _():
            post(0, 1)

        @pl.when(a == 2)
        def _():
            post(2, 3)

        @pl.when(a == 3)
        def _():
            post(4, 5)
            rs_go(0, 1)

        lax.fori_loop(0, 2, lambda j, c: (expert(j), c)[1], 0)
        lax.fori_loop(0, 4, lambda q, c: (spread(a, q), c)[1], 0)
        for b in range(2):
            sib_push(2 * a + b).start()

        @pl.when(a == 0)
        def _():
            hop(3).wait_recv()
            hop(4).wait_recv()
            hop(7).start()
            relay(6).start()
            for ci in (2, 3):
                relay(ci).wait_recv()

        @pl.when(a == 1)
        def _():
            for n, ci in ((5, 5), (6, 4)):
                hop(n).wait_recv()
                relay(ci).start()
            for ci in (4, 5):
                relay(ci).wait_recv()

        @pl.when(a == 2)
        def _():
            hop(7).wait_recv()
            relay(7).start()
            for ci in (6, 7):
                relay(ci).wait_recv()

        return carry

    lax.fori_loop(0, 4, step, 0)
    def round_rows(place):
        w_full[place, :] = acc[place, :].astype(jnp.bfloat16)

    z, y = tensor // 2, tensor % 2
    up, down, pair = (
        (dp, ctx, ((z + 1) % 4) * 2 + y),
        (dp, ctx, ((z + 3) % 4) * 2 + y),
        (dp, ctx, z * 2 + 1 - y),
    )

    def grad_hop(n):
        place, dst, device = (
            (first_half(z, y, 2, 0), ra_0.at[0], up),
            (first_half(z, y, 2, 1), ra_0.at[1], down),
            (first_half(z, y, 1, 1), ra_1.at[0], up),
            (first_half(z, y, 3, 0), ra_1.at[1], down),
            (second_half(z, y, 2, 1 - y), rb.at[0], pair),
            (second_half(z, y, 1, 1 - y), rb.at[1], pair),
            (second_half(z, y, 3, 1 - y), rb.at[2], pair),
        )[n]
        return copy_to(w_full.at[place], dst, r_send.at[n], r_recv.at[n], device)

    for n in range(2):
        round_rows(first_half(z, y, 2, n))
        grad_hop(n).start()
    post(7, 6)
    rs_go(2)
    for n, k in ((2, 1), (3, 3)):
        round_rows(first_half(z, y, k, 3 - n))
        grad_hop(n).start()
    rs_got(0, 1)
    plus(2, slice(None), rs_a[0], rs_a[1])
    rs_go(3)
    for k, c in ((1, 0), (3, 1), (0, 0), (0, 1)):
        round_rows(first_half(z, y, k, c))
    for k in range(4):
        for c in range(2):
            round_rows(second_half(z, y, k, c))

    def keep(n, place):
        return pltpu.make_async_copy(w_full.at[place], grad_ref.at[place], keep_sem.at[n])

    first_places = [first_half(z, y, k, c) for k, c in ((1, 1), (3, 0), (2, 0), (2, 1))]
    first_places += [second_half(z, y, k, 1 - y) for k in range(4)] + [second_half(z, y, 0, y)]
    last_places = [
        first_half(z, y, 1, 0),
        first_half(z, y, 3, 1),
        second_half(z, y, 2, y),
        first_half(z, y, 0, 1),
        first_half(z, y, 0, 0),
        second_half(z, y, 1, y),
        second_half(z, y, 3, y),
    ]
    for n, place in enumerate(first_places):
        keep(n, place).start()
    rs_got(2)
    plus(12, slice(None), rs_b[...])
    rs_go(4, 5)
    grad_hop(4).start()
    grad_hop(5).start()
    grad_hop(6).start()
    rs_got(4)
    plus(4, low, rs_d[0])
    rs_go(6)
    rs_got(5)
    plus(6, high, rs_d[1])
    rs_go(7)
    for i in range(1, 8):
        t = (tensor + i) % 8
        w_arrival(t, ctx).wait_recv()
        w_relay(t).start()
    for n in range(8):
        hop(n).wait_send()
        relay(n).wait_send()
    for r in range(1, 16):
        gate_push(r // 4, (r // 2) % 2, r % 2).wait_send()
    store_out = pltpu.make_async_copy(out_all, out_part_ref, store_sem.at[0])
    store_out.start()

    for r in range(1, 16):
        a, b, flip = r // 4, (r // 2) % 2, r % 2
        dg_push(a, b, flip).wait()
    dg_in[0] = dg_out[0]
    d_gate = jnp.zeros((32, 128), jnp.float32)
    for r in range(16):
        d, c = across(r // 4, (r // 2) % 2, r % 2)
        got = dg_in[r]
        for j in range(2):
            d_gate = jnp.where(expert_row == (d * 2 + c) * 2 + j, got[j : j + 1], d_gate)
    d_gate_ref[...] = d_gate
    for ci in range(8):
        sib_push(ci).wait_send()
    rs_got(3, 6, 7)
    total = din_all[0].astype(jnp.float32) + rs_c[...].astype(jnp.float32)
    d_rows_ref[...] = total + rs_e[0].astype(jnp.float32) + rs_e[1].astype(jnp.float32)
    for n in range(8):
        rs_hop(n).wait_send()
    for i in range(1, 8):
        t = (tensor + i) % 8
        w_arrival(t, 1 - ctx).wait_recv()
        w_push(i).wait_send()
        w_relay(t).wait_send()
    w_own.wait()
    for n, (arrived, got) in enumerate(
        ((0, ra_0.at[0]), (1, ra_0.at[1]), (4, rb.at[0]), (2, ra_1.at[0]), (3, ra_1.at[1]), (5, rb.at[1]), (6, rb.at[2]))
    ):
        grad_hop(arrived).wait_recv()
        add_rows(w_full, last_places[n], got[...])
        keep(9 + n, last_places[n]).start()
    for n in range(7):
        grad_hop(n).wait_send()
    store_out.wait()
    for n, place in enumerate(first_places + last_places):
        keep(n, place).wait()


def moe(rows, gates, dy, w_gate, w_up, w_down, w_t):
    bf, f32 = jnp.bfloat16, jnp.float32
    vmem, hbm = pl.BlockSpec(memory_space=pltpu.VMEM), pl.BlockSpec(memory_space=pl.ANY)
    sem = pltpu.SemaphoreType.DMA
    return pl.pallas_call(
        moe_kernel,
        out_shape=(
            jax.ShapeDtypeStruct((128, 1024), f32),
            jax.ShapeDtypeStruct((32, 128), f32),
            jax.ShapeDtypeStruct((16, 128, 1024), bf),
            jax.ShapeDtypeStruct((3072, 1024), bf),
            jax.ShapeDtypeStruct((8, 256, 1024), bf),
        ),
        in_specs=[vmem] * 2 + [hbm] * 4 + [vmem],
        out_specs=(vmem, vmem, hbm, hbm, hbm),
        scratch_shapes=[
            pltpu.VMEM((16, 128, 1024), bf),
            pltpu.VMEM((16, 32, 128), f32),
            pltpu.VMEM((16, 128, 1024), bf),
            pltpu.VMEM((3072, 1024), bf),
            pltpu.VMEM((3072, 1024), f32),
            pltpu.VMEM((16, 128, 1024), bf),
            pltpu.VMEM((16, 128, 1024), bf),
            pltpu.VMEM((8, 128, 1024), bf),
            pltpu.VMEM((2, 128, 1024), bf),
            pltpu.VMEM((128, 1024), bf),
            pltpu.VMEM((128, 1024), bf),
            pltpu.VMEM((2, 64, 1024), bf),
            pltpu.VMEM((2, 128, 1024), bf),
            pltpu.VMEM((16, 8, 128), f32),
            pltpu.VMEM((16, 8, 128), f32),
            pltpu.VMEM((4, 128, 128), bf),
            pltpu.VMEM((2, 256, 1024), bf),
            pltpu.VMEM((2, 256, 1024), bf),
            pltpu.VMEM((2, 256, 1024), bf),
            pltpu.VMEM((2, 256, 1024), bf),
            pltpu.VMEM((2, 256, 1024), bf),
            pltpu.VMEM((2, 256, 1), f32),
            pltpu.VMEM((2, 256, 1), f32),
            sem((8,)),
            sem((16,)),
            sem((16,)),
            sem((16,)),
            sem((16,)),
            sem((8,)),
            sem((8,)),
            sem((8,)),
            sem((8,)),
            sem((16,)),
            sem((16,)),
            sem((2,)),
            sem((16,)),
            sem((8, 2)),
            pltpu.VMEM((2, 304, 1024), bf),
            pltpu.VMEM((2, 304, 1024), bf),
            pltpu.VMEM((3, 80, 1024), bf),
            sem((7,)),
            sem((7,)),
            sem((16,)),
        ],
        compiler_params=pltpu.CompilerParams(
            collective_id=1, has_side_effects=True, vmem_limit_bytes=60 << 20
        ),
        cost_estimate=pl.CostEstimate(
            flops=20_000_000_000, bytes_accessed=30_000_000, transcendentals=2_000_000
        ),
    )(rows, gates, dy, w_gate, w_up, w_down, w_t)


def attention_kernel(
    x_ref,
    dy_ref,
    segment_ref,
    norm1_ref,
    q_gain_ref,
    k_gain_ref,
    norm2_ref,
    router_ref,
    routes_ref,
    w_q_ref,
    w_k_ref,
    w_v_ref,
    w_out_ref,
    table_ref,
    rows2_ref,
    gates_ref,
    resid_ref,
    rows1_ref,
    raw_ref,
    inv_ref,
    q_ref,
    kv_ref,
    lse_ref,
    heads_ref,
    w_out_all_ref,
    dy_all_ref,
    w_t_ref,
    heads_all_ref,
    h_all,
    dy_all,
    w_all,
    w_q,
    w_t,
    raw,
    table,
    stat,
    stats,
    q_t,
    kv_own,
    kv_sib,
    k_own,
    k_sib,
    starts,
    heads,
    heads_all,
    load_sem,
    h_send,
    h_recv,
    dy_send,
    dy_recv,
    w_send,
    w_recv,
    s_send,
    s_recv,
    kv_sem,
    o_send,
    o_recv,
    store_sem,
):
    f32, bf = jnp.float32, jnp.bfloat16
    dp, ctx, me = lax.axis_index("dp"), lax.axis_index("ctx"), lax.axis_index("tensor")

    def side(i):
        return (dp, ctx, (me + i) % 8)

    def to(a, b, flip):
        d, c = across(a, b, flip)
        return (d, c, me)

    sibling = (dp, 1 - ctx, me)
    loads = [
        pltpu.make_async_copy(w_q_ref, w_q, load_sem.at[0]),
        pltpu.make_async_copy(w_k_ref, w_t.at[pl.ds(128, 64)], load_sem.at[1]),
        pltpu.make_async_copy(w_v_ref, w_t.at[pl.ds(192, 64)], load_sem.at[2]),
        pltpu.make_async_copy(w_out_ref, w_all.at[me], load_sem.at[3]),
        pltpu.make_async_copy(table_ref.at[ctx], table, load_sem.at[4]),
    ]
    for load in loads:
        load.start()
    barrier = pltpu.get_barrier_semaphore()
    for i in range(1, 8):
        pl.semaphore_signal(barrier, inc=1, device_id=side(i), device_id_type=MESH)
    for a in range(4):
        for b in range(2):
            if (a, b) != (0, 0):
                pl.semaphore_signal(barrier, inc=1, device_id=to(a, b, 0), device_id_type=MESH)
    pl.semaphore_signal(barrier, inc=1, device_id=sibling, device_id_type=MESH)
    x = x_ref[...].astype(f32)
    inv_one = lax.rsqrt(jnp.mean(x * x, -1, keepdims=True) + EPS)
    h_all[me] = (x * inv_one * norm1_ref[...]).astype(bf)
    dy_all[0] = dy_ref[...]
    pl.semaphore_wait(barrier, 15)

    z, y = me // 2, me % 2
    up, down, pair = (
        (dp, ctx, ((z + 1) % 4) * 2 + y),
        (dp, ctx, ((z + 3) % 4) * 2 + y),
        (dp, ctx, z * 2 + 1 - y),
    )
    low, high = pl.ds(0, 64), pl.ds(64, 64)

    def block_at(k, flip):
        return ((z + k) % 4) * 2 + (y + flip) % 2

    def h_hop(n):
        place, device = (
            (h_all.at[me], up),
            (h_all.at[me], down),
            (h_all.at[me], pair),
            (h_all.at[block_at(3, 0), low], up),
            (h_all.at[block_at(1, 0), high], down),
            (h_all.at[block_at(0, 1)], up),
            (h_all.at[block_at(0, 1)], down),
            (h_all.at[block_at(2, 0)], pair),
        )[n]
        return copy_to(place, place, h_send.at[n], h_recv.at[n], device)

    right, left, partner = to(1, 0, 0), to(1, 1, 0), to(0, 1, 0)

    def dy_hop(n):
        src, dst, device = (
            (dy_all.at[0], dy_all.at[6], right),
            (dy_all.at[0], dy_all.at[4], left),
            (dy_all.at[0], dy_all.at[2], partner),
            (dy_all.at[6, low], dy_all.at[12, low], right),
            (dy_all.at[4, high], dy_all.at[12, high], left),
            (dy_all.at[2], dy_all.at[10], right),
            (dy_all.at[2], dy_all.at[8], left),
            (dy_all.at[12], dy_all.at[14], partner),
        )[n]
        return copy_to(src, dst, dy_send.at[n], dy_recv.at[n], device)

    def dy_relay(ci):
        r = 2 * ci
        return copy_to(
            dy_all.at[r], dy_all.at[r + 1], dy_send.at[8 + ci], dy_recv.at[8 + ci], sibling
        )

    for n in range(3):
        h_hop(n).start()
    for n in range(3):
        dy_hop(n).start()
    dy_relay(0).start()

    for load in loads:
        load.wait()
    w_t[0:128, :] = jnp.transpose(w_q[...])
    seg = segment_ref[...]
    start = jnp.zeros((16, 128), f32)
    for s in range(1, 8):
        below = jnp.where(seg < s, 1.0, 0.0)
        count = jnp.sum(jnp.sum(below, 1, keepdims=True), 0, keepdims=True)
        start = jnp.where(seg == s, count, start)
    start = jnp.where(ctx == 0, start[:8], start[8:])
    for t in range(8):
        starts[0:1, 128 * t : 128 * t + 128] = start[t : t + 1]

    def project(t):
        value = dot_nt(w_t[...], h_all[t])
        raw[t] = value
        square = value * value
        stat[0, pl.ds(t, 1), :] = jnp.sum(square[0:128], 0, keepdims=True)
        stat[1, pl.ds(t, 1), :] = jnp.sum(square[128:192], 0, keepdims=True)

    project(me)
    for n in range(2):
        h_hop(n).wait_recv()
        h_hop(3 + n).start()
    h_hop(2).wait_recv()
    h_hop(5).start()
    h_hop(6).start()
    for k, flip in ((3, 0), (1, 0), (0, 1)):
        project(block_at(k, flip))
    h_hop(3).wait_recv()
    h_hop(4).wait_recv()
    h_hop(7).start()
    project(block_at(2, 0))
    for n, k in ((5, 3), (6, 1), (7, 2)):
        h_hop(n).wait_recv()
        project(block_at(k, 1))
    stats[me] = stat[...]

    def s_push(i):
        return copy_to(stats.at[me], stats.at[me], s_send.at[i], s_recv.at[me], side(i))

    def s_arrival(t):
        return copy_to(stats.at[t], stats.at[t], s_send.at[0], s_recv.at[t], sibling)

    for i in range(1, 8):
        s_push(i).start()
    store_rows = pltpu.make_async_copy(h_all, rows1_ref, store_sem.at[0])
    store_raw = pltpu.make_async_copy(raw, raw_ref, store_sem.at[1])
    store_wt = pltpu.make_async_copy(w_t, w_t_ref, store_sem.at[8])
    store_rows.start()
    store_raw.start()
    store_wt.start()

    def w_push(i):
        half = w_all.at[me, pl.ds(pl.multiple_of(ctx * 64, 64), 64)]
        return copy_to(half, half, w_send.at[i], w_recv.at[me, ctx], side(i))

    def w_relay(t):
        half = w_all.at[t, pl.ds(pl.multiple_of(ctx * 64, 64), 64)]
        return copy_to(half, half, w_send.at[8 + t], w_recv.at[t, ctx], sibling)

    def w_arrival(t, c):
        half = w_all.at[t, pl.ds(pl.multiple_of(c * 64, 64), 64)]
        return copy_to(half, half, w_send.at[0], w_recv.at[t, c], sibling)

    for n, ci in ((0, 3), (1, 2)):
        dy_hop(n).wait_recv()
        dy_hop(3 + n).start()
        dy_relay(ci).start()
    dy_hop(2).wait_recv()
    dy_hop(5).start()
    dy_hop(6).start()
    dy_relay(1).start()
    for i in (1, 7, 2, 6, 3, 5, 4):
        w_push(i).start()
    gain_q = column(q_gain_ref[...])
    gain_k = column(jnp.concatenate([k_gain_ref[...], jnp.zeros((1, 64), f32)], 1))[:64]
    for i in range(1, 8):
        s_arrival((me + i) % 8).wait_recv()

    def finish(t, carry):
        at = pl.ds(pl.multiple_of(t * 128, 128), 128)
        rows = []
        for n, width in enumerate((1024.0, 512.0)):
            total = stats[0, n, pl.ds(t, 1), :]
            for s in range(1, 8):
                total = total + stats[s, n, pl.ds(t, 1), :]
            rows.append(lax.rsqrt(total / width + EPS))
        inv = jnp.concatenate(rows + [jnp.zeros((6, 128), f32)], 0)
        inv_ref[t] = inv
        value = raw[t]
        cos_part, sin_part = table[0, :, at], table[1, :, at]
        queries = turn(value[0:128] * inv[0:1] * gain_q, cos_part, sin_part).astype(bf)
        keys = turn(value[128:192] * inv[1:2] * gain_k, cos_part, sin_part).astype(bf)
        q_t[:, at] = queries
        kv_own[0:64, at] = keys
        kv_own[64:128, at] = value[192:256].astype(bf)
        k_own[at, :] = jnp.transpose(keys)
        return carry

    lax.fori_loop(0, 8, finish, 0)
    kv_push = copy_to(kv_own, kv_sib, kv_sem.at[0], kv_sem.at[1], sibling)
    kv_push.start()

    key_row = lax.broadcasted_iota(jnp.int32, (256, 512), 0).astype(f32)
    query_lane = (lax.broadcasted_iota(jnp.int32, (256, 512), 1) % 256).astype(f32)
    base = (ctx * 1024).astype(f32)

    def attend(i, carry):
        at = pl.ds(pl.multiple_of(i * 256, 256), 256)
        q = jnp.concatenate([q_t[0:64, at], q_t[64:128, at]], 1) * 0.125
        begin = jnp.concatenate([starts[0:1, at]] * 2, 1)

        def block(keys, values, first_key, state, causal):
            top, total, acc = state
            s = jnp.dot(keys, q, preferred_element_type=f32)
            ok = key_row >= begin - first_key
            if causal:
                ok = ok & (key_row <= query_lane)
            s = jnp.where(ok, s, MASKED)
            new_top = jnp.maximum(top, jnp.max(s, 0, keepdims=True))
            e = jnp.exp(s - new_top)
            shrink = jnp.exp(top - new_top)
            total = total * shrink + jnp.sum(e, 0, keepdims=True)
            acc = acc * shrink + jnp.dot(values, e.astype(bf), preferred_element_type=f32)
            return new_top, total, acc

        state = (jnp.full((1, 512), MASKED, f32), jnp.zeros((1, 512), f32), jnp.zeros((64, 512), f32))
        state = block(
            k_own[at, :], kv_own[64:128, at], base + (i * 256).astype(f32), state, True
        )

        def own(j, state):
            ks = pl.ds(pl.multiple_of(j * 256, 256), 256)
            return block(k_own[ks, :], kv_own[64:128, ks], base + (j * 256).astype(f32), state, False)

        state = lax.fori_loop(0, i, own, state)

        def other(j, state):
            ks = pl.ds(pl.multiple_of(j * 256, 256), 256)
            return block(k_sib[ks, :], kv_sib[64:128, ks], (j * 256).astype(f32), state, False)

        top, total, acc = lax.fori_loop(0, 4 * ctx, other, state)
        out = (acc / total).astype(bf)
        lse = top + jnp.log(total)
        for h in range(2):
            for n in range(2):
                heads[2 * i + n, 64 * h : 64 * h + 64, :] = out[
                    :, 256 * h + 128 * n : 256 * h + 128 * n + 128
                ]
            lse_ref[h, 0:1, at] = lse[:, 256 * h : 256 * h + 256]
        return carry

    kv_push.wait()

    def straighten(t, carry):
        at = pl.ds(pl.multiple_of(t * 128, 128), 128)
        k_sib[at, :] = jnp.transpose(kv_sib[0:64, at])
        return carry

    dy_hop(3).wait_recv()
    dy_hop(4).wait_recv()
    dy_hop(7).start()
    dy_relay(6).start()
    lax.fori_loop(0, 8, straighten, 0)
    lax.fori_loop(0, 4, attend, 0)

    def o_push(i):
        return copy_to(
            heads.at[(me + i) % 8], heads_all.at[me], o_send.at[i], o_recv.at[me], side(i)
        )

    def o_arrival(t):
        return copy_to(heads_all.at[t], heads_all.at[t], o_send.at[0], o_recv.at[t], sibling)

    for i in range(1, 8):
        o_push(i).start()
    heads_all[me] = heads[me]
    stores = [
        pltpu.make_async_copy(q_t, q_ref, store_sem.at[2]),
        pltpu.make_async_copy(kv_own, kv_ref.at[0], store_sem.at[3]),
        pltpu.make_async_copy(kv_sib, kv_ref.at[1], store_sem.at[4]),
        pltpu.make_async_copy(heads, heads_ref, store_sem.at[5]),
    ]
    for store in stores:
        store.start()

    def pass_on(i, carry):
        t = (me + i) % 8
        w_arrival(t, ctx).wait_recv()
        w_relay(t).start()
        return carry

    lax.fori_loop(1, 8, pass_on, 0)

    for n, ci in ((5, 5), (6, 4), (7, 7)):
        dy_hop(n).wait_recv()
        dy_relay(ci).start()
    for i in range(1, 8):
        t = (me + i) % 8
        w_arrival(t, 1 - ctx).wait_recv()
        o_arrival(t).wait_recv()
    store_w = pltpu.make_async_copy(w_all, w_out_all_ref, store_sem.at[6])
    store_w.start()
    store_heads = pltpu.make_async_copy(heads_all, heads_all_ref, store_sem.at[9])
    store_heads.start()
    attended = dot_tn(heads_all[...].reshape(1024, 128), w_all[...].reshape(1024, 1024))
    resid = x + attended
    resid_ref[...] = resid
    inv_two = lax.rsqrt(jnp.mean(resid * resid, -1, keepdims=True) + EPS)
    rows2 = (resid * inv_two * norm2_ref[...]).astype(bf)
    rows2_ref[...] = rows2
    logits = dot_nt(router_ref[...], rows2)
    expert_row = lax.broadcasted_iota(jnp.int32, (32, 128), 0)
    routes = routes_ref[...]
    named = routes[0:1] == expert_row
    for k in range(1, 8):
        named = named | (routes[k : k + 1] == expert_row)
    chosen = jnp.where(named, logits, MASKED)
    weight = jnp.where(named, jnp.exp(chosen - jnp.max(chosen, 0, keepdims=True)), 0.0)
    gates_ref[...] = weight / jnp.sum(weight, 0, keepdims=True)

    for ci in range(8):
        dy_relay(ci).wait_recv()
    store_dy = pltpu.make_async_copy(dy_all, dy_all_ref, store_sem.at[7])
    store_dy.start()
    for i in range(1, 8):
        s_push(i).wait_send()
        w_push(i).wait_send()
        w_relay((me + i) % 8).wait_send()
        o_push(i).wait_send()
    for n in range(8):
        h_hop(n).wait_send()
        dy_hop(n).wait_send()
        dy_relay(n).wait_send()
    for store in [store_rows, store_raw, store_wt, store_w, store_dy, store_heads] + stores:
        store.wait()


def attention(x, dy, segment, norm1, q_gain, k_gain, norm2, router, routes, w_q, w_k, w_v, w_out):
    bf, f32 = jnp.bfloat16, jnp.float32
    vmem, hbm = pl.BlockSpec(memory_space=pltpu.VMEM), pl.BlockSpec(memory_space=pl.ANY)
    sem = pltpu.SemaphoreType.DMA
    shape = jax.ShapeDtypeStruct
    table = jnp.asarray(rope_constants(2048, 32))
    return pl.pallas_call(
        attention_kernel,
        out_shape=(
            shape((128, 1024), bf),
            shape((32, 128), f32),
            shape((128, 1024), f32),
            shape((8, 128, 1024), bf),
            shape((8, 256, 128), f32),
            shape((8, 8, 128), f32),
            shape((128, 1024), bf),
            shape((2, 128, 1024), bf),
            shape((2, 8, 1024), f32),
            shape((8, 128, 128), bf),
            shape((8, 128, 1024), bf),
            shape((16, 128, 1024), bf),
            shape((256, 1024), bf),
            shape((8, 128, 128), bf),
        ),
        in_specs=[vmem] * 9 + [hbm] * 5,
        out_specs=(vmem, vmem, vmem, hbm, hbm, vmem, hbm, hbm, vmem, hbm, hbm, hbm, hbm, hbm),
        scratch_shapes=[
            pltpu.VMEM((8, 128, 1024), bf),
            pltpu.VMEM((16, 128, 1024), bf),
            pltpu.VMEM((8, 128, 1024), bf),
            pltpu.VMEM((1024, 128), bf),
            pltpu.VMEM((256, 1024), bf),
            pltpu.VMEM((8, 256, 128), f32),
            pltpu.VMEM((2, 32, 1024), f32),
            pltpu.VMEM((2, 8, 128), f32),
            pltpu.VMEM((8, 2, 8, 128), f32),
            pltpu.VMEM((128, 1024), bf),
            pltpu.VMEM((128, 1024), bf),
            pltpu.VMEM((128, 1024), bf),
            pltpu.VMEM((1024, 64), bf),
            pltpu.VMEM((1024, 64), bf),
            pltpu.VMEM((8, 1024), f32),
            pltpu.VMEM((8, 128, 128), bf),
            pltpu.VMEM((8, 128, 128), bf),
            sem((5,)),
            sem((8,)),
            sem((8,)),
            sem((16,)),
            sem((16,)),
            sem((16,)),
            sem((8, 2)),
            sem((8,)),
            sem((8,)),
            sem((2,)),
            sem((8,)),
            sem((8,)),
            sem((10,)),
        ],
        compiler_params=pltpu.CompilerParams(
            collective_id=2, has_side_effects=True, vmem_limit_bytes=56 << 20
        ),
        cost_estimate=pl.CostEstimate(
            flops=5_000_000_000, bytes_accessed=20_000_000, transcendentals=4_000_000
        ),
    )(
        x,
        dy,
        segment.reshape(16, 128),
        norm1.reshape(1, 1024),
        q_gain.reshape(1, 128),
        k_gain.reshape(1, 64),
        norm2.reshape(1, 1024),
        router.T,
        routes.T,
        w_q,
        w_k.T,
        w_v.T,
        w_out,
        table,
    )


def backward_kernel(
    x_ref,
    dy_ref,
    d_rows_ref,
    d_gate_ref,
    gates_ref,
    rows2_ref,
    resid_ref,
    router_ref,
    norm1_ref,
    norm2_ref,
    q_gain_ref,
    k_gain_ref,
    segment_ref,
    inv_ref,
    lse_ref,
    rows1_ref,
    raw_ref,
    q_ref,
    kv_ref,
    heads_ref,
    heads_all_ref,
    w_out_ref,
    w_all_ref,
    grads_ref,
    out_part_ref,
    table_ref,
    grad_x_ref,
    norm1_out_ref,
    pack_ref,
    output_ref,
    reduced_ref,
    rows1,
    raw,
    q_t,
    kv_own,
    kv_sib,
    heads,
    w_out,
    w_all,
    table,
    starts,
    d_resid,
    heads_all,
    wo_part,
    wo_in,
    dh_send,
    dh_all,
    tiny,
    q_cat,
    q_nat,
    d_cat,
    d_nat,
    lanes,
    k_nat,
    v_nat,
    dq_acc,
    dk_acc,
    dv_acc,
    dkv_out,
    dkv_in,
    terms,
    stat,
    stats,
    dqkv,
    dqkv_all,
    pack,
    pack_sib,
    pack_in,
    result,
    n1,
    n1_chips,
    n1_sib,
    load_sem,
    a_send,
    a_recv,
    dh_send_sem,
    dh_recv,
    t_send,
    t_recv,
    s_send,
    s_recv,
    dkv_sem,
    o_send,
    o_recv,
    p_sem,
    rs_send,
    rs_recv,
    g_send,
    g_recv,
    gs_send,
    gs_recv,
    n_send,
    n_recv,
    m_send,
    m_recv,
    ns_sem,
    grads,
    reduced,
    ra2,
    ra4,
    rb1,
    rb2,
    rb3,
    r_send,
    r_recv,
    out_own,
    out_sib,
    out_a,
    out_b,
    out_c,
    os_sem,
    out_send,
    out_recv,
    keep_sem,
):
    f32, bf = jnp.float32, jnp.bfloat16
    dp, ctx, me = lax.axis_index("dp"), lax.axis_index("ctx"), lax.axis_index("tensor")
    sibling = (dp, 1 - ctx, me)

    def side(i):
        return (dp, ctx, (me + i) % 8)

    def chip(i):
        return ((dp + i) % 8, ctx, me)

    z, y = me // 2, me % 2
    other = 1 - y
    up, down, pair = (
        (dp, ctx, ((z + 1) % 4) * 2 + y),
        (dp, ctx, ((z + 3) % 4) * 2 + y),
        (dp, ctx, z * 2 + other),
    )

    def a_rows(k, c, s=0):
        start = 304 * (((z + k) % 4) * 2 + c) + 160 * s
        return pl.ds(pl.multiple_of(start, 16), (160, 144)[s])

    def of_part(s):
        return pl.ds(160 * s, (160, 144)[s])

    def b_rows(k, c):
        return second_half(z, y, k, c)

    def hop(n, s=0):
        if n < 2:
            src, dst = grads.at[a_rows((1, 3)[n], n, s)], ra2.at[n, of_part(s)]
            to = (up, down)[n]
        elif n == 2:
            src, dst, to = grads.at[b_rows(0, other)], rb1, pair
        elif n < 5:
            part = n - 3
            src, to = grads.at[piece(z, y, 2, y, part)], (up, down)[part]
            dst = (rb2.at[pl.ds(0, 48)], rb2.at[pl.ds(48, 32)])[part]
        elif n == 5:
            src, dst, to = grads.at[a_rows(0, other, s)], ra4.at[of_part(s)], pair
        elif n == 6:
            src, dst, to = grads.at[b_rows(1, y)], rb3.at[0], up
        elif n == 7:
            src, dst, to = grads.at[b_rows(3, y)], rb3.at[1], down
        else:
            place, to = (
                (a_rows(0, y, s), pair),
                (a_rows(0, y, s), up),
                (a_rows(0, y, s), down),
                (a_rows(0, other, s), up),
                (a_rows(0, other, s), down),
                (a_rows(3, 0, s), up),
                (a_rows(1, 1, s), down),
                (b_rows(0, y), up),
                (b_rows(0, y), down),
                (piece(z, y, 3, y, 0), up),
                (piece(z, y, 1, y, 1), down),
                (b_rows(0, y), pair),
                (b_rows(3, y), pair),
                (b_rows(1, y), pair),
                (b_rows(2, y), pair),
            )[n - 8]
            src = dst = reduced.at[place]
        return copy_to(src, dst, r_send.at[n + 23 * s], r_recv.at[n + 23 * s], to)

    def go(*hops, s=0):
        for n in hops:
            hop(n, s).start()

    def got(*hops, s=0):
        for n in hops:
            hop(n, s).wait_recv()

    def reduce_0():
        go(0, 1, 3, 4, 2)

    def reduce_1(s):
        got(0, 1, s=s)
        for c in range(2):
            add_rows(grads, a_rows(0, c, s), ra2[c, of_part(s)])
        go(5, s=s)

    def reduce_2():
        got(3, 4)
        add_rows(grads, piece(z, y, 1, y, 0), rb2[0:48])
        add_rows(grads, piece(z, y, 3, y, 1), rb2[48:80])
        go(6, 7)

    def reduce_3(s):
        got(5, s=s)
        add_rows(grads, a_rows(0, y, s), ra4[of_part(s)])
        reduced[a_rows(0, y, s), :] = grads[a_rows(0, y, s), :]
        go(8, 9, 10, s=s)

    def reduce_4():
        got(6, 7, 2)
        add_rows(grads, b_rows(0, y), rb1[...], rb3[0], rb3[1])
        reduced[b_rows(0, y), :] = grads[b_rows(0, y), :]
        go(15, 16, 19)

    def reduce_5(s):
        got(8, s=s)
        go(11, 12, s=s)

    def reduce_6():
        got(15)
        go(17, 20)
        got(16)
        go(18, 21)

    def reduce_7(s):
        @pl.when(y == 0)
        def _():
            got(9, 12, s=s)

        @pl.when(y == 1)
        def _():
            got(11, 10, s=s)

        go(13, 14, s=s)

    def reduce_8():
        got(17, 18)
        go(22)

    def keep(n, place):
        return pltpu.make_async_copy(reduced.at[place], reduced_ref.at[place], keep_sem.at[n])

    keep_places = (
        [a_rows(0, c, s) for c in range(2) for s in range(2)]
        + [a_rows(k, c, s) for k in (1, 3) for c in range(2) for s in range(2)]
        + [a_rows(2, c, s) for c in range(2) for s in range(2)]
        + [pl.ds(2432, 640)]
    )

    def reduce_9():
        for n in range(4):
            keep(n, keep_places[n]).start()
        for s in range(2):

            @pl.when(y == 0)
            def _():
                got(10, 11, s=s)

            @pl.when(y == 1)
            def _():
                got(9, 12, s=s)

        for n in range(4, 12):
            keep(n, keep_places[n]).start()
        got(19, 20, 21, 22)
        keep(16, keep_places[16]).start()
        for s in range(2):
            got(13, 14, s=s)
        for n in range(12, 16):
            keep(n, keep_places[n]).start()
        for n in range(23):
            hop(n).wait_send()
        for n in (0, 1, 5, 8, 9, 10, 11, 12, 13, 14):
            hop(n, 1).wait_send()

    def x_side(i):
        return ((dp // 4) * 4 + (dp + i) % 4, ctx, me)

    right, left, partner = x_side(1), x_side(3), ((dp + 4) % 8, ctx, me)
    theirs_out = out_part_ref.at[pl.ds(pl.multiple_of((1 - ctx) * 8, 8), 8)]
    os_push = copy_to(
        theirs_out, out_sib.at[:, :, pl.ds(0, 1024)], os_sem.at[0], os_sem.at[1], sibling
    )
    wo_push = copy_to(
        wo_part.at[1 - ctx],
        out_sib.at[:, :, pl.ds(1024, 512)],
        os_sem.at[2],
        os_sem.at[3],
        sibling,
    )

    def out_at(i, b):
        return (dp // 4 + b) % 2 * 4 + (dp + i) % 4

    def out_hop(n):
        b = n % 2
        if n < 2:
            src, dst, to = out_own.at[out_at(2, b), pl.ds(0, 64)], out_a.at[0, b], right
        elif n < 4:
            src, dst, to = out_own.at[out_at(2, b), pl.ds(64, 64)], out_a.at[1, b], left
        elif n < 6:
            src, dst, to = out_own.at[out_at(1, b)], out_b.at[0, b], right
        elif n < 8:
            src, dst, to = out_own.at[out_at(3, b)], out_b.at[1, b], left
        else:
            src, dst, to = out_own.at[out_at(0, 1)], out_c, partner
        return copy_to(src, dst, out_send.at[n], out_recv.at[n], to)

    def out_0():
        os_push.wait()
        wo_push.wait()

        def add_sib(d, carry):
            left_part = out_own[d, :, 0:1024].astype(f32)
            right_part = wo_part[ctx, d].astype(f32)
            total = jnp.concatenate([left_part, right_part], 1) + out_sib[d].astype(f32)
            out_own[d] = total.astype(bf)
            return carry

        lax.fori_loop(0, 8, add_sib, 0)
        for n in range(4):
            out_hop(n).start()

    def out_add(at, rows, *parts):
        total = out_own[at, rows].astype(f32)
        for part in parts:
            total = total + part.astype(f32)
        out_own[at, rows] = total.astype(bf)

    def out_1():
        for b in range(2):
            out_hop(b).wait_recv()
            out_add(out_at(1, b), pl.ds(0, 64), out_a[0, b])
            out_hop(4 + b).start()
            out_hop(2 + b).wait_recv()
            out_add(out_at(3, b), pl.ds(64, 64), out_a[1, b])
            out_hop(6 + b).start()

    def out_2():
        for b in (1, 0):
            out_hop(4 + b).wait_recv()
            out_hop(6 + b).wait_recv()
            out_add(out_at(0, b), slice(None), out_b[0, b], out_b[1, b])
            if b == 1:
                out_hop(8).start()

    def out_3():
        out_hop(8).wait_recv()
        total = out_own[dp].astype(f32) + out_c[...].astype(f32)
        output_ref[...] = (resid_ref[...] + total[:, 0:1024]).astype(bf)
        wo_sum = total[:, 1024:1536].astype(bf)
        for t in range(8):
            wo_part[0, 0, 16 * t : 16 * t + 16, :] = wo_sum[16 * t : 16 * t + 16]
        for i in range(1, 8):
            wo_hop(i).start()
        wo_in[me] = wo_part[0, 0, pl.ds(pl.multiple_of(me * 16, 16), 16), :]
        for n in range(9):
            out_hop(n).wait_send()

    def wo_hop(i):
        rows = pl.ds(pl.multiple_of((me + i) % 8 * 16, 16), 16)
        return copy_to(wo_part.at[0, 0, rows], wo_in.at[me], a_send.at[i], a_recv.at[me], side(i))

    def wo_arrival(t):
        return copy_to(wo_in.at[t], wo_in.at[t], a_send.at[0], a_recv.at[t], sibling)

    early = pltpu.make_async_copy(grads_ref, grads, load_sem.at[9])
    early.start()
    sources = (rows1_ref, raw_ref, q_ref, kv_ref.at[0], kv_ref.at[1], heads_ref, w_out_ref)
    targets = (rows1, raw, q_t, kv_own, kv_sib, heads, w_out)
    loads = [
        pltpu.make_async_copy(s, t, load_sem.at[n])
        for n, (s, t) in enumerate(zip(sources, targets, strict=True))
    ]
    loads.append(pltpu.make_async_copy(w_all_ref, w_all, load_sem.at[7]))
    loads.append(pltpu.make_async_copy(table_ref.at[ctx], table, load_sem.at[8]))
    loads.append(early)
    loads.append(pltpu.make_async_copy(heads_all_ref, heads_all, load_sem.at[11]))
    own_blocks = out_part_ref.at[pl.ds(pl.multiple_of(ctx * 8, 8), 8)]
    loads.append(pltpu.make_async_copy(own_blocks, out_own.at[:, :, pl.ds(0, 1024)], load_sem.at[10]))
    for n, load in enumerate(loads):
        if n != 9:
            load.start()
    barrier = pltpu.get_barrier_semaphore()
    for i in range(1, 8):
        pl.semaphore_signal(barrier, inc=1, device_id=side(i), device_id_type=MESH)
        pl.semaphore_signal(barrier, inc=1, device_id=chip(i), device_id_type=MESH)
    pl.semaphore_signal(barrier, inc=1, device_id=sibling, device_id_type=MESH)

    pl.semaphore_wait(barrier, 15)
    early.wait()
    reduce_0()
    gates, d_gate = gates_ref[...], d_gate_ref[...]
    d_logits = gates * (d_gate - jnp.sum(gates * d_gate, 0, keepdims=True))
    d_normed = d_rows_ref[...] + lax.dot_general(
        jnp.transpose(d_logits),
        router_ref[...].astype(f32),
        (((1,), (0,)), ((), ())),
        preferred_element_type=f32,
        precision=lax.Precision.HIGHEST,
    )
    resid = resid_ref[...]
    inv_two = lax.rsqrt(jnp.mean(resid * resid, -1, keepdims=True) + EPS)
    res_hat = resid * inv_two
    scaled = d_normed * norm2_ref[...]
    d_res = dy_ref[...].astype(f32) + inv_two * (
        scaled - res_hat * jnp.mean(scaled * res_hat, -1, keepdims=True)
    )
    d_resid[...] = d_res
    datt = d_res.astype(bf)
    for n in (6,):
        loads[n].wait()
    d_heads = dot_nt(w_out[...].reshape(1024, 1024), datt).astype(bf)
    dh_send[...] = d_heads.reshape(8, 128, 128)
    dh_all[me] = dh_send[me]

    def dh_push(i):
        return copy_to(
            dh_send.at[(me + i) % 8], dh_all.at[me], dh_send_sem.at[i], dh_recv.at[me], side(i)
        )

    def dh_arrival(t):
        return copy_to(dh_all.at[t], dh_all.at[t], dh_send_sem.at[0], dh_recv.at[t], sibling)

    for i in range(1, 8):
        dh_push(i).start()

    norm2_part = jnp.sum(d_normed * res_hat, 0, keepdims=True)
    router_part = jnp.dot(
        d_logits,
        rows2_ref[...].astype(f32),
        preferred_element_type=f32,
        precision=lax.Precision.HIGHEST,
    )
    def pack_rows(place, value):
        for c in range(2):
            pack[c, place, :] = value[:, 512 * c : 512 * c + 512].astype(bf)

    pack_rows(pl.ds(256, 32), router_part)
    pack_rows(pl.ds(288, 16), jnp.concatenate([norm2_part, jnp.zeros((15, 1024), f32)], 0))
    pack_rows(pl.ds(320, 64), jnp.zeros((64, 1024), f32))

    os_push.start()
    loads[10].wait()

    def wo_rows(t, carry):
        value = jnp.dot(heads_all[t], datt, preferred_element_type=f32).astype(bf)
        rows = pl.ds(pl.multiple_of(t * 16, 16), 16)
        for d in range(8):
            for c in range(2):
                wo_part[c, d, rows, :] = value[16 * d : 16 * d + 16, 512 * c : 512 * c + 512]
        return carry

    lax.fori_loop(0, 8, wo_rows, 0)
    wo_push.start()
    go(0, 1, s=1)
    for n in (0, 1, 2, 3, 4, 5, 7, 8, 11):
        loads[n].wait()
    seg = segment_ref[...]
    start = jnp.zeros((16, 128), f32)
    for s in range(1, 8):
        below = jnp.where(seg < s, 1.0, 0.0)
        count = jnp.sum(jnp.sum(below, 1, keepdims=True), 0, keepdims=True)
        start = jnp.where(seg == s, count, start)
    start = jnp.where(ctx == 0, start[:8], start[8:])
    for t in range(8):
        starts[0:1, 128 * t : 128 * t + 128] = start[t : t + 1]

    def lay_out(t, carry):
        at = pl.ds(pl.multiple_of(t * 128, 128), 128)
        i, half = t // 2, t % 2
        q = q_t[:, at] * 0.125
        for h in range(2):
            spot = pl.ds(pl.multiple_of(h * 256 + half * 128, 128), 128)
            q_h = q[64 * h : 64 * h + 64]
            q_cat[i, :, spot] = q_h
            q_nat[i, spot, :] = jnp.transpose(q_h)
            lanes[i, 0:1, spot] = lse_ref[h, 0:1, at]
            lanes[i, 2:3, spot] = starts[0:1, at]
        for n, kv in enumerate((kv_own, kv_sib)):
            k_nat[n, at, :] = jnp.transpose(kv[0:64, at])
            v_nat[n, at, :] = jnp.transpose(kv[64:128, at])
        return carry

    lax.fori_loop(0, 8, lay_out, 0)
    dk_acc[...] = jnp.zeros_like(dk_acc)
    dv_acc[...] = jnp.zeros_like(dv_acc)
    dq_acc[...] = jnp.zeros_like(dq_acc)
    for i in range(1, 8):
        dh_arrival((me + i) % 8).wait_recv()

    def lay_dh(t, carry):
        i, half = t // 2, t % 2
        d, o = dh_all[t], heads[t]
        product = d.astype(f32) * o.astype(f32)
        for h in range(2):
            spot = pl.ds(pl.multiple_of(h * 256 + half * 128, 128), 128)
            d_h = d[64 * h : 64 * h + 64]
            d_cat[i, :, spot] = d_h
            d_nat[i, spot, :] = jnp.transpose(d_h)
            lanes[i, 1:2, spot] = jnp.sum(product[64 * h : 64 * h + 64], 0, keepdims=True)
        return carry

    lax.fori_loop(0, 8, lay_dh, 0)
    reduce_1(0)
    key_row = lax.broadcasted_iota(jnp.int32, (256, 512), 0).astype(f32)
    query_lane = (lax.broadcasted_iota(jnp.int32, (256, 512), 1) % 256).astype(f32)
    base = (ctx * 1024).astype(f32)

    def block(n, i, j, first_key, causal):
        ks = pl.ds(pl.multiple_of(j * 256, 256), 256)
        kv = (kv_own, kv_sib)[n]
        s = jnp.dot(k_nat[n, ks, :], q_cat[i], preferred_element_type=f32)
        ok = key_row >= lanes[i, 2:3, :] - first_key
        if causal:
            ok = ok & (key_row <= query_lane)
        p = jnp.exp(jnp.where(ok, s, MASKED) - lanes[i, 0:1, :])
        dp_ = jnp.dot(v_nat[n, ks, :], d_cat[i], preferred_element_type=f32)
        ds = (p * (dp_ - lanes[i, 1:2, :])).astype(bf)
        dv_acc[n, ks, :] += jnp.dot(p.astype(bf), d_nat[i], preferred_element_type=f32)
        dk_acc[n, ks, :] += jnp.dot(ds, q_nat[i], preferred_element_type=f32)
        dq_acc[i] += jnp.dot(kv[0:64, ks], ds, preferred_element_type=f32)

    def hook_0():
        reduce_2()
        reduce_1(1)

    def hook_1():
        out_0()
        reduce_3(0)

    def hook_2():
        reduce_4()

    def hook_3():
        reduce_3(1)
        out_1()

    for i in range(4):

        def cross(j, carry, i=i):
            block(1, i, j, (j * 256).astype(f32), False)
            return carry

        lax.fori_loop(0, 4 * ctx, cross, 0)
        (hook_0, hook_1, hook_2, hook_3)[i]()
    dkv_push = copy_to(dkv_out, dkv_in, dkv_sem.at[0], dkv_sem.at[1], sibling)

    def upright(t, carry):
        at = pl.ds(pl.multiple_of(t * 128, 128), 128)
        dkv_out[0:64, at] = jnp.transpose(dk_acc[1, at, :]).astype(bf)
        dkv_out[64:128, at] = jnp.transpose(dv_acc[1, at, :]).astype(bf)
        return carry

    lax.fori_loop(0, 8, upright, 0)
    dkv_push.start()

    def within(i):
        def full(j, c):
            block(0, i, j, base + (j * 256).astype(f32), False)
            return c

        lax.fori_loop(0, i, full, 0)
        block(0, i, i, base + 256.0 * i, True)

    within(0)
    within(1)
    within(2)
    within(3)
    reduce_5(0)
    reduce_6()
    gain_q = column(q_gain_ref[...])
    gain_k = column(jnp.concatenate([k_gain_ref[...], jnp.zeros((1, 64), f32)], 1))[:64]
    dkv_push.wait()

    def unturn(t, sums):
        at = pl.ds(pl.multiple_of(t * 128, 128), 128)
        i, half = t // 2, t % 2
        parts = [
            dq_acc[i, :, pl.ds(pl.multiple_of(h * 256 + half * 128, 128), 128)] for h in range(2)
        ]
        cos_part, sin_part = table[0, :, at], -table[1, :, at]
        inv = inv_ref[t]
        d_q = turn(jnp.concatenate(parts, 0) * 0.125, cos_part, sin_part)
        came = dkv_in[:, at].astype(f32)
        d_k = turn(jnp.transpose(dk_acc[0, at, :]) + came[0:64], cos_part, sin_part)
        d_v = jnp.transpose(dv_acc[0, at, :]) + came[64:128]
        q_hat, k_hat = raw[t, 0:128] * inv[0:1], raw[t, 128:192] * inv[1:2]
        q_sum, k_sum = sums[0] + d_q * q_hat, sums[1] + d_k * k_hat
        q_term, k_term = d_q * gain_q, d_k * gain_k
        terms[t, 0:128] = q_term
        terms[t, 128:192] = k_term
        dqkv[t, 192:256] = d_v.astype(bf)
        stat[0, pl.ds(t, 1), :] = jnp.sum(q_term * q_hat, 0, keepdims=True)
        stat[1, pl.ds(t, 1), :] = jnp.sum(k_term * k_hat, 0, keepdims=True)
        return q_sum, k_sum

    q_sum, k_sum = lax.fori_loop(
        0, 8, unturn, (jnp.zeros((128, 128), f32), jnp.zeros((64, 128), f32))
    )
    stats[me] = stat[...]

    def s_push(i):
        return copy_to(stats.at[me], stats.at[me], s_send.at[i], s_recv.at[me], side(i))

    def s_arrival(t):
        return copy_to(stats.at[t], stats.at[t], s_send.at[0], s_recv.at[t], sibling)

    for i in range(1, 8):
        s_push(i).start()
    out_2()
    q_row = jnp.sum(jnp.transpose(q_sum), 0, keepdims=True)
    k_row = jnp.sum(jnp.transpose(k_sum), 0, keepdims=True)
    gain_row = jnp.concatenate([q_row, k_row, jnp.zeros((1, 1024 - 192), f32)], 1)
    pack_rows(pl.ds(304, 16), jnp.concatenate([gain_row, jnp.zeros((15, 1024), f32)], 0))
    reduce_5(1)
    for i in range(1, 8):
        s_arrival((me + i) % 8).wait_recv()

    def finish(t, carry):
        at = pl.ds(pl.multiple_of(t * 128, 128), 128)
        inner = []
        for n in range(2):
            part = stats[0, n, pl.ds(t, 1), :]
            for s in range(1, 8):
                part = part + stats[s, n, pl.ds(t, 1), :]
            inner.append(part)
        inv = inv_ref[t]
        q_hat, k_hat = raw[t, 0:128] * inv[0:1], raw[t, 128:192] * inv[1:2]
        d_q = inv[0:1] * (terms[t, 0:128] - q_hat * (inner[0] / 1024.0))
        d_k = inv[1:2] * (terms[t, 128:192] - k_hat * (inner[1] / 512.0))
        dqkv[t, 0:128] = d_q.astype(bf)
        dqkv[t, 128:192] = d_k.astype(bf)
        return carry

    lax.fori_loop(0, 8, finish, 0)

    def o_push(i):
        return copy_to(
            dqkv.at[(me + i) % 8], dqkv_all.at[me], o_send.at[i], o_recv.at[me], side(i)
        )

    def o_arrival(t):
        return copy_to(dqkv_all.at[t], dqkv_all.at[t], o_send.at[0], o_recv.at[t], sibling)

    for i in range(1, 8):
        o_push(i).start()
    dqkv_all[me] = dqkv[me]
    grad_qkv = jnp.zeros((256, 1024), f32)
    for t in range(8):
        grad_qkv = grad_qkv + jnp.dot(dqkv[t], rows1[t], preferred_element_type=f32)
    pack_rows(pl.ds(0, 256), grad_qkv)
    p_push = copy_to(pack.at[1 - ctx], pack_sib, p_sem.at[0], p_sem.at[1], sibling)
    p_push.start()
    reduce_7(0)
    for i in range(1, 8):
        o_arrival((me + i) % 8).wait_recv()
    d_rows1 = dot_tn(dqkv_all[...].reshape(2048, 128), w_all[...].reshape(2048, 1024))
    x = x_ref[...].astype(f32)
    inv_one = lax.rsqrt(jnp.mean(x * x, -1, keepdims=True) + EPS)
    x_hat = x * inv_one
    norm1_part = jnp.sum(d_rows1 * x_hat, 0, keepdims=True)
    n1[me] = jnp.concatenate([norm1_part[:, 128 * t : 128 * t + 128] for t in range(8)], 0)

    def n_push(i):
        return copy_to(n1.at[me], n1.at[me], n_send.at[i], n_recv.at[me], side(i))

    def n_arrival(t):
        return copy_to(n1.at[t], n1.at[t], n_send.at[0], n_recv.at[t], sibling)

    for i in range(1, 8):
        n_push(i).start()
    p_push.wait()
    pack[ctx] = (pack[ctx].astype(f32) + pack_sib[...].astype(f32)).astype(bf)
    out_3()

    def rs_push(i):
        to = (dp + i) % 8
        rows = pack.at[ctx, pl.ds(pl.multiple_of(to * 48, 16), 48)]
        return copy_to(rows, pack_in.at[dp], rs_send.at[i], rs_recv.at[dp], chip(i))

    def rs_arrival(d):
        return copy_to(pack_in.at[d], pack_in.at[d], rs_send.at[0], rs_recv.at[d], sibling)

    for i in range(1, 8):
        rs_push(i).start()
    scaled = d_rows1 * norm1_ref[...]
    grad_x_ref[...] = (
        d_resid[...] + inv_one * (scaled - x_hat * jnp.mean(scaled * x_hat, -1, keepdims=True))
    ).astype(bf)
    reduce_8()
    reduce_7(1)
    for i in range(1, 8):
        n_arrival((me + i) % 8).wait_recv()
    norm1_sum = n1[0]
    for t in range(1, 8):
        norm1_sum = norm1_sum + n1[t]
    n1_chips[dp] = norm1_sum

    def m_push(i):
        return copy_to(n1_chips.at[dp], n1_chips.at[dp], m_send.at[i], m_recv.at[dp], chip(i))

    def m_arrival(d):
        return copy_to(n1_chips.at[d], n1_chips.at[d], m_send.at[0], m_recv.at[d], sibling)

    for i in range(1, 8):
        m_push(i).start()
    pack_in[dp] = pack[ctx, pl.ds(pl.multiple_of(dp * 48, 16), 48), :]
    for i in range(1, 8):
        rs_arrival((dp + i) % 8).wait_recv()
    owned = pack_in[0].astype(f32)
    for d in range(1, 8):
        owned = owned + pack_in[d].astype(f32)
    top = pl.ds(0, 48)
    result[ctx, dp, top] = owned.astype(bf)
    wide = (dp == 5) | (dp == 6)

    def t_push(i):
        return copy_to(result.at[ctx, dp, top], tiny.at[me], t_send.at[i], t_recv.at[me], side(i))

    def t_arrival(t):
        return copy_to(tiny.at[t], tiny.at[t], t_send.at[0], t_recv.at[t], sibling)

    @pl.when(wide)
    def _():
        for i in range(1, 8):
            t_push(i).start()
        tiny[me] = result[ctx, dp, top]
        for i in range(1, 8):
            t_arrival((me + i) % 8).wait_recv()
            t_push(i).wait_send()
        total = tiny[0].astype(f32)
        for t in range(1, 8):
            total = total + tiny[t].astype(f32)
        row = lax.broadcasted_iota(jnp.int32, (48, 512), 0)
        shared = ((dp == 5) & (row >= 16)) | ((dp == 6) & (row < 16))
        result[ctx, dp, top] = jnp.where(shared, total, owned).astype(bf)

    for i in range(1, 8):
        wo_arrival((me + i) % 8).wait_recv()
    total = wo_in[0].astype(f32)
    for t in range(1, 8):
        total = total + wo_in[t].astype(f32)
    result[ctx, dp, pl.ds(48, 16)] = total.astype(bf)


    def g_push(i):
        return copy_to(
            result.at[ctx, dp], result.at[ctx, dp], g_send.at[i], g_recv.at[dp], chip(i)
        )

    def g_arrival(d):
        return copy_to(result.at[ctx, d], result.at[ctx, d], g_send.at[0], g_recv.at[d], sibling)

    def g_relay(d):
        return copy_to(
            result.at[ctx, d], result.at[ctx, d], gs_send.at[d], gs_recv.at[d], sibling
        )

    def g_sib_arrival(d):
        place = result.at[1 - ctx, d]
        return copy_to(place, place, gs_send.at[d], gs_recv.at[d], sibling)

    for i in range(1, 8):
        g_push(i).start()
    g_relay(dp).start()
    for i in range(1, 8):
        m_arrival((dp + i) % 8).wait_recv()
    norm1_sum = n1_chips[0]
    for d in range(1, 8):
        norm1_sum = norm1_sum + n1_chips[d]
    n1_sib[0] = norm1_sum
    ns_push = copy_to(n1_sib.at[0], n1_sib.at[1], ns_sem.at[0], ns_sem.at[1], sibling)
    ns_push.start()

    def pass_on(i, carry):
        d = (dp + i) % 8
        g_arrival(d).wait_recv()
        g_relay(d).start()
        return carry

    lax.fori_loop(1, 8, pass_on, 0)
    ns_push.wait()
    norm1_out_ref[...] = n1_sib[0] + n1_sib[1]
    for d in range(8):
        g_sib_arrival(d).wait_recv()
        g_relay(d).wait_send()
    reduce_9()
    pack_ref[...] = result[...]
    for i in range(1, 8):
        dh_push(i).wait_send()
        s_push(i).wait_send()
        o_push(i).wait_send()
        n_push(i).wait_send()
        rs_push(i).wait_send()
        m_push(i).wait_send()
        g_push(i).wait_send()
    for i in range(1, 8):
        wo_hop(i).wait_send()
    for n, place in enumerate(keep_places):
        keep(n, place).wait()


def backward(small, large):
    bf, f32 = jnp.bfloat16, jnp.float32
    vmem, hbm = pl.BlockSpec(memory_space=pltpu.VMEM), pl.BlockSpec(memory_space=pl.ANY)
    sem = pltpu.SemaphoreType.DMA
    shape = jax.ShapeDtypeStruct
    table = jnp.asarray(rope_constants(2048, 32))
    return pl.pallas_call(
        backward_kernel,
        out_shape=(
            shape((128, 1024), bf),
            shape((8, 128), f32),
            shape((2, 8, 64, 512), bf),
            shape((128, 1024), bf),
            shape((3072, 1024), bf),
        ),
        in_specs=[vmem] * 15 + [hbm] * 11,
        out_specs=(vmem, vmem, vmem, vmem, hbm),
        scratch_shapes=[
            pltpu.VMEM((8, 128, 1024), bf),
            pltpu.VMEM((8, 256, 128), f32),
            pltpu.VMEM((128, 1024), bf),
            pltpu.VMEM((128, 1024), bf),
            pltpu.VMEM((128, 1024), bf),
            pltpu.VMEM((8, 128, 128), bf),
            pltpu.VMEM((8, 128, 1024), bf),
            pltpu.VMEM((8, 256, 1024), bf),
            pltpu.VMEM((2, 32, 1024), f32),
            pltpu.VMEM((8, 1024), f32),
            pltpu.VMEM((128, 1024), f32),
            pltpu.VMEM((8, 128, 128), bf),
            pltpu.VMEM((2, 8, 128, 512), bf),
            pltpu.VMEM((8, 16, 512), bf),
            pltpu.VMEM((8, 128, 128), bf),
            pltpu.VMEM((8, 128, 128), bf),
            pltpu.VMEM((8, 48, 512), bf),
            pltpu.VMEM((4, 64, 512), bf),
            pltpu.VMEM((4, 512, 64), bf),
            pltpu.VMEM((4, 64, 512), bf),
            pltpu.VMEM((4, 512, 64), bf),
            pltpu.VMEM((4, 8, 512), f32),
            pltpu.VMEM((2, 1024, 64), bf),
            pltpu.VMEM((2, 1024, 64), bf),
            pltpu.VMEM((4, 64, 512), f32),
            pltpu.VMEM((2, 1024, 64), f32),
            pltpu.VMEM((2, 1024, 64), f32),
            pltpu.VMEM((128, 1024), bf),
            pltpu.VMEM((128, 1024), bf),
            pltpu.VMEM((8, 192, 128), f32),
            pltpu.VMEM((2, 8, 128), f32),
            pltpu.VMEM((8, 2, 8, 128), f32),
            pltpu.VMEM((8, 256, 128), bf),
            pltpu.VMEM((8, 256, 128), bf),
            pltpu.VMEM((2, 384, 512), bf),
            pltpu.VMEM((384, 512), bf),
            pltpu.VMEM((8, 48, 512), bf),
            pltpu.VMEM((2, 8, 64, 512), bf),
            pltpu.VMEM((8, 8, 128), f32),
            pltpu.VMEM((8, 8, 128), f32),
            pltpu.VMEM((2, 8, 128), f32),
            sem((12,)),
        ]
        + [sem((8,))] * 8
        + [sem((2,))]
        + [sem((8,))] * 2
        + [sem((2,))]
        + [sem((8,))] * 10
        + [sem((2,))]
        + [
            pltpu.VMEM((3072, 1024), bf),
            pltpu.VMEM((3072, 1024), bf),
            pltpu.VMEM((2, 304, 1024), bf),
            pltpu.VMEM((304, 1024), bf),
            pltpu.VMEM((80, 1024), bf),
            pltpu.VMEM((80, 1024), bf),
            pltpu.VMEM((2, 80, 1024), bf),
            sem((46,)),
            sem((46,)),
            pltpu.VMEM((8, 128, 1536), bf),
            pltpu.VMEM((8, 128, 1536), bf),
            pltpu.VMEM((2, 2, 64, 1536), bf),
            pltpu.VMEM((2, 2, 128, 1536), bf),
            pltpu.VMEM((128, 1536), bf),
            sem((4,)),
            sem((9,)),
            sem((9,)),
            sem((17,)),
        ],
        compiler_params=pltpu.CompilerParams(
            collective_id=3, has_side_effects=True, vmem_limit_bytes=56 << 20
        ),
        cost_estimate=pl.CostEstimate(
            flops=10_000_000_000, bytes_accessed=20_000_000, transcendentals=4_000_000
        ),
    )(*small, *large, table)


def finish_kernel(
    reduced_ref,
    out_ref,
    grad_x_ref,
    pack_ref,
    norm1_ref,
    gate_ref,
    up_ref,
    down_ref,
    out_copy_ref,
    grad_x_copy_ref,
    w_q_ref,
    w_k_ref,
    w_v_ref,
    q_gain_ref,
    k_gain_ref,
    w_out_ref,
    norm2_ref,
    router_ref,
    norm1_copy_ref,
    rounded,
    wide,
    load_sem,
    store_sem,
):
    f32 = jnp.float32
    loads = [
        pltpu.make_async_copy(reduced_ref.at[pl.ds(256 * n, 256)], rounded.at[n], load_sem.at[n])
        for n in range(12)
    ]
    passed = [
        pltpu.make_async_copy(out_ref, out_copy_ref, load_sem.at[12]),
        pltpu.make_async_copy(grad_x_ref, grad_x_copy_ref, load_sem.at[13]),
    ]
    for copy in loads + passed:
        copy.start()
    def rows(start, count):
        parts = []
        for c in range(2):
            pieces = []
            for d in range(start // 48, (start + count - 1) // 48 + 1):
                first, last = max(start, 48 * d) - 48 * d, min(start + count, 48 * d + 48) - 48 * d
                pieces.append(pack_ref[c, d, first:last, :])
            parts.append(jnp.concatenate(pieces, 0))
        return jnp.concatenate(parts, 1).astype(f32)

    w_q_ref[...] = jnp.transpose(rows(0, 128))
    w_k_ref[...] = rows(128, 64)
    w_v_ref[...] = rows(192, 64)
    router_ref[...] = rows(256, 32)
    norm2_ref[...] = rows(288, 16)[0:1]
    gains = rows(304, 16)
    q_gain_ref[...] = gains[0:1, 0:128]
    k_gain_ref[...] = gains[0:1, 128:192]
    for d in range(8):
        for c in range(2):
            w_out_ref[16 * d : 16 * d + 16, 512 * c : 512 * c + 512] = pack_ref[c, d, 48:64, :].astype(f32)
    norm1_copy_ref[...] = norm1_ref[...]
    stores = []
    for n in range(12):
        loads[n].wait()
        wide[n] = rounded[n].astype(f32)
        if n < 8:
            rows = pl.ds(256 * (n % 4), 256)
            for m, ref in enumerate((gate_ref, up_ref)):
                src = wide.at[n, :, pl.ds(512 * m, 512)]
                stores.append(pltpu.make_async_copy(src, ref.at[n // 4, rows], store_sem.at[2 * n + m]))
        else:
            rows = pl.ds(256 * (n % 2), 256)
            stores.append(
                pltpu.make_async_copy(wide.at[n], down_ref.at[n // 2 - 4, rows], store_sem.at[n + 8])
            )
        for store in stores[-2:] if n < 8 else stores[-1:]:
            store.start()
    for copy in stores + passed:
        copy.wait()


def finish(reduced, out, grad_x, pack, norm1):
    bf, f32 = jnp.bfloat16, jnp.float32
    vmem, hbm = pl.BlockSpec(memory_space=pltpu.VMEM), pl.BlockSpec(memory_space=pl.ANY)
    shape = jax.ShapeDtypeStruct
    return pl.pallas_call(
        finish_kernel,
        out_shape=(
            shape((2, 1024, 512), f32),
            shape((2, 1024, 512), f32),
            shape((2, 512, 1024), f32),
            shape((128, 1024), bf),
            shape((128, 1024), bf),
            shape((1024, 128), f32),
            shape((64, 1024), f32),
            shape((64, 1024), f32),
            shape((1, 128), f32),
            shape((1, 64), f32),
            shape((128, 1024), f32),
            shape((1, 1024), f32),
            shape((32, 1024), f32),
            shape((8, 128), f32),
        ),
        in_specs=[hbm] + [vmem] * 4,
        out_specs=(hbm,) * 5 + (vmem,) * 9,
        scratch_shapes=[
            pltpu.VMEM((12, 256, 1024), bf),
            pltpu.VMEM((12, 256, 1024), f32),
            pltpu.SemaphoreType.DMA((14,)),
            pltpu.SemaphoreType.DMA((20,)),
        ],
        compiler_params=pltpu.CompilerParams(vmem_limit_bytes=62 << 20),
    )(reduced, out, grad_x, pack, norm1)


def shards(
    hidden_in,
    segment,
    norm1_gain,
    w_query,
    w_key,
    w_value,
    q_gain,
    k_gain,
    w_out,
    norm2_gain,
    router,
    w_gate,
    w_up,
    w_down,
    routes,
    cotangent,
):
    f32, bf = jnp.float32, jnp.bfloat16
    rows2, gates, resid, rows1, raw, inv, q_t, kv, lse, heads, w_out_all, dy_all, w_t, heads_all = attention(
        hidden_in,
        cotangent,
        segment,
        norm1_gain,
        q_gain,
        k_gain,
        norm2_gain,
        router,
        routes,
        w_query,
        w_key,
        w_value,
        w_out,
    )
    d_rows, d_gate, out_part, grads, w_all = moe(
        rows2, gates, dy_all, w_gate, w_up, w_down, w_t
    )
    grad_x, norm1_sum, pack, output, grads = backward(
        (
            hidden_in,
            cotangent,
            d_rows,
            d_gate,
            gates,
            rows2,
            resid,
            router.T,
            norm1_gain.reshape(1, 1024),
            norm2_gain.reshape(1, 1024),
            q_gain.reshape(1, 128),
            k_gain.reshape(1, 64),
            segment.reshape(16, 128),
            inv,
            lse,
        ),
        (rows1, raw, q_t, kv, heads, heads_all, w_out_all, w_all, grads, out_part),
    )
    (
        gate,
        up,
        down,
        output,
        grad_x,
        w_q,
        w_k,
        w_v,
        q_g,
        k_g,
        w_o,
        norm2_sum,
        grad_router,
        norm1_sum,
    ) = finish(grads, output, grad_x, pack, norm1_sum)
    return (
        output,
        grad_x,
        norm1_sum.reshape(1024),
        w_q,
        w_k.T,
        w_v.T,
        q_g.reshape(128),
        k_g.reshape(64),
        w_o,
        norm2_sum.reshape(1024),
        grad_router.T,
        gate,
        up,
        down,
    )


def solution(mesh):
    return jax.shard_map(
        shards,
        mesh=mesh,
        in_specs=(
            P(("dp", "ctx", "tensor"), None),
            P("dp"),
            P(),
            P(None, "tensor"),
            P(None, "tensor"),
            P(None, "tensor"),
            P("tensor"),
            P("tensor"),
            P("tensor", None),
            P(),
            P(),
            P(("dp", "ctx"), None, None),
            P(("dp", "ctx"), None, None),
            P(("dp", "ctx"), None, None),
            P(("dp", "ctx", "tensor"), None),
            P(("dp", "ctx", "tensor"), None),
        ),
        out_specs=(
            P(("dp", "ctx", "tensor"), None),
            P(("dp", "ctx", "tensor"), None),
            P(),
            P(None, "tensor"),
            P(None, "tensor"),
            P(None, "tensor"),
            P("tensor"),
            P("tensor"),
            P("tensor", None),
            P(),
            P(),
            P(("dp", "ctx"), None, None),
            P(("dp", "ctx"), None, None),
            P(("dp", "ctx"), None, None),
        ),
        check_vma=False,
    )
```

```python
import jax
import jax.numpy as jnp
import numpy as np
from jax import lax
from jax.experimental import pallas as pl
from jax.experimental.pallas import tpu as pltpu
from jax.sharding import PartitionSpec as P

EPS = 1e-06
THETA = 10000.0
MASKED = -1e30
MESH = pl.DeviceIdType.MESH


def rope_constants(length, half_dim):
    inverse = THETA ** (-(np.arange(half_dim, dtype=np.float64) * 2.0 / (2 * half_dim)))
    angles = inverse[:, None] * np.arange(length, dtype=np.float64)[None, :]
    table = np.stack([np.cos(angles), np.sin(angles)]).astype(np.float32)
    return np.ascontiguousarray(table.reshape(2, half_dim, 2, length // 2).transpose(2, 0, 1, 3))


def turn(value, cos_part, sin_part):
    parts = []
    for h in range(value.shape[0] // 64):
        a, b = value[64 * h : 64 * h + 32], value[64 * h + 32 : 64 * h + 64]
        parts += [a * cos_part - b * sin_part, b * cos_part + a * sin_part]
    return jnp.concatenate(parts, 0)


def column(row):
    return jnp.transpose(jnp.broadcast_to(row, (128, 128)))


def copy_to(src, dst, send, recv, device):
    return pltpu.make_async_remote_copy(
        src_ref=src, dst_ref=dst, send_sem=send, recv_sem=recv, device_id=device, device_id_type=MESH
    )


def dot_nt(left, right):
    return lax.dot_general(
        left, right, (((1,), (1,)), ((), ())), preferred_element_type=jnp.float32
    )


def dot_tn(left, right):
    return lax.dot_general(
        left, right, (((0,), (0,)), ((), ())), preferred_element_type=jnp.float32
    )


def across(a, b, flip):
    dp, ctx = lax.axis_index("dp"), lax.axis_index("ctx")
    x, y = dp % 4, dp // 4
    mid = ((a + 1) // 2) % 2
    by_x = mid * (1 + 2 * b) + (1 - mid) * 2 * (a // 3)
    by_y = mid * (a // 2) + (1 - mid) * b
    return ((y + by_y) % 2) * 4 + (x + by_x) % 4, (ctx + flip) % 2


def opposite(a, b):
    return b + (((a + 1) // 2) % 2) * (1 - 2 * b)


def first_half(z, y, k, c):
    return pl.ds(pl.multiple_of(304 * (((z + k) % 4) * 2 + c), 16), 304)


def second_half(z, y, k, c):
    return pl.ds(pl.multiple_of(2432 + 80 * (((z + k) % 4) * 2 + c), 16), 80)


def piece(z, y, k, c, part):
    start = 2432 + 80 * (((z + k) % 4) * 2 + c) + 48 * part
    return pl.ds(pl.multiple_of(start, 16), (48, 32)[part])


def add_rows(ref, place, *parts):
    total = ref[place, :].astype(jnp.float32)
    for part in parts:
        total = total + part.astype(jnp.float32)
    ref[place, :] = total.astype(jnp.bfloat16)


def moe_kernel(
    rows_ref,
    gate_ref,
    dy_ref,
    w_gate_ref,
    w_up_ref,
    w_down_ref,
    w_t_ref,
    d_rows_ref,
    d_gate_ref,
    out_part_ref,
    grad_ref,
    w_all_ref,
    rows_all,
    gate_all,
    dy_all,
    w_full,
    acc,
    out_all,
    din_all,
    sib,
    rs_a,
    rs_b,
    rs_c,
    rs_d,
    rs_e,
    dg_out,
    dg_in,
    places,
    x_buf,
    y_buf,
    d_buf,
    o_buf,
    i_buf,
    gs_buf,
    dgs_buf,
    load_sem,
    ag_send,
    ag_recv,
    g_send,
    g_recv,
    sib_send,
    sib_recv,
    rs_send,
    rs_recv,
    dg_send,
    dg_recv,
    store_sem,
    w_send,
    w_recv,
    ra_0,
    ra_1,
    rb,
    r_send,
    r_recv,
    keep_sem,
):
    tensor = lax.axis_index("tensor")
    dp, ctx = lax.axis_index("dp"), lax.axis_index("ctx")
    me = dp * 2 + ctx

    def to(a, b, flip):
        d, c = across(a, b, flip)
        return (d, c, tensor)

    def side(i):
        return (dp, ctx, (tensor + i) % 8)

    loads = []
    for j in range(2):
        loads.append(
            pltpu.make_async_copy(w_gate_ref.at[j], w_full.at[pl.ds(1024 * j, 1024), pl.ds(0, 512)], load_sem.at[3 * j])
        )
        loads.append(
            pltpu.make_async_copy(
                w_up_ref.at[j], w_full.at[pl.ds(1024 * j, 1024), pl.ds(512, 512)], load_sem.at[3 * j + 1]
            )
        )
        loads.append(pltpu.make_async_copy(w_down_ref.at[j], w_full.at[pl.ds(2048 + 512 * j, 512)], load_sem.at[3 * j + 2]))
    loads.append(pltpu.make_async_copy(dy_ref, dy_all, load_sem.at[6]))
    for load in loads:
        load.start()

    barrier = pltpu.get_barrier_semaphore()
    for a in range(4):
        for b in range(2):
            for flip in range(2):
                if (a, b, flip) != (0, 0, 0):
                    pl.semaphore_signal(
                        barrier, inc=1, device_id=to(a, b, flip), device_id_type=MESH
                    )
    for i in range(1, 8):
        pl.semaphore_signal(barrier, inc=1, device_id=side(i), device_id_type=MESH)
    pl.semaphore_wait(barrier, 22)

    right, left, partner = to(1, 0, 0), to(1, 1, 0), to(0, 1, 0)
    sibling = to(0, 0, 1)
    low, high = pl.ds(0, 64), pl.ds(64, 64)

    def hop(n):
        src, dst, device = (
            (rows_all.at[0], rows_all.at[6], right),
            (rows_all.at[0], rows_all.at[4], left),
            (rows_all.at[0], rows_all.at[2], partner),
            (rows_all.at[6, low], rows_all.at[12, low], right),
            (rows_all.at[4, high], rows_all.at[12, high], left),
            (rows_all.at[2], rows_all.at[10], right),
            (rows_all.at[2], rows_all.at[8], left),
            (rows_all.at[12], rows_all.at[14], partner),
        )[n]
        return copy_to(src, dst, ag_send.at[n], ag_recv.at[n], device)

    def relay(ci):
        r = 2 * ci
        return copy_to(
            rows_all.at[r], rows_all.at[r + 1], ag_send.at[8 + ci], ag_recv.at[8 + ci], sibling
        )

    def gate_push(a, b, flip):
        r = 4 * a + 2 * b + flip
        back = 4 * a + 2 * opposite(a, b) + flip
        return copy_to(
            gate_all.at[0], gate_all.at[back], g_send.at[r], g_recv.at[back], to(a, b, flip)
        )

    rows_all[0] = rows_ref[...]
    gate_all[0] = gate_ref[...]
    for n in range(3):
        hop(n).start()
    relay(0).start()
    for r in range(1, 16):
        gate_push(r // 4, (r // 2) % 2, r % 2).start()

    acc[...] = jnp.zeros_like(acc)

    half = pl.ds(pl.multiple_of(ctx * 128, 128), 128)

    def w_push(i):
        return copy_to(
            w_t_ref.at[half],
            w_all_ref.at[tensor, half],
            w_send.at[i],
            w_recv.at[tensor, ctx],
            side(i),
        )

    def w_relay(t):
        place = w_all_ref.at[t, half]
        return copy_to(place, place, w_send.at[8 + t], w_recv.at[t, ctx], to(0, 0, 1))

    def w_arrival(t, c):
        place = w_all_ref.at[t, pl.ds(pl.multiple_of(c * 128, 128), 128)]
        return copy_to(place, place, w_send.at[0], w_recv.at[t, c], to(0, 0, 1))

    w_own = pltpu.make_async_copy(w_t_ref, w_all_ref.at[tensor], load_sem.at[7])
    w_own.start()

    def sib_push(ci):
        return copy_to(
            din_all.at[2 * ci + 1], sib.at[ci], sib_send.at[ci], sib_recv.at[ci], sibling
        )

    def rs_hop(n):
        src, dst, device = (
            (din_all.at[8], rs_a.at[0], right),
            (din_all.at[10], rs_a.at[1], left),
            (din_all.at[14], rs_b, partner),
            (din_all.at[2], rs_c, partner),
            (din_all.at[12, low], rs_d.at[0], right),
            (din_all.at[12, high], rs_d.at[1], left),
            (din_all.at[4], rs_e.at[0], right),
            (din_all.at[6], rs_e.at[1], left),
        )[n]
        return copy_to(src, dst, rs_send.at[n], rs_recv.at[n], device)

    def rs_go(*hops):
        for n in hops:
            rs_hop(n).start()

    def rs_got(*hops):
        for n in hops:
            rs_hop(n).wait_recv()

    def plus(r, rows, *parts):
        total = din_all[r, rows].astype(jnp.float32)
        for part in parts:
            total = total + part.astype(jnp.float32)
        din_all[r, rows] = total.astype(jnp.bfloat16)

    def post(*cis):
        for ci in cis:
            sib_push(ci).wait_recv()
            plus(2 * ci, slice(None), sib[ci])

    def dg_push(a, b, flip):
        r = 4 * a + 2 * b + flip
        back = 4 * a + 2 * opposite(a, b) + flip
        return pltpu.make_async_remote_copy(
            src_ref=dg_out.at[r],
            dst_ref=dg_in.at[back],
            send_sem=dg_send.at[r],
            recv_sem=dg_recv.at[back],
            device_id=to(a, b, flip),
            device_id_type=MESH,
        )

    expert_row = lax.broadcasted_iota(jnp.int32, (32, 128), 0)
    slot_row = lax.broadcasted_iota(jnp.int32, (64, 128), 0).astype(jnp.float32)
    before = (
        lax.broadcasted_iota(jnp.int32, (128, 128), 0)
        < lax.broadcasted_iota(jnp.int32, (128, 128), 1)
    ).astype(jnp.float32)
    before = before.astype(jnp.bfloat16)

    def gather(a, q):
        r = 4 * a + q
        gates = gate_all[r]
        at = pl.ds(pl.multiple_of(q * 64, 64), 64)
        rows = [
            jnp.sum(jnp.where(expert_row == 2 * me + j, gates, 0.0), 0, keepdims=True)
            for j in range(2)
        ]
        both = jnp.concatenate(rows + [jnp.zeros((6, 128), jnp.float32)], 0)
        named = jnp.where(both > 0.0, 1.0, 0.0).astype(jnp.bfloat16)
        slots = jnp.dot(named, before, preferred_element_type=jnp.float32)
        hits = [
            jnp.where((slot_row == slots[j : j + 1]) & (rows[j] > 0.0), 1.0, 0.0) for j in range(2)
        ]
        place = jnp.concatenate(hits, 0).astype(jnp.bfloat16)
        places[q] = place
        x = jnp.dot(place, rows_all[r], preferred_element_type=jnp.float32).astype(jnp.bfloat16)
        y = jnp.dot(place, dy_all[r], preferred_element_type=jnp.float32)
        for j in range(2):
            gs = jnp.sum(hits[j] * rows[j], 1, keepdims=True)
            y_j = y[64 * j : 64 * j + 64]
            x_buf[j, at, :] = x[64 * j : 64 * j + 64]
            y_buf[j, at, :] = y_j.astype(jnp.bfloat16)
            d_buf[j, at, :] = (y_j * gs).astype(jnp.bfloat16)
            gs_buf[j, at, :] = gs

    def expert(j):
        of_gu = pl.ds(pl.multiple_of(j * 1024, 1024), 1024)
        of_dn = pl.ds(pl.multiple_of(2048 + j * 512, 512), 512)
        x = x_buf[j]
        gu = jnp.dot(x, w_full[of_gu, :], preferred_element_type=jnp.float32)
        g, u = gu[:, :512], gu[:, 512:]
        s = jax.nn.sigmoid(g)
        silu = g * s
        act = (silu * u).astype(jnp.bfloat16)
        eout = (
            jnp.dot(act, w_full[of_dn, :], preferred_element_type=jnp.float32)
            .astype(jnp.bfloat16)
            .astype(jnp.float32)
        )
        dgs_buf[j] = jnp.sum(y_buf[j].astype(jnp.float32) * eout, 1, keepdims=True)
        o_buf[j] = (eout * gs_buf[j]).astype(jnp.bfloat16)
        d = d_buf[j]
        d_act = dot_nt(d, w_full[of_dn, :])
        d_g = (d_act * u * s * (1.0 + g * (1.0 - s))).astype(jnp.bfloat16)
        d_u = (d_act * silu).astype(jnp.bfloat16)
        d_gu = jnp.concatenate([d_g, d_u], 1)
        i_buf[j] = dot_nt(d_gu, w_full[of_gu, :]).astype(jnp.bfloat16)
        acc[of_gu, :] += dot_tn(x, d_gu)
        acc[of_dn, :] += dot_tn(act, d)

    def spread(a, q):
        r = 4 * a + q
        b, flip = q // 2, q % 2
        at = pl.ds(pl.multiple_of(q * 64, 64), 64)
        place = places[q]
        d, c = across(a, b, flip)
        o = jnp.concatenate([o_buf[0, at, :], o_buf[1, at, :]], 0)
        out_all[c * 8 + d] = dot_tn(place, o).astype(jnp.bfloat16)
        i = jnp.concatenate([i_buf[0, at, :], i_buf[1, at, :]], 0)
        din_all[r] = dot_tn(place, i).astype(jnp.bfloat16)
        hits = place.astype(jnp.float32)
        back = [
            jnp.sum(hits[64 * j : 64 * j + 64] * dgs_buf[j, at, :], 0, keepdims=True)
            for j in range(2)
        ]
        dg_out[r] = jnp.concatenate(back + [jnp.zeros((6, 128), jnp.float32)], 0)

        @pl.when(r > 0)
        def _():
            dg_push(a, b, flip).start()

    for n, ci in ((0, 3), (1, 2)):
        hop(n).wait_recv()
        hop(3 + n).start()
        relay(ci).start()
    hop(2).wait_recv()
    hop(5).start()
    hop(6).start()
    relay(1).start()
    relay(0).wait_recv()
    for r in range(1, 16):
        gate_push(r // 4, (r // 2) % 2, r % 2).wait_recv()
    for load in loads:
        load.wait()
    relay(1).wait_recv()
    for i in (1, 7, 2, 6, 3, 5, 4):
        w_push(i).start()

    def step(a, carry):
        lax.fori_loop(0, 4, lambda q, c: (gather(a, q), c)[1], 0)

        @pl.when(a == 1)
        def _():
            post(0, 1)

        @pl.when(a == 2)
        def _():
            post(2, 3)

        @pl.when(a == 3)
        def _():
            post(4, 5)
            rs_go(0, 1)

        lax.fori_loop(0, 2, lambda j, c: (expert(j), c)[1], 0)
        lax.fori_loop(0, 4, lambda q, c: (spread(a, q), c)[1], 0)
        for b in range(2):
            sib_push(2 * a + b).start()

        @pl.when(a == 0)
        def _():
            hop(3).wait_recv()
            hop(4).wait_recv()
            hop(7).start()
            relay(6).start()
            for ci in (2, 3):
                relay(ci).wait_recv()

        @pl.when(a == 1)
        def _():
            for n, ci in ((5, 5), (6, 4)):
                hop(n).wait_recv()
                relay(ci).start()
            for ci in (4, 5):
                relay(ci).wait_recv()

        @pl.when(a == 2)
        def _():
            hop(7).wait_recv()
            relay(7).start()
            for ci in (6, 7):
                relay(ci).wait_recv()

        return carry

    lax.fori_loop(0, 4, step, 0)
    def round_rows(place):
        w_full[place, :] = acc[place, :].astype(jnp.bfloat16)

    z, y = tensor // 2, tensor % 2
    up, down, pair = (
        (dp, ctx, ((z + 1) % 4) * 2 + y),
        (dp, ctx, ((z + 3) % 4) * 2 + y),
        (dp, ctx, z * 2 + 1 - y),
    )

    def grad_hop(n):
        place, dst, device = (
            (first_half(z, y, 2, 0), ra_0.at[0], up),
            (first_half(z, y, 2, 1), ra_0.at[1], down),
            (first_half(z, y, 1, 1), ra_1.at[0], up),
            (first_half(z, y, 3, 0), ra_1.at[1], down),
            (second_half(z, y, 2, 1 - y), rb.at[0], pair),
            (second_half(z, y, 1, 1 - y), rb.at[1], pair),
            (second_half(z, y, 3, 1 - y), rb.at[2], pair),
        )[n]
        return copy_to(w_full.at[place], dst, r_send.at[n], r_recv.at[n], device)

    for n in range(2):
        round_rows(first_half(z, y, 2, n))
        grad_hop(n).start()
    post(7, 6)
    rs_go(2)
    for n, k in ((2, 1), (3, 3)):
        round_rows(first_half(z, y, k, 3 - n))
        grad_hop(n).start()
    rs_got(0, 1)
    plus(2, slice(None), rs_a[0], rs_a[1])
    rs_go(3)
    for k, c in ((1, 0), (3, 1), (0, 0), (0, 1)):
        round_rows(first_half(z, y, k, c))
    for k in range(4):
        for c in range(2):
            round_rows(second_half(z, y, k, c))

    def keep(n, place):
        return pltpu.make_async_copy(w_full.at[place], grad_ref.at[place], keep_sem.at[n])

    first_places = [first_half(z, y, k, c) for k, c in ((1, 1), (3, 0), (2, 0), (2, 1))]
    first_places += [second_half(z, y, k, 1 - y) for k in range(4)] + [second_half(z, y, 0, y)]
    last_places = [
        first_half(z, y, 1, 0),
        first_half(z, y, 3, 1),
        second_half(z, y, 2, y),
        first_half(z, y, 0, 1),
        first_half(z, y, 0, 0),
        second_half(z, y, 1, y),
        second_half(z, y, 3, y),
    ]
    for n, place in enumerate(first_places):
        keep(n, place).start()
    rs_got(2)
    plus(12, slice(None), rs_b[...])
    rs_go(4, 5)
    grad_hop(4).start()
    grad_hop(5).start()
    grad_hop(6).start()
    rs_got(4)
    plus(4, low, rs_d[0])
    rs_go(6)
    rs_got(5)
    plus(6, high, rs_d[1])
    rs_go(7)
    for i in range(1, 8):
        t = (tensor + i) % 8
        w_arrival(t, ctx).wait_recv()
        w_relay(t).start()
    for n in range(8):
        hop(n).wait_send()
        relay(n).wait_send()
    for r in range(1, 16):
        gate_push(r // 4, (r // 2) % 2, r % 2).wait_send()
    store_out = pltpu.make_async_copy(out_all, out_part_ref, store_sem.at[0])
    store_out.start()

    for r in range(1, 16):
        a, b, flip = r // 4, (r // 2) % 2, r % 2
        dg_push(a, b, flip).wait()
    dg_in[0] = dg_out[0]
    d_gate = jnp.zeros((32, 128), jnp.float32)
    for r in range(16):
        d, c = across(r // 4, (r // 2) % 2, r % 2)
        got = dg_in[r]
        for j in range(2):
            d_gate = jnp.where(expert_row == (d * 2 + c) * 2 + j, got[j : j + 1], d_gate)
    d_gate_ref[...] = d_gate
    for ci in range(8):
        sib_push(ci).wait_send()
    rs_got(3, 6, 7)
    total = din_all[0].astype(jnp.float32) + rs_c[...].astype(jnp.float32)
    d_rows_ref[...] = total + rs_e[0].astype(jnp.float32) + rs_e[1].astype(jnp.float32)
    for n in range(8):
        rs_hop(n).wait_send()
    for i in range(1, 8):
        t = (tensor + i) % 8
        w_arrival(t, 1 - ctx).wait_recv()
        w_push(i).wait_send()
        w_relay(t).wait_send()
    w_own.wait()
    for n, (arrived, got) in enumerate(
        ((0, ra_0.at[0]), (1, ra_0.at[1]), (4, rb.at[0]), (2, ra_1.at[0]), (3, ra_1.at[1]), (5, rb.at[1]), (6, rb.at[2]))
    ):
        grad_hop(arrived).wait_recv()
        add_rows(w_full, last_places[n], got[...])
        keep(9 + n, last_places[n]).start()
    for n in range(7):
        grad_hop(n).wait_send()
    store_out.wait()
    for n, place in enumerate(first_places + last_places):
        keep(n, place).wait()


def moe(rows, gates, dy, w_gate, w_up, w_down, w_t):
    bf, f32 = jnp.bfloat16, jnp.float32
    vmem, hbm = pl.BlockSpec(memory_space=pltpu.VMEM), pl.BlockSpec(memory_space=pl.ANY)
    sem = pltpu.SemaphoreType.DMA
    return pl.pallas_call(
        moe_kernel,
        out_shape=(
            jax.ShapeDtypeStruct((128, 1024), f32),
            jax.ShapeDtypeStruct((32, 128), f32),
            jax.ShapeDtypeStruct((16, 128, 1024), bf),
            jax.ShapeDtypeStruct((3072, 1024), bf),
            jax.ShapeDtypeStruct((8, 256, 1024), bf),
        ),
        in_specs=[vmem] * 2 + [hbm] * 4 + [vmem],
        out_specs=(vmem, vmem, hbm, hbm, hbm),
        scratch_shapes=[
            pltpu.VMEM((16, 128, 1024), bf),
            pltpu.VMEM((16, 32, 128), f32),
            pltpu.VMEM((16, 128, 1024), bf),
            pltpu.VMEM((3072, 1024), bf),
            pltpu.VMEM((3072, 1024), f32),
            pltpu.VMEM((16, 128, 1024), bf),
            pltpu.VMEM((16, 128, 1024), bf),
            pltpu.VMEM((8, 128, 1024), bf),
            pltpu.VMEM((2, 128, 1024), bf),
            pltpu.VMEM((128, 1024), bf),
            pltpu.VMEM((128, 1024), bf),
            pltpu.VMEM((2, 64, 1024), bf),
            pltpu.VMEM((2, 128, 1024), bf),
            pltpu.VMEM((16, 8, 128), f32),
            pltpu.VMEM((16, 8, 128), f32),
            pltpu.VMEM((4, 128, 128), bf),
            pltpu.VMEM((2, 256, 1024), bf),
            pltpu.VMEM((2, 256, 1024), bf),
            pltpu.VMEM((2, 256, 1024), bf),
            pltpu.VMEM((2, 256, 1024), bf),
            pltpu.VMEM((2, 256, 1024), bf),
            pltpu.VMEM((2, 256, 1), f32),
            pltpu.VMEM((2, 256, 1), f32),
            sem((8,)),
            sem((16,)),
            sem((16,)),
            sem((16,)),
            sem((16,)),
            sem((8,)),
            sem((8,)),
            sem((8,)),
            sem((8,)),
            sem((16,)),
            sem((16,)),
            sem((2,)),
            sem((16,)),
            sem((8, 2)),
            pltpu.VMEM((2, 304, 1024), bf),
            pltpu.VMEM((2, 304, 1024), bf),
            pltpu.VMEM((3, 80, 1024), bf),
            sem((7,)),
            sem((7,)),
            sem((16,)),
        ],
        compiler_params=pltpu.CompilerParams(
            collective_id=1, has_side_effects=True, vmem_limit_bytes=60 << 20
        ),
        cost_estimate=pl.CostEstimate(
            flops=20_000_000_000, bytes_accessed=30_000_000, transcendentals=2_000_000
        ),
    )(rows, gates, dy, w_gate, w_up, w_down, w_t)


def attention_kernel(
    x_ref,
    dy_ref,
    segment_ref,
    norm1_ref,
    q_gain_ref,
    k_gain_ref,
    norm2_ref,
    router_ref,
    routes_ref,
    w_q_ref,
    w_k_ref,
    w_v_ref,
    w_out_ref,
    table_ref,
    rows2_ref,
    gates_ref,
    resid_ref,
    rows1_ref,
    raw_ref,
    inv_ref,
    q_ref,
    kv_ref,
    lse_ref,
    heads_ref,
    w_out_all_ref,
    dy_all_ref,
    w_t_ref,
    heads_all_ref,
    h_all,
    dy_all,
    w_all,
    w_q,
    w_t,
    raw,
    table,
    stat,
    stats,
    q_t,
    kv_own,
    kv_sib,
    k_own,
    k_sib,
    starts,
    heads,
    heads_all,
    load_sem,
    h_send,
    h_recv,
    dy_send,
    dy_recv,
    w_send,
    w_recv,
    s_send,
    s_recv,
    kv_sem,
    o_send,
    o_recv,
    store_sem,
):
    f32, bf = jnp.float32, jnp.bfloat16
    dp, ctx, me = lax.axis_index("dp"), lax.axis_index("ctx"), lax.axis_index("tensor")

    def side(i):
        return (dp, ctx, (me + i) % 8)

    def to(a, b, flip):
        d, c = across(a, b, flip)
        return (d, c, me)

    sibling = (dp, 1 - ctx, me)
    loads = [
        pltpu.make_async_copy(w_q_ref, w_q, load_sem.at[0]),
        pltpu.make_async_copy(w_k_ref, w_t.at[pl.ds(128, 64)], load_sem.at[1]),
        pltpu.make_async_copy(w_v_ref, w_t.at[pl.ds(192, 64)], load_sem.at[2]),
        pltpu.make_async_copy(w_out_ref, w_all.at[me], load_sem.at[3]),
        pltpu.make_async_copy(table_ref.at[ctx], table, load_sem.at[4]),
    ]
    for load in loads:
        load.start()
    barrier = pltpu.get_barrier_semaphore()
    for i in range(1, 8):
        pl.semaphore_signal(barrier, inc=1, device_id=side(i), device_id_type=MESH)
    for a in range(4):
        for b in range(2):
            if (a, b) != (0, 0):
                pl.semaphore_signal(barrier, inc=1, device_id=to(a, b, 0), device_id_type=MESH)
    pl.semaphore_signal(barrier, inc=1, device_id=sibling, device_id_type=MESH)
    x = x_ref[...].astype(f32)
    inv_one = lax.rsqrt(jnp.mean(x * x, -1, keepdims=True) + EPS)
    h_all[me] = (x * inv_one * norm1_ref[...]).astype(bf)
    dy_all[0] = dy_ref[...]
    pl.semaphore_wait(barrier, 15)

    z, y = me // 2, me % 2
    up, down, pair = (
        (dp, ctx, ((z + 1) % 4) * 2 + y),
        (dp, ctx, ((z + 3) % 4) * 2 + y),
        (dp, ctx, z * 2 + 1 - y),
    )
    low, high = pl.ds(0, 64), pl.ds(64, 64)

    def block_at(k, flip):
        return ((z + k) % 4) * 2 + (y + flip) % 2

    def h_hop(n):
        place, device = (
            (h_all.at[me], up),
            (h_all.at[me], down),
            (h_all.at[me], pair),
            (h_all.at[block_at(3, 0), low], up),
            (h_all.at[block_at(1, 0), high], down),
            (h_all.at[block_at(0, 1)], up),
            (h_all.at[block_at(0, 1)], down),
            (h_all.at[block_at(2, 0)], pair),
        )[n]
        return copy_to(place, place, h_send.at[n], h_recv.at[n], device)

    right, left, partner = to(1, 0, 0), to(1, 1, 0), to(0, 1, 0)

    def dy_hop(n):
        src, dst, device = (
            (dy_all.at[0], dy_all.at[6], right),
            (dy_all.at[0], dy_all.at[4], left),
            (dy_all.at[0], dy_all.at[2], partner),
            (dy_all.at[6, low], dy_all.at[12, low], right),
            (dy_all.at[4, high], dy_all.at[12, high], left),
            (dy_all.at[2], dy_all.at[10], right),
            (dy_all.at[2], dy_all.at[8], left),
            (dy_all.at[12], dy_all.at[14], partner),
        )[n]
        return copy_to(src, dst, dy_send.at[n], dy_recv.at[n], device)

    def dy_relay(ci):
        r = 2 * ci
        return copy_to(
            dy_all.at[r], dy_all.at[r + 1], dy_send.at[8 + ci], dy_recv.at[8 + ci], sibling
        )

    for n in range(3):
        h_hop(n).start()
    for n in range(3):
        dy_hop(n).start()
    dy_relay(0).start()

    for load in loads:
        load.wait()
    w_t[0:128, :] = jnp.transpose(w_q[...])
    seg = segment_ref[...]
    start = jnp.zeros((16, 128), f32)
    for s in range(1, 8):
        below = jnp.where(seg < s, 1.0, 0.0)
        count = jnp.sum(jnp.sum(below, 1, keepdims=True), 0, keepdims=True)
        start = jnp.where(seg == s, count, start)
    start = jnp.where(ctx == 0, start[:8], start[8:])
    for t in range(8):
        starts[0:1, 128 * t : 128 * t + 128] = start[t : t + 1]

    def project(t):
        value = dot_nt(w_t[...], h_all[t])
        raw[t] = value
        square = value * value
        stat[0, pl.ds(t, 1), :] = jnp.sum(square[0:128], 0, keepdims=True)
        stat[1, pl.ds(t, 1), :] = jnp.sum(square[128:192], 0, keepdims=True)

    project(me)
    for n in range(2):
        h_hop(n).wait_recv()
        h_hop(3 + n).start()
    h_hop(2).wait_recv()
    h_hop(5).start()
    h_hop(6).start()
    for k, flip in ((3, 0), (1, 0), (0, 1)):
        project(block_at(k, flip))
    h_hop(3).wait_recv()
    h_hop(4).wait_recv()
    h_hop(7).start()
    project(block_at(2, 0))
    for n, k in ((5, 3), (6, 1), (7, 2)):
        h_hop(n).wait_recv()
        project(block_at(k, 1))
    stats[me] = stat[...]

    def s_push(i):
        return copy_to(stats.at[me], stats.at[me], s_send.at[i], s_recv.at[me], side(i))

    def s_arrival(t):
        return copy_to(stats.at[t], stats.at[t], s_send.at[0], s_recv.at[t], sibling)

    for i in range(1, 8):
        s_push(i).start()
    store_rows = pltpu.make_async_copy(h_all, rows1_ref, store_sem.at[0])
    store_raw = pltpu.make_async_copy(raw, raw_ref, store_sem.at[1])
    store_wt = pltpu.make_async_copy(w_t, w_t_ref, store_sem.at[8])
    store_rows.start()
    store_raw.start()
    store_wt.start()

    def w_push(i):
        half = w_all.at[me, pl.ds(pl.multiple_of(ctx * 64, 64), 64)]
        return copy_to(half, half, w_send.at[i], w_recv.at[me, ctx], side(i))

    def w_relay(t):
        half = w_all.at[t, pl.ds(pl.multiple_of(ctx * 64, 64), 64)]
        return copy_to(half, half, w_send.at[8 + t], w_recv.at[t, ctx], sibling)

    def w_arrival(t, c):
        half = w_all.at[t, pl.ds(pl.multiple_of(c * 64, 64), 64)]
        return copy_to(half, half, w_send.at[0], w_recv.at[t, c], sibling)

    for n, ci in ((0, 3), (1, 2)):
        dy_hop(n).wait_recv()
        dy_hop(3 + n).start()
        dy_relay(ci).start()
    dy_hop(2).wait_recv()
    dy_hop(5).start()
    dy_hop(6).start()
    dy_relay(1).start()
    for i in (1, 7, 2, 6, 3, 5, 4):
        w_push(i).start()
    gain_q = column(q_gain_ref[...])
    gain_k = column(jnp.concatenate([k_gain_ref[...], jnp.zeros((1, 64), f32)], 1))[:64]
    for i in range(1, 8):
        s_arrival((me + i) % 8).wait_recv()

    def finish(t, carry):
        at = pl.ds(pl.multiple_of(t * 128, 128), 128)
        rows = []
        for n, width in enumerate((1024.0, 512.0)):
            total = stats[0, n, pl.ds(t, 1), :]
            for s in range(1, 8):
                total = total + stats[s, n, pl.ds(t, 1), :]
            rows.append(lax.rsqrt(total / width + EPS))
        inv = jnp.concatenate(rows + [jnp.zeros((6, 128), f32)], 0)
        inv_ref[t] = inv
        value = raw[t]
        cos_part, sin_part = table[0, :, at], table[1, :, at]
        queries = turn(value[0:128] * inv[0:1] * gain_q, cos_part, sin_part).astype(bf)
        keys = turn(value[128:192] * inv[1:2] * gain_k, cos_part, sin_part).astype(bf)
        q_t[:, at] = queries
        kv_own[0:64, at] = keys
        kv_own[64:128, at] = value[192:256].astype(bf)
        k_own[at, :] = jnp.transpose(keys)
        return carry

    lax.fori_loop(0, 8, finish, 0)
    kv_push = copy_to(kv_own, kv_sib, kv_sem.at[0], kv_sem.at[1], sibling)
    kv_push.start()

    key_row = lax.broadcasted_iota(jnp.int32, (256, 512), 0).astype(f32)
    query_lane = (lax.broadcasted_iota(jnp.int32, (256, 512), 1) % 256).astype(f32)
    base = (ctx * 1024).astype(f32)

    def attend(i, carry):
        at = pl.ds(pl.multiple_of(i * 256, 256), 256)
        q = jnp.concatenate([q_t[0:64, at], q_t[64:128, at]], 1) * 0.125
        begin = jnp.concatenate([starts[0:1, at]] * 2, 1)

        def block(keys, values, first_key, state, causal):
            top, total, acc = state
            s = jnp.dot(keys, q, preferred_element_type=f32)
            ok = key_row >= begin - first_key
            if causal:
                ok = ok & (key_row <= query_lane)
            s = jnp.where(ok, s, MASKED)
            new_top = jnp.maximum(top, jnp.max(s, 0, keepdims=True))
            e = jnp.exp(s - new_top)
            shrink = jnp.exp(top - new_top)
            total = total * shrink + jnp.sum(e, 0, keepdims=True)
            acc = acc * shrink + jnp.dot(values, e.astype(bf), preferred_element_type=f32)
            return new_top, total, acc

        state = (jnp.full((1, 512), MASKED, f32), jnp.zeros((1, 512), f32), jnp.zeros((64, 512), f32))
        state = block(
            k_own[at, :], kv_own[64:128, at], base + (i * 256).astype(f32), state, True
        )

        def own(j, state):
            ks = pl.ds(pl.multiple_of(j * 256, 256), 256)
            return block(k_own[ks, :], kv_own[64:128, ks], base + (j * 256).astype(f32), state, False)

        state = lax.fori_loop(0, i, own, state)

        def other(j, state):
            ks = pl.ds(pl.multiple_of(j * 256, 256), 256)
            return block(k_sib[ks, :], kv_sib[64:128, ks], (j * 256).astype(f32), state, False)

        top, total, acc = lax.fori_loop(0, 4 * ctx, other, state)
        out = (acc / total).astype(bf)
        lse = top + jnp.log(total)
        for h in range(2):
            for n in range(2):
                heads[2 * i + n, 64 * h : 64 * h + 64, :] = out[
                    :, 256 * h + 128 * n : 256 * h + 128 * n + 128
                ]
            lse_ref[h, 0:1, at] = lse[:, 256 * h : 256 * h + 256]
        return carry

    kv_push.wait()

    def straighten(t, carry):
        at = pl.ds(pl.multiple_of(t * 128, 128), 128)
        k_sib[at, :] = jnp.transpose(kv_sib[0:64, at])
        return carry

    dy_hop(3).wait_recv()
    dy_hop(4).wait_recv()
    dy_hop(7).start()
    dy_relay(6).start()
    lax.fori_loop(0, 8, straighten, 0)
    lax.fori_loop(0, 4, attend, 0)

    def o_push(i):
        return copy_to(
            heads.at[(me + i) % 8], heads_all.at[me], o_send.at[i], o_recv.at[me], side(i)
        )

    def o_arrival(t):
        return copy_to(heads_all.at[t], heads_all.at[t], o_send.at[0], o_recv.at[t], sibling)

    for i in range(1, 8):
        o_push(i).start()
    heads_all[me] = heads[me]
    stores = [
        pltpu.make_async_copy(q_t, q_ref, store_sem.at[2]),
        pltpu.make_async_copy(kv_own, kv_ref.at[0], store_sem.at[3]),
        pltpu.make_async_copy(kv_sib, kv_ref.at[1], store_sem.at[4]),
        pltpu.make_async_copy(heads, heads_ref, store_sem.at[5]),
    ]
    for store in stores:
        store.start()

    def pass_on(i, carry):
        t = (me + i) % 8
        w_arrival(t, ctx).wait_recv()
        w_relay(t).start()
        return carry

    lax.fori_loop(1, 8, pass_on, 0)

    for n, ci in ((5, 5), (6, 4), (7, 7)):
        dy_hop(n).wait_recv()
        dy_relay(ci).start()
    for i in range(1, 8):
        t = (me + i) % 8
        w_arrival(t, 1 - ctx).wait_recv()
        o_arrival(t).wait_recv()
    store_w = pltpu.make_async_copy(w_all, w_out_all_ref, store_sem.at[6])
    store_w.start()
    store_heads = pltpu.make_async_copy(heads_all, heads_all_ref, store_sem.at[9])
    store_heads.start()
    attended = dot_tn(heads_all[...].reshape(1024, 128), w_all[...].reshape(1024, 1024))
    resid = x + attended
    resid_ref[...] = resid
    inv_two = lax.rsqrt(jnp.mean(resid * resid, -1, keepdims=True) + EPS)
    rows2 = (resid * inv_two * norm2_ref[...]).astype(bf)
    rows2_ref[...] = rows2
    logits = dot_nt(router_ref[...], rows2)
    expert_row = lax.broadcasted_iota(jnp.int32, (32, 128), 0)
    routes = routes_ref[...]
    named = routes[0:1] == expert_row
    for k in range(1, 8):
        named = named | (routes[k : k + 1] == expert_row)
    chosen = jnp.where(named, logits, MASKED)
    weight = jnp.where(named, jnp.exp(chosen - jnp.max(chosen, 0, keepdims=True)), 0.0)
    gates_ref[...] = weight / jnp.sum(weight, 0, keepdims=True)

    for ci in range(8):
        dy_relay(ci).wait_recv()
    store_dy = pltpu.make_async_copy(dy_all, dy_all_ref, store_sem.at[7])
    store_dy.start()
    for i in range(1, 8):
        s_push(i).wait_send()
        w_push(i).wait_send()
        w_relay((me + i) % 8).wait_send()
        o_push(i).wait_send()
    for n in range(8):
        h_hop(n).wait_send()
        dy_hop(n).wait_send()
        dy_relay(n).wait_send()
    for store in [store_rows, store_raw, store_wt, store_w, store_dy, store_heads] + stores:
        store.wait()


def attention(x, dy, segment, norm1, q_gain, k_gain, norm2, router, routes, w_q, w_k, w_v, w_out):
    bf, f32 = jnp.bfloat16, jnp.float32
    vmem, hbm = pl.BlockSpec(memory_space=pltpu.VMEM), pl.BlockSpec(memory_space=pl.ANY)
    sem = pltpu.SemaphoreType.DMA
    shape = jax.ShapeDtypeStruct
    table = jnp.asarray(rope_constants(2048, 32))
    return pl.pallas_call(
        attention_kernel,
        out_shape=(
            shape((128, 1024), bf),
            shape((32, 128), f32),
            shape((128, 1024), f32),
            shape((8, 128, 1024), bf),
            shape((8, 256, 128), f32),
            shape((8, 8, 128), f32),
            shape((128, 1024), bf),
            shape((2, 128, 1024), bf),
            shape((2, 8, 1024), f32),
            shape((8, 128, 128), bf),
            shape((8, 128, 1024), bf),
            shape((16, 128, 1024), bf),
            shape((256, 1024), bf),
            shape((8, 128, 128), bf),
        ),
        in_specs=[vmem] * 9 + [hbm] * 5,
        out_specs=(vmem, vmem, vmem, hbm, hbm, vmem, hbm, hbm, vmem, hbm, hbm, hbm, hbm, hbm),
        scratch_shapes=[
            pltpu.VMEM((8, 128, 1024), bf),
            pltpu.VMEM((16, 128, 1024), bf),
            pltpu.VMEM((8, 128, 1024), bf),
            pltpu.VMEM((1024, 128), bf),
            pltpu.VMEM((256, 1024), bf),
            pltpu.VMEM((8, 256, 128), f32),
            pltpu.VMEM((2, 32, 1024), f32),
            pltpu.VMEM((2, 8, 128), f32),
            pltpu.VMEM((8, 2, 8, 128), f32),
            pltpu.VMEM((128, 1024), bf),
            pltpu.VMEM((128, 1024), bf),
            pltpu.VMEM((128, 1024), bf),
            pltpu.VMEM((1024, 64), bf),
            pltpu.VMEM((1024, 64), bf),
            pltpu.VMEM((8, 1024), f32),
            pltpu.VMEM((8, 128, 128), bf),
            pltpu.VMEM((8, 128, 128), bf),
            sem((5,)),
            sem((8,)),
            sem((8,)),
            sem((16,)),
            sem((16,)),
            sem((16,)),
            sem((8, 2)),
            sem((8,)),
            sem((8,)),
            sem((2,)),
            sem((8,)),
            sem((8,)),
            sem((10,)),
        ],
        compiler_params=pltpu.CompilerParams(
            collective_id=2, has_side_effects=True, vmem_limit_bytes=56 << 20
        ),
        cost_estimate=pl.CostEstimate(
            flops=5_000_000_000, bytes_accessed=20_000_000, transcendentals=4_000_000
        ),
    )(
        x,
        dy,
        segment.reshape(16, 128),
        norm1.reshape(1, 1024),
        q_gain.reshape(1, 128),
        k_gain.reshape(1, 64),
        norm2.reshape(1, 1024),
        router.T,
        routes.T,
        w_q,
        w_k.T,
        w_v.T,
        w_out,
        table,
    )


def backward_kernel(
    x_ref,
    dy_ref,
    d_rows_ref,
    d_gate_ref,
    gates_ref,
    rows2_ref,
    resid_ref,
    router_ref,
    norm1_ref,
    norm2_ref,
    q_gain_ref,
    k_gain_ref,
    segment_ref,
    inv_ref,
    lse_ref,
    rows1_ref,
    raw_ref,
    q_ref,
    kv_ref,
    heads_ref,
    heads_all_ref,
    w_out_ref,
    w_all_ref,
    grads_ref,
    out_part_ref,
    table_ref,
    grad_x_ref,
    norm1_out_ref,
    pack_ref,
    output_ref,
    reduced_ref,
    rows1,
    raw,
    q_t,
    kv_own,
    kv_sib,
    heads,
    w_out,
    w_all,
    table,
    starts,
    d_resid,
    heads_all,
    wo_part,
    wo_in,
    dh_send,
    dh_all,
    tiny,
    q_cat,
    q_nat,
    d_cat,
    d_nat,
    lanes,
    k_nat,
    v_nat,
    dq_acc,
    dk_acc,
    dv_acc,
    dkv_out,
    dkv_in,
    terms,
    stat,
    stats,
    dqkv,
    dqkv_all,
    pack,
    pack_sib,
    pack_in,
    result,
    n1,
    n1_chips,
    n1_sib,
    load_sem,
    a_send,
    a_recv,
    dh_send_sem,
    dh_recv,
    t_send,
    t_recv,
    s_send,
    s_recv,
    dkv_sem,
    o_send,
    o_recv,
    p_sem,
    rs_send,
    rs_recv,
    g_send,
    g_recv,
    gs_send,
    gs_recv,
    n_send,
    n_recv,
    m_send,
    m_recv,
    ns_sem,
    grads,
    reduced,
    ra2,
    ra4,
    rb1,
    rb2,
    rb3,
    r_send,
    r_recv,
    out_own,
    out_sib,
    out_a,
    out_b,
    out_c,
    os_sem,
    out_send,
    out_recv,
    keep_sem,
):
    f32, bf = jnp.float32, jnp.bfloat16
    dp, ctx, me = lax.axis_index("dp"), lax.axis_index("ctx"), lax.axis_index("tensor")
    sibling = (dp, 1 - ctx, me)

    def side(i):
        return (dp, ctx, (me + i) % 8)

    def chip(i):
        return ((dp + i) % 8, ctx, me)

    z, y = me // 2, me % 2
    other = 1 - y
    up, down, pair = (
        (dp, ctx, ((z + 1) % 4) * 2 + y),
        (dp, ctx, ((z + 3) % 4) * 2 + y),
        (dp, ctx, z * 2 + other),
    )

    def a_rows(k, c, s=0):
        start = 304 * (((z + k) % 4) * 2 + c) + 160 * s
        return pl.ds(pl.multiple_of(start, 16), (160, 144)[s])

    def of_part(s):
        return pl.ds(160 * s, (160, 144)[s])

    def b_rows(k, c):
        return second_half(z, y, k, c)

    def hop(n, s=0):
        if n < 2:
            src, dst = grads.at[a_rows((1, 3)[n], n, s)], ra2.at[n, of_part(s)]
            to = (up, down)[n]
        elif n == 2:
            src, dst, to = grads.at[b_rows(0, other)], rb1, pair
        elif n < 5:
            part = n - 3
            src, to = grads.at[piece(z, y, 2, y, part)], (up, down)[part]
            dst = (rb2.at[pl.ds(0, 48)], rb2.at[pl.ds(48, 32)])[part]
        elif n == 5:
            src, dst, to = grads.at[a_rows(0, other, s)], ra4.at[of_part(s)], pair
        elif n == 6:
            src, dst, to = grads.at[b_rows(1, y)], rb3.at[0], up
        elif n == 7:
            src, dst, to = grads.at[b_rows(3, y)], rb3.at[1], down
        else:
            place, to = (
                (a_rows(0, y, s), pair),
                (a_rows(0, y, s), up),
                (a_rows(0, y, s), down),
                (a_rows(0, other, s), up),
                (a_rows(0, other, s), down),
                (a_rows(3, 0, s), up),
                (a_rows(1, 1, s), down),
                (b_rows(0, y), up),
                (b_rows(0, y), down),
                (piece(z, y, 3, y, 0), up),
                (piece(z, y, 1, y, 1), down),
                (b_rows(0, y), pair),
                (b_rows(3, y), pair),
                (b_rows(1, y), pair),
                (b_rows(2, y), pair),
            )[n - 8]
            src = dst = reduced.at[place]
        return copy_to(src, dst, r_send.at[n + 23 * s], r_recv.at[n + 23 * s], to)

    def go(*hops, s=0):
        for n in hops:
            hop(n, s).start()

    def got(*hops, s=0):
        for n in hops:
            hop(n, s).wait_recv()

    def reduce_0():
        go(0, 1, 3, 4, 2)

    def reduce_1(s):
        got(0, 1, s=s)
        for c in range(2):
            add_rows(grads, a_rows(0, c, s), ra2[c, of_part(s)])
        go(5, s=s)

    def reduce_2():
        got(3, 4)
        add_rows(grads, piece(z, y, 1, y, 0), rb2[0:48])
        add_rows(grads, piece(z, y, 3, y, 1), rb2[48:80])
        go(6, 7)

    def reduce_3(s):
        got(5, s=s)
        add_rows(grads, a_rows(0, y, s), ra4[of_part(s)])
        reduced[a_rows(0, y, s), :] = grads[a_rows(0, y, s), :]
        go(8, 9, 10, s=s)

    def reduce_4():
        got(6, 7, 2)
        add_rows(grads, b_rows(0, y), rb1[...], rb3[0], rb3[1])
        reduced[b_rows(0, y), :] = grads[b_rows(0, y), :]
        go(15, 16, 19)

    def reduce_5(s):
        got(8, s=s)
        go(11, 12, s=s)

    def reduce_6():
        got(15)
        go(17, 20)
        got(16)
        go(18, 21)

    def reduce_7(s):
        @pl.when(y == 0)
        def _():
            got(9, 12, s=s)

        @pl.when(y == 1)
        def _():
            got(11, 10, s=s)

        go(13, 14, s=s)

    def reduce_8():
        got(17, 18)
        go(22)

    def keep(n, place):
        return pltpu.make_async_copy(reduced.at[place], reduced_ref.at[place], keep_sem.at[n])

    keep_places = (
        [a_rows(0, c, s) for c in range(2) for s in range(2)]
        + [a_rows(k, c, s) for k in (1, 3) for c in range(2) for s in range(2)]
        + [a_rows(2, c, s) for c in range(2) for s in range(2)]
        + [pl.ds(2432, 640)]
    )

    def reduce_9():
        for n in range(4):
            keep(n, keep_places[n]).start()
        for s in range(2):

            @pl.when(y == 0)
            def _():
                got(10, 11, s=s)

            @pl.when(y == 1)
            def _():
                got(9, 12, s=s)

        for n in range(4, 12):
            keep(n, keep_places[n]).start()
        got(19, 20, 21, 22)
        keep(16, keep_places[16]).start()
        for s in range(2):
            got(13, 14, s=s)
        for n in range(12, 16):
            keep(n, keep_places[n]).start()
        for n in range(23):
            hop(n).wait_send()
        for n in (0, 1, 5, 8, 9, 10, 11, 12, 13, 14):
            hop(n, 1).wait_send()

    def x_side(i):
        return ((dp // 4) * 4 + (dp + i) % 4, ctx, me)

    right, left, partner = x_side(1), x_side(3), ((dp + 4) % 8, ctx, me)
    theirs_out = out_part_ref.at[pl.ds(pl.multiple_of((1 - ctx) * 8, 8), 8)]
    os_push = copy_to(
        theirs_out, out_sib.at[:, :, pl.ds(0, 1024)], os_sem.at[0], os_sem.at[1], sibling
    )
    wo_push = copy_to(
        wo_part.at[1 - ctx],
        out_sib.at[:, :, pl.ds(1024, 512)],
        os_sem.at[2],
        os_sem.at[3],
        sibling,
    )

    def out_at(i, b):
        return (dp // 4 + b) % 2 * 4 + (dp + i) % 4

    def out_hop(n):
        b = n % 2
        if n < 2:
            src, dst, to = out_own.at[out_at(2, b), pl.ds(0, 64)], out_a.at[0, b], right
        elif n < 4:
            src, dst, to = out_own.at[out_at(2, b), pl.ds(64, 64)], out_a.at[1, b], left
        elif n < 6:
            src, dst, to = out_own.at[out_at(1, b)], out_b.at[0, b], right
        elif n < 8:
            src, dst, to = out_own.at[out_at(3, b)], out_b.at[1, b], left
        else:
            src, dst, to = out_own.at[out_at(0, 1)], out_c, partner
        return copy_to(src, dst, out_send.at[n], out_recv.at[n], to)

    def out_0():
        os_push.wait()
        wo_push.wait()

        def add_sib(d, carry):
            left_part = out_own[d, :, 0:1024].astype(f32)
            right_part = wo_part[ctx, d].astype(f32)
            total = jnp.concatenate([left_part, right_part], 1) + out_sib[d].astype(f32)
            out_own[d] = total.astype(bf)
            return carry

        lax.fori_loop(0, 8, add_sib, 0)
        for n in range(4):
            out_hop(n).start()

    def out_add(at, rows, *parts):
        total = out_own[at, rows].astype(f32)
        for part in parts:
            total = total + part.astype(f32)
        out_own[at, rows] = total.astype(bf)

    def out_1():
        for b in range(2):
            out_hop(b).wait_recv()
            out_add(out_at(1, b), pl.ds(0, 64), out_a[0, b])
            out_hop(4 + b).start()
            out_hop(2 + b).wait_recv()
            out_add(out_at(3, b), pl.ds(64, 64), out_a[1, b])
            out_hop(6 + b).start()

    def out_2():
        for b in (1, 0):
            out_hop(4 + b).wait_recv()
            out_hop(6 + b).wait_recv()
            out_add(out_at(0, b), slice(None), out_b[0, b], out_b[1, b])
            if b == 1:
                out_hop(8).start()

    def out_3():
        out_hop(8).wait_recv()
        total = out_own[dp].astype(f32) + out_c[...].astype(f32)
        output_ref[...] = (resid_ref[...] + total[:, 0:1024]).astype(bf)
        wo_sum = total[:, 1024:1536].astype(bf)
        for t in range(8):
            wo_part[0, 0, 16 * t : 16 * t + 16, :] = wo_sum[16 * t : 16 * t + 16]
        for i in range(1, 8):
            wo_hop(i).start()
        wo_in[me] = wo_part[0, 0, pl.ds(pl.multiple_of(me * 16, 16), 16), :]
        for n in range(9):
            out_hop(n).wait_send()

    def wo_hop(i):
        rows = pl.ds(pl.multiple_of((me + i) % 8 * 16, 16), 16)
        return copy_to(wo_part.at[0, 0, rows], wo_in.at[me], a_send.at[i], a_recv.at[me], side(i))

    def wo_arrival(t):
        return copy_to(wo_in.at[t], wo_in.at[t], a_send.at[0], a_recv.at[t], sibling)

    early = pltpu.make_async_copy(grads_ref, grads, load_sem.at[9])
    early.start()
    sources = (rows1_ref, raw_ref, q_ref, kv_ref.at[0], kv_ref.at[1], heads_ref, w_out_ref)
    targets = (rows1, raw, q_t, kv_own, kv_sib, heads, w_out)
    loads = [
        pltpu.make_async_copy(s, t, load_sem.at[n])
        for n, (s, t) in enumerate(zip(sources, targets, strict=True))
    ]
    loads.append(pltpu.make_async_copy(w_all_ref, w_all, load_sem.at[7]))
    loads.append(pltpu.make_async_copy(table_ref.at[ctx], table, load_sem.at[8]))
    loads.append(early)
    loads.append(pltpu.make_async_copy(heads_all_ref, heads_all, load_sem.at[11]))
    own_blocks = out_part_ref.at[pl.ds(pl.multiple_of(ctx * 8, 8), 8)]
    loads.append(pltpu.make_async_copy(own_blocks, out_own.at[:, :, pl.ds(0, 1024)], load_sem.at[10]))
    for n, load in enumerate(loads):
        if n != 9:
            load.start()
    barrier = pltpu.get_barrier_semaphore()
    for i in range(1, 8):
        pl.semaphore_signal(barrier, inc=1, device_id=side(i), device_id_type=MESH)
        pl.semaphore_signal(barrier, inc=1, device_id=chip(i), device_id_type=MESH)
    pl.semaphore_signal(barrier, inc=1, device_id=sibling, device_id_type=MESH)

    pl.semaphore_wait(barrier, 15)
    early.wait()
    reduce_0()
    gates, d_gate = gates_ref[...], d_gate_ref[...]
    d_logits = gates * (d_gate - jnp.sum(gates * d_gate, 0, keepdims=True))
    d_normed = d_rows_ref[...] + lax.dot_general(
        jnp.transpose(d_logits),
        router_ref[...].astype(f32),
        (((1,), (0,)), ((), ())),
        preferred_element_type=f32,
        precision=lax.Precision.HIGHEST,
    )
    resid = resid_ref[...]
    inv_two = lax.rsqrt(jnp.mean(resid * resid, -1, keepdims=True) + EPS)
    res_hat = resid * inv_two
    scaled = d_normed * norm2_ref[...]
    d_res = dy_ref[...].astype(f32) + inv_two * (
        scaled - res_hat * jnp.mean(scaled * res_hat, -1, keepdims=True)
    )
    d_resid[...] = d_res
    datt = d_res.astype(bf)
    for n in (6,):
        loads[n].wait()
    d_heads = dot_nt(w_out[...].reshape(1024, 1024), datt).astype(bf)
    dh_send[...] = d_heads.reshape(8, 128, 128)
    dh_all[me] = dh_send[me]

    def dh_push(i):
        return copy_to(
            dh_send.at[(me + i) % 8], dh_all.at[me], dh_send_sem.at[i], dh_recv.at[me], side(i)
        )

    def dh_arrival(t):
        return copy_to(dh_all.at[t], dh_all.at[t], dh_send_sem.at[0], dh_recv.at[t], sibling)

    for i in range(1, 8):
        dh_push(i).start()

    norm2_part = jnp.sum(d_normed * res_hat, 0, keepdims=True)
    router_part = jnp.dot(
        d_logits,
        rows2_ref[...].astype(f32),
        preferred_element_type=f32,
        precision=lax.Precision.HIGHEST,
    )
    def pack_rows(place, value):
        for c in range(2):
            pack[c, place, :] = value[:, 512 * c : 512 * c + 512].astype(bf)

    pack_rows(pl.ds(256, 32), router_part)
    pack_rows(pl.ds(288, 16), jnp.concatenate([norm2_part, jnp.zeros((15, 1024), f32)], 0))
    pack_rows(pl.ds(320, 64), jnp.zeros((64, 1024), f32))

    os_push.start()
    loads[10].wait()

    def wo_rows(t, carry):
        value = jnp.dot(heads_all[t], datt, preferred_element_type=f32).astype(bf)
        rows = pl.ds(pl.multiple_of(t * 16, 16), 16)
        for d in range(8):
            for c in range(2):
                wo_part[c, d, rows, :] = value[16 * d : 16 * d + 16, 512 * c : 512 * c + 512]
        return carry

    lax.fori_loop(0, 8, wo_rows, 0)
    wo_push.start()
    go(0, 1, s=1)
    for n in (0, 1, 2, 3, 4, 5, 7, 8, 11):
        loads[n].wait()
    seg = segment_ref[...]
    start = jnp.zeros((16, 128), f32)
    for s in range(1, 8):
        below = jnp.where(seg < s, 1.0, 0.0)
        count = jnp.sum(jnp.sum(below, 1, keepdims=True), 0, keepdims=True)
        start = jnp.where(seg == s, count, start)
    start = jnp.where(ctx == 0, start[:8], start[8:])
    for t in range(8):
        starts[0:1, 128 * t : 128 * t + 128] = start[t : t + 1]

    def lay_out(t, carry):
        at = pl.ds(pl.multiple_of(t * 128, 128), 128)
        i, half = t // 2, t % 2
        q = q_t[:, at] * 0.125
        for h in range(2):
            spot = pl.ds(pl.multiple_of(h * 256 + half * 128, 128), 128)
            q_h = q[64 * h : 64 * h + 64]
            q_cat[i, :, spot] = q_h
            q_nat[i, spot, :] = jnp.transpose(q_h)
            lanes[i, 0:1, spot] = lse_ref[h, 0:1, at]
            lanes[i, 2:3, spot] = starts[0:1, at]
        for n, kv in enumerate((kv_own, kv_sib)):
            k_nat[n, at, :] = jnp.transpose(kv[0:64, at])
            v_nat[n, at, :] = jnp.transpose(kv[64:128, at])
        return carry

    lax.fori_loop(0, 8, lay_out, 0)
    dk_acc[...] = jnp.zeros_like(dk_acc)
    dv_acc[...] = jnp.zeros_like(dv_acc)
    dq_acc[...] = jnp.zeros_like(dq_acc)
    for i in range(1, 8):
        dh_arrival((me + i) % 8).wait_recv()

    def lay_dh(t, carry):
        i, half = t // 2, t % 2
        d, o = dh_all[t], heads[t]
        product = d.astype(f32) * o.astype(f32)
        for h in range(2):
            spot = pl.ds(pl.multiple_of(h * 256 + half * 128, 128), 128)
            d_h = d[64 * h : 64 * h + 64]
            d_cat[i, :, spot] = d_h
            d_nat[i, spot, :] = jnp.transpose(d_h)
            lanes[i, 1:2, spot] = jnp.sum(product[64 * h : 64 * h + 64], 0, keepdims=True)
        return carry

    lax.fori_loop(0, 8, lay_dh, 0)
    reduce_1(0)
    key_row = lax.broadcasted_iota(jnp.int32, (256, 512), 0).astype(f32)
    query_lane = (lax.broadcasted_iota(jnp.int32, (256, 512), 1) % 256).astype(f32)
    base = (ctx * 1024).astype(f32)

    def block(n, i, j, first_key, causal):
        ks = pl.ds(pl.multiple_of(j * 256, 256), 256)
        kv = (kv_own, kv_sib)[n]
        s = jnp.dot(k_nat[n, ks, :], q_cat[i], preferred_element_type=f32)
        ok = key_row >= lanes[i, 2:3, :] - first_key
        if causal:
            ok = ok & (key_row <= query_lane)
        p = jnp.exp(jnp.where(ok, s, MASKED) - lanes[i, 0:1, :])
        dp_ = jnp.dot(v_nat[n, ks, :], d_cat[i], preferred_element_type=f32)
        ds = (p * (dp_ - lanes[i, 1:2, :])).astype(bf)
        dv_acc[n, ks, :] += jnp.dot(p.astype(bf), d_nat[i], preferred_element_type=f32)
        dk_acc[n, ks, :] += jnp.dot(ds, q_nat[i], preferred_element_type=f32)
        dq_acc[i] += jnp.dot(kv[0:64, ks], ds, preferred_element_type=f32)

    def hook_0():
        reduce_2()
        reduce_1(1)

    def hook_1():
        out_0()
        reduce_3(0)

    def hook_2():
        reduce_4()

    def hook_3():
        reduce_3(1)
        out_1()

    for i in range(4):

        def cross(j, carry, i=i):
            block(1, i, j, (j * 256).astype(f32), False)
            return carry

        lax.fori_loop(0, 4 * ctx, cross, 0)
        (hook_0, hook_1, hook_2, hook_3)[i]()
    dkv_push = copy_to(dkv_out, dkv_in, dkv_sem.at[0], dkv_sem.at[1], sibling)

    def upright(t, carry):
        at = pl.ds(pl.multiple_of(t * 128, 128), 128)
        dkv_out[0:64, at] = jnp.transpose(dk_acc[1, at, :]).astype(bf)
        dkv_out[64:128, at] = jnp.transpose(dv_acc[1, at, :]).astype(bf)
        return carry

    lax.fori_loop(0, 8, upright, 0)
    dkv_push.start()

    def within(i):
        def full(j, c):
            block(0, i, j, base + (j * 256).astype(f32), False)
            return c

        lax.fori_loop(0, i, full, 0)
        block(0, i, i, base + 256.0 * i, True)

    within(0)
    within(1)
    within(2)
    within(3)
    reduce_5(0)
    reduce_6()
    gain_q = column(q_gain_ref[...])
    gain_k = column(jnp.concatenate([k_gain_ref[...], jnp.zeros((1, 64), f32)], 1))[:64]
    dkv_push.wait()

    def unturn(t, sums):
        at = pl.ds(pl.multiple_of(t * 128, 128), 128)
        i, half = t // 2, t % 2
        parts = [
            dq_acc[i, :, pl.ds(pl.multiple_of(h * 256 + half * 128, 128), 128)] for h in range(2)
        ]
        cos_part, sin_part = table[0, :, at], -table[1, :, at]
        inv = inv_ref[t]
        d_q = turn(jnp.concatenate(parts, 0) * 0.125, cos_part, sin_part)
        came = dkv_in[:, at].astype(f32)
        d_k = turn(jnp.transpose(dk_acc[0, at, :]) + came[0:64], cos_part, sin_part)
        d_v = jnp.transpose(dv_acc[0, at, :]) + came[64:128]
        q_hat, k_hat = raw[t, 0:128] * inv[0:1], raw[t, 128:192] * inv[1:2]
        q_sum, k_sum = sums[0] + d_q * q_hat, sums[1] + d_k * k_hat
        q_term, k_term = d_q * gain_q, d_k * gain_k
        terms[t, 0:128] = q_term
        terms[t, 128:192] = k_term
        dqkv[t, 192:256] = d_v.astype(bf)
        stat[0, pl.ds(t, 1), :] = jnp.sum(q_term * q_hat, 0, keepdims=True)
        stat[1, pl.ds(t, 1), :] = jnp.sum(k_term * k_hat, 0, keepdims=True)
        return q_sum, k_sum

    q_sum, k_sum = lax.fori_loop(
        0, 8, unturn, (jnp.zeros((128, 128), f32), jnp.zeros((64, 128), f32))
    )
    stats[me] = stat[...]

    def s_push(i):
        return copy_to(stats.at[me], stats.at[me], s_send.at[i], s_recv.at[me], side(i))

    def s_arrival(t):
        return copy_to(stats.at[t], stats.at[t], s_send.at[0], s_recv.at[t], sibling)

    for i in range(1, 8):
        s_push(i).start()
    out_2()
    q_row = jnp.sum(jnp.transpose(q_sum), 0, keepdims=True)
    k_row = jnp.sum(jnp.transpose(k_sum), 0, keepdims=True)
    gain_row = jnp.concatenate([q_row, k_row, jnp.zeros((1, 1024 - 192), f32)], 1)
    pack_rows(pl.ds(304, 16), jnp.concatenate([gain_row, jnp.zeros((15, 1024), f32)], 0))
    reduce_5(1)
    for i in range(1, 8):
        s_arrival((me + i) % 8).wait_recv()

    def finish(t, carry):
        at = pl.ds(pl.multiple_of(t * 128, 128), 128)
        inner = []
        for n in range(2):
            part = stats[0, n, pl.ds(t, 1), :]
            for s in range(1, 8):
                part = part + stats[s, n, pl.ds(t, 1), :]
            inner.append(part)
        inv = inv_ref[t]
        q_hat, k_hat = raw[t, 0:128] * inv[0:1], raw[t, 128:192] * inv[1:2]
        d_q = inv[0:1] * (terms[t, 0:128] - q_hat * (inner[0] / 1024.0))
        d_k = inv[1:2] * (terms[t, 128:192] - k_hat * (inner[1] / 512.0))
        dqkv[t, 0:128] = d_q.astype(bf)
        dqkv[t, 128:192] = d_k.astype(bf)
        return carry

    lax.fori_loop(0, 8, finish, 0)

    def o_push(i):
        return copy_to(
            dqkv.at[(me + i) % 8], dqkv_all.at[me], o_send.at[i], o_recv.at[me], side(i)
        )

    def o_arrival(t):
        return copy_to(dqkv_all.at[t], dqkv_all.at[t], o_send.at[0], o_recv.at[t], sibling)

    for i in range(1, 8):
        o_push(i).start()
    dqkv_all[me] = dqkv[me]
    grad_qkv = jnp.zeros((256, 1024), f32)
    for t in range(8):
        grad_qkv = grad_qkv + jnp.dot(dqkv[t], rows1[t], preferred_element_type=f32)
    pack_rows(pl.ds(0, 256), grad_qkv)
    p_push = copy_to(pack.at[1 - ctx], pack_sib, p_sem.at[0], p_sem.at[1], sibling)
    p_push.start()
    reduce_7(0)
    for i in range(1, 8):
        o_arrival((me + i) % 8).wait_recv()
    d_rows1 = dot_tn(dqkv_all[...].reshape(2048, 128), w_all[...].reshape(2048, 1024))
    x = x_ref[...].astype(f32)
    inv_one = lax.rsqrt(jnp.mean(x * x, -1, keepdims=True) + EPS)
    x_hat = x * inv_one
    norm1_part = jnp.sum(d_rows1 * x_hat, 0, keepdims=True)
    n1[me] = jnp.concatenate([norm1_part[:, 128 * t : 128 * t + 128] for t in range(8)], 0)

    def n_push(i):
        return copy_to(n1.at[me], n1.at[me], n_send.at[i], n_recv.at[me], side(i))

    def n_arrival(t):
        return copy_to(n1.at[t], n1.at[t], n_send.at[0], n_recv.at[t], sibling)

    for i in range(1, 8):
        n_push(i).start()
    p_push.wait()
    pack[ctx] = (pack[ctx].astype(f32) + pack_sib[...].astype(f32)).astype(bf)
    out_3()

    def rs_push(i):
        to = (dp + i) % 8
        rows = pack.at[ctx, pl.ds(pl.multiple_of(to * 48, 16), 48)]
        return copy_to(rows, pack_in.at[dp], rs_send.at[i], rs_recv.at[dp], chip(i))

    def rs_arrival(d):
        return copy_to(pack_in.at[d], pack_in.at[d], rs_send.at[0], rs_recv.at[d], sibling)

    for i in range(1, 8):
        rs_push(i).start()
    scaled = d_rows1 * norm1_ref[...]
    grad_x_ref[...] = (
        d_resid[...] + inv_one * (scaled - x_hat * jnp.mean(scaled * x_hat, -1, keepdims=True))
    ).astype(bf)
    reduce_8()
    reduce_7(1)
    for i in range(1, 8):
        n_arrival((me + i) % 8).wait_recv()
    norm1_sum = n1[0]
    for t in range(1, 8):
        norm1_sum = norm1_sum + n1[t]
    n1_chips[dp] = norm1_sum

    def m_push(i):
        return copy_to(n1_chips.at[dp], n1_chips.at[dp], m_send.at[i], m_recv.at[dp], chip(i))

    def m_arrival(d):
        return copy_to(n1_chips.at[d], n1_chips.at[d], m_send.at[0], m_recv.at[d], sibling)

    for i in range(1, 8):
        m_push(i).start()
    pack_in[dp] = pack[ctx, pl.ds(pl.multiple_of(dp * 48, 16), 48), :]
    for i in range(1, 8):
        rs_arrival((dp + i) % 8).wait_recv()
    owned = pack_in[0].astype(f32)
    for d in range(1, 8):
        owned = owned + pack_in[d].astype(f32)
    top = pl.ds(0, 48)
    result[ctx, dp, top] = owned.astype(bf)
    wide = (dp == 5) | (dp == 6)

    def t_push(i):
        return copy_to(result.at[ctx, dp, top], tiny.at[me], t_send.at[i], t_recv.at[me], side(i))

    def t_arrival(t):
        return copy_to(tiny.at[t], tiny.at[t], t_send.at[0], t_recv.at[t], sibling)

    @pl.when(wide)
    def _():
        for i in range(1, 8):
            t_push(i).start()
        tiny[me] = result[ctx, dp, top]
        for i in range(1, 8):
            t_arrival((me + i) % 8).wait_recv()
            t_push(i).wait_send()
        total = tiny[0].astype(f32)
        for t in range(1, 8):
            total = total + tiny[t].astype(f32)
        row = lax.broadcasted_iota(jnp.int32, (48, 512), 0)
        shared = ((dp == 5) & (row >= 16)) | ((dp == 6) & (row < 16))
        result[ctx, dp, top] = jnp.where(shared, total, owned).astype(bf)

    for i in range(1, 8):
        wo_arrival((me + i) % 8).wait_recv()
    total = wo_in[0].astype(f32)
    for t in range(1, 8):
        total = total + wo_in[t].astype(f32)
    result[ctx, dp, pl.ds(48, 16)] = total.astype(bf)


    def g_push(i):
        return copy_to(
            result.at[ctx, dp], result.at[ctx, dp], g_send.at[i], g_recv.at[dp], chip(i)
        )

    def g_arrival(d):
        return copy_to(result.at[ctx, d], result.at[ctx, d], g_send.at[0], g_recv.at[d], sibling)

    def g_relay(d):
        return copy_to(
            result.at[ctx, d], result.at[ctx, d], gs_send.at[d], gs_recv.at[d], sibling
        )

    def g_sib_arrival(d):
        place = result.at[1 - ctx, d]
        return copy_to(place, place, gs_send.at[d], gs_recv.at[d], sibling)

    for i in range(1, 8):
        g_push(i).start()
    g_relay(dp).start()
    for i in range(1, 8):
        m_arrival((dp + i) % 8).wait_recv()
    norm1_sum = n1_chips[0]
    for d in range(1, 8):
        norm1_sum = norm1_sum + n1_chips[d]
    n1_sib[0] = norm1_sum
    ns_push = copy_to(n1_sib.at[0], n1_sib.at[1], ns_sem.at[0], ns_sem.at[1], sibling)
    ns_push.start()

    def pass_on(i, carry):
        d = (dp + i) % 8
        g_arrival(d).wait_recv()
        g_relay(d).start()
        return carry

    lax.fori_loop(1, 8, pass_on, 0)
    ns_push.wait()
    norm1_out_ref[...] = n1_sib[0] + n1_sib[1]
    for d in range(8):
        g_sib_arrival(d).wait_recv()
        g_relay(d).wait_send()
    reduce_9()
    pack_ref[...] = result[...]
    for i in range(1, 8):
        dh_push(i).wait_send()
        s_push(i).wait_send()
        o_push(i).wait_send()
        n_push(i).wait_send()
        rs_push(i).wait_send()
        m_push(i).wait_send()
        g_push(i).wait_send()
    for i in range(1, 8):
        wo_hop(i).wait_send()
    for n, place in enumerate(keep_places):
        keep(n, place).wait()


def backward(small, large):
    bf, f32 = jnp.bfloat16, jnp.float32
    vmem, hbm = pl.BlockSpec(memory_space=pltpu.VMEM), pl.BlockSpec(memory_space=pl.ANY)
    sem = pltpu.SemaphoreType.DMA
    shape = jax.ShapeDtypeStruct
    table = jnp.asarray(rope_constants(2048, 32))
    return pl.pallas_call(
        backward_kernel,
        out_shape=(
            shape((128, 1024), bf),
            shape((8, 128), f32),
            shape((2, 8, 64, 512), bf),
            shape((128, 1024), bf),
            shape((3072, 1024), bf),
        ),
        in_specs=[vmem] * 15 + [hbm] * 11,
        out_specs=(vmem, vmem, vmem, vmem, hbm),
        scratch_shapes=[
            pltpu.VMEM((8, 128, 1024), bf),
            pltpu.VMEM((8, 256, 128), f32),
            pltpu.VMEM((128, 1024), bf),
            pltpu.VMEM((128, 1024), bf),
            pltpu.VMEM((128, 1024), bf),
            pltpu.VMEM((8, 128, 128), bf),
            pltpu.VMEM((8, 128, 1024), bf),
            pltpu.VMEM((8, 256, 1024), bf),
            pltpu.VMEM((2, 32, 1024), f32),
            pltpu.VMEM((8, 1024), f32),
            pltpu.VMEM((128, 1024), f32),
            pltpu.VMEM((8, 128, 128), bf),
            pltpu.VMEM((2, 8, 128, 512), bf),
            pltpu.VMEM((8, 16, 512), bf),
            pltpu.VMEM((8, 128, 128), bf),
            pltpu.VMEM((8, 128, 128), bf),
            pltpu.VMEM((8, 48, 512), bf),
            pltpu.VMEM((4, 64, 512), bf),
            pltpu.VMEM((4, 512, 64), bf),
            pltpu.VMEM((4, 64, 512), bf),
            pltpu.VMEM((4, 512, 64), bf),
            pltpu.VMEM((4, 8, 512), f32),
            pltpu.VMEM((2, 1024, 64), bf),
            pltpu.VMEM((2, 1024, 64), bf),
            pltpu.VMEM((4, 64, 512), f32),
            pltpu.VMEM((2, 1024, 64), f32),
            pltpu.VMEM((2, 1024, 64), f32),
            pltpu.VMEM((128, 1024), bf),
            pltpu.VMEM((128, 1024), bf),
            pltpu.VMEM((8, 192, 128), f32),
            pltpu.VMEM((2, 8, 128), f32),
            pltpu.VMEM((8, 2, 8, 128), f32),
            pltpu.VMEM((8, 256, 128), bf),
            pltpu.VMEM((8, 256, 128), bf),
            pltpu.VMEM((2, 384, 512), bf),
            pltpu.VMEM((384, 512), bf),
            pltpu.VMEM((8, 48, 512), bf),
            pltpu.VMEM((2, 8, 64, 512), bf),
            pltpu.VMEM((8, 8, 128), f32),
            pltpu.VMEM((8, 8, 128), f32),
            pltpu.VMEM((2, 8, 128), f32),
            sem((12,)),
        ]
        + [sem((8,))] * 8
        + [sem((2,))]
        + [sem((8,))] * 2
        + [sem((2,))]
        + [sem((8,))] * 10
        + [sem((2,))]
        + [
            pltpu.VMEM((3072, 1024), bf),
            pltpu.VMEM((3072, 1024), bf),
            pltpu.VMEM((2, 304, 1024), bf),
            pltpu.VMEM((304, 1024), bf),
            pltpu.VMEM((80, 1024), bf),
            pltpu.VMEM((80, 1024), bf),
            pltpu.VMEM((2, 80, 1024), bf),
            sem((46,)),
            sem((46,)),
            pltpu.VMEM((8, 128, 1536), bf),
            pltpu.VMEM((8, 128, 1536), bf),
            pltpu.VMEM((2, 2, 64, 1536), bf),
            pltpu.VMEM((2, 2, 128, 1536), bf),
            pltpu.VMEM((128, 1536), bf),
            sem((4,)),
            sem((9,)),
            sem((9,)),
            sem((17,)),
        ],
        compiler_params=pltpu.CompilerParams(
            collective_id=3, has_side_effects=True, vmem_limit_bytes=56 << 20
        ),
        cost_estimate=pl.CostEstimate(
            flops=10_000_000_000, bytes_accessed=20_000_000, transcendentals=4_000_000
        ),
    )(*small, *large, table)


def finish_kernel(
    reduced_ref,
    out_ref,
    grad_x_ref,
    pack_ref,
    norm1_ref,
    gate_ref,
    up_ref,
    down_ref,
    out_copy_ref,
    grad_x_copy_ref,
    w_q_ref,
    w_k_ref,
    w_v_ref,
    q_gain_ref,
    k_gain_ref,
    w_out_ref,
    norm2_ref,
    router_ref,
    norm1_copy_ref,
    rounded,
    wide,
    load_sem,
    store_sem,
):
    f32 = jnp.float32
    loads = [
        pltpu.make_async_copy(reduced_ref.at[pl.ds(256 * n, 256)], rounded.at[n], load_sem.at[n])
        for n in range(12)
    ]
    passed = [
        pltpu.make_async_copy(out_ref, out_copy_ref, load_sem.at[12]),
        pltpu.make_async_copy(grad_x_ref, grad_x_copy_ref, load_sem.at[13]),
    ]
    for copy in loads + passed:
        copy.start()
    def rows(start, count):
        parts = []
        for c in range(2):
            pieces = []
            for d in range(start // 48, (start + count - 1) // 48 + 1):
                first, last = max(start, 48 * d) - 48 * d, min(start + count, 48 * d + 48) - 48 * d
                pieces.append(pack_ref[c, d, first:last, :])
            parts.append(jnp.concatenate(pieces, 0))
        return jnp.concatenate(parts, 1).astype(f32)

    w_q_ref[...] = jnp.transpose(rows(0, 128))
    w_k_ref[...] = rows(128, 64)
    w_v_ref[...] = rows(192, 64)
    router_ref[...] = rows(256, 32)
    norm2_ref[...] = rows(288, 16)[0:1]
    gains = rows(304, 16)
    q_gain_ref[...] = gains[0:1, 0:128]
    k_gain_ref[...] = gains[0:1, 128:192]
    for d in range(8):
        for c in range(2):
            w_out_ref[16 * d : 16 * d + 16, 512 * c : 512 * c + 512] = pack_ref[c, d, 48:64, :].astype(f32)
    norm1_copy_ref[...] = norm1_ref[...]
    stores = []
    for n in range(12):
        loads[n].wait()
        wide[n] = rounded[n].astype(f32)
        if n < 8:
            rows = pl.ds(256 * (n % 4), 256)
            for m, ref in enumerate((gate_ref, up_ref)):
                src = wide.at[n, :, pl.ds(512 * m, 512)]
                stores.append(pltpu.make_async_copy(src, ref.at[n // 4, rows], store_sem.at[2 * n + m]))
        else:
            rows = pl.ds(256 * (n % 2), 256)
            stores.append(
                pltpu.make_async_copy(wide.at[n], down_ref.at[n // 2 - 4, rows], store_sem.at[n + 8])
            )
        for store in stores[-2:] if n < 8 else stores[-1:]:
            store.start()
    for copy in stores + passed:
        copy.wait()


def finish(reduced, out, grad_x, pack, norm1):
    bf, f32 = jnp.bfloat16, jnp.float32
    vmem, hbm = pl.BlockSpec(memory_space=pltpu.VMEM), pl.BlockSpec(memory_space=pl.ANY)
    shape = jax.ShapeDtypeStruct
    return pl.pallas_call(
        finish_kernel,
        out_shape=(
            shape((2, 1024, 512), f32),
            shape((2, 1024, 512), f32),
            shape((2, 512, 1024), f32),
            shape((128, 1024), bf),
            shape((128, 1024), bf),
            shape((1024, 128), f32),
            shape((64, 1024), f32),
            shape((64, 1024), f32),
            shape((1, 128), f32),
            shape((1, 64), f32),
            shape((128, 1024), f32),
            shape((1, 1024), f32),
            shape((32, 1024), f32),
            shape((8, 128), f32),
        ),
        in_specs=[hbm] + [vmem] * 4,
        out_specs=(hbm,) * 5 + (vmem,) * 9,
        scratch_shapes=[
            pltpu.VMEM((12, 256, 1024), bf),
            pltpu.VMEM((12, 256, 1024), f32),
            pltpu.SemaphoreType.DMA((14,)),
            pltpu.SemaphoreType.DMA((20,)),
        ],
        compiler_params=pltpu.CompilerParams(vmem_limit_bytes=62 << 20),
    )(reduced, out, grad_x, pack, norm1)


def shards(
    hidden_in,
    segment,
    norm1_gain,
    w_query,
    w_key,
    w_value,
    q_gain,
    k_gain,
    w_out,
    norm2_gain,
    router,
    w_gate,
    w_up,
    w_down,
    routes,
    cotangent,
):
    f32, bf = jnp.float32, jnp.bfloat16
    rows2, gates, resid, rows1, raw, inv, q_t, kv, lse, heads, w_out_all, dy_all, w_t, heads_all = attention(
        hidden_in,
        cotangent,
        segment,
        norm1_gain,
        q_gain,
        k_gain,
        norm2_gain,
        router,
        routes,
        w_query,
        w_key,
        w_value,
        w_out,
    )
    d_rows, d_gate, out_part, grads, w_all = moe(
        rows2, gates, dy_all, w_gate, w_up, w_down, w_t
    )
    grad_x, norm1_sum, pack, output, grads = backward(
        (
            hidden_in,
            cotangent,
            d_rows,
            d_gate,
            gates,
            rows2,
            resid,
            router.T,
            norm1_gain.reshape(1, 1024),
            norm2_gain.reshape(1, 1024),
            q_gain.reshape(1, 128),
            k_gain.reshape(1, 64),
            segment.reshape(16, 128),
            inv,
            lse,
        ),
        (rows1, raw, q_t, kv, heads, heads_all, w_out_all, w_all, grads, out_part),
    )
    (
        gate,
        up,
        down,
        output,
        grad_x,
        w_q,
        w_k,
        w_v,
        q_g,
        k_g,
        w_o,
        norm2_sum,
        grad_router,
        norm1_sum,
    ) = finish(grads, output, grad_x, pack, norm1_sum)
    return (
        output,
        grad_x,
        norm1_sum.reshape(1024),
        w_q,
        w_k.T,
        w_v.T,
        q_g.reshape(128),
        k_g.reshape(64),
        w_o,
        norm2_sum.reshape(1024),
        grad_router.T,
        gate,
        up,
        down,
    )


def solution(mesh):
    return jax.shard_map(
        shards,
        mesh=mesh,
        in_specs=(
            P(("dp", "ctx", "tensor"), None),
            P("dp"),
            P(),
            P(None, "tensor"),
            P(None, "tensor"),
            P(None, "tensor"),
            P("tensor"),
            P("tensor"),
            P("tensor", None),
            P(),
            P(),
            P(("dp", "ctx"), None, None),
            P(("dp", "ctx"), None, None),
            P(("dp", "ctx"), None, None),
            P(("dp", "ctx", "tensor"), None),
            P(("dp", "ctx", "tensor"), None),
        ),
        out_specs=(
            P(("dp", "ctx", "tensor"), None),
            P(("dp", "ctx", "tensor"), None),
            P(),
            P(None, "tensor"),
            P(None, "tensor"),
            P(None, "tensor"),
            P("tensor"),
            P("tensor"),
            P("tensor", None),
            P(),
            P(),
            P(("dp", "ctx"), None, None),
            P(("dp", "ctx"), None, None),
            P(("dp", "ctx"), None, None),
        ),
        check_vma=False,
    )
```
